32 devices in a mesh: gx: 4 (over x, core), gy: 4 (over z), gz: 2 (over y).
Axes of the slice: x: 2, y: 2, z: 4, core: 2. Of those that a mesh axis runs over, the one named last changes fastest.
Arguments:
- fields: float32 [4, 32, 128, 256], P(None, 'gx', 'gy', 'gz'), may hold values from -6 to 6
- viscosity: float32 [32, 128, 256], P('gx', 'gy', 'gz'), may hold values from 0.02 to 0.6
- samples: int32 [4, 4, 2, 8], P('gx', 'gy', 'gz'), may hold values from 0 to 511
- trainers: int32 [4, 4, 2, 8, 1], P('gx', 'gy', 'gz'), may hold values from 0 to 3; in each aligned block of 8 rows (0 to 7, 8 to 15, ..., all dimensions but the last counted through in order) at most 2 rows name the same one
- conv_first: bfloat16 [32, 108], replicated, may hold values from -0.625 to 0.625
- conv_second: bfloat16 [32, 864], replicated, may hold values from -0.21875 to 0.21875
- conv_third: bfloat16 [6, 32], replicated, may hold values from -1 to 1
Outputs:
- advanced: float32 [4, 32, 128, 256], P(None, 'gx', 'gy', 'gz')
- block_losses: float32 [4, 4, 2, 8], P('gx', 'gy', 'gz')
- first_grad: float32 [32, 108], replicated
- second_grad: float32 [32, 864], replicated
- third_grad: float32 [6, 32], replicated
The draws below stay inside these ranges and needn't reach their ends.
Inputs may be any that keep to these rules, and one draw needn't show every extreme that they name: `trainers`: among the 8 samples of one device no trainer occurs more than 2 times, and on some device one occurs exactly 2 times.
All inputs are finite; a program needn't handle non-finite values.
Results may differ from the reference program's by a relative error of at most 0.0036.
The reference program's roundings to bfloat16 on the way (of `chosen`, `stack`, `hidden_first`, `hidden_second`, `grad_pred`, `grad_mid` and `grad_entry`) count: a program that leaves them out, or rounds other values in their place, can miss the bound.
Values may be sent and summed in bfloat16 or wider, within the bound.
No kernel may reach another device: no remote copies, remote signals or barrier semaphores. Data moves between devices by JAX's collectives and lax.ppermute only.
A program may use at most 128 MiB of HBM per device.

```python
import math
from functools import reduce
import jax
import jax.numpy as jnp
import numpy as np
from jax import lax

CX = 8
CY = 32
CZ = 128
SAMP = 8
BLK = 4
CAP = 2
NF = 4
NOUT = 6
CH = 32
NX = 32
NY = 128
NZ = 256
NB = 512
SLOTS = 8
WORKERS = 32
N_GX = 4
N_GY = 4
N_GZ = 2


def place_ends(entries, key, smallest, high):
    dims = entries.shape
    index_at = [jax.random.randint(jax.random.fold_in(key, axis), (), 0, dims[axis]) for axis in range(len(dims))]
    entries = entries.at[tuple(index_at)].set(smallest)
    longest = dims.index(max(dims))
    index_at[longest] = (index_at[longest] + 1) % dims[longest]
    return entries.at[tuple(index_at)].set(high)


def levels(key, extent, split, smallest, largest):
    def one(position, parts):
        heights = jax.random.uniform(jax.random.fold_in(jax.random.fold_in(key, 6), position), (parts,), jnp.float32, smallest / len(split), largest / len(split))
        return jnp.repeat(jnp.exp(heights), extent[position] // parts).reshape((-1,) + (1,) * (len(extent) - position - 1))

    gain = one(*split[0])
    for cut in split[1:]:
        gain = gain * one(*cut)
    return gain


def deal_out(own_key, own, number, rows, amount, top, bound, skew):
    order = jax.random.permutation(own_key, amount)
    packed, ordinary = shares(amount, rows * top, bound, skew, True), shares(amount, rows * top, bound, skew, False)
    places = jnp.arange(amount)

    def named(tallies, turn):
        used = int((tallies > 0).sum())
        fixed = max(1, used // 4)
        shifted = fixed + (places - fixed + turn * (used - fixed)) % max(1, amount - fixed)
        return jnp.zeros((amount,), jnp.int32).at[order[jnp.where(places < fixed, places, shifted)]].set(jnp.asarray(tallies, jnp.int32))

    tallies = jnp.where(number % 4 == 0, named(packed, number // 4), named(ordinary, number - number // 4 - 1))
    mixed = jax.random.permutation(jax.random.fold_in(own, 3), amount)
    donor, sink = mixed[0:amount // 2 * 2:2], mixed[1:amount // 2 * 2:2]
    room = jnp.minimum(tallies[donor] - 1, bound - tallies[sink]) // 2
    room = jnp.where((donor == order[0]) | (sink == order[0]) | (tallies[sink] == 0), 0, jnp.maximum(room, 0))
    shifted = jax.random.randint(jax.random.fold_in(own, 4), (amount // 2,), 0, 1 << 20) % (room + 1)
    tallies = tallies.at[donor].add(-shifted).at[sink].add(shifted)
    items = jnp.searchsorted(jnp.cumsum(tallies), jnp.arange(rows * top), side="right").astype(jnp.int32)
    table = items.reshape(top, rows).T
    table = table[jax.random.permutation(jax.random.fold_in(own, 1), rows)]
    turn = jax.random.randint(jax.random.fold_in(own, 2), (rows, 1), 0, top)
    return jnp.take_along_axis(table, (jnp.arange(top)[None, :] + turn) % top, axis=1)


def shares(number_of, total, most, lean, full):
    weights = [(1 << 20) // math.isqrt(standing ** lean) + 1 for standing in range(1, number_of + 1)]
    largest = most if full else min(most, max(-(-total // number_of), total * weights[0] // sum(weights)))
    least = 1 if total - largest >= number_of - 1 else 0
    given, surplus = [largest] + [least] * (number_of - 1), total - largest - least * (number_of - 1)
    while surplus > 0:
        free = [i for i in range(1, number_of) if given[i] < largest] or [i for i in range(1, number_of) if given[i] < most]
        mass, remaining = sum([weights[i] for i in free]), surplus
        for i in free:
            more = min(most - given[i], max(1, remaining * weights[i] // mass), surplus)
            given[i] = given[i] + more
            surplus = surplus - more
    return np.array(given)


def gaussian(stream_key, extent, scale, most, split=(), kind=jnp.bfloat16):
    factor_of = levels(stream_key, extent, split, -0.22, 0.18) if split else 1.0
    values = jax.random.normal(stream_key, extent, jnp.float32) * scale * factor_of
    return jnp.minimum(jnp.maximum(values, -most), most).astype(kind)


def setup_inputs(seed: int = 0) -> dict:
    key_list = jax.random.split(jax.random.key(seed), 8)
    fields = gaussian(key_list[0], (NF, NX, NY, NZ), 1.0, 6.0, ((1, 4), (2, 4), (3, 2)), jnp.float32)
    viscosity = jnp.clip(jnp.exp(math.log(0.6) - 3.4011974 * jax.random.uniform(key_list[1], (NX, NY, NZ), jnp.float32) ** levels(key_list[1], (NX, NY, NZ), ((0, 4), (1, 4), (2, 2)), -0.2, 0.2)), 0.02, 0.6)
    samples = place_ends(jax.random.randint(key_list[2], (N_GX, N_GY, N_GZ, SAMP), 0, NB), jax.random.fold_in(key_list[2], 1), 0, NB - 1).astype(jnp.int32)
    trainers_keys = jax.random.split(jax.random.fold_in(key_list[3], 1), N_GX * N_GY * N_GZ * SAMP // SAMP)
    trainers_turns = jax.random.permutation(jax.random.fold_in(key_list[3], 3), N_GX * N_GY * N_GZ * SAMP // SAMP)
    trainers = jax.vmap(lambda own, number: deal_out(jax.random.fold_in(key_list[3], 2), own, number, SAMP, N_GY, 1, CAP, 2))(trainers_keys, trainers_turns).reshape((N_GX, N_GY, N_GZ, SAMP, 1))
    conv_first = gaussian(key_list[4], (CH, 27 * NF), (27 * NF) ** -0.5, 0.625)
    conv_second = gaussian(key_list[5], (CH, 27 * CH), (27 * CH) ** -0.5, 0.21875)
    conv_third = gaussian(key_list[6], (NOUT, CH), CH ** -0.5, 1.0)
    return dict(fields=fields, viscosity=viscosity, samples=samples, trainers=trainers, conv_first=conv_first, conv_second=conv_second, conv_third=conv_third)


time_step = 0.25
buoyancy = 0.5


def advance(fields, viscosity):
    summed_div = None
    for dimension in range(3):
        ahead = jnp.roll(fields, -1, dimension + 1)
        face_speed = fields[dimension] + ahead[dimension]
        face_visc = viscosity + jnp.roll(viscosity, -1, dimension)
        face_flux = 0.25 * face_speed * (fields + ahead) - 0.5 * face_visc * (ahead - fields)
        diverge = face_flux - jnp.roll(face_flux, 1, dimension + 1)
        summed_div = diverge if summed_div is None else summed_div + diverge
    updated = fields - time_step * summed_div
    return updated.at[2].add(time_step * buoyancy * fields[3])


def shifted_copies(values, block_edge, direction):
    length = values.shape[-1]
    within = jnp.arange(length, dtype=jnp.int32) % (block_edge * block_edge * block_edge)
    coord_x = within // (block_edge * block_edge)
    coord_y = (within // block_edge) % block_edge
    coord_z = within % block_edge
    pieces = []
    for step_x in (-1, 0, 1):
        for step_y in (-1, 0, 1):
            for step_z in (-1, 0, 1):
                move_x = direction * step_x
                move_y = direction * step_y
                move_z = direction * step_z
                inside = ((coord_x + move_x >= 0) & (coord_x + move_x < block_edge)
                          & (coord_y + move_y >= 0) & (coord_y + move_y < block_edge)
                          & (coord_z + move_z >= 0) & (coord_z + move_z < block_edge))
                rolled = jnp.roll(values, -(move_x * block_edge * block_edge + move_y * block_edge + move_z), axis=1)
                pieces.append(jnp.where(inside[None, :], rolled, jnp.zeros_like(rolled)))
    return pieces


def silu_slope(values):
    sigmoid_v = jax.nn.sigmoid(values)
    return sigmoid_v * (1.0 + values * (1.0 - sigmoid_v))


def subgrid_stress(fields, block_edge):
    velocity = fields[:3]
    products = jnp.stack([velocity[0] * velocity[0], velocity[1] * velocity[1], velocity[2] * velocity[2],
                          velocity[0] * velocity[1], velocity[0] * velocity[2], velocity[1] * velocity[2]])
    joined = jnp.concatenate([velocity, products], 0)
    filtered = reduce(jnp.add, shifted_copies(joined, block_edge, 1)) / 27.0
    smooth = filtered[:3]
    return filtered[3:] - jnp.stack([smooth[0] * smooth[0], smooth[1] * smooth[1], smooth[2] * smooth[2],
                                     smooth[0] * smooth[1], smooth[0] * smooth[2], smooth[1] * smooth[2]])


def closure_step(inputs, slot_weight, conv_first, conv_second, conv_third, block_edge):
    volume = block_edge ** 3
    slots_here = inputs.shape[1] // volume
    contract = (((1,), (1,)), ((), ()))
    stack_in = jnp.concatenate(shifted_copies(inputs, block_edge, 1), 0)
    pre_first = jnp.dot(conv_first, stack_in, preferred_element_type=jnp.float32)
    hidden_first = jax.nn.silu(pre_first).astype(jnp.bfloat16)
    stack_mid = jnp.concatenate(shifted_copies(hidden_first, block_edge, 1), 0)
    pre_second = jnp.dot(conv_second, stack_mid, preferred_element_type=jnp.float32)
    hidden_second = jax.nn.silu(pre_second).astype(jnp.bfloat16)
    predicted = jnp.dot(conv_third, hidden_second, preferred_element_type=jnp.float32)
    target = subgrid_stress(inputs.astype(jnp.float32), block_edge)
    misfit = predicted - target
    out_rows = misfit.shape[0]
    shaped = misfit.reshape(out_rows, slots_here, volume)
    losses = jnp.sum(shaped * shaped, axis=(0, 2)) / (out_rows * volume)
    scale_slot = slot_weight * (2.0 / (out_rows * volume))
    grad_pred = (shaped * scale_slot[None, :, None]).reshape(misfit.shape).astype(jnp.bfloat16)
    grad_third = lax.dot_general(grad_pred, hidden_second, contract, preferred_element_type=jnp.float32)
    grad_upper = lax.dot_general(conv_third, grad_pred, (((0,), (0,)), ((), ())), preferred_element_type=jnp.float32)
    grad_mid = (grad_upper * silu_slope(pre_second)).astype(jnp.bfloat16)
    grad_second = lax.dot_general(grad_mid, stack_mid, contract, preferred_element_type=jnp.float32)
    back_stack = jnp.concatenate(shifted_copies(grad_mid, block_edge, -1), 0)
    channels = conv_second.shape[0]
    turned = conv_second.reshape(channels, 27, channels).transpose(2, 1, 0).reshape(channels, 27 * channels)
    grad_lower = jnp.dot(turned, back_stack, preferred_element_type=jnp.float32)
    grad_entry = (grad_lower * silu_slope(pre_first)).astype(jnp.bfloat16)
    grad_first = lax.dot_general(grad_entry, stack_in, contract, preferred_element_type=jnp.float32)
    return losses, (grad_first, grad_second, grad_third)


def reference(fields, viscosity, samples, trainers, conv_first, conv_second, conv_third):
    middle = advance(fields, viscosity)
    advanced = advance(middle, viscosity)
    volume = BLK ** 3
    blocks = advanced.reshape(NF, NX // BLK, BLK, NY // BLK, BLK, NZ // BLK, BLK)
    blocks = blocks.transpose(0, 1, 3, 5, 2, 4, 6).reshape(NF, NX // BLK, NY // BLK, NZ // BLK, volume)
    local_x = CX // BLK
    local_y = CY // BLK
    local_z = CZ // BLK
    pos_x = jnp.arange(N_GX, dtype=jnp.int32).reshape(N_GX, 1, 1, 1)
    pos_y = jnp.arange(N_GY, dtype=jnp.int32).reshape(1, N_GY, 1, 1)
    pos_z = jnp.arange(N_GZ, dtype=jnp.int32).reshape(1, 1, N_GZ, 1)
    block_x = pos_x * local_x + samples // (local_y * local_z)
    block_y = pos_y * local_y + (samples // local_z) % local_y
    block_z = pos_z * local_z + samples % local_z
    chosen = blocks[:, block_x, block_y, block_z].astype(jnp.bfloat16)
    owners = trainers[..., 0]
    owner_hot = (owners[..., None] == jnp.arange(N_GY, dtype=jnp.int32)).astype(jnp.float32)
    load_sums = jnp.sum(owner_hot, axis=(1, 3))
    load_of = jnp.sum(owner_hot * load_sums[:, None, :, None, :], axis=-1)
    sample_share = 1.0 / (WORKERS * jnp.maximum(load_of, 1.0))
    positions = jnp.arange(SAMP, dtype=jnp.int32)
    earlier = (owners[..., :, None] == owners[..., None, :]) & (positions[:, None] < positions[None, :])
    rank_of = jnp.sum(earlier.astype(jnp.int32), axis=-2)
    batched = chosen.reshape(NF, WORKERS, SAMP, volume).transpose(1, 0, 2, 3)
    weights = sample_share.reshape(WORKERS, SAMP)

    def per_device(summed, device_items):
        inputs, weight_here = device_items
        losses, gradients = closure_step(inputs.reshape(NF, SAMP * volume), weight_here,
                                         conv_first, conv_second, conv_third, BLK)
        return jax.tree.map(jnp.add, summed, gradients), losses

    starting = (jnp.zeros((CH, 27 * NF), jnp.float32), jnp.zeros((CH, 27 * CH), jnp.float32),
                jnp.zeros((NOUT, CH), jnp.float32))
    summed, losses = lax.scan(per_device, starting, (batched, weights))
    shape_four = (N_GX, N_GY, N_GZ, SAMP)
    index_x = jnp.broadcast_to(pos_x, shape_four)
    index_y = jnp.broadcast_to(pos_y, shape_four)
    index_z = jnp.broadcast_to(pos_z, shape_four)
    slot_losses = jnp.zeros((N_GX, N_GY, N_GZ, SLOTS), jnp.float32)
    slot_losses = slot_losses.at[index_x, owners, index_z, index_y * CAP + rank_of].set(losses.reshape(shape_four))
    return advanced, slot_losses, summed[0], summed[1], summed[2]
```

```python
import functools

import jax
import jax.numpy as jnp
import numpy as np
from jax import lax
from jax.experimental import pallas as pl
from jax.experimental.pallas import tpu as pltpu
from jax.sharding import PartitionSpec as P

BLK = 4
CAP = 2
NF = 4
VOL = BLK**3
TAPS = [(x, y, z) for x in (-1, 0, 1) for y in (-1, 0, 1) for z in (-1, 0, 1)]
LANES = 128
ROWS = 8
NOUT = 6
CH = 32

time_step = 0.25
buoyancy = 0.5

VMEM = pl.BlockSpec(memory_space=pltpu.VMEM)
SMEM = pl.BlockSpec(memory_space=pltpu.SMEM)
PARAMS = pltpu.CompilerParams(vmem_limit_bytes=24 * 1024 * 1024)
FULL = (((1,), (1,)), ((), ()))


def iota(shape, axis):
    return lax.broadcasted_iota(jnp.int32, shape, axis)


def pair_of(f, x, c, planes, chunks):
    k = (f * planes + x) * chunks + c
    return k // (LANES // 2), 2 * (k % (LANES // 2))


def add_pair(packed, tile, lane):
    moved = pltpu.roll(tile, lane + 1, 1)
    at = iota(tile.shape, 1)
    return jnp.where((at == lane) | (at == lane + 1), moved, packed)


def counts_of(trainers_ref, count):
    at = iota((ROWS, LANES), 1)
    total = jnp.zeros((ROWS, LANES), jnp.float32)
    for j in range(count):
        total = total + jnp.where(at == trainers_ref[0, 0, 0, j, 0], 1.0, 0.0)
    return total


def pack_faces(fields, visc, trainers, x_first, x_last, y_first, y_last, z_both):
    _, planes, rows, _ = fields.shape
    chunks = rows // ROWS
    arrays = [fields.at[f] for f in range(NF)] + [visc]
    packed = [jnp.zeros((ROWS, LANES), jnp.float32) for _ in range(z_both.shape[0])]
    for f, array in enumerate(arrays):
        x_first[f] = array[0]
        x_last[f] = array[planes - 1]
        y_first[f] = array[:, 0, :]
        y_last[f] = array[:, rows - 1, :]
        for x in range(planes):
            for c in range(chunks):
                tile, lane = pair_of(f, x, c, planes, chunks)
                packed[tile] = add_pair(packed[tile], array[x, ROWS * c : ROWS * c + ROWS], lane)
    for tile, value in enumerate(packed):
        z_both[tile] = value
    counts = counts_of(trainers, trainers.shape[3])
    y_first[NF + 1] = counts
    y_last[NF + 1] = counts


def flux(lower, upper, dimension, visc_lower, visc_upper):
    speed = 0.25 * (lower[dimension] + upper[dimension])
    mean_visc = 0.5 * (visc_lower + visc_upper)
    return [speed * (a + b) - mean_visc * (b - a) for a, b in zip(lower, upper)]


def advance(fields, visc, halo, visc_halo, emit):
    _, planes, rows, _ = fields.shape
    chunks = rows // ROWS
    row = iota((ROWS, LANES), 0)
    lane_at = iota((ROWS, LANES), 1)

    def cell(f, x, part):
        return fields[f, x, part, :] if f < NF else visc[x, part, :]

    def face(f, which, *index):
        side = halo[which] if f < NF else visc_halo[which]
        return side[(f,) + index]

    every = range(NF + 1)
    for c in range(chunks):
        part = slice(ROWS * c, ROWS * c + ROWS)
        before = [face(f, "x_prev", part) for f in every]
        here = [cell(f, 0, part) for f in every]
        flux_lower = flux(before[:NF], here[:NF], 0, before[NF], here[NF])
        for x in range(planes):
            if x + 1 < planes:
                after = [cell(f, x + 1, part) for f in every]
            else:
                after = [face(f, "x_next", part) for f in every]
            flux_upper = flux(here[:NF], after[:NF], 0, here[NF], after[NF])
            total = [b - a for a, b in zip(flux_lower, flux_upper)]
            flux_lower = flux_upper
            below, above = [], []
            for f in every:
                if c > 0:
                    edge = cell(f, x, slice(ROWS * c - 1, ROWS * c))
                else:
                    edge = face(f, "y_prev", slice(x, x + 1))
                below.append(jnp.where(row == 0, edge, pltpu.roll(here[f], 1, 0)))
                if c + 1 < chunks:
                    edge = cell(f, x, slice(ROWS * c + ROWS, ROWS * c + ROWS + 1))
                else:
                    edge = face(f, "y_next", slice(x, x + 1))
                above.append(jnp.where(row == ROWS - 1, edge, pltpu.roll(here[f], ROWS - 1, 0)))
            lower = flux(below[:NF], here[:NF], 1, below[NF], here[NF])
            upper = flux(here[:NF], above[:NF], 1, here[NF], above[NF])
            total = [t + (b - a) for t, a, b in zip(total, lower, upper)]
            left, right = [], []
            for f in every:
                tile, lane = pair_of(f, x, c, planes, chunks)
                both = pltpu.roll(face(f, "z_both", tile), LANES - 1 - lane, 1)
                left.append(pltpu.roll(jnp.where(lane_at == LANES - 1, both, here[f]), 1, 1))
                right.append(pltpu.roll(jnp.where(lane_at == 0, both, here[f]), LANES - 1, 1))
            lower = flux(left[:NF], here[:NF], 2, left[NF], here[NF])
            upper = flux(here[:NF], right[:NF], 2, here[NF], right[NF])
            total = [t + (b - a) for t, a, b in zip(total, lower, upper)]
            updated = [q - time_step * t for q, t in zip(here[:NF], total)]
            updated[2] = updated[2] + (time_step * buoyancy) * here[3]
            emit(x, c, updated)
            here = after


class Side:
    def __init__(self, ref):
        self.ref = ref

    def __getitem__(self, index):
        return self.ref[index[1]]


def halo_of(x_prev, x_next, y_prev, y_next, z_both):
    return dict(x_prev=x_prev, x_next=x_next, y_prev=y_prev, y_next=y_next, z_both=Side(z_both))


def first_step(fields, visc, x_prev, x_next, y_prev, y_next, z_other,
               middle, x_first, x_last, y_first, y_last, z_both):
    _, planes, rows, _ = fields.shape
    chunks = rows // ROWS
    halo = halo_of(x_prev, x_next, y_prev, y_next, z_other)
    packed = [jnp.zeros((ROWS, LANES), jnp.float32) for _ in range(z_both.shape[0])]

    def emit(x, c, tiles):
        for f, tile in enumerate(tiles):
            middle[f, x, ROWS * c : ROWS * c + ROWS, :] = tile
            if x == 0:
                x_first[f, ROWS * c : ROWS * c + ROWS, :] = tile
            if x == planes - 1:
                x_last[f, ROWS * c : ROWS * c + ROWS, :] = tile
            if c == 0:
                y_first[f, x : x + 1, :] = tile[:1]
            if c == chunks - 1:
                y_last[f, x : x + 1, :] = tile[ROWS - 1 :]
            at, lane = pair_of(f, x, c, planes, chunks)
            packed[at] = add_pair(packed[at], tile, lane)

    advance(fields, visc, halo, halo, emit)
    for at, value in enumerate(packed):
        z_both[at] = value
    y_last[NF] = y_prev[NF + 1]


def inside_masks():
    at = iota((1, LANES), 1) % VOL
    coords = (at // (BLK * BLK), at // BLK % BLK, at % BLK)
    along = []
    for coord in coords:
        along.append({
            -1: jnp.where(coord > 0, 1.0, 0.0),
            0: jnp.ones((1, LANES), jnp.float32),
            1: jnp.where(coord < BLK - 1, 1.0, 0.0),
        })
    return along


def move_of(tap):
    return tap[0] * BLK * BLK + tap[1] * BLK + tap[2]


def shifted(tile, tap, along):
    move = move_of(tap)
    if move == 0:
        return tile
    mask = along[0][tap[0]] * along[1][tap[1]] * along[2][tap[2]]
    return pltpu.roll(tile, (-move) % LANES, 1) * mask


def box(tile, along):
    for dimension, step in enumerate((BLK * BLK, BLK, 1)):
        ahead = pltpu.roll(tile, LANES - step, 1) * along[dimension][1]
        behind = pltpu.roll(tile, step, 1) * along[dimension][-1]
        tile = (behind + tile) + ahead
    return tile / 27.0


def sigmoid(values):
    return 1.0 / (1.0 + jnp.exp(-values))


def pick_blocks(advanced, samples, pick, count):
    _, _, rows, lanes = advanced.shape
    along_y, along_z = rows // BLK, lanes // BLK
    row = iota((ROWS, LANES), 0)
    lane_at = iota((ROWS, LANES), 1)
    out = []
    for j in range(0, count, 2):
        parts = [jnp.zeros((ROWS, LANES), jnp.float32) for _ in range(NF)]
        uppers = []
        for half in range(2):
            block = samples[0, 0, 0, j + half]
            block_x = block // (along_y * along_z)
            block_y = block // along_z % along_y
            block_z = block % along_z
            uppers.append(block_y % 2)
            start = pl.multiple_of(block_y // 2 * ROWS, ROWS)
            for x in range(BLK):
                turn = lax.rem(VOL * half + BLK * BLK * x - BLK * block_z + LANES, LANES)
                wanted = lane_at // BLK == (VOL * half + BLK * BLK * x) // BLK
                for f in range(NF):
                    tile = advanced[f, block_x * BLK + x, pl.ds(start, ROWS), :]
                    parts[f] = jnp.where(wanted, pltpu.roll(tile, turn, 1), parts[f])
        upper = jnp.where(lane_at < VOL, uppers[0], uppers[1])
        valid = row // BLK == upper
        for f in range(NF):
            for bit in (1, 2):
                moved = pltpu.roll(parts[f], BLK * bit, 1)
                parts[f] = jnp.where(row // bit % 2 == 1, moved, parts[f])
            parts[f] = jnp.where(valid, parts[f], 0.0)
        stacked = jnp.concatenate(parts, 0).astype(jnp.bfloat16)
        out.append(jnp.dot(pick, stacked, preferred_element_type=jnp.float32))
    return out


def closure(advanced, samples, trainers, counts, pick, w_first, w_second, w_second_t, w_third,
            w_third_t, devices_all, stack_first, stack_mid, send, slots, inline, place):
    count = samples.shape[3]
    pairs = count // 2
    cols = [slice(LANES * m, LANES * m + LANES) for m in range(pairs)]
    along = inside_masks()
    lane_at = iota((ROWS, LANES), 1)
    row = iota((ROWS, LANES), 0)

    picked = pick_blocks(advanced, samples, pick, count)
    values = [p[:ROWS] for p in picked]
    targets = []
    for p in picked:
        first, second = p[ROWS : 2 * ROWS], p[2 * ROWS : 3 * ROWS]
        targets.append(box(first * second, along) - box(first, along) * box(second, along))

    for m, tile in enumerate(values):
        for t in range(0, 28, 2):
            piece = shifted(tile, TAPS[t], along)
            later = shifted(tile, TAPS[t + 1], along) if t + 1 < 27 else jnp.zeros_like(tile)
            stack_first[BLK * t : BLK * t + ROWS, cols[m]] = jnp.where(row < NF, piece, later)
    stack_in = stack_first[...].astype(jnp.bfloat16)
    pre_first = jnp.dot(w_first, stack_in, preferred_element_type=jnp.float32)
    gate_first = sigmoid(pre_first)
    hidden_first = (pre_first * gate_first).astype(jnp.bfloat16).astype(jnp.float32)
    for m in range(pairs):
        tile = hidden_first[:, cols[m]]
        for k, tap in enumerate(TAPS):
            stack_mid[CH * k : CH * k + CH, cols[m]] = shifted(tile, tap, along).astype(jnp.bfloat16)
    pre_second = jnp.dot(w_second, stack_mid[...], preferred_element_type=jnp.float32)
    gate_second = sigmoid(pre_second)
    hidden_second = (pre_second * gate_second).astype(jnp.bfloat16)
    predicted = jnp.dot(w_third, hidden_second, preferred_element_type=jnp.float32)

    misfit = predicted[:ROWS] - jnp.concatenate(targets, 1)
    square = jnp.sum(misfit * misfit, axis=0, keepdims=True)
    sample_at = iota((ROWS, count * VOL), 1) // VOL
    mine = sample_at == iota((ROWS, count * VOL), 0)
    losses = jnp.sum(jnp.where(mine, square, 0.0), axis=1, keepdims=True) / (NOUT * VOL)
    owner = jnp.zeros((ROWS, LANES), jnp.int32)
    for j in range(count):
        owner = jnp.where(row == j, trainers[0, 0, 0, j, 0], owner)
    load = jnp.sum(jnp.where(lane_at == owner, counts, 0.0), axis=1, keepdims=True)
    share = 1.0 / (devices_all * jnp.maximum(load, 1.0))
    scale = share * (2.0 / (NOUT * VOL))
    scale_at = jnp.sum(jnp.where(mine, scale, 0.0), axis=0, keepdims=True)
    grad_pred = (misfit * scale_at).astype(jnp.bfloat16)
    grad_pred = jnp.concatenate([grad_pred, jnp.zeros_like(grad_pred)], 0)

    upper = jnp.dot(w_third_t, grad_pred, preferred_element_type=jnp.float32)
    slope = gate_second * (1.0 + pre_second * (1.0 - gate_second))
    grad_mid = (upper * slope).astype(jnp.bfloat16)
    grad_second = lax.dot_general(grad_mid, stack_mid[...], FULL, preferred_element_type=jnp.float32)
    third = jnp.concatenate([grad_pred, jnp.zeros((LANES - 16, count * VOL), jnp.bfloat16)], 0)
    grad_third = lax.dot_general(hidden_second, third, FULL, preferred_element_type=jnp.float32)

    grad_wide = grad_mid.astype(jnp.float32)
    for m in range(pairs):
        tile = grad_wide[:, cols[m]]
        for k, tap in enumerate(TAPS):
            back = shifted(tile, tuple(-o for o in tap), along)
            stack_mid[CH * k : CH * k + CH, cols[m]] = back.astype(jnp.bfloat16)
    lower = jnp.dot(w_second_t, stack_mid[...], preferred_element_type=jnp.float32)
    slope = gate_first * (1.0 + pre_first * (1.0 - gate_first))
    grad_entry = (lower * slope).astype(jnp.bfloat16)
    grad_first = lax.dot_general(grad_entry, stack_in, FULL, preferred_element_type=jnp.float32)

    whole = CH * 27 // LANES
    rest = CH * 27 - whole * LANES
    for t in range(whole):
        send[:, t, :] = grad_second[:, LANES * t : LANES * t + LANES]
    mixed = jnp.concatenate([grad_second[:, whole * LANES :], jnp.zeros((CH, LANES - rest), jnp.float32)], 1)
    mixed = mixed + pltpu.roll(grad_third, rest, 1)
    tail = LANES - grad_first.shape[1]
    send[:, whole + 1, :] = jnp.concatenate([grad_first, jnp.zeros((CH, tail), jnp.float32)], 1)

    pos_x, pos_y, pos_z, count_y, count_z = place
    offset = rest + ROWS if inline else 0
    height = CH if inline else slots.shape[0]
    slot_rows = iota((height, LANES), 0)
    slot_lanes = iota((height, LANES), 1)
    placed = jnp.zeros((height, LANES), jnp.float32)
    for j in range(count):
        name = trainers[0, 0, 0, j, 0]
        rank = jnp.int32(0)
        for i in range(j):
            rank = rank + jnp.where(trainers[0, 0, 0, i, 0] == name, 1, 0)
        target = (pos_x * count_y + name) * count_z + pos_z
        slot = offset + pos_y * CAP + rank
        hit = (slot_rows == target) & (slot_lanes == slot)
        placed = jnp.where(hit, losses[j : j + 1, :], placed)
    if inline:
        mixed = mixed + placed
    else:
        slots[:, 0, :] = placed
    send[:, whole, :] = mixed


def second_step(sizes, inline, samples, trainers, middle, visc, vx_prev, vx_next, vy_prev, vy_next,
                vz_other, x_prev, x_next, y_prev, y_next, z_other, counts, pick, w_first, w_second,
                w_second_t, w_third, w_third_t, advanced, send, *rest):
    slots = None if inline else rest[0]
    stack_first, stack_mid = rest[-2:]
    halo = halo_of(x_prev, x_next, y_prev, y_next, z_other)
    visc_halo = halo_of(vx_prev, vx_next, vy_prev, vy_next, vz_other)

    def emit(x, c, tiles):
        for f, tile in enumerate(tiles):
            advanced[f, x, ROWS * c : ROWS * c + ROWS, :] = tile

    advance(middle, visc, halo, visc_halo, emit)
    if sizes["gy"] == 4:
        total = counts_of(trainers, trainers.shape[3]) + vy_prev[NF + 1] + vy_next[NF + 1] + y_prev[NF]
    else:
        total = counts[...]
    place = (lax.axis_index("gx"), lax.axis_index("gy"), lax.axis_index("gz"), sizes["gy"], sizes["gz"])
    closure(advanced, samples, trainers, total, pick[...], w_first[...], w_second[...],
            w_second_t[...], w_third[...], w_third_t[...],
            float(sizes["gx"] * sizes["gy"] * sizes["gz"]), stack_first, stack_mid, send, slots,
            inline, place)


def add_up(arrived, spread, own):
    total = jnp.sum(arrived[...], axis=0)
    own[...] = total
    for i in range(spread.shape[0]):
        spread[i] = total


def unpack(gathered, first, second, third):
    whole = second.shape[1] // LANES
    rest = second.shape[1] - whole * LANES
    for t in range(whole):
        second[:, LANES * t : LANES * t + LANES] = gathered[:, t, :]
    mixed = gathered[:, whole, :]
    second[:, LANES * whole :] = mixed[:, :rest]
    third[...] = mixed[:, rest : rest + ROWS].T[:NOUT]
    first[...] = gathered[:, whole + 1, :][:, : first.shape[1]]


def pick_rows():
    wanted = [0, 1, 2, 3, 0, 1, 2, 3, 0, 1, 2, 0, 0, 1, -1, -1, 0, 1, 2, 1, 2, 2, -1, -1]
    table = np.zeros((32, NF * ROWS), np.float32)
    for i, f in enumerate(wanted):
        if f >= 0:
            table[i, f * ROWS : f * ROWS + ROWS] = 1.0
    return table


def shape_of(*dims, dtype=jnp.float32):
    return jax.ShapeDtypeStruct(dims, dtype)


def exchange(x_first, x_last, y_first, y_last, z_both, sizes):
    def ring(axis, step):
        count = sizes[axis]
        return [(i, (i + step) % count) for i in range(count)]

    x_prev = lax.ppermute(x_last, "gx", ring("gx", 1))
    x_next = lax.ppermute(x_first, "gx", ring("gx", -1))
    y_prev = lax.ppermute(y_last, "gy", ring("gy", 1))
    y_next = lax.ppermute(y_first, "gy", ring("gy", -1))
    z_other = lax.ppermute(z_both, "gz", ring("gz", 1))
    return x_prev, x_next, y_prev, y_next, z_other


def on_device(sizes, fields, visc, samples, trainers, conv_first, conv_second, conv_third):
    _, planes, rows, lanes = fields.shape
    axes = ("gx", "gy", "gz")
    devices_all = sizes["gx"] * sizes["gy"] * sizes["gz"]
    pairs = planes * rows // ROWS
    half = LANES // 2

    faces = pl.pallas_call(
        pack_faces,
        out_shape=[
            shape_of(NF + 1, rows, lanes),
            shape_of(NF + 1, rows, lanes),
            shape_of(NF + 2, planes, lanes),
            shape_of(NF + 2, planes, lanes),
            shape_of(-(-(NF + 1) * pairs // half), ROWS, LANES),
        ],
        in_specs=[VMEM, VMEM, SMEM],
        out_specs=[VMEM] * 5,
        compiler_params=PARAMS,
        name="pack_faces",
    )(fields, visc, trainers)
    halo = exchange(*faces, sizes)

    if sizes["gy"] == 4:
        counts = jnp.zeros((1, LANES), jnp.float32)
    else:
        named = trainers.reshape(-1, 1) == jnp.arange(LANES, dtype=jnp.int32)[None, :]
        counts = lax.psum(jnp.sum(named.astype(jnp.float32), axis=0, keepdims=True), "gy")
    counts = jnp.broadcast_to(counts, (ROWS, LANES))
    w_first = jnp.pad(conv_first, ((0, 0), (0, 28 * NF - conv_first.shape[1])))
    w_second_t = conv_second.reshape(CH, 27, CH).transpose(2, 1, 0).reshape(CH, 27 * CH)
    w_third = jnp.pad(conv_third, ((0, 16 - NOUT), (0, 0)))
    w_third_t = w_third.T

    middle, *faces = pl.pallas_call(
        first_step,
        out_shape=[
            shape_of(*fields.shape),
            shape_of(NF, rows, lanes),
            shape_of(NF, rows, lanes),
            shape_of(NF, planes, lanes),
            shape_of(NF + 1, planes, lanes),
            shape_of(-(-NF * pairs // half), ROWS, LANES),
        ],
        in_specs=[VMEM] * 7,
        out_specs=[VMEM] * 6,
        compiler_params=PARAMS,
        name="first_step",
    )(fields, visc, *halo)
    later = exchange(*faces, sizes)

    count = samples.shape[3]
    slot_total = sizes["gy"] * CAP
    tiles = -(-27 * CH // LANES) + 1
    parts = devices_all // CH
    inline = parts == 1 and slot_total <= 24
    out_shape = [shape_of(*fields.shape), shape_of(CH, tiles, LANES)]
    if not inline:
        out_shape.append(shape_of(devices_all, 1, LANES))
    advanced, send, *slots = pl.pallas_call(
        functools.partial(second_step, sizes, inline),
        out_shape=out_shape,
        in_specs=[SMEM] * 2 + [VMEM] * 19,
        out_specs=[VMEM] * len(out_shape),
        scratch_shapes=[
            pltpu.VMEM((28 * NF, count * VOL), jnp.float32),
            pltpu.VMEM((27 * CH, count * VOL), jnp.bfloat16),
        ],
        compiler_params=PARAMS,
        name="second_step",
    )(samples, trainers, middle, visc, *halo, *later, counts, jnp.asarray(pick_rows(), jnp.bfloat16),
      w_first, conv_second, w_second_t, w_third, w_third_t)

    if not inline:
        send = jnp.concatenate([send.reshape(devices_all, tiles // parts, LANES), slots[0]], 1)
    arrived = lax.all_to_all(send, axes, split_axis=0, concat_axis=0, tiled=True)
    spread, own = pl.pallas_call(
        add_up,
        out_shape=[shape_of(*send.shape), shape_of(*send.shape[1:])],
        in_specs=[VMEM],
        out_specs=[VMEM] * 2,
        compiler_params=PARAMS,
        name="add_up",
    )(arrived)
    if inline:
        offset = 27 * CH % LANES + ROWS
        block_losses = own[27 * CH // LANES, offset : offset + slot_total]
    else:
        block_losses = own[-1, :slot_total]
        spread = spread[:, :-1, :]
    gathered = lax.all_to_all(spread, axes, split_axis=0, concat_axis=0, tiled=True)
    first, second, third = pl.pallas_call(
        unpack,
        out_shape=[shape_of(*conv_first.shape), shape_of(*conv_second.shape), shape_of(*conv_third.shape)],
        in_specs=[VMEM],
        out_specs=[VMEM] * 3,
        compiler_params=PARAMS,
        name="unpack",
    )(gathered.reshape(CH, tiles, LANES))
    return advanced, block_losses.reshape(1, 1, 1, slot_total), first, second, third


def solution(mesh):
    sizes = dict(mesh.shape)
    in_specs = (
        P(None, "gx", "gy", "gz"),
        P("gx", "gy", "gz"),
        P("gx", "gy", "gz", None),
        P("gx", "gy", "gz", None, None),
        P(),
        P(),
        P(),
    )
    out_specs = (P(None, "gx", "gy", "gz"), P("gx", "gy", "gz", None), P(), P(), P())
    return jax.shard_map(
        functools.partial(on_device, sizes), mesh=mesh, in_specs=in_specs, out_specs=out_specs,
        check_vma=False,
    )
```

```python
import functools

import jax
import jax.numpy as jnp
import numpy as np
from jax import lax
from jax.experimental import pallas as pl
from jax.experimental.pallas import tpu as pltpu
from jax.sharding import PartitionSpec as P

BLK = 4
CAP = 2
NF = 4
VOL = BLK**3
TAPS = [(x, y, z) for x in (-1, 0, 1) for y in (-1, 0, 1) for z in (-1, 0, 1)]
LANES = 128
ROWS = 8
NOUT = 6
CH = 32

time_step = 0.25
buoyancy = 0.5

VMEM = pl.BlockSpec(memory_space=pltpu.VMEM)
SMEM = pl.BlockSpec(memory_space=pltpu.SMEM)
HBM = pl.BlockSpec(memory_space=pltpu.HBM)
PARAMS = pltpu.CompilerParams(vmem_limit_bytes=24 * 1024 * 1024)
PACK = pltpu.CompilerParams(vmem_limit_bytes=60 * 1024 * 1024)
FULL = (((1,), (1,)), ((), ()))


def iota(shape, axis):
    return lax.broadcasted_iota(jnp.int32, shape, axis)


def pair_of(f, c, planes, chunks):
    k = (c * NF + f) * planes if f < NF else (NF * chunks + c) * planes
    return k // (LANES // 2), 2 * (k % (LANES // 2))


def add_pair(packed, tile, lane):
    moved = pltpu.roll(tile, lane + 1, 1)
    at = iota(tile.shape, 1)
    return jnp.where((at == lane) | (at == lane + 1), moved, packed)


def counts_of(trainers_ref, count):
    at = iota((ROWS, LANES), 1)
    total = jnp.zeros((ROWS, LANES), jnp.float32)
    for j in range(count):
        total = total + jnp.where(at == trainers_ref[j], 1.0, 0.0)
    return total


def pack_faces(fields_far, visc_far, trainers, x_first, x_last, y_first, y_last, z_both, fields, visc, sems):
    _, planes, rows, _ = fields.shape
    chunks = rows // ROWS
    copies = [pltpu.make_async_copy(fields_far.at[f], fields.at[f], sems.at[f]) for f in range(NF)]
    copies.append(pltpu.make_async_copy(visc_far, visc, sems.at[NF]))
    for copy in copies:
        copy.start()
    counts = counts_of(trainers, trainers.shape[0])
    y_first[NF + 1] = counts
    y_last[NF + 1] = counts
    arrays = [fields.at[f] for f in range(NF)] + [visc]
    packed = [jnp.zeros((ROWS, LANES), jnp.float32) for _ in range(z_both.shape[0])]
    for f, array in enumerate(arrays):
        copies[f].wait()
        x_first[f] = array[0]
        x_last[f] = array[planes - 1]
        y_first[f] = array[:, 0, :]
        y_last[f] = array[:, rows - 1, :]
        for c in range(chunks):
            tile, lane = pair_of(f, c, planes, chunks)
            for x in range(planes):
                cells = array[x, ROWS * c : ROWS * c + ROWS]
                packed[tile] = add_pair(packed[tile], cells, lane + 2 * x)
    for tile, value in enumerate(packed):
        z_both[tile] = value


def flux(lower, upper, dimension, visc_lower, visc_upper):
    speed = 0.25 * (lower[dimension] + upper[dimension])
    mean_visc = 0.5 * (visc_lower + visc_upper)
    return [speed * (a + b) - mean_visc * (b - a) for a, b in zip(lower, upper)]


def advance(fields, visc, halo, visc_halo, emit, state):
    _, planes, rows, _ = fields.shape
    chunks = rows // ROWS
    row = iota((ROWS, LANES), 0)
    lane_at = iota((ROWS, LANES), 1)
    parts = [slice(ROWS * c, ROWS * c + ROWS) for c in range(chunks)]
    every = range(NF + 1)

    def cell(f, x, part):
        return fields[f, x, part, :] if f < NF else visc[x, part, :]

    def face(f, which, *index):
        side = halo[which] if f < NF else visc_halo[which]
        return side[(f,) + index]

    def plane(x, carry):
        lowers, state = carry
        uppers = []
        last = x == planes - 1
        beyond = jnp.minimum(x + 1, planes - 1)
        for c, part in enumerate(parts):
            here = [cell(f, x, part) for f in every]
            after = [jnp.where(last, face(f, "x_next", part), cell(f, beyond, part)) for f in every]
            upper = flux(here[:NF], after[:NF], 0, here[NF], after[NF])
            total = [b - a for a, b in zip(lowers[c], upper)]
            uppers.append(upper)
            below, above = [], []
            for f in every:
                if c > 0:
                    edge = cell(f, x, slice(ROWS * c - 1, ROWS * c))
                else:
                    edge = face(f, "y_prev", pl.ds(x, 1))
                below.append(jnp.where(row == 0, edge, pltpu.roll(here[f], 1, 0)))
                if c + 1 < chunks:
                    edge = cell(f, x, slice(ROWS * c + ROWS, ROWS * c + ROWS + 1))
                else:
                    edge = face(f, "y_next", pl.ds(x, 1))
                above.append(jnp.where(row == ROWS - 1, edge, pltpu.roll(here[f], ROWS - 1, 0)))
            lower = flux(below[:NF], here[:NF], 1, below[NF], here[NF])
            upper = flux(here[:NF], above[:NF], 1, here[NF], above[NF])
            total = [t + (b - a) for t, a, b in zip(total, lower, upper)]
            left, right = [], []
            for f in every:
                tile, lane = pair_of(f, c, planes, chunks)
                both = pltpu.roll(face(f, "z_both", tile), LANES - 1 - lane - 2 * x, 1)
                left.append(pltpu.roll(jnp.where(lane_at == LANES - 1, both, here[f]), 1, 1))
                right.append(pltpu.roll(jnp.where(lane_at == 0, both, here[f]), LANES - 1, 1))
            lower = flux(left[:NF], here[:NF], 2, left[NF], here[NF])
            upper = flux(here[:NF], right[:NF], 2, here[NF], right[NF])
            total = [t + (b - a) for t, a, b in zip(total, lower, upper)]
            updated = [q - time_step * t for q, t in zip(here[:NF], total)]
            updated[2] = updated[2] + (time_step * buoyancy) * here[3]
            state = emit(x, c, updated, state)
        return uppers, state

    lowers = []
    for part in parts:
        before = [face(f, "x_prev", part) for f in every]
        here = [cell(f, 0, part) for f in every]
        lowers.append(flux(before[:NF], here[:NF], 0, before[NF], here[NF]))
    return lax.fori_loop(0, planes, plane, (lowers, state))[1]


class Side:
    def __init__(self, ref):
        self.ref = ref

    def __getitem__(self, index):
        return self.ref[index[1]]


def halo_of(x_prev, x_next, y_prev, y_next, z_both):
    return dict(x_prev=x_prev, x_next=x_next, y_prev=y_prev, y_next=y_next, z_both=Side(z_both))


def first_step(fields, visc, x_prev, x_next, y_prev, y_next, z_other,
               middle, x_first, x_last, y_first, y_last, z_both):
    _, planes, rows, _ = fields.shape
    chunks = rows // ROWS
    halo = halo_of(x_prev, x_next, y_prev, y_next, z_other)
    packed = [jnp.zeros((ROWS, LANES), jnp.float32) for _ in range(z_both.shape[0])]

    def emit(x, c, tiles, packed):
        packed = list(packed)
        for f, tile in enumerate(tiles):
            middle[f, x, ROWS * c : ROWS * c + ROWS, :] = tile
            at, lane = pair_of(f, c, planes, chunks)
            packed[at] = add_pair(packed[at], tile, lane + 2 * x)
        return packed

    packed = advance(fields, visc, halo, halo, emit, packed)
    for at, value in enumerate(packed):
        z_both[at] = value
    x_first[...] = middle[:, 0]
    x_last[...] = middle[:, planes - 1]
    for f in range(NF):
        y_first[f] = middle[f, :, 0, :]
        y_last[f] = middle[f, :, rows - 1, :]
    y_last[NF] = y_prev[NF + 1]


def inside_masks():
    at = iota((1, LANES), 1) % VOL
    coords = (at // (BLK * BLK), at // BLK % BLK, at % BLK)
    along = []
    for coord in coords:
        along.append({
            -1: jnp.where(coord > 0, 1.0, 0.0),
            0: jnp.ones((1, LANES), jnp.float32),
            1: jnp.where(coord < BLK - 1, 1.0, 0.0),
        })
    return along


def move_of(tap):
    return tap[0] * BLK * BLK + tap[1] * BLK + tap[2]


def shifted(tile, tap, along):
    move = move_of(tap)
    if move == 0:
        return tile
    mask = along[0][tap[0]] * along[1][tap[1]] * along[2][tap[2]]
    return pltpu.roll(tile, (-move) % LANES, 1) * mask


def box(tile, along):
    for dimension, step in enumerate((BLK * BLK, BLK, 1)):
        ahead = pltpu.roll(tile, LANES - step, 1) * along[dimension][1]
        behind = pltpu.roll(tile, step, 1) * along[dimension][-1]
        tile = (behind + tile) + ahead
    return tile / 27.0


def sigmoid(values):
    return 1.0 / (1.0 + jnp.exp(-values))


def pick_blocks(advanced, samples, pick, count):
    _, _, rows, lanes = advanced.shape
    along_y, along_z = rows // BLK, lanes // BLK
    row = iota((ROWS, LANES), 0)
    lane_at = iota((ROWS, LANES), 1)
    out = []
    for j in range(0, count, 2):
        parts = [jnp.zeros((ROWS, LANES), jnp.float32) for _ in range(NF)]
        uppers = []
        for half in range(2):
            block = samples[j + half]
            block_x = block // (along_y * along_z)
            block_y = block // along_z % along_y
            block_z = block % along_z
            uppers.append(block_y % 2)
            start = pl.multiple_of(block_y // 2 * ROWS, ROWS)
            for x in range(BLK):
                turn = lax.rem(VOL * half + BLK * BLK * x - BLK * block_z + LANES, LANES)
                wanted = lane_at // BLK == (VOL * half + BLK * BLK * x) // BLK
                for f in range(NF):
                    tile = advanced[f, block_x * BLK + x, pl.ds(start, ROWS), :]
                    parts[f] = jnp.where(wanted, pltpu.roll(tile, turn, 1), parts[f])
        upper = jnp.where(lane_at < VOL, uppers[0], uppers[1])
        valid = row // BLK == upper
        for f in range(NF):
            for bit in (1, 2):
                moved = pltpu.roll(parts[f], BLK * bit, 1)
                parts[f] = jnp.where(row // bit % 2 == 1, moved, parts[f])
            parts[f] = jnp.where(valid, parts[f], 0.0)
        stacked = jnp.concatenate(parts, 0).astype(jnp.bfloat16)
        out.append(jnp.dot(pick, stacked, preferred_element_type=jnp.float32))
    return out


def closure(advanced, samples, trainers, counts, pick, w_first, w_second, w_second_t, w_third,
            w_third_t, devices_all, stack_first, stack_mid, send, slots, inline, place):
    count = samples.shape[0]
    pairs = count // 2
    cols = [slice(LANES * m, LANES * m + LANES) for m in range(pairs)]
    along = inside_masks()
    lane_at = iota((ROWS, LANES), 1)
    row = iota((ROWS, LANES), 0)

    picked = pick_blocks(advanced, samples, pick, count)
    values = [p[:ROWS] for p in picked]
    targets = []
    for p in picked:
        first, second = p[ROWS : 2 * ROWS], p[2 * ROWS : 3 * ROWS]
        targets.append(box(first * second, along) - box(first, along) * box(second, along))

    for m, tile in enumerate(values):
        for t in range(0, 28, 2):
            piece = shifted(tile, TAPS[t], along)
            later = shifted(tile, TAPS[t + 1], along) if t + 1 < 27 else jnp.zeros_like(tile)
            stack_first[BLK * t : BLK * t + ROWS, cols[m]] = jnp.where(row < NF, piece, later)
    stack_in = stack_first[...].astype(jnp.bfloat16)
    pre_first = jnp.dot(w_first, stack_in, preferred_element_type=jnp.float32)
    gate_first = sigmoid(pre_first)
    hidden_first = (pre_first * gate_first).astype(jnp.bfloat16).astype(jnp.float32)
    for m in range(pairs):
        tile = hidden_first[:, cols[m]]
        for k, tap in enumerate(TAPS):
            stack_mid[CH * k : CH * k + CH, cols[m]] = shifted(tile, tap, along).astype(jnp.bfloat16)
    pre_second = jnp.dot(w_second, stack_mid[...], preferred_element_type=jnp.float32)
    gate_second = sigmoid(pre_second)
    hidden_second = (pre_second * gate_second).astype(jnp.bfloat16)
    predicted = jnp.dot(w_third, hidden_second, preferred_element_type=jnp.float32)

    misfit = predicted[:ROWS] - jnp.concatenate(targets, 1)
    square = jnp.sum(misfit * misfit, axis=0, keepdims=True)
    sample_at = iota((ROWS, count * VOL), 1) // VOL
    mine = sample_at == iota((ROWS, count * VOL), 0)
    losses = jnp.sum(jnp.where(mine, square, 0.0), axis=1, keepdims=True) / (NOUT * VOL)
    owner = jnp.zeros((ROWS, LANES), jnp.int32)
    for j in range(count):
        owner = jnp.where(row == j, trainers[j], owner)
    load = jnp.sum(jnp.where(lane_at == owner, counts, 0.0), axis=1, keepdims=True)
    share = 1.0 / (devices_all * jnp.maximum(load, 1.0))
    scale = share * (2.0 / (NOUT * VOL))
    scale_at = jnp.sum(jnp.where(mine, scale, 0.0), axis=0, keepdims=True)
    grad_pred = (misfit * scale_at).astype(jnp.bfloat16)
    grad_pred = jnp.concatenate([grad_pred, jnp.zeros_like(grad_pred)], 0)

    upper = jnp.dot(w_third_t, grad_pred, preferred_element_type=jnp.float32)
    slope = gate_second * (1.0 + pre_second * (1.0 - gate_second))
    grad_mid = (upper * slope).astype(jnp.bfloat16)
    grad_second = lax.dot_general(grad_mid, stack_mid[...], FULL, preferred_element_type=jnp.float32)
    third = jnp.concatenate([grad_pred, jnp.zeros((LANES - 16, count * VOL), jnp.bfloat16)], 0)
    grad_third = lax.dot_general(hidden_second, third, FULL, preferred_element_type=jnp.float32)

    grad_wide = grad_mid.astype(jnp.float32)
    for m in range(pairs):
        tile = grad_wide[:, cols[m]]
        for k, tap in enumerate(TAPS):
            back = shifted(tile, tuple(-o for o in tap), along)
            stack_mid[CH * k : CH * k + CH, cols[m]] = back.astype(jnp.bfloat16)
    lower = jnp.dot(w_second_t, stack_mid[...], preferred_element_type=jnp.float32)
    slope = gate_first * (1.0 + pre_first * (1.0 - gate_first))
    grad_entry = (lower * slope).astype(jnp.bfloat16)
    grad_first = lax.dot_general(grad_entry, stack_in, FULL, preferred_element_type=jnp.float32)

    whole = CH * 27 // LANES
    rest = CH * 27 - whole * LANES
    for t in range(whole):
        send[:, t, :] = grad_second[:, LANES * t : LANES * t + LANES]
    mixed = jnp.concatenate([grad_second[:, whole * LANES :], jnp.zeros((CH, LANES - rest), jnp.float32)], 1)
    mixed = mixed + pltpu.roll(grad_third, rest, 1)
    tail = LANES - grad_first.shape[1]
    send[:, whole + 1, :] = jnp.concatenate([grad_first, jnp.zeros((CH, tail), jnp.float32)], 1)

    pos_x, pos_y, pos_z, count_y, count_z = place
    offset = rest + ROWS if inline else 0
    height = CH if inline else slots.shape[0]
    slot_rows = iota((height, LANES), 0)
    slot_lanes = iota((height, LANES), 1)
    placed = jnp.zeros((height, LANES), jnp.float32)
    for j in range(count):
        name = trainers[j]
        rank = jnp.int32(0)
        for i in range(j):
            rank = rank + jnp.where(trainers[i] == name, 1, 0)
        target = (pos_x * count_y + name) * count_z + pos_z
        slot = offset + pos_y * CAP + rank
        hit = (slot_rows == target) & (slot_lanes == slot)
        placed = jnp.where(hit, losses[j : j + 1, :], placed)
    if inline:
        mixed = mixed + placed
    else:
        slots[:, 0, :] = placed
    send[:, whole, :] = mixed


def second_step(sizes, inline, samples, trainers, middle, visc, vx_prev, vx_next, vy_prev, vy_next,
                vz_other, x_prev, x_next, y_prev, y_next, z_other, counts, pick, w_first, w_second,
                w_second_t, w_third, w_third_t, advanced, send, *rest):
    slots = None if inline else rest[0]
    stack_first, stack_mid = rest[-2:]
    halo = halo_of(x_prev, x_next, y_prev, y_next, z_other)
    visc_halo = halo_of(vx_prev, vx_next, vy_prev, vy_next, vz_other)

    def emit(x, c, tiles, state):
        for f, tile in enumerate(tiles):
            advanced[f, x, ROWS * c : ROWS * c + ROWS, :] = tile
        return state

    advance(middle, visc, halo, visc_halo, emit, ())
    if sizes["gy"] == 4:
        total = counts_of(trainers, trainers.shape[0]) + vy_prev[NF + 1] + vy_next[NF + 1] + y_prev[NF]
    else:
        total = counts[...]
    place = (lax.axis_index("gx"), lax.axis_index("gy"), lax.axis_index("gz"), sizes["gy"], sizes["gz"])
    closure(advanced, samples, trainers, total, pick[...], w_first[...], w_second[...],
            w_second_t[...], w_third[...], w_third_t[...],
            float(sizes["gx"] * sizes["gy"] * sizes["gz"]), stack_first, stack_mid, send, slots,
            inline, place)


def add_up(where, arrived, spread, losses):
    total = jnp.sum(arrived[...], axis=0)
    row, lane = where
    losses[0, 0] = total[row : row + 1, lane : lane + losses.shape[3]]
    for i in range(spread.shape[0]):
        spread[i] = total


def unpack(gathered, first, second, third):
    whole = second.shape[1] // LANES
    rest = second.shape[1] - whole * LANES
    for t in range(whole):
        second[:, LANES * t : LANES * t + LANES] = gathered[:, t, :]
    mixed = gathered[:, whole, :]
    second[:, LANES * whole :] = mixed[:, :rest]
    third[...] = mixed[:, rest : rest + ROWS].T[:NOUT]
    first[...] = gathered[:, whole + 1, :][:, : first.shape[1]]


def pick_rows():
    wanted = [0, 1, 2, 3, 0, 1, 2, 3, 0, 1, 2, 0, 0, 1, -1, -1, 0, 1, 2, 1, 2, 2, -1, -1]
    table = np.zeros((32, NF * ROWS), np.float32)
    for i, f in enumerate(wanted):
        if f >= 0:
            table[i, f * ROWS : f * ROWS + ROWS] = 1.0
    return table


def shape_of(*dims, dtype=jnp.float32):
    return jax.ShapeDtypeStruct(dims, dtype)


def exchange(x_first, x_last, y_first, y_last, z_both, sizes):
    def ring(axis, step):
        count = sizes[axis]
        return [(i, (i + step) % count) for i in range(count)]

    x_prev = lax.ppermute(x_last, "gx", ring("gx", 1))
    x_next = lax.ppermute(x_first, "gx", ring("gx", -1))
    y_prev = lax.ppermute(y_last, "gy", ring("gy", 1))
    y_next = lax.ppermute(y_first, "gy", ring("gy", -1))
    z_other = lax.ppermute(z_both, "gz", ring("gz", 1))
    return x_prev, x_next, y_prev, y_next, z_other


def on_device(sizes, fields, visc, samples, trainers, conv_first, conv_second, conv_third):
    _, planes, rows, lanes = fields.shape
    axes = ("gx", "gy", "gz")
    devices_all = sizes["gx"] * sizes["gy"] * sizes["gz"]
    pairs = planes * rows // ROWS
    half = LANES // 2
    samples = samples.reshape(-1)
    trainers = trainers.reshape(-1)

    faces = pl.pallas_call(
        pack_faces,
        out_shape=[
            shape_of(NF + 1, rows, lanes),
            shape_of(NF + 1, rows, lanes),
            shape_of(NF + 2, planes, lanes),
            shape_of(NF + 2, planes, lanes),
            shape_of(-(-(NF + 1) * pairs // half), ROWS, LANES),
        ],
        in_specs=[HBM, HBM, SMEM],
        out_specs=[VMEM] * 5,
        scratch_shapes=[
            pltpu.VMEM(fields.shape, jnp.float32),
            pltpu.VMEM(visc.shape, jnp.float32),
            pltpu.SemaphoreType.DMA((NF + 1,)),
        ],
        compiler_params=PACK,
        name="pack_faces",
    )(fields, visc, trainers)
    halo = exchange(*faces, sizes)

    if sizes["gy"] == 4:
        counts = jnp.zeros((1, LANES), jnp.float32)
    else:
        named = trainers.reshape(-1, 1) == jnp.arange(LANES, dtype=jnp.int32)[None, :]
        counts = lax.psum(jnp.sum(named.astype(jnp.float32), axis=0, keepdims=True), "gy")
    counts = jnp.broadcast_to(counts, (ROWS, LANES))
    w_first = jnp.pad(conv_first, ((0, 0), (0, 28 * NF - conv_first.shape[1])))
    w_second_t = conv_second.reshape(CH, 27, CH).transpose(2, 1, 0).reshape(CH, 27 * CH)
    w_third = jnp.pad(conv_third, ((0, 16 - NOUT), (0, 0)))
    w_third_t = w_third.T

    middle, *faces = pl.pallas_call(
        first_step,
        out_shape=[
            shape_of(*fields.shape),
            shape_of(NF, rows, lanes),
            shape_of(NF, rows, lanes),
            shape_of(NF, planes, lanes),
            shape_of(NF + 1, planes, lanes),
            shape_of(-(-NF * pairs // half), ROWS, LANES),
        ],
        in_specs=[VMEM] * 7,
        out_specs=[VMEM] * 6,
        compiler_params=PARAMS,
        name="first_step",
    )(fields, visc, *halo)
    later = exchange(*faces, sizes)

    count = samples.shape[0]
    slot_total = sizes["gy"] * CAP
    tiles = -(-27 * CH // LANES) + 1
    parts = devices_all // CH
    inline = parts == 1 and slot_total <= 24
    out_shape = [shape_of(*fields.shape), shape_of(CH, tiles, LANES)]
    if not inline:
        out_shape.append(shape_of(devices_all, 1, LANES))
    advanced, send, *slots = pl.pallas_call(
        functools.partial(second_step, sizes, inline),
        out_shape=out_shape,
        in_specs=[SMEM] * 2 + [VMEM] * 19,
        out_specs=[VMEM] * len(out_shape),
        scratch_shapes=[
            pltpu.VMEM((28 * NF, count * VOL), jnp.float32),
            pltpu.VMEM((27 * CH, count * VOL), jnp.bfloat16),
        ],
        compiler_params=PARAMS,
        name="second_step",
    )(samples, trainers, middle, visc, *halo, *later, counts, jnp.asarray(pick_rows(), jnp.bfloat16),
      w_first, conv_second, w_second_t, w_third, w_third_t)

    if not inline:
        send = jnp.concatenate([send.reshape(devices_all, tiles // parts, LANES), slots[0]], 1)
    arrived = lax.all_to_all(send, axes, split_axis=0, concat_axis=0, tiled=True)
    if inline:
        where = (27 * CH // LANES, 27 * CH % LANES + ROWS)
    else:
        where = (send.shape[1] - 1, 0)
    spread, block_losses = pl.pallas_call(
        functools.partial(add_up, where),
        out_shape=[shape_of(*send.shape), shape_of(1, 1, 1, slot_total)],
        in_specs=[VMEM],
        out_specs=[VMEM] * 2,
        compiler_params=PARAMS,
        name="add_up",
    )(arrived)
    if not inline:
        spread = spread[:, :-1, :]
    gathered = lax.all_to_all(spread, axes, split_axis=0, concat_axis=0, tiled=True)
    first, second, third = pl.pallas_call(
        unpack,
        out_shape=[shape_of(*conv_first.shape), shape_of(*conv_second.shape), shape_of(*conv_third.shape)],
        in_specs=[VMEM],
        out_specs=[VMEM] * 3,
        compiler_params=PARAMS,
        name="unpack",
    )(gathered.reshape(CH, tiles, LANES))
    return advanced, block_losses, first, second, third


def solution(mesh):
    sizes = dict(mesh.shape)
    in_specs = (
        P(None, "gx", "gy", "gz"),
        P("gx", "gy", "gz"),
        P("gx", "gy", "gz", None),
        P("gx", "gy", "gz", None, None),
        P(),
        P(),
        P(),
    )
    out_specs = (P(None, "gx", "gy", "gz"), P("gx", "gy", "gz", None), P(), P(), P())
    return jax.shard_map(
        functools.partial(on_device, sizes), mesh=mesh, in_specs=in_specs, out_specs=out_specs,
        check_vma=False,
    )
```

```python
import functools

import jax
import jax.numpy as jnp
import numpy as np
from jax import lax
from jax.experimental import pallas as pl
from jax.experimental.pallas import tpu as pltpu
from jax.sharding import PartitionSpec as P

BLK = 4
CAP = 2
NF = 4
VOL = BLK**3
TAPS = [(x, y, z) for x in (-1, 0, 1) for y in (-1, 0, 1) for z in (-1, 0, 1)]
LANES = 128
ROWS = 8
NOUT = 6
CH = 32

time_step = 0.25
buoyancy = 0.5

VMEM = pl.BlockSpec(memory_space=pltpu.VMEM)
SMEM = pl.BlockSpec(memory_space=pltpu.SMEM)
HBM = pl.BlockSpec(memory_space=pltpu.HBM)
PARAMS = pltpu.CompilerParams(vmem_limit_bytes=24 * 1024 * 1024)
PACK = pltpu.CompilerParams(vmem_limit_bytes=60 * 1024 * 1024)
FULL = (((1,), (1,)), ((), ()))


def iota(shape, axis):
    return lax.broadcasted_iota(jnp.int32, shape, axis)


def pair_of(f, c, planes, chunks):
    k = (c * NF + f) * planes if f < NF else (NF * chunks + c) * planes
    return k // (LANES // 2), 2 * (k % (LANES // 2))


def add_pair(packed, tile, lane):
    moved = pltpu.roll(tile, lane + 1, 1)
    at = iota(tile.shape, 1)
    return jnp.where((at == lane) | (at == lane + 1), moved, packed)


def counts_of(trainers_ref, count):
    at = iota((ROWS, LANES), 1)
    total = jnp.zeros((ROWS, LANES), jnp.float32)
    for j in range(count):
        total = total + jnp.where(at == trainers_ref[j], 1.0, 0.0)
    return total


def pack_faces(fields_far, visc_far, trainers, x_first, x_last, y_first, y_last, z_both, fields, visc, sems):
    _, planes, rows, _ = fields.shape
    chunks = rows // ROWS
    copies = [pltpu.make_async_copy(fields_far.at[f], fields.at[f], sems.at[f]) for f in range(NF)]
    copies.append(pltpu.make_async_copy(visc_far, visc, sems.at[NF]))
    for copy in copies:
        copy.start()
    counts = counts_of(trainers, trainers.shape[0])
    y_first[NF + 1] = counts
    y_last[NF + 1] = counts
    arrays = [fields.at[f] for f in range(NF)] + [visc]
    packed = [jnp.zeros((ROWS, LANES), jnp.float32) for _ in range(z_both.shape[0])]
    for f, array in enumerate(arrays):
        copies[f].wait()
        x_first[f] = array[0]
        x_last[f] = array[planes - 1]
        y_first[f] = array[:, 0, :]
        y_last[f] = array[:, rows - 1, :]
        for c in range(chunks):
            tile, lane = pair_of(f, c, planes, chunks)
            for x in range(planes):
                cells = array[x, ROWS * c : ROWS * c + ROWS]
                packed[tile] = add_pair(packed[tile], cells, lane + 2 * x)
    for tile, value in enumerate(packed):
        z_both[tile] = value


def flux(lower, upper, dimension, visc_lower, visc_upper):
    speed = 0.25 * (lower[dimension] + upper[dimension])
    mean_visc = 0.5 * (visc_lower + visc_upper)
    return [speed * (a + b) - mean_visc * (b - a) for a, b in zip(lower, upper)]


def advance(fields, visc, halo, visc_halo, emit, state):
    _, planes, rows, _ = fields.shape
    chunks = rows // ROWS
    row = iota((ROWS, LANES), 0)
    lane_at = iota((ROWS, LANES), 1)
    parts = [slice(ROWS * c, ROWS * c + ROWS) for c in range(chunks)]
    every = range(NF + 1)

    def cell(f, x, part):
        return fields[f, x, part, :] if f < NF else visc[x, part, :]

    def face(f, which, *index):
        side = halo[which] if f < NF else visc_halo[which]
        return side[(f,) + index]

    def plane(x, carry):
        lowers, state = carry
        uppers = []
        last = x == planes - 1
        beyond = jnp.minimum(x + 1, planes - 1)
        for c, part in enumerate(parts):
            here = [cell(f, x, part) for f in every]
            after = [jnp.where(last, face(f, "x_next", part), cell(f, beyond, part)) for f in every]
            upper = flux(here[:NF], after[:NF], 0, here[NF], after[NF])
            total = [b - a for a, b in zip(lowers[c], upper)]
            uppers.append(upper)
            below, above = [], []
            for f in every:
                if c > 0:
                    edge = cell(f, x, slice(ROWS * c - 1, ROWS * c))
                else:
                    edge = face(f, "y_prev", pl.ds(x, 1))
                below.append(jnp.where(row == 0, edge, pltpu.roll(here[f], 1, 0)))
                if c + 1 < chunks:
                    edge = cell(f, x, slice(ROWS * c + ROWS, ROWS * c + ROWS + 1))
                else:
                    edge = face(f, "y_next", pl.ds(x, 1))
                above.append(jnp.where(row == ROWS - 1, edge, pltpu.roll(here[f], ROWS - 1, 0)))
            lower = flux(below[:NF], here[:NF], 1, below[NF], here[NF])
            upper = flux(here[:NF], above[:NF], 1, here[NF], above[NF])
            total = [t + (b - a) for t, a, b in zip(total, lower, upper)]
            left, right = [], []
            for f in every:
                tile, lane = pair_of(f, c, planes, chunks)
                both = pltpu.roll(face(f, "z_both", tile), LANES - 1 - lane - 2 * x, 1)
                left.append(pltpu.roll(jnp.where(lane_at == LANES - 1, both, here[f]), 1, 1))
                right.append(pltpu.roll(jnp.where(lane_at == 0, both, here[f]), LANES - 1, 1))
            lower = flux(left[:NF], here[:NF], 2, left[NF], here[NF])
            upper = flux(here[:NF], right[:NF], 2, here[NF], right[NF])
            total = [t + (b - a) for t, a, b in zip(total, lower, upper)]
            updated = [q - time_step * t for q, t in zip(here[:NF], total)]
            updated[2] = updated[2] + (time_step * buoyancy) * here[3]
            state = emit(x, c, updated, state)
        return uppers, state

    lowers = []
    for part in parts:
        before = [face(f, "x_prev", part) for f in every]
        here = [cell(f, 0, part) for f in every]
        lowers.append(flux(before[:NF], here[:NF], 0, before[NF], here[NF]))
    return lax.fori_loop(0, planes, plane, (lowers, state))[1]


class Side:
    def __init__(self, ref):
        self.ref = ref

    def __getitem__(self, index):
        return self.ref[index[1]]


def halo_of(x_prev, x_next, y_prev, y_next, z_both):
    return dict(x_prev=x_prev, x_next=x_next, y_prev=y_prev, y_next=y_next, z_both=Side(z_both))


def first_step(fields, visc, x_prev, x_next, y_prev, y_next, z_other,
               middle, x_first, x_last, y_first, y_last, z_both):
    _, planes, rows, _ = fields.shape
    chunks = rows // ROWS
    halo = halo_of(x_prev, x_next, y_prev, y_next, z_other)
    packed = [jnp.zeros((ROWS, LANES), jnp.float32) for _ in range(z_both.shape[0])]

    def emit(x, c, tiles, packed):
        packed = list(packed)
        for f, tile in enumerate(tiles):
            middle[f, x, ROWS * c : ROWS * c + ROWS, :] = tile
            at, lane = pair_of(f, c, planes, chunks)
            packed[at] = add_pair(packed[at], tile, lane + 2 * x)
        return packed

    packed = advance(fields, visc, halo, halo, emit, packed)
    for at, value in enumerate(packed):
        z_both[at] = value
    x_first[...] = middle[:, 0]
    x_last[...] = middle[:, planes - 1]
    for f in range(NF):
        y_first[f] = middle[f, :, 0, :]
        y_last[f] = middle[f, :, rows - 1, :]
    y_last[NF] = y_prev[NF + 1]


def inside_masks():
    at = iota((1, LANES), 1) % VOL
    coords = (at // (BLK * BLK), at // BLK % BLK, at % BLK)
    along = []
    for coord in coords:
        along.append({
            -1: jnp.where(coord > 0, 1.0, 0.0),
            0: jnp.ones((1, LANES), jnp.float32),
            1: jnp.where(coord < BLK - 1, 1.0, 0.0),
        })
    return along


def move_of(tap):
    return tap[0] * BLK * BLK + tap[1] * BLK + tap[2]


def shifted(tile, tap, along):
    move = move_of(tap)
    if move == 0:
        return tile
    mask = along[0][tap[0]] * along[1][tap[1]] * along[2][tap[2]]
    return pltpu.roll(tile, (-move) % LANES, 1) * mask


def box(tile, along):
    for dimension, step in enumerate((BLK * BLK, BLK, 1)):
        ahead = pltpu.roll(tile, LANES - step, 1) * along[dimension][1]
        behind = pltpu.roll(tile, step, 1) * along[dimension][-1]
        tile = (behind + tile) + ahead
    return tile / 27.0


def sigmoid(values):
    return 1.0 / (1.0 + jnp.exp(-values))


def pick_blocks(advanced, samples, pick, count):
    _, _, rows, lanes = advanced.shape
    along_y, along_z = rows // BLK, lanes // BLK
    row = iota((ROWS, LANES), 0)
    lane_at = iota((ROWS, LANES), 1)
    out = []
    for j in range(0, count, 2):
        parts = [jnp.zeros((ROWS, LANES), jnp.float32) for _ in range(NF)]
        uppers = []
        for half in range(2):
            block = samples[j + half]
            block_x = block // (along_y * along_z)
            block_y = block // along_z % along_y
            block_z = block % along_z
            uppers.append(block_y % 2)
            start = pl.multiple_of(block_y // 2 * ROWS, ROWS)
            for x in range(BLK):
                turn = lax.rem(VOL * half + BLK * BLK * x - BLK * block_z + LANES, LANES)
                wanted = lane_at // BLK == (VOL * half + BLK * BLK * x) // BLK
                for f in range(NF):
                    tile = advanced[f, block_x * BLK + x, pl.ds(start, ROWS), :]
                    parts[f] = jnp.where(wanted, pltpu.roll(tile, turn, 1), parts[f])
        upper = jnp.where(lane_at < VOL, uppers[0], uppers[1])
        valid = row // BLK == upper
        for f in range(NF):
            for bit in (1, 2):
                moved = pltpu.roll(parts[f], BLK * bit, 1)
                parts[f] = jnp.where(row // bit % 2 == 1, moved, parts[f])
            parts[f] = jnp.where(valid, parts[f], 0.0)
        stacked = jnp.concatenate(parts, 0).astype(jnp.bfloat16)
        out.append(jnp.dot(pick, stacked, preferred_element_type=jnp.float32))
    return out


def closure(advanced, samples, trainers, counts, pick, w_first, w_second, w_second_t, w_third,
            w_third_t, devices_all, stack_first, stack_mid, rows_out, send, slots, inline, place):
    count = samples.shape[0]
    pairs = count // 2
    cols = [slice(LANES * m, LANES * m + LANES) for m in range(pairs)]
    along = inside_masks()
    lane_at = iota((ROWS, LANES), 1)
    row = iota((ROWS, LANES), 0)

    picked = pick_blocks(advanced, samples, pick, count)
    values = [p[:ROWS] for p in picked]
    targets = []
    for p in picked:
        first, second = p[ROWS : 2 * ROWS], p[2 * ROWS : 3 * ROWS]
        targets.append(box(first * second, along) - box(first, along) * box(second, along))

    for m, tile in enumerate(values):
        for t in range(0, 28, 2):
            piece = shifted(tile, TAPS[t], along)
            later = shifted(tile, TAPS[t + 1], along) if t + 1 < 27 else jnp.zeros_like(tile)
            stack_first[BLK * t : BLK * t + ROWS, cols[m]] = jnp.where(row < NF, piece, later)
    stack_in = stack_first[...].astype(jnp.bfloat16)
    pre_first = jnp.dot(w_first, stack_in, preferred_element_type=jnp.float32)
    gate_first = sigmoid(pre_first)
    hidden_first = (pre_first * gate_first).astype(jnp.bfloat16).astype(jnp.float32)
    for m in range(pairs):
        tile = hidden_first[:, cols[m]]
        for k, tap in enumerate(TAPS):
            stack_mid[CH * k : CH * k + CH, cols[m]] = shifted(tile, tap, along).astype(jnp.bfloat16)
    pre_second = jnp.dot(w_second, stack_mid[...], preferred_element_type=jnp.float32)
    gate_second = sigmoid(pre_second)
    hidden_second = (pre_second * gate_second).astype(jnp.bfloat16)
    predicted = jnp.dot(w_third, hidden_second, preferred_element_type=jnp.float32)

    misfit = predicted[:ROWS] - jnp.concatenate(targets, 1)
    square = jnp.sum(misfit * misfit, axis=0, keepdims=True)
    sample_at = iota((ROWS, count * VOL), 1) // VOL
    mine = sample_at == iota((ROWS, count * VOL), 0)
    losses = jnp.sum(jnp.where(mine, square, 0.0), axis=1, keepdims=True) / (NOUT * VOL)
    owner = jnp.zeros((ROWS, LANES), jnp.int32)
    for j in range(count):
        owner = jnp.where(row == j, trainers[j], owner)
    load = jnp.sum(jnp.where(lane_at == owner, counts, 0.0), axis=1, keepdims=True)
    share = 1.0 / (devices_all * jnp.maximum(load, 1.0))
    scale = share * (2.0 / (NOUT * VOL))
    scale_at = jnp.sum(jnp.where(mine, scale, 0.0), axis=0, keepdims=True)
    grad_pred = (misfit * scale_at).astype(jnp.bfloat16)
    grad_pred = jnp.concatenate([grad_pred, jnp.zeros_like(grad_pred)], 0)

    upper = jnp.dot(w_third_t, grad_pred, preferred_element_type=jnp.float32)
    slope = gate_second * (1.0 + pre_second * (1.0 - gate_second))
    grad_mid = (upper * slope).astype(jnp.bfloat16)
    grad_second = lax.dot_general(grad_mid, stack_mid[...], FULL, preferred_element_type=jnp.float32)
    third = jnp.concatenate([grad_pred, jnp.zeros((LANES - 16, count * VOL), jnp.bfloat16)], 0)
    grad_third = lax.dot_general(hidden_second, third, FULL, preferred_element_type=jnp.float32)

    grad_wide = grad_mid.astype(jnp.float32)
    for m in range(pairs):
        tile = grad_wide[:, cols[m]]
        for k, tap in enumerate(TAPS):
            back = shifted(tile, tuple(-o for o in tap), along)
            stack_mid[CH * k : CH * k + CH, cols[m]] = back.astype(jnp.bfloat16)
    lower = jnp.dot(w_second_t, stack_mid[...], preferred_element_type=jnp.float32)
    slope = gate_first * (1.0 + pre_first * (1.0 - gate_first))
    grad_entry = (lower * slope).astype(jnp.bfloat16)
    grad_first = lax.dot_general(grad_entry, stack_in, FULL, preferred_element_type=jnp.float32)

    whole = CH * 27 // LANES
    rest = CH * 27 - whole * LANES
    for t in range(whole):
        rows_out[:, t, :] = grad_second[:, LANES * t : LANES * t + LANES]
    mixed = jnp.concatenate([grad_second[:, whole * LANES :], jnp.zeros((CH, LANES - rest), jnp.float32)], 1)
    mixed = mixed + pltpu.roll(grad_third, rest, 1)
    tail = LANES - grad_first.shape[1]
    rows_out[:, whole + 1, :] = jnp.concatenate([grad_first, jnp.zeros((CH, tail), jnp.float32)], 1)

    pos_x, pos_y, pos_z, count_y, count_z = place
    offset = rest + ROWS if inline else 0
    height = CH if inline else slots.shape[0]
    slot_rows = iota((height, LANES), 0)
    slot_lanes = iota((height, LANES), 1)
    placed = jnp.zeros((height, LANES), jnp.float32)
    for j in range(count):
        name = trainers[j]
        rank = jnp.int32(0)
        for i in range(j):
            rank = rank + jnp.where(trainers[i] == name, 1, 0)
        target = (pos_x * count_y + name) * count_z + pos_z
        slot = offset + pos_y * CAP + rank
        hit = (slot_rows == target) & (slot_lanes == slot)
        placed = jnp.where(hit, losses[j : j + 1, :], placed)
    high = placed.astype(jnp.bfloat16).astype(jnp.float32)
    placed = high + pltpu.roll(placed - high, count_y * CAP, 1)
    if inline:
        mixed = mixed + placed
    else:
        slots[:, 0, :] = placed.astype(jnp.bfloat16)
    rows_out[:, whole, :] = mixed
    send[...] = rows_out[...].astype(jnp.bfloat16)


def second_step(sizes, inline, samples, trainers, middle, visc, vx_prev, vx_next, vy_prev, vy_next,
                vz_other, x_prev, x_next, y_prev, y_next, z_other, counts, pick, w_first, w_second,
                w_second_t, w_third, w_third_t, advanced, send, *rest):
    slots = None if inline else rest[0]
    stack_first, stack_mid, rows_out = rest[-3:]
    halo = halo_of(x_prev, x_next, y_prev, y_next, z_other)
    visc_halo = halo_of(vx_prev, vx_next, vy_prev, vy_next, vz_other)

    def emit(x, c, tiles, state):
        for f, tile in enumerate(tiles):
            advanced[f, x, ROWS * c : ROWS * c + ROWS, :] = tile
        return state

    advance(middle, visc, halo, visc_halo, emit, ())
    if sizes["gy"] == 4:
        total = counts_of(trainers, trainers.shape[0]) + vy_prev[NF + 1] + vy_next[NF + 1] + y_prev[NF]
    else:
        total = counts[...]
    place = (lax.axis_index("gx"), lax.axis_index("gy"), lax.axis_index("gz"), sizes["gy"], sizes["gz"])
    closure(advanced, samples, trainers, total, pick[...], w_first[...], w_second[...],
            w_second_t[...], w_third[...], w_third_t[...],
            float(sizes["gx"] * sizes["gy"] * sizes["gz"]), stack_first, stack_mid, rows_out,
            send, slots, inline, place)


def add_up(where, arrived, spread, losses):
    total = jnp.sum(arrived[...].astype(jnp.float32), axis=0)
    row, lane = where
    count = losses.shape[3]
    high = total[row : row + 1, lane : lane + count]
    losses[0, 0] = high + total[row : row + 1, lane + count : lane + 2 * count]
    rounded = total.astype(jnp.bfloat16)
    for i in range(spread.shape[0]):
        spread[i] = rounded


def unpack(gathered, first, second, third, wide):
    wide[...] = gathered[...].astype(jnp.float32)
    whole = second.shape[1] // LANES
    rest = second.shape[1] - whole * LANES
    for t in range(whole):
        second[:, LANES * t : LANES * t + LANES] = wide[:, t, :]
    mixed = wide[:, whole, :]
    second[:, LANES * whole :] = mixed[:, :rest]
    third[...] = mixed[:, rest : rest + ROWS].T[:NOUT]
    first[...] = wide[:, whole + 1, :][:, : first.shape[1]]


def pick_rows():
    wanted = [0, 1, 2, 3, 0, 1, 2, 3, 0, 1, 2, 0, 0, 1, -1, -1, 0, 1, 2, 1, 2, 2, -1, -1]
    table = np.zeros((32, NF * ROWS), np.float32)
    for i, f in enumerate(wanted):
        if f >= 0:
            table[i, f * ROWS : f * ROWS + ROWS] = 1.0
    return table


def shape_of(*dims, dtype=jnp.float32):
    return jax.ShapeDtypeStruct(dims, dtype)


def exchange(x_first, x_last, y_first, y_last, z_both, sizes):
    def ring(axis, step):
        count = sizes[axis]
        return [(i, (i + step) % count) for i in range(count)]

    x_prev = lax.ppermute(x_last, "gx", ring("gx", 1))
    x_next = lax.ppermute(x_first, "gx", ring("gx", -1))
    y_prev = lax.ppermute(y_last, "gy", ring("gy", 1))
    y_next = lax.ppermute(y_first, "gy", ring("gy", -1))
    z_other = lax.ppermute(z_both, "gz", ring("gz", 1))
    return x_prev, x_next, y_prev, y_next, z_other


def on_device(sizes, fields, visc, samples, trainers, conv_first, conv_second, conv_third):
    _, planes, rows, lanes = fields.shape
    axes = ("gx", "gy", "gz")
    devices_all = sizes["gx"] * sizes["gy"] * sizes["gz"]
    pairs = planes * rows // ROWS
    half = LANES // 2
    samples = samples.reshape(-1)
    trainers = trainers.reshape(-1)

    faces = pl.pallas_call(
        pack_faces,
        out_shape=[
            shape_of(NF + 1, rows, lanes),
            shape_of(NF + 1, rows, lanes),
            shape_of(NF + 2, planes, lanes),
            shape_of(NF + 2, planes, lanes),
            shape_of(-(-(NF + 1) * pairs // half), ROWS, LANES),
        ],
        in_specs=[HBM, HBM, SMEM],
        out_specs=[VMEM] * 5,
        scratch_shapes=[
            pltpu.VMEM(fields.shape, jnp.float32),
            pltpu.VMEM(visc.shape, jnp.float32),
            pltpu.SemaphoreType.DMA((NF + 1,)),
        ],
        compiler_params=PACK,
        name="pack_faces",
    )(fields, visc, trainers)
    halo = exchange(*faces, sizes)

    if sizes["gy"] == 4:
        counts = jnp.zeros((1, LANES), jnp.float32)
    else:
        named = trainers.reshape(-1, 1) == jnp.arange(LANES, dtype=jnp.int32)[None, :]
        counts = lax.psum(jnp.sum(named.astype(jnp.float32), axis=0, keepdims=True), "gy")
    counts = jnp.broadcast_to(counts, (ROWS, LANES))
    w_first = jnp.pad(conv_first, ((0, 0), (0, 28 * NF - conv_first.shape[1])))
    w_second_t = conv_second.reshape(CH, 27, CH).transpose(2, 1, 0).reshape(CH, 27 * CH)
    w_third = jnp.pad(conv_third, ((0, 16 - NOUT), (0, 0)))
    w_third_t = w_third.T
    weights = (w_first, conv_second, w_second_t, w_third, w_third_t)
    halo, weights = lax.optimization_barrier((halo, weights))

    middle, *faces = pl.pallas_call(
        first_step,
        out_shape=[
            shape_of(*fields.shape),
            shape_of(NF, rows, lanes),
            shape_of(NF, rows, lanes),
            shape_of(NF, planes, lanes),
            shape_of(NF + 1, planes, lanes),
            shape_of(-(-NF * pairs // half), ROWS, LANES),
        ],
        in_specs=[VMEM] * 7,
        out_specs=[VMEM] * 6,
        compiler_params=PARAMS,
        name="first_step",
    )(fields, visc, *halo)
    later = exchange(*faces, sizes)

    count = samples.shape[0]
    slot_total = sizes["gy"] * CAP
    tiles = -(-27 * CH // LANES) + 1
    parts = devices_all // CH
    inline = parts == 1 and slot_total <= 12
    out_shape = [shape_of(*fields.shape), shape_of(CH, tiles, LANES, dtype=jnp.bfloat16)]
    if not inline:
        out_shape.append(shape_of(devices_all, 1, LANES, dtype=jnp.bfloat16))
    advanced, send, *slots = pl.pallas_call(
        functools.partial(second_step, sizes, inline),
        out_shape=out_shape,
        in_specs=[SMEM] * 2 + [VMEM] * 19,
        out_specs=[VMEM] * len(out_shape),
        scratch_shapes=[
            pltpu.VMEM((28 * NF, count * VOL), jnp.float32),
            pltpu.VMEM((27 * CH, count * VOL), jnp.bfloat16),
            pltpu.VMEM((CH, tiles, LANES), jnp.float32),
        ],
        compiler_params=PARAMS,
        name="second_step",
    )(samples, trainers, middle, visc, *halo, *later, counts, jnp.asarray(pick_rows(), jnp.bfloat16),
      *weights)

    if not inline:
        send = jnp.concatenate([send.reshape(devices_all, tiles // parts, LANES), slots[0]], 1)
    arrived = lax.all_to_all(send, axes, split_axis=0, concat_axis=0, tiled=True)
    if inline:
        where = (27 * CH // LANES, 27 * CH % LANES + ROWS)
    else:
        where = (send.shape[1] - 1, 0)
    spread, block_losses = pl.pallas_call(
        functools.partial(add_up, where),
        out_shape=[shape_of(*send.shape, dtype=jnp.bfloat16), shape_of(1, 1, 1, slot_total)],
        in_specs=[VMEM],
        out_specs=[VMEM] * 2,
        compiler_params=PARAMS,
        name="add_up",
    )(arrived)
    if not inline:
        spread = spread[:, :-1, :]
    gathered = lax.all_to_all(spread, axes, split_axis=0, concat_axis=0, tiled=True)
    first, second, third = pl.pallas_call(
        unpack,
        out_shape=[shape_of(*conv_first.shape), shape_of(*conv_second.shape), shape_of(*conv_third.shape)],
        in_specs=[VMEM],
        out_specs=[VMEM] * 3,
        scratch_shapes=[pltpu.VMEM((CH, tiles, LANES), jnp.float32)],
        compiler_params=PARAMS,
        name="unpack",
    )(gathered.reshape(CH, tiles, LANES))
    return advanced, block_losses, first, second, third


def solution(mesh):
    sizes = dict(mesh.shape)
    in_specs = (
        P(None, "gx", "gy", "gz"),
        P("gx", "gy", "gz"),
        P("gx", "gy", "gz", None),
        P("gx", "gy", "gz", None, None),
        P(),
        P(),
        P(),
    )
    out_specs = (P(None, "gx", "gy", "gz"), P("gx", "gy", "gz", None), P(), P(), P())
    return jax.shard_map(
        functools.partial(on_device, sizes), mesh=mesh, in_specs=in_specs, out_specs=out_specs,
        check_vma=False,
    )
```

```python
import functools

import jax
import jax.numpy as jnp
import numpy as np
from jax import lax
from jax.experimental import pallas as pl
from jax.experimental.pallas import tpu as pltpu
from jax.sharding import PartitionSpec as P

BLK = 4
CAP = 2
NF = 4
VOL = BLK**3
TAPS = [(x, y, z) for x in (-1, 0, 1) for y in (-1, 0, 1) for z in (-1, 0, 1)]
LANES = 128
ROWS = 8
NOUT = 6
CH = 32

time_step = 0.25
buoyancy = 0.5

VMEM = pl.BlockSpec(memory_space=pltpu.VMEM)
SMEM = pl.BlockSpec(memory_space=pltpu.SMEM)
HBM = pl.BlockSpec(memory_space=pltpu.HBM)
PARAMS = pltpu.CompilerParams(vmem_limit_bytes=24 * 1024 * 1024)
PACK = pltpu.CompilerParams(vmem_limit_bytes=54784 * 1024)
FULL = (((1,), (1,)), ((), ()))


def iota(shape, axis):
    return lax.broadcasted_iota(jnp.int32, shape, axis)


def pair_of(f, c, planes, chunks):
    span = 2 * planes * chunks
    return f * span // LANES, f * span % LANES + 2 * planes * c


def add_pair(packed, tile, lane):
    moved = pltpu.roll(tile, lane + 1, 1)
    at = iota(tile.shape, 1)
    return jnp.where((at == lane) | (at == lane + 1), moved, packed)


def counts_of(trainers_ref, count):
    at = iota((ROWS, LANES), 1)
    total = jnp.zeros((ROWS, LANES), jnp.float32)
    for j in range(count):
        total = total + jnp.where(at == trainers_ref[j], 1.0, 0.0)
    return total


def pack_faces(fields_far, visc_far, trainers, x_first, x_last, y_first, y_last, z_both, fields, visc, sems):
    _, planes, rows, _ = fields.shape
    chunks = rows // ROWS
    copies = [pltpu.make_async_copy(fields_far.at[f], fields.at[f], sems.at[f]) for f in range(NF)]
    copies.append(pltpu.make_async_copy(visc_far, visc, sems.at[NF]))
    for copy in copies:
        copy.start()
    counts = counts_of(trainers, trainers.shape[0])
    y_first[NF + 1] = counts
    y_last[NF + 1] = counts
    arrays = [fields.at[f] for f in range(NF)] + [visc]
    packed = [jnp.zeros((ROWS, LANES), jnp.float32) for _ in range(z_both.shape[0])]
    for f, array in enumerate(arrays):
        copies[f].wait()
        x_first[f] = array[0]
        x_last[f] = array[planes - 1]
        y_first[f] = array[:, 0, :]
        y_last[f] = array[:, rows - 1, :]
        for c in range(chunks):
            tile, lane = pair_of(f, c, planes, chunks)
            for x in range(planes):
                cells = array[x, ROWS * c : ROWS * c + ROWS]
                packed[tile] = add_pair(packed[tile], cells, lane + 2 * x)
    for tile, value in enumerate(packed):
        z_both[tile] = value


def flux(lower, upper, dimension):
    speed = 0.25 * (lower[dimension] + upper[dimension])
    mean_visc = 0.5 * (lower[NF] + upper[NF])
    return [speed * (a + b) - mean_visc * (b - a) for a, b in zip(lower[:NF], upper[:NF])]


def interior(fields, visc, partial):
    _, planes, rows, _ = fields.shape
    chunks = rows // ROWS
    end_row = iota((ROWS, LANES), 0) == ROWS - 1
    end_lane = iota((ROWS, LANES), 1) == LANES - 1
    every = range(NF + 1)

    def cell(f, x, part):
        return fields[f, x, part, :] if f < NF else visc[x, part, :]

    def plane(x, lowers):
        uppers = []
        last = x == planes - 1
        beyond = jnp.minimum(x + 1, planes - 1)
        behind = [jnp.zeros((ROWS, LANES), jnp.float32)] * NF
        for c in range(chunks):
            part = slice(ROWS * c, ROWS * c + ROWS)
            here = [cell(f, x, part) for f in every]
            after = [cell(f, beyond, part) for f in every]
            upper = flux(here, after, 0)
            upper = [jnp.where(last, 0.0, u) for u in upper]
            total = [b - a for a, b in zip(lowers[c], upper)]
            uppers.append(upper)
            above = [pltpu.roll(h, ROWS - 1, 0) for h in here]
            if c + 1 < chunks:
                first = slice(ROWS * c + ROWS, ROWS * c + ROWS + 1)
                above = [jnp.where(end_row, cell(f, x, first), above[f]) for f in every]
            upper = flux(here, above, 1)
            lower = [pltpu.roll(jnp.where(end_row, b, u), 1, 0) for b, u in zip(behind, upper)]
            if c + 1 == chunks:
                upper = [jnp.where(end_row, 0.0, u) for u in upper]
            behind = upper
            total = [t + (b - a) for t, a, b in zip(total, lower, upper)]
            right = [pltpu.roll(h, LANES - 1, 1) for h in here]
            upper = [jnp.where(end_lane, 0.0, u) for u in flux(here, right, 2)]
            lower = [pltpu.roll(u, 1, 1) for u in upper]
            total = [t + (b - a) for t, a, b in zip(total, lower, upper)]
            updated = [q - time_step * t for q, t in zip(here[:NF], total)]
            updated[2] = updated[2] + (time_step * buoyancy) * here[3]
            for f in range(NF):
                partial[f, x, part, :] = updated[f]
        return uppers

    zeros = [[jnp.zeros((ROWS, LANES), jnp.float32)] * NF for _ in range(chunks)]
    lax.fori_loop(0, planes, plane, zeros)


def z_terms(own, other, visc_own, visc_other):
    lane = iota((ROWS, LANES), 1)
    second = lane % 2 == 1
    span = LANES // 2

    def ends(mine, theirs):
        lower = jnp.where(second, pltpu.roll(theirs, 1, 1), mine)
        return lower, jnp.where(second, mine, pltpu.roll(theirs, LANES - 1, 1))

    def twice(tile):
        return jnp.where(lane < span, tile, pltpu.roll(tile, span, 1))

    pairs = [ends(a, b) for a, b in zip(own, other)]
    speed = [twice(end) for end in pairs[2 * span // LANES]]
    visc = [twice(end) for end in ends(visc_own, visc_other)]
    speed = 0.25 * (speed[0] + speed[1])
    mean_visc = 0.5 * (visc[0] + visc[1])
    through = [speed * (a + b) - mean_visc * (b - a) for a, b in pairs]
    return [jnp.where(second, time_step, -time_step) * t for t in through]


def close(fields, visc, partial, halo, visc_halo, z_own, visc_z_own, y_terms, emit):
    _, planes, rows, _ = fields.shape
    chunks = rows // ROWS
    every = range(NF + 1)
    row = iota((ROWS, LANES), 0)
    lane_at = iota((ROWS, LANES), 1)
    ends = (lane_at == 0) | (lane_at == LANES - 1)

    def cell(f, *index):
        return fields[(f,) + index] if f < NF else visc[index]

    def face(f, which, *index):
        return (halo if f < NF else visc_halo)[which][(f,) + index]

    lower = flux([face(f, "y_prev") for f in every], [cell(f, slice(None), 0) for f in every], 1)
    upper = flux([cell(f, slice(None), rows - 1) for f in every], [face(f, "y_next") for f in every], 1)
    for f in range(NF):
        y_terms[0, f] = time_step * lower[f]
        y_terms[1, f] = -time_step * upper[f]
    tiles = z_own.shape[0] if z_own.shape[0] * LANES == 2 * NF * planes * chunks else z_own.shape[0] - 1
    terms = z_terms([z_own[t] for t in range(tiles)], [halo["z_both"][t] for t in range(tiles)],
                    visc_z_own[tiles], visc_halo["z_both"][tiles])
    for c in range(chunks):
        part = slice(ROWS * c, ROWS * c + ROWS)
        low = flux([face(f, "x_prev", part) for f in every], [cell(f, 0, part) for f in every], 0)
        high = flux([cell(f, planes - 1, part) for f in every], [face(f, "x_next", part) for f in every], 0)
        for x in range(planes):
            for f in range(NF):
                tile, lane = pair_of(f, c, planes, chunks)
                moved = pltpu.roll(terms[tile], LANES - 1 - lane - 2 * x, 1)
                value = partial[f, x, part, :] + jnp.where(ends, moved, 0.0)
                if x == 0:
                    value = value + time_step * low[f]
                if x == planes - 1:
                    value = value - time_step * high[f]
                if c == 0:
                    value = value + jnp.where(row == 0, y_terms[0, f, x : x + 1, :], 0.0)
                if c == chunks - 1:
                    value = value + jnp.where(row == ROWS - 1, y_terms[1, f, x : x + 1, :], 0.0)
                emit(f, x, c, value)


def halo_of(x_prev, x_next, y_prev, y_next, z_both):
    return dict(x_prev=x_prev, x_next=x_next, y_prev=y_prev, y_next=y_next, z_both=z_both)


def close_first(fields, visc, partial, x_prev, x_next, y_prev, y_next, z_other, z_own,
                middle, x_first, x_last, y_first, y_last, z_both, y_terms):
    _, planes, rows, _ = fields.shape
    chunks = rows // ROWS
    halo = halo_of(x_prev, x_next, y_prev, y_next, z_other)
    packed = [jnp.zeros((ROWS, LANES), jnp.float32) for _ in range(z_both.shape[0])]

    def emit(f, x, c, tile):
        middle[f, x, ROWS * c : ROWS * c + ROWS, :] = tile
        at, lane = pair_of(f, c, planes, chunks)
        packed[at] = add_pair(packed[at], tile, lane + 2 * x)

    close(fields, visc, partial, halo, halo, z_own, z_own, y_terms, emit)
    for at, value in enumerate(packed):
        z_both[at] = value
    x_first[...] = middle[:, 0]
    x_last[...] = middle[:, planes - 1]
    for f in range(NF):
        y_first[f] = middle[f, :, 0, :]
        y_last[f] = middle[f, :, rows - 1, :]
    y_last[NF] = y_prev[NF + 1]


def inside_masks():
    at = iota((1, LANES), 1) % VOL
    coords = (at // (BLK * BLK), at // BLK % BLK, at % BLK)
    along = []
    for coord in coords:
        along.append({
            -1: jnp.where(coord > 0, 1.0, 0.0),
            0: jnp.ones((1, LANES), jnp.float32),
            1: jnp.where(coord < BLK - 1, 1.0, 0.0),
        })
    return along


def move_of(tap):
    return tap[0] * BLK * BLK + tap[1] * BLK + tap[2]


def shifted(tile, tap, along):
    move = move_of(tap)
    if move == 0:
        return tile
    mask = along[0][tap[0]] * along[1][tap[1]] * along[2][tap[2]]
    return pltpu.roll(tile, (-move) % LANES, 1) * mask


def box(tile, along):
    for dimension, step in enumerate((BLK * BLK, BLK, 1)):
        ahead = pltpu.roll(tile, LANES - step, 1) * along[dimension][1]
        behind = pltpu.roll(tile, step, 1) * along[dimension][-1]
        tile = (behind + tile) + ahead
    return tile / 27.0


def sigmoid(values):
    return 1.0 / (1.0 + jnp.exp(-values))


def pick_blocks(advanced, samples, pick, count):
    _, _, rows, lanes = advanced.shape
    along_y, along_z = rows // BLK, lanes // BLK
    row = iota((ROWS, LANES), 0)
    lane_at = iota((ROWS, LANES), 1)
    out = []
    for j in range(0, count, 2):
        parts = [jnp.zeros((ROWS, LANES), jnp.float32) for _ in range(NF)]
        uppers = []
        for half in range(2):
            block = samples[j + half]
            block_x = block // (along_y * along_z)
            block_y = block // along_z % along_y
            block_z = block % along_z
            uppers.append(block_y % 2)
            start = pl.multiple_of(block_y // 2 * ROWS, ROWS)
            for x in range(BLK):
                turn = lax.rem(VOL * half + BLK * BLK * x - BLK * block_z + LANES, LANES)
                wanted = lane_at // BLK == (VOL * half + BLK * BLK * x) // BLK
                for f in range(NF):
                    tile = advanced[f, block_x * BLK + x, pl.ds(start, ROWS), :]
                    parts[f] = jnp.where(wanted, pltpu.roll(tile, turn, 1), parts[f])
        upper = jnp.where(lane_at < VOL, uppers[0], uppers[1])
        valid = row // BLK == upper
        for f in range(NF):
            for bit in (1, 2):
                moved = pltpu.roll(parts[f], BLK * bit, 1)
                parts[f] = jnp.where(row // bit % 2 == 1, moved, parts[f])
            parts[f] = jnp.where(valid, parts[f], 0.0)
        stacked = jnp.concatenate(parts, 0).astype(jnp.bfloat16)
        out.append(jnp.dot(pick, stacked, preferred_element_type=jnp.float32))
    return out


def closure(advanced, samples, trainers, counts, pick, w_first, w_second, w_second_t, w_third,
            w_third_t, devices_all, stack_first, stack_mid, rows_out, send, slots, inline, place):
    count = samples.shape[0]
    pairs = count // 2
    cols = [slice(LANES * m, LANES * m + LANES) for m in range(pairs)]
    along = inside_masks()
    lane_at = iota((ROWS, LANES), 1)
    row = iota((ROWS, LANES), 0)

    picked = pick_blocks(advanced, samples, pick, count)
    values = [p[:ROWS] for p in picked]
    targets = []
    for p in picked:
        first, second = p[ROWS : 2 * ROWS], p[2 * ROWS : 3 * ROWS]
        targets.append(box(first * second, along) - box(first, along) * box(second, along))

    for m, tile in enumerate(values):
        for t in range(0, 28, 2):
            piece = shifted(tile, TAPS[t], along)
            later = shifted(tile, TAPS[t + 1], along) if t + 1 < 27 else jnp.zeros_like(tile)
            stack_first[BLK * t : BLK * t + ROWS, cols[m]] = jnp.where(row < NF, piece, later)
    stack_in = stack_first[...].astype(jnp.bfloat16)
    pre_first = jnp.dot(w_first, stack_in, preferred_element_type=jnp.float32)
    gate_first = sigmoid(pre_first)
    hidden_first = (pre_first * gate_first).astype(jnp.bfloat16).astype(jnp.float32)
    for m in range(pairs):
        tile = hidden_first[:, cols[m]]
        for k, tap in enumerate(TAPS):
            stack_mid[CH * k : CH * k + CH, cols[m]] = shifted(tile, tap, along).astype(jnp.bfloat16)
    pre_second = jnp.dot(w_second, stack_mid[...], preferred_element_type=jnp.float32)
    gate_second = sigmoid(pre_second)
    hidden_second = (pre_second * gate_second).astype(jnp.bfloat16)
    predicted = jnp.dot(w_third, hidden_second, preferred_element_type=jnp.float32)

    misfit = predicted[:ROWS] - jnp.concatenate(targets, 1)
    square = jnp.sum(misfit * misfit, axis=0, keepdims=True)
    sample_at = iota((ROWS, count * VOL), 1) // VOL
    mine = sample_at == iota((ROWS, count * VOL), 0)
    losses = jnp.sum(jnp.where(mine, square, 0.0), axis=1, keepdims=True) / (NOUT * VOL)
    owner = jnp.zeros((ROWS, LANES), jnp.int32)
    for j in range(count):
        owner = jnp.where(row == j, trainers[j], owner)
    load = jnp.sum(jnp.where(lane_at == owner, counts, 0.0), axis=1, keepdims=True)
    share = 1.0 / (devices_all * jnp.maximum(load, 1.0))
    scale = share * (2.0 / (NOUT * VOL))
    scale_at = jnp.sum(jnp.where(mine, scale, 0.0), axis=0, keepdims=True)
    grad_pred = (misfit * scale_at).astype(jnp.bfloat16)
    grad_pred = jnp.concatenate([grad_pred, jnp.zeros_like(grad_pred)], 0)

    upper = jnp.dot(w_third_t, grad_pred, preferred_element_type=jnp.float32)
    slope = gate_second * (1.0 + pre_second * (1.0 - gate_second))
    grad_mid = (upper * slope).astype(jnp.bfloat16)
    grad_second = lax.dot_general(grad_mid, stack_mid[...], FULL, preferred_element_type=jnp.float32)
    third = jnp.concatenate([grad_pred, jnp.zeros((LANES - 16, count * VOL), jnp.bfloat16)], 0)
    grad_third = lax.dot_general(hidden_second, third, FULL, preferred_element_type=jnp.float32)

    grad_wide = grad_mid.astype(jnp.float32)
    for m in range(pairs):
        tile = grad_wide[:, cols[m]]
        for k, tap in enumerate(TAPS):
            back = shifted(tile, tuple(-o for o in tap), along)
            stack_mid[CH * k : CH * k + CH, cols[m]] = back.astype(jnp.bfloat16)
    lower = jnp.dot(w_second_t, stack_mid[...], preferred_element_type=jnp.float32)
    slope = gate_first * (1.0 + pre_first * (1.0 - gate_first))
    grad_entry = (lower * slope).astype(jnp.bfloat16)
    grad_first = lax.dot_general(grad_entry, stack_in, FULL, preferred_element_type=jnp.float32)

    whole = CH * 27 // LANES
    rest = CH * 27 - whole * LANES
    for t in range(whole):
        rows_out[:, t, :] = grad_second[:, LANES * t : LANES * t + LANES]
    mixed = jnp.concatenate([grad_second[:, whole * LANES :], jnp.zeros((CH, LANES - rest), jnp.float32)], 1)
    mixed = mixed + pltpu.roll(grad_third, rest, 1)
    tail = LANES - grad_first.shape[1]
    rows_out[:, whole + 1, :] = jnp.concatenate([grad_first, jnp.zeros((CH, tail), jnp.float32)], 1)

    pos_x, pos_y, pos_z, count_y, count_z = place
    offset = rest + ROWS if inline else 0
    height = CH if inline else slots.shape[0]
    slot_rows = iota((height, LANES), 0)
    slot_lanes = iota((height, LANES), 1)
    placed = jnp.zeros((height, LANES), jnp.float32)
    for j in range(count):
        name = trainers[j]
        rank = jnp.int32(0)
        for i in range(j):
            rank = rank + jnp.where(trainers[i] == name, 1, 0)
        target = (pos_x * count_y + name) * count_z + pos_z
        slot = offset + pos_y * CAP + rank
        hit = (slot_rows == target) & (slot_lanes == slot)
        placed = jnp.where(hit, losses[j : j + 1, :], placed)
    high = placed.astype(jnp.bfloat16).astype(jnp.float32)
    placed = high + pltpu.roll(placed - high, count_y * CAP, 1)
    if inline:
        mixed = mixed + placed
    else:
        slots[:, 0, :] = placed.astype(jnp.bfloat16)
    rows_out[:, whole, :] = mixed
    send[...] = rows_out[...].astype(jnp.bfloat16)


def second_step(sizes, inline, samples, trainers, middle, visc, partial, vx_prev, vx_next, vy_prev,
                vy_next, vz_other, vz_own, x_prev, x_next, y_prev, y_next, z_other, z_own, counts, pick,
                w_first, w_second, w_second_t, w_third, w_third_t, advanced, send, *rest):
    slots = None if inline else rest[0]
    stack_first, stack_mid, rows_out, y_terms = rest[-4:]
    halo = halo_of(x_prev, x_next, y_prev, y_next, z_other)
    visc_halo = halo_of(vx_prev, vx_next, vy_prev, vy_next, vz_other)

    def emit(f, x, c, tile):
        advanced[f, x, ROWS * c : ROWS * c + ROWS, :] = tile

    close(middle, visc, partial, halo, visc_halo, z_own, vz_own, y_terms, emit)
    if sizes["gy"] == 4:
        total = counts_of(trainers, trainers.shape[0]) + vy_prev[NF + 1] + vy_next[NF + 1] + y_prev[NF]
    else:
        total = counts[...]
    place = (lax.axis_index("gx"), lax.axis_index("gy"), lax.axis_index("gz"), sizes["gy"], sizes["gz"])
    closure(advanced, samples, trainers, total, pick[...], w_first[...], w_second[...],
            w_second_t[...], w_third[...], w_third_t[...],
            float(sizes["gx"] * sizes["gy"] * sizes["gz"]), stack_first, stack_mid, rows_out,
            send, slots, inline, place)


def add_up(where, arrived, spread, losses):
    total = jnp.sum(arrived[...].astype(jnp.float32), axis=0)
    row, lane = where
    count = losses.shape[3]
    high = total[row : row + 1, lane : lane + count]
    losses[0, 0] = high + total[row : row + 1, lane + count : lane + 2 * count]
    rounded = total.astype(jnp.bfloat16)
    for i in range(spread.shape[0]):
        spread[i] = rounded


def unpack(gathered, first, second, third, wide):
    wide[...] = gathered[...].astype(jnp.float32)
    whole = second.shape[1] // LANES
    rest = second.shape[1] - whole * LANES
    for t in range(whole):
        second[:, LANES * t : LANES * t + LANES] = wide[:, t, :]
    mixed = wide[:, whole, :]
    second[:, LANES * whole :] = mixed[:, :rest]
    third[...] = mixed[:, rest : rest + ROWS].T[:NOUT]
    first[...] = wide[:, whole + 1, :][:, : first.shape[1]]


def pick_rows():
    wanted = [0, 1, 2, 3, 0, 1, 2, 3, 0, 1, 2, 0, 0, 1, -1, -1, 0, 1, 2, 1, 2, 2, -1, -1]
    table = np.zeros((32, NF * ROWS), np.float32)
    for i, f in enumerate(wanted):
        if f >= 0:
            table[i, f * ROWS : f * ROWS + ROWS] = 1.0
    return table


def shape_of(*dims, dtype=jnp.float32):
    return jax.ShapeDtypeStruct(dims, dtype)


def exchange(x_first, x_last, y_first, y_last, z_both, sizes):
    def ring(axis, step):
        count = sizes[axis]
        return [(i, (i + step) % count) for i in range(count)]

    x_prev = lax.ppermute(x_last, "gx", ring("gx", 1))
    x_next = lax.ppermute(x_first, "gx", ring("gx", -1))
    y_prev = lax.ppermute(y_last, "gy", ring("gy", 1))
    y_next = lax.ppermute(y_first, "gy", ring("gy", -1))
    z_other = lax.ppermute(z_both, "gz", ring("gz", 1))
    return x_prev, x_next, y_prev, y_next, z_other


def without_border(fields, visc):
    cells = visc.size
    return pl.pallas_call(
        interior,
        out_shape=shape_of(*fields.shape),
        in_specs=[VMEM] * 2,
        out_specs=VMEM,
        compiler_params=PARAMS,
        cost_estimate=pl.CostEstimate(flops=120 * cells, bytes_accessed=36 * cells, transcendentals=0),
        name="interior",
    )(fields, visc)


def on_device(sizes, fields, visc, samples, trainers, conv_first, conv_second, conv_third):
    _, planes, rows, lanes = fields.shape
    axes = ("gx", "gy", "gz")
    devices_all = sizes["gx"] * sizes["gy"] * sizes["gz"]
    pairs = planes * rows // ROWS
    half = LANES // 2
    samples = samples.reshape(-1)
    trainers = trainers.reshape(-1)

    faces = pl.pallas_call(
        pack_faces,
        out_shape=[
            shape_of(NF + 1, rows, lanes),
            shape_of(NF + 1, rows, lanes),
            shape_of(NF + 2, planes, lanes),
            shape_of(NF + 2, planes, lanes),
            shape_of(-(-(NF + 1) * pairs // half), ROWS, LANES),
        ],
        in_specs=[HBM, HBM, SMEM],
        out_specs=[VMEM] * 5,
        scratch_shapes=[
            pltpu.VMEM(fields.shape, jnp.float32),
            pltpu.VMEM(visc.shape, jnp.float32),
            pltpu.SemaphoreType.DMA((NF + 1,)),
        ],
        compiler_params=PACK,
        name="pack_faces",
    )(fields, visc, trainers)
    halo = exchange(*faces, sizes)

    if sizes["gy"] == 4:
        counts = jnp.zeros((1, LANES), jnp.float32)
    else:
        named = trainers.reshape(-1, 1) == jnp.arange(LANES, dtype=jnp.int32)[None, :]
        counts = lax.psum(jnp.sum(named.astype(jnp.float32), axis=0, keepdims=True), "gy")
    counts = jnp.broadcast_to(counts, (ROWS, LANES))
    w_first = jnp.pad(conv_first, ((0, 0), (0, 28 * NF - conv_first.shape[1])))
    w_second_t = conv_second.reshape(CH, 27, CH).transpose(2, 1, 0).reshape(CH, 27 * CH)
    w_third = jnp.pad(conv_third, ((0, 16 - NOUT), (0, 0)))
    w_third_t = w_third.T
    weights = (w_first, conv_second, w_second_t, w_third, w_third_t)

    z_own = faces[4]
    y_terms = pltpu.VMEM((2, NF, planes, lanes), jnp.float32)
    middle, *faces = pl.pallas_call(
        close_first,
        out_shape=[
            shape_of(*fields.shape),
            shape_of(NF, rows, lanes),
            shape_of(NF, rows, lanes),
            shape_of(NF, planes, lanes),
            shape_of(NF + 1, planes, lanes),
            shape_of(-(-NF * pairs // half), ROWS, LANES),
        ],
        in_specs=[VMEM] * 9,
        out_specs=[VMEM] * 6,
        scratch_shapes=[y_terms],
        compiler_params=PARAMS,
        name="close_first",
    )(fields, visc, without_border(fields, visc), *halo, z_own)
    later = exchange(*faces, sizes)

    count = samples.shape[0]
    slot_total = sizes["gy"] * CAP
    tiles = -(-27 * CH // LANES) + 1
    parts = devices_all // CH
    inline = parts == 1 and slot_total <= 12
    out_shape = [shape_of(*fields.shape), shape_of(CH, tiles, LANES, dtype=jnp.bfloat16)]
    if not inline:
        out_shape.append(shape_of(devices_all, 1, LANES, dtype=jnp.bfloat16))
    advanced, send, *slots = pl.pallas_call(
        functools.partial(second_step, sizes, inline),
        out_shape=out_shape,
        in_specs=[SMEM] * 2 + [VMEM] * 22,
        out_specs=[VMEM] * len(out_shape),
        scratch_shapes=[
            pltpu.VMEM((28 * NF, count * VOL), jnp.float32),
            pltpu.VMEM((27 * CH, count * VOL), jnp.bfloat16),
            pltpu.VMEM((CH, tiles, LANES), jnp.float32),
            y_terms,
        ],
        compiler_params=PARAMS,
        name="second_step",
    )(samples, trainers, middle, visc, without_border(middle, visc), *halo, z_own, *later, faces[4], counts, jnp.asarray(pick_rows(), jnp.bfloat16),
      *weights)

    if not inline:
        send = jnp.concatenate([send.reshape(devices_all, tiles // parts, LANES), slots[0]], 1)
    arrived = lax.all_to_all(send, axes, split_axis=0, concat_axis=0, tiled=True)
    if inline:
        where = (27 * CH // LANES, 27 * CH % LANES + ROWS)
    else:
        where = (send.shape[1] - 1, 0)
    spread, block_losses = pl.pallas_call(
        functools.partial(add_up, where),
        out_shape=[shape_of(*send.shape, dtype=jnp.bfloat16), shape_of(1, 1, 1, slot_total)],
        in_specs=[VMEM],
        out_specs=[VMEM] * 2,
        compiler_params=PARAMS,
        name="add_up",
    )(arrived)
    if not inline:
        spread = spread[:, :-1, :]
    gathered = lax.all_to_all(spread, axes, split_axis=0, concat_axis=0, tiled=True)
    first, second, third = pl.pallas_call(
        unpack,
        out_shape=[shape_of(*conv_first.shape), shape_of(*conv_second.shape), shape_of(*conv_third.shape)],
        in_specs=[VMEM],
        out_specs=[VMEM] * 3,
        scratch_shapes=[pltpu.VMEM((CH, tiles, LANES), jnp.float32)],
        compiler_params=PARAMS,
        name="unpack",
    )(gathered.reshape(CH, tiles, LANES))
    return advanced, block_losses, first, second, third


def solution(mesh):
    sizes = dict(mesh.shape)
    in_specs = (
        P(None, "gx", "gy", "gz"),
        P("gx", "gy", "gz"),
        P("gx", "gy", "gz", None),
        P("gx", "gy", "gz", None, None),
        P(),
        P(),
        P(),
    )
    out_specs = (P(None, "gx", "gy", "gz"), P("gx", "gy", "gz", None), P(), P(), P())
    return jax.shard_map(
        functools.partial(on_device, sizes), mesh=mesh, in_specs=in_specs, out_specs=out_specs,
        check_vma=False,
    )
```

```python
import functools

import jax
import jax.numpy as jnp
import numpy as np
from jax import lax
from jax.experimental import pallas as pl
from jax.experimental.pallas import tpu as pltpu
from jax.sharding import PartitionSpec as P

BLK = 4
CAP = 2
NF = 4
VOL = BLK**3
TAPS = [(x, y, z) for x in (-1, 0, 1) for y in (-1, 0, 1) for z in (-1, 0, 1)]
LANES = 128
ROWS = 8
NOUT = 6
CH = 32

time_step = 0.25
buoyancy = 0.5

VMEM = pl.BlockSpec(memory_space=pltpu.VMEM)
SMEM = pl.BlockSpec(memory_space=pltpu.SMEM)
HBM = pl.BlockSpec(memory_space=pltpu.HBM)
PARAMS = pltpu.CompilerParams(vmem_limit_bytes=24 * 1024 * 1024)
PACK = pltpu.CompilerParams(vmem_limit_bytes=60 * 1024 * 1024)
FULL = (((1,), (1,)), ((), ()))


def iota(shape, axis):
    return lax.broadcasted_iota(jnp.int32, shape, axis)


def pair_of(f, c, planes, chunks):
    span = 2 * planes * chunks
    return f * span // LANES, f * span % LANES + 2 * planes * c


def add_pair(packed, tile, lane):
    moved = pltpu.roll(tile, lane + 1, 1)
    at = iota(tile.shape, 1)
    return jnp.where((at == lane) | (at == lane + 1), moved, packed)


def counts_of(trainers_ref, count):
    at = iota((ROWS, LANES), 1)
    total = jnp.zeros((ROWS, LANES), jnp.float32)
    for j in range(count):
        total = total + jnp.where(at == trainers_ref[j], 1.0, 0.0)
    return total


def pack_faces(fields_far, visc_far, trainers, x_first, x_last, y_first, y_last, z_both, fields, visc, sems):
    _, planes, rows, _ = fields.shape
    chunks = rows // ROWS
    copies = [pltpu.make_async_copy(fields_far.at[f], fields.at[f], sems.at[f]) for f in range(NF)]
    copies.append(pltpu.make_async_copy(visc_far, visc, sems.at[NF]))
    for copy in copies:
        copy.start()
    counts = counts_of(trainers, trainers.shape[0])
    y_first[NF + 1] = counts
    y_last[NF + 1] = counts
    arrays = [fields.at[f] for f in range(NF)] + [visc]
    packed = [jnp.zeros((ROWS, LANES), jnp.float32) for _ in range(z_both.shape[0])]
    for f, array in enumerate(arrays):
        copies[f].wait()
        x_first[f] = array[0]
        x_last[f] = array[planes - 1]
        y_first[f] = array[:, 0, :]
        y_last[f] = array[:, rows - 1, :]
        for c in range(chunks):
            tile, lane = pair_of(f, c, planes, chunks)
            for x in range(planes):
                cells = array[x, ROWS * c : ROWS * c + ROWS]
                packed[tile] = add_pair(packed[tile], cells, lane + 2 * x)
    for tile, value in enumerate(packed):
        z_both[tile] = value


def flux(lower, upper, dimension):
    speed = 0.25 * (lower[dimension] + upper[dimension])
    mean_visc = 0.5 * (lower[NF] + upper[NF])
    return [speed * (a + b) - mean_visc * (b - a) for a, b in zip(lower[:NF], upper[:NF])]


def interior(fields, visc, partial):
    _, planes, rows, _ = fields.shape
    chunks = rows // ROWS
    end_row = iota((ROWS, LANES), 0) == ROWS - 1
    end_lane = iota((ROWS, LANES), 1) == LANES - 1
    every = range(NF + 1)

    def cell(f, x, part):
        return fields[f, x, part, :] if f < NF else visc[x, part, :]

    def plane(x, lowers):
        uppers = []
        last = x == planes - 1
        beyond = jnp.minimum(x + 1, planes - 1)
        behind = [jnp.zeros((ROWS, LANES), jnp.float32)] * NF
        for c in range(chunks):
            part = slice(ROWS * c, ROWS * c + ROWS)
            here = [cell(f, x, part) for f in every]
            after = [cell(f, beyond, part) for f in every]
            upper = flux(here, after, 0)
            upper = [jnp.where(last, 0.0, u) for u in upper]
            total = [b - a for a, b in zip(lowers[c], upper)]
            uppers.append(upper)
            above = [pltpu.roll(h, ROWS - 1, 0) for h in here]
            if c + 1 < chunks:
                first = slice(ROWS * c + ROWS, ROWS * c + ROWS + 1)
                above = [jnp.where(end_row, cell(f, x, first), above[f]) for f in every]
            upper = flux(here, above, 1)
            lower = [pltpu.roll(jnp.where(end_row, b, u), 1, 0) for b, u in zip(behind, upper)]
            if c + 1 == chunks:
                upper = [jnp.where(end_row, 0.0, u) for u in upper]
            behind = upper
            total = [t + (b - a) for t, a, b in zip(total, lower, upper)]
            right = [pltpu.roll(h, LANES - 1, 1) for h in here]
            upper = [jnp.where(end_lane, 0.0, u) for u in flux(here, right, 2)]
            lower = [pltpu.roll(u, 1, 1) for u in upper]
            total = [t + (b - a) for t, a, b in zip(total, lower, upper)]
            updated = [q - time_step * t for q, t in zip(here[:NF], total)]
            updated[2] = updated[2] + (time_step * buoyancy) * here[3]
            for f in range(NF):
                partial[f, x, part, :] = updated[f]
        return uppers

    zeros = [[jnp.zeros((ROWS, LANES), jnp.float32)] * NF for _ in range(chunks)]
    lax.fori_loop(0, planes, plane, zeros)


def interior_and_weights(samples, trainers, fields, visc, conv_first, conv_second, conv_third, partial,
                         w_first, w_second_t, w_third, w_third_t, drawn):
    at, row = iota((ROWS, LANES), 1), iota((ROWS, LANES), 0)
    table = jnp.zeros((ROWS, LANES), jnp.int32)
    for j in range(samples.shape[0]):
        table = jnp.where(at == j, jnp.where(row == 0, samples[j], trainers[j]), table)
    drawn[...] = table
    interior(fields, visc, partial)
    ahead = conv_first.shape[1]
    w_first[:, :ahead] = conv_first[...]
    w_first[:, ahead:] = jnp.zeros((CH, w_first.shape[1] - ahead), jnp.bfloat16)
    w_second_t[...] = conv_second[...].astype(jnp.float32).T.astype(jnp.bfloat16)
    third = conv_third[...].astype(jnp.float32)
    third = jnp.concatenate([third, jnp.zeros((w_third.shape[0] - NOUT, CH), jnp.float32)], 0)
    w_third[...] = third.astype(jnp.bfloat16)
    w_third_t[...] = third.T.astype(jnp.bfloat16)


def z_terms(own, other, visc_own, visc_other):
    lane = iota((ROWS, LANES), 1)
    second = lane % 2 == 1
    span = LANES // 2

    def ends(mine, theirs):
        lower = jnp.where(second, pltpu.roll(theirs, 1, 1), mine)
        return lower, jnp.where(second, mine, pltpu.roll(theirs, LANES - 1, 1))

    def twice(tile):
        return jnp.where(lane < span, tile, pltpu.roll(tile, span, 1))

    pairs = [ends(a, b) for a, b in zip(own, other)]
    speed = [twice(end) for end in pairs[2 * span // LANES]]
    visc = [twice(end) for end in ends(visc_own, visc_other)]
    speed = 0.25 * (speed[0] + speed[1])
    mean_visc = 0.5 * (visc[0] + visc[1])
    through = [speed * (a + b) - mean_visc * (b - a) for a, b in pairs]
    return [jnp.where(second, time_step, -time_step) * t for t in through]


def close(fields, visc, partial, halo, visc_halo, z_own, visc_z_own, y_terms, emit):
    _, planes, rows, _ = fields.shape
    chunks = rows // ROWS
    every = range(NF + 1)
    row = iota((ROWS, LANES), 0)
    lane_at = iota((ROWS, LANES), 1)
    ends = (lane_at == 0) | (lane_at == LANES - 1)

    def cell(f, *index):
        return fields[(f,) + index] if f < NF else visc[index]

    def face(f, which, *index):
        return (halo if f < NF else visc_halo)[which][(f,) + index]

    lower = flux([face(f, "y_prev") for f in every], [cell(f, slice(None), 0) for f in every], 1)
    upper = flux([cell(f, slice(None), rows - 1) for f in every], [face(f, "y_next") for f in every], 1)
    for f in range(NF):
        y_terms[0, f] = time_step * lower[f]
        y_terms[1, f] = -time_step * upper[f]
    tiles = z_own.shape[0] if z_own.shape[0] * LANES == 2 * NF * planes * chunks else z_own.shape[0] - 1
    terms = z_terms([z_own[t] for t in range(tiles)], [halo["z_both"][t] for t in range(tiles)],
                    visc_z_own[tiles], visc_halo["z_both"][tiles])
    for c in range(chunks):
        part = slice(ROWS * c, ROWS * c + ROWS)
        low = flux([face(f, "x_prev", part) for f in every], [cell(f, 0, part) for f in every], 0)
        high = flux([cell(f, planes - 1, part) for f in every], [face(f, "x_next", part) for f in every], 0)
        for x in range(planes):
            for f in range(NF):
                tile, lane = pair_of(f, c, planes, chunks)
                moved = pltpu.roll(terms[tile], LANES - 1 - lane - 2 * x, 1)
                value = partial[f, x, part, :] + jnp.where(ends, moved, 0.0)
                if x == 0:
                    value = value + time_step * low[f]
                if x == planes - 1:
                    value = value - time_step * high[f]
                if c == 0:
                    value = value + jnp.where(row == 0, y_terms[0, f, x : x + 1, :], 0.0)
                if c == chunks - 1:
                    value = value + jnp.where(row == ROWS - 1, y_terms[1, f, x : x + 1, :], 0.0)
                emit(f, x, c, value)


def halo_of(x_prev, x_next, y_prev, y_next, z_both):
    return dict(x_prev=x_prev, x_next=x_next, y_prev=y_prev, y_next=y_next, z_both=z_both)


def close_first(fields, visc, partial, x_prev, x_next, y_prev, y_next, z_other, z_own,
                middle, x_first, x_last, y_first, y_last, z_both, y_terms):
    _, planes, rows, _ = fields.shape
    chunks = rows // ROWS
    halo = halo_of(x_prev, x_next, y_prev, y_next, z_other)
    packed = [jnp.zeros((ROWS, LANES), jnp.float32) for _ in range(z_both.shape[0])]

    def emit(f, x, c, tile):
        middle[f, x, ROWS * c : ROWS * c + ROWS, :] = tile
        at, lane = pair_of(f, c, planes, chunks)
        packed[at] = add_pair(packed[at], tile, lane + 2 * x)

    close(fields, visc, partial, halo, halo, z_own, z_own, y_terms, emit)
    for at, value in enumerate(packed):
        z_both[at] = value
    x_first[...] = middle[:, 0]
    x_last[...] = middle[:, planes - 1]
    for f in range(NF):
        y_first[f] = middle[f, :, 0, :]
        y_last[f] = middle[f, :, rows - 1, :]
    y_last[NF] = y_prev[NF + 1]


def inside_masks():
    at = iota((1, LANES), 1) % VOL
    coords = (at // (BLK * BLK), at // BLK % BLK, at % BLK)
    along = []
    for coord in coords:
        along.append({
            -1: jnp.where(coord > 0, 1.0, 0.0),
            0: jnp.ones((1, LANES), jnp.float32),
            1: jnp.where(coord < BLK - 1, 1.0, 0.0),
        })
    return along


def move_of(tap):
    return tap[0] * BLK * BLK + tap[1] * BLK + tap[2]


def shifted(tile, tap, along):
    move = move_of(tap)
    if move == 0:
        return tile
    mask = along[0][tap[0]] * along[1][tap[1]] * along[2][tap[2]]
    return pltpu.roll(tile, (-move) % LANES, 1) * mask


def box(tile, along):
    for dimension, step in enumerate((BLK * BLK, BLK, 1)):
        ahead = pltpu.roll(tile, LANES - step, 1) * along[dimension][1]
        behind = pltpu.roll(tile, step, 1) * along[dimension][-1]
        tile = (behind + tile) + ahead
    return tile / 27.0


def sigmoid(values):
    return 1.0 / (1.0 + jnp.exp(-values))


def pick_blocks(advanced, samples, pick, count):
    _, _, rows, lanes = advanced.shape
    along_y, along_z = rows // BLK, lanes // BLK
    row = iota((ROWS, LANES), 0)
    lane_at = iota((ROWS, LANES), 1)
    out = []
    for j in range(0, count, 2):
        parts = [jnp.zeros((ROWS, LANES), jnp.float32) for _ in range(NF)]
        uppers = []
        for half in range(2):
            block = samples[j + half]
            block_x = block // (along_y * along_z)
            block_y = block // along_z % along_y
            block_z = block % along_z
            uppers.append(block_y % 2)
            start = pl.multiple_of(block_y // 2 * ROWS, ROWS)
            for x in range(BLK):
                turn = lax.rem(VOL * half + BLK * BLK * x - BLK * block_z + LANES, LANES)
                wanted = lane_at // BLK == (VOL * half + BLK * BLK * x) // BLK
                for f in range(NF):
                    tile = advanced[f, block_x * BLK + x, pl.ds(start, ROWS), :]
                    parts[f] = jnp.where(wanted, pltpu.roll(tile, turn, 1), parts[f])
        upper = jnp.where(lane_at < VOL, uppers[0], uppers[1])
        valid = row // BLK == upper
        for f in range(NF):
            for bit in (1, 2):
                moved = pltpu.roll(parts[f], BLK * bit, 1)
                parts[f] = jnp.where(row // bit % 2 == 1, moved, parts[f])
            parts[f] = jnp.where(valid, parts[f], 0.0)
        stacked = jnp.concatenate(parts, 0).astype(jnp.bfloat16)
        out.append(jnp.dot(pick, stacked, preferred_element_type=jnp.float32))
    return out


def closure(advanced, samples, trainers, counts, pick, w_first, w_second, w_second_t, w_third,
            w_third_t, devices_all, stack_first, stack_mid, rows_out, send, slots, inline, place):
    count = len(samples)
    pairs = count // 2
    cols = [slice(LANES * m, LANES * m + LANES) for m in range(pairs)]
    along = inside_masks()
    lane_at = iota((ROWS, LANES), 1)
    row = iota((ROWS, LANES), 0)

    picked = pick_blocks(advanced, samples, pick, count)
    values = [p[:ROWS] for p in picked]
    targets = []
    for p in picked:
        first, second = p[ROWS : 2 * ROWS], p[2 * ROWS : 3 * ROWS]
        targets.append(box(first * second, along) - box(first, along) * box(second, along))

    for m, tile in enumerate(values):
        for t in range(0, 28, 2):
            piece = shifted(tile, TAPS[t], along)
            later = shifted(tile, TAPS[t + 1], along) if t + 1 < 27 else jnp.zeros_like(tile)
            stack_first[BLK * t : BLK * t + ROWS, cols[m]] = jnp.where(row < NF, piece, later)
    stack_in = stack_first[...].astype(jnp.bfloat16)
    pre_first = jnp.dot(w_first, stack_in, preferred_element_type=jnp.float32)
    gate_first = sigmoid(pre_first)
    hidden_first = (pre_first * gate_first).astype(jnp.bfloat16).astype(jnp.float32)
    for m in range(pairs):
        tile = hidden_first[:, cols[m]]
        for k, tap in enumerate(TAPS):
            stack_mid[CH * k : CH * k + CH, cols[m]] = shifted(tile, tap, along).astype(jnp.bfloat16)
    pre_second = jnp.dot(w_second, stack_mid[...], preferred_element_type=jnp.float32)
    gate_second = sigmoid(pre_second)
    hidden_second = (pre_second * gate_second).astype(jnp.bfloat16)
    predicted = jnp.dot(w_third, hidden_second, preferred_element_type=jnp.float32)

    misfit = predicted[:ROWS] - jnp.concatenate(targets, 1)
    square = jnp.sum(misfit * misfit, axis=0, keepdims=True)
    sample_at = iota((ROWS, count * VOL), 1) // VOL
    mine = sample_at == iota((ROWS, count * VOL), 0)
    losses = jnp.sum(jnp.where(mine, square, 0.0), axis=1, keepdims=True) / (NOUT * VOL)
    owner = jnp.zeros((ROWS, LANES), jnp.int32)
    for j in range(count):
        owner = jnp.where(row == j, trainers[j], owner)
    load = jnp.sum(jnp.where(lane_at == owner, counts, 0.0), axis=1, keepdims=True)
    share = 1.0 / (devices_all * jnp.maximum(load, 1.0))
    scale = share * (2.0 / (NOUT * VOL))
    scale_at = jnp.sum(jnp.where(mine, scale, 0.0), axis=0, keepdims=True)
    grad_pred = (misfit * scale_at).astype(jnp.bfloat16)
    grad_pred = jnp.concatenate([grad_pred, jnp.zeros_like(grad_pred)], 0)

    upper = jnp.dot(w_third_t, grad_pred, preferred_element_type=jnp.float32)
    slope = gate_second * (1.0 + pre_second * (1.0 - gate_second))
    grad_mid = (upper * slope).astype(jnp.bfloat16)
    grad_second = lax.dot_general(grad_mid, stack_mid[...], FULL, preferred_element_type=jnp.float32)
    third = jnp.concatenate([grad_pred, jnp.zeros((LANES - 16, count * VOL), jnp.bfloat16)], 0)
    grad_third = lax.dot_general(hidden_second, third, FULL, preferred_element_type=jnp.float32)

    spread = jnp.dot(w_second_t, grad_mid, preferred_element_type=jnp.float32)
    lower = []
    for m in range(pairs):
        terms = [
            shifted(spread[CH * k : CH * k + CH, cols[m]], tuple(-o for o in tap), along)
            for k, tap in enumerate(TAPS)
        ]
        lower.append(functools.reduce(jnp.add, terms))
    lower = jnp.concatenate(lower, 1)
    slope = gate_first * (1.0 + pre_first * (1.0 - gate_first))
    grad_entry = (lower * slope).astype(jnp.bfloat16)
    grad_first = lax.dot_general(grad_entry, stack_in, FULL, preferred_element_type=jnp.float32)

    whole = CH * 27 // LANES
    rest = CH * 27 - whole * LANES
    for t in range(whole):
        rows_out[:, t, :] = grad_second[:, LANES * t : LANES * t + LANES]
    mixed = jnp.concatenate([grad_second[:, whole * LANES :], jnp.zeros((CH, LANES - rest), jnp.float32)], 1)
    mixed = mixed + pltpu.roll(grad_third, rest, 1)
    tail = LANES - grad_first.shape[1]
    rows_out[:, whole + 1, :] = jnp.concatenate([grad_first, jnp.zeros((CH, tail), jnp.float32)], 1)

    pos_x, pos_y, pos_z, count_y, count_z = place
    offset = rest + ROWS if inline else 0
    height = CH if inline else slots.shape[0]
    slot_rows = iota((height, LANES), 0)
    slot_lanes = iota((height, LANES), 1)
    placed = jnp.zeros((height, LANES), jnp.float32)
    for j in range(count):
        name = trainers[j]
        rank = jnp.int32(0)
        for i in range(j):
            rank = rank + jnp.where(trainers[i] == name, 1, 0)
        target = (pos_x * count_y + name) * count_z + pos_z
        slot = offset + pos_y * CAP + rank
        hit = (slot_rows == target) & (slot_lanes == slot)
        placed = jnp.where(hit, losses[j : j + 1, :], placed)
    high = placed.astype(jnp.bfloat16).astype(jnp.float32)
    placed = high + pltpu.roll(placed - high, count_y * CAP, 1)
    if inline:
        mixed = mixed + placed
    else:
        slots[:, 0, :] = placed.astype(jnp.bfloat16)
    rows_out[:, whole, :] = mixed
    send[...] = rows_out[...].astype(jnp.bfloat16)


def second_step(sizes, inline, drawn, middle, visc, partial, vx_prev, vx_next, vy_prev,
                vy_next, vz_other, vz_own, x_prev, x_next, y_prev, y_next, z_other, z_own, *rest):
    counts = None if sizes["gy"] == 4 else rest[0]
    rest = rest if counts is None else rest[1:]
    pick, w_first, w_second, w_second_t, w_third, w_third_t, advanced, send = rest[:8]
    slots = None if inline else rest[8]
    stack_first, stack_mid, rows_out, y_terms = rest[-4:]
    halo = halo_of(x_prev, x_next, y_prev, y_next, z_other)
    visc_halo = halo_of(vx_prev, vx_next, vy_prev, vy_next, vz_other)
    count = stack_mid.shape[1] // VOL
    samples = [drawn[0, j] for j in range(count)]
    trainers = [drawn[1, j] for j in range(count)]

    def emit(f, x, c, tile):
        advanced[f, x, ROWS * c : ROWS * c + ROWS, :] = tile

    close(middle, visc, partial, halo, visc_halo, z_own, vz_own, y_terms, emit)
    if counts is None:
        total = counts_of(trainers, count) + vy_prev[NF + 1] + vy_next[NF + 1] + y_prev[NF]
    else:
        total = counts[...]
    place = (lax.axis_index("gx"), lax.axis_index("gy"), lax.axis_index("gz"), sizes["gy"], sizes["gz"])
    closure(advanced, samples, trainers, total, pick[...], w_first[...], w_second[...],
            w_second_t[...], w_third[...], w_third_t[...],
            float(sizes["gx"] * sizes["gy"] * sizes["gz"]), stack_first, stack_mid, rows_out,
            send, slots, inline, place)


def add_up(where, arrived, spread, losses):
    total = jnp.sum(arrived[...].astype(jnp.float32), axis=0)
    row, lane = where
    count = losses.shape[3]
    high = total[row : row + 1, lane : lane + count]
    losses[0, 0] = high + total[row : row + 1, lane + count : lane + 2 * count]
    rounded = total.astype(jnp.bfloat16)
    for i in range(spread.shape[0]):
        spread[i] = rounded


def unpack(gathered, first, second, third, wide):
    wide[...] = gathered[...].astype(jnp.float32)
    whole = second.shape[1] // LANES
    rest = second.shape[1] - whole * LANES
    for t in range(whole):
        second[:, LANES * t : LANES * t + LANES] = wide[:, t, :]
    mixed = wide[:, whole, :]
    second[:, LANES * whole :] = mixed[:, :rest]
    third[...] = mixed[:, rest : rest + ROWS].T[:NOUT]
    first[...] = wide[:, whole + 1, :][:, : first.shape[1]]


def pick_rows():
    wanted = [0, 1, 2, 3, 0, 1, 2, 3, 0, 1, 2, 0, 0, 1, -1, -1, 0, 1, 2, 1, 2, 2, -1, -1]
    table = np.zeros((32, NF * ROWS), np.float32)
    for i, f in enumerate(wanted):
        if f >= 0:
            table[i, f * ROWS : f * ROWS + ROWS] = 1.0
    return table


def shape_of(*dims, dtype=jnp.float32):
    return jax.ShapeDtypeStruct(dims, dtype)


def exchange(x_first, x_last, y_first, y_last, z_both, sizes):
    def ring(axis, step):
        count = sizes[axis]
        return [(i, (i + step) % count) for i in range(count)]

    x_prev = lax.ppermute(x_last, "gx", ring("gx", 1))
    x_next = lax.ppermute(x_first, "gx", ring("gx", -1))
    y_prev = lax.ppermute(y_last, "gy", ring("gy", 1))
    y_next = lax.ppermute(y_first, "gy", ring("gy", -1))
    z_other = lax.ppermute(z_both, "gz", ring("gz", 1))
    return x_prev, x_next, y_prev, y_next, z_other


def without_border(kernel, fields, visc, index=(), weights=()):
    cells = visc.size
    out_shape = [shape_of(*fields.shape)]
    if weights:
        sizes = ((CH, 28 * NF), (27 * CH, CH), (16, CH), (CH, 16))
        out_shape += [shape_of(*size, dtype=jnp.bfloat16) for size in sizes]
        out_shape.append(shape_of(ROWS, LANES, dtype=jnp.int32))
    return pl.pallas_call(
        kernel,
        out_shape=out_shape,
        in_specs=[SMEM] * len(index) + [VMEM] * (2 + len(weights)),
        out_specs=[VMEM] * len(out_shape),
        compiler_params=PARAMS,
        cost_estimate=pl.CostEstimate(flops=120 * cells, bytes_accessed=36 * cells, transcendentals=0),
        name=kernel.__name__,
    )(*index, fields, visc, *weights)


def on_device(sizes, fields, visc, samples, trainers, conv_first, conv_second, conv_third):
    _, planes, rows, lanes = fields.shape
    axes = ("gx", "gy", "gz")
    devices_all = sizes["gx"] * sizes["gy"] * sizes["gz"]
    pairs = planes * rows // ROWS
    half = LANES // 2
    samples = samples.reshape(-1)
    trainers = trainers.reshape(-1)

    faces = pl.pallas_call(
        pack_faces,
        out_shape=[
            shape_of(NF + 1, rows, lanes),
            shape_of(NF + 1, rows, lanes),
            shape_of(NF + 2, planes, lanes),
            shape_of(NF + 2, planes, lanes),
            shape_of(-(-(NF + 1) * pairs // half), ROWS, LANES),
        ],
        in_specs=[HBM, HBM, SMEM],
        out_specs=[VMEM] * 5,
        scratch_shapes=[
            pltpu.VMEM(fields.shape, jnp.float32),
            pltpu.VMEM(visc.shape, jnp.float32),
            pltpu.SemaphoreType.DMA((NF + 1,)),
        ],
        compiler_params=PACK,
        name="pack_faces",
    )(fields, visc, trainers)
    halo = exchange(*faces, sizes)

    own_counts = sizes["gy"] == 4
    counts = []
    if not own_counts:
        named = trainers.reshape(-1, 1) == jnp.arange(LANES, dtype=jnp.int32)[None, :]
        total = lax.psum(jnp.sum(named.astype(jnp.float32), axis=0, keepdims=True), "gy")
        counts = [jnp.broadcast_to(total, (ROWS, LANES))]
    z_own = faces[4]
    y_terms = pltpu.VMEM((2, NF, planes, lanes), jnp.float32)
    middle, *faces = pl.pallas_call(
        close_first,
        out_shape=[
            shape_of(*fields.shape),
            shape_of(NF, rows, lanes),
            shape_of(NF, rows, lanes),
            shape_of(NF, planes, lanes),
            shape_of(NF + 1, planes, lanes),
            shape_of(-(-NF * pairs // half), ROWS, LANES),
        ],
        in_specs=[VMEM] * 9,
        out_specs=[VMEM] * 6,
        scratch_shapes=[y_terms],
        compiler_params=PARAMS,
        name="close_first",
    )(fields, visc, *without_border(interior, fields, visc), *halo, z_own)
    later = exchange(*faces, sizes)
    partial, w_first, w_second_t, w_third, w_third_t, drawn = without_border(
        interior_and_weights, middle, visc, (samples, trainers), (conv_first, conv_second, conv_third)
    )

    count = samples.shape[0]
    slot_total = sizes["gy"] * CAP
    tiles = -(-27 * CH // LANES) + 1
    parts = devices_all // CH
    inline = parts == 1 and slot_total <= 12
    out_shape = [shape_of(*fields.shape), shape_of(CH, tiles, LANES, dtype=jnp.bfloat16)]
    if not inline:
        out_shape.append(shape_of(devices_all, 1, LANES, dtype=jnp.bfloat16))
    advanced, send, *slots = pl.pallas_call(
        functools.partial(second_step, sizes, inline),
        out_shape=out_shape,
        in_specs=[VMEM] * (22 if own_counts else 23),
        out_specs=[VMEM] * len(out_shape),
        scratch_shapes=[
            pltpu.VMEM((28 * NF, count * VOL), jnp.float32),
            pltpu.VMEM((27 * CH, count * VOL), jnp.bfloat16),
            pltpu.VMEM((CH, tiles, LANES), jnp.float32),
            y_terms,
        ],
        compiler_params=PARAMS,
        name="second_step",
    )(drawn, middle, visc, partial, *halo, z_own, *later, faces[4], *counts, jnp.asarray(pick_rows(), jnp.bfloat16),
      w_first, conv_second, w_second_t, w_third, w_third_t)

    if not inline:
        send = jnp.concatenate([send.reshape(devices_all, tiles // parts, LANES), slots[0]], 1)
    arrived = lax.all_to_all(send, axes, split_axis=0, concat_axis=0, tiled=True)
    if inline:
        where = (27 * CH // LANES, 27 * CH % LANES + ROWS)
    else:
        where = (send.shape[1] - 1, 0)
    spread, block_losses = pl.pallas_call(
        functools.partial(add_up, where),
        out_shape=[shape_of(*send.shape, dtype=jnp.bfloat16), shape_of(1, 1, 1, slot_total)],
        in_specs=[VMEM],
        out_specs=[VMEM] * 2,
        compiler_params=PARAMS,
        name="add_up",
    )(arrived)
    if not inline:
        spread = spread[:, :-1, :]
    gathered = lax.all_to_all(spread, axes, split_axis=0, concat_axis=0, tiled=True)
    first, second, third = pl.pallas_call(
        unpack,
        out_shape=[shape_of(*conv_first.shape), shape_of(*conv_second.shape), shape_of(*conv_third.shape)],
        in_specs=[VMEM],
        out_specs=[VMEM] * 3,
        scratch_shapes=[pltpu.VMEM((CH, tiles, LANES), jnp.float32)],
        compiler_params=PARAMS,
        name="unpack",
    )(gathered.reshape(CH, tiles, LANES))
    return advanced, block_losses, first, second, third


def solution(mesh):
    sizes = dict(mesh.shape)
    in_specs = (
        P(None, "gx", "gy", "gz"),
        P("gx", "gy", "gz"),
        P("gx", "gy", "gz", None),
        P("gx", "gy", "gz", None, None),
        P(),
        P(),
        P(),
    )
    out_specs = (P(None, "gx", "gy", "gz"), P("gx", "gy", "gz", None), P(), P(), P())
    return jax.shard_map(
        functools.partial(on_device, sizes), mesh=mesh, in_specs=in_specs, out_specs=out_specs,
        check_vma=False,
    )
```

```python
import functools

import jax
import jax.numpy as jnp
from jax import lax
from jax.experimental import pallas as pl
from jax.experimental.pallas import tpu as pltpu
from jax.sharding import PartitionSpec as P

BLK = 4
CAP = 2
NF = 4
VOL = BLK**3
TAPS = [(x, y, z) for x in (-1, 0, 1) for y in (-1, 0, 1) for z in (-1, 0, 1)]
LANES = 128
ROWS = 8
NOUT = 6
CH = 32

time_step = 0.25
buoyancy = 0.5

VMEM = pl.BlockSpec(memory_space=pltpu.VMEM)
SMEM = pl.BlockSpec(memory_space=pltpu.SMEM)
HBM = pl.BlockSpec(memory_space=pltpu.HBM)
PARAMS = pltpu.CompilerParams(vmem_limit_bytes=24 * 1024 * 1024)
PACK = pltpu.CompilerParams(vmem_limit_bytes=60 * 1024 * 1024)
FULL = (((1,), (1,)), ((), ()))


def iota(shape, axis):
    return lax.broadcasted_iota(jnp.int32, shape, axis)


def pair_of(f, c, planes, chunks):
    span = 2 * planes * chunks
    return f * span // LANES, f * span % LANES + 2 * planes * c


def add_pair(packed, tile, lane):
    moved = pltpu.roll(tile, lane + 1, 1)
    at = iota(tile.shape, 1)
    return jnp.where((at == lane) | (at == lane + 1), moved, packed)


def counts_of(trainers_ref, count):
    at = iota((ROWS, LANES), 1)
    total = jnp.zeros((ROWS, LANES), jnp.float32)
    for j in range(count):
        total = total + jnp.where(at == trainers_ref[j], 1.0, 0.0)
    return total


def pack_faces(fields_far, visc_far, trainers, x_first, x_last, y_first, y_last, z_both, fields, visc, sems):
    _, planes, rows, _ = fields.shape
    chunks = rows // ROWS
    copies = [pltpu.make_async_copy(fields_far.at[f], fields.at[f], sems.at[f]) for f in range(NF)]
    copies.append(pltpu.make_async_copy(visc_far, visc, sems.at[NF]))
    for copy in copies:
        copy.start()
    counts = counts_of(trainers, trainers.shape[0])
    y_first[NF + 1] = counts
    y_last[NF + 1] = counts
    arrays = [fields.at[f] for f in range(NF)] + [visc]
    packed = [jnp.zeros((ROWS, LANES), jnp.float32) for _ in range(z_both.shape[0])]
    for f, array in enumerate(arrays):
        copies[f].wait()
        x_first[f] = array[0]
        x_last[f] = array[planes - 1]
        y_first[f] = array[:, 0, :]
        y_last[f] = array[:, rows - 1, :]
        for c in range(chunks):
            tile, lane = pair_of(f, c, planes, chunks)
            for x in range(planes):
                cells = array[x, ROWS * c : ROWS * c + ROWS]
                packed[tile] = add_pair(packed[tile], cells, lane + 2 * x)
    for tile, value in enumerate(packed):
        z_both[tile] = value


def flux(lower, upper, dimension):
    speed = 0.25 * (lower[dimension] + upper[dimension])
    mean_visc = 0.5 * (lower[NF] + upper[NF])
    return [speed * (a + b) - mean_visc * (b - a) for a, b in zip(lower[:NF], upper[:NF])]


def interior(fields, visc, partial):
    _, planes, rows, _ = fields.shape
    chunks = rows // ROWS
    end_row = iota((ROWS, LANES), 0) == ROWS - 1
    end_lane = iota((ROWS, LANES), 1) == LANES - 1
    every = range(NF + 1)

    def cell(f, x, part):
        return fields[f, x, part, :] if f < NF else visc[x, part, :]

    def plane(x, lowers):
        uppers = []
        last = x == planes - 1
        beyond = jnp.minimum(x + 1, planes - 1)
        behind = [jnp.zeros((ROWS, LANES), jnp.float32)] * NF
        for c in range(chunks):
            part = slice(ROWS * c, ROWS * c + ROWS)
            here = [cell(f, x, part) for f in every]
            after = [cell(f, beyond, part) for f in every]
            upper = flux(here, after, 0)
            upper = [jnp.where(last, 0.0, u) for u in upper]
            total = [b - a for a, b in zip(lowers[c], upper)]
            uppers.append(upper)
            above = [pltpu.roll(h, ROWS - 1, 0) for h in here]
            if c + 1 < chunks:
                first = slice(ROWS * c + ROWS, ROWS * c + ROWS + 1)
                above = [jnp.where(end_row, cell(f, x, first), above[f]) for f in every]
            upper = flux(here, above, 1)
            lower = [pltpu.roll(jnp.where(end_row, b, u), 1, 0) for b, u in zip(behind, upper)]
            if c + 1 == chunks:
                upper = [jnp.where(end_row, 0.0, u) for u in upper]
            behind = upper
            total = [t + (b - a) for t, a, b in zip(total, lower, upper)]
            right = [pltpu.roll(h, LANES - 1, 1) for h in here]
            upper = [jnp.where(end_lane, 0.0, u) for u in flux(here, right, 2)]
            lower = [pltpu.roll(u, 1, 1) for u in upper]
            total = [t + (b - a) for t, a, b in zip(total, lower, upper)]
            updated = [q - time_step * t for q, t in zip(here[:NF], total)]
            updated[2] = updated[2] + (time_step * buoyancy) * here[3]
            for f in range(NF):
                partial[f, x, part, :] = updated[f]
        return uppers

    zeros = [[jnp.zeros((ROWS, LANES), jnp.float32)] * NF for _ in range(chunks)]
    lax.fori_loop(0, planes, plane, zeros)


def interior_and_weights(samples, trainers, fields, visc, conv_first, conv_second, conv_third, partial,
                         w_first, w_second_t, w_third, w_third_t, drawn):
    at, row = iota((ROWS, LANES), 1), iota((ROWS, LANES), 0)
    table = jnp.zeros((ROWS, LANES), jnp.int32)
    for j in range(samples.shape[0]):
        table = jnp.where(at == j, jnp.where(row == 0, samples[j], trainers[j]), table)
    drawn[...] = table
    interior(fields, visc, partial)
    ahead = conv_first.shape[1]
    w_first[:, :ahead] = conv_first[...]
    w_first[:, ahead:] = jnp.zeros((CH, w_first.shape[1] - ahead), jnp.bfloat16)
    w_second_t[...] = conv_second[...].astype(jnp.float32).T.astype(jnp.bfloat16)
    third = conv_third[...].astype(jnp.float32)
    third = jnp.concatenate([third, jnp.zeros((w_third.shape[0] - NOUT, CH), jnp.float32)], 0)
    w_third[...] = third.astype(jnp.bfloat16)
    w_third_t[...] = third.T.astype(jnp.bfloat16)


def z_terms(own, other, visc_own, visc_other):
    lane = iota((ROWS, LANES), 1)
    second = lane % 2 == 1
    span = LANES // 2

    def ends(mine, theirs):
        lower = jnp.where(second, pltpu.roll(theirs, 1, 1), mine)
        return lower, jnp.where(second, mine, pltpu.roll(theirs, LANES - 1, 1))

    def twice(tile):
        return jnp.where(lane < span, tile, pltpu.roll(tile, span, 1))

    pairs = [ends(a, b) for a, b in zip(own, other)]
    speed = [twice(end) for end in pairs[2 * span // LANES]]
    visc = [twice(end) for end in ends(visc_own, visc_other)]
    speed = 0.25 * (speed[0] + speed[1])
    mean_visc = 0.5 * (visc[0] + visc[1])
    through = [speed * (a + b) - mean_visc * (b - a) for a, b in pairs]
    return [jnp.where(second, time_step, -time_step) * t for t in through]


def close(fields, visc, partial, halo, visc_halo, z_own, visc_z_own, y_terms, emit):
    _, planes, rows, _ = fields.shape
    chunks = rows // ROWS
    every = range(NF + 1)
    row = iota((ROWS, LANES), 0)
    lane_at = iota((ROWS, LANES), 1)
    ends = (lane_at == 0) | (lane_at == LANES - 1)

    def cell(f, *index):
        return fields[(f,) + index] if f < NF else visc[index]

    def face(f, which, *index):
        return (halo if f < NF else visc_halo)[which][(f,) + index]

    lower = flux([face(f, "y_prev") for f in every], [cell(f, slice(None), 0) for f in every], 1)
    upper = flux([cell(f, slice(None), rows - 1) for f in every], [face(f, "y_next") for f in every], 1)
    for f in range(NF):
        y_terms[0, f] = time_step * lower[f]
        y_terms[1, f] = -time_step * upper[f]
    tiles = z_own.shape[0] if z_own.shape[0] * LANES == 2 * NF * planes * chunks else z_own.shape[0] - 1
    terms = z_terms([z_own[t] for t in range(tiles)], [halo["z_both"][t] for t in range(tiles)],
                    visc_z_own[tiles], visc_halo["z_both"][tiles])
    for c in range(chunks):
        part = slice(ROWS * c, ROWS * c + ROWS)
        low = flux([face(f, "x_prev", part) for f in every], [cell(f, 0, part) for f in every], 0)
        high = flux([cell(f, planes - 1, part) for f in every], [face(f, "x_next", part) for f in every], 0)
        for x in range(planes):
            for f in range(NF):
                tile, lane = pair_of(f, c, planes, chunks)
                moved = pltpu.roll(terms[tile], LANES - 1 - lane - 2 * x, 1)
                value = partial[f, x, part, :] + jnp.where(ends, moved, 0.0)
                if x == 0:
                    value = value + time_step * low[f]
                if x == planes - 1:
                    value = value - time_step * high[f]
                if c == 0:
                    value = value + jnp.where(row == 0, y_terms[0, f, x : x + 1, :], 0.0)
                if c == chunks - 1:
                    value = value + jnp.where(row == ROWS - 1, y_terms[1, f, x : x + 1, :], 0.0)
                emit(f, x, c, value)


def halo_of(x_prev, x_next, y_prev, y_next, z_both):
    return dict(x_prev=x_prev, x_next=x_next, y_prev=y_prev, y_next=y_next, z_both=z_both)


def close_first(fields, visc, partial, x_prev, x_next, y_prev, y_next, z_other, z_own,
                middle, x_first, x_last, y_first, y_last, z_both, y_terms):
    _, planes, rows, _ = fields.shape
    chunks = rows // ROWS
    halo = halo_of(x_prev, x_next, y_prev, y_next, z_other)
    packed = [jnp.zeros((ROWS, LANES), jnp.float32) for _ in range(z_both.shape[0])]

    def emit(f, x, c, tile):
        middle[f, x, ROWS * c : ROWS * c + ROWS, :] = tile
        at, lane = pair_of(f, c, planes, chunks)
        packed[at] = add_pair(packed[at], tile, lane + 2 * x)

    close(fields, visc, partial, halo, halo, z_own, z_own, y_terms, emit)
    for at, value in enumerate(packed):
        z_both[at] = value
    x_first[...] = middle[:, 0]
    x_last[...] = middle[:, planes - 1]
    for f in range(NF):
        y_first[f] = middle[f, :, 0, :]
        y_last[f] = middle[f, :, rows - 1, :]
    y_last[NF] = y_prev[NF + 1]


def inside_masks():
    at = iota((1, LANES), 1) % VOL
    coords = (at // (BLK * BLK), at // BLK % BLK, at % BLK)
    along = []
    for coord in coords:
        along.append({
            -1: jnp.where(coord > 0, 1.0, 0.0),
            0: jnp.ones((1, LANES), jnp.float32),
            1: jnp.where(coord < BLK - 1, 1.0, 0.0),
        })
    return along


def move_of(tap):
    return tap[0] * BLK * BLK + tap[1] * BLK + tap[2]


def shifted(tile, tap, along):
    move = move_of(tap)
    if move == 0:
        return tile
    mask = along[0][tap[0]] * along[1][tap[1]] * along[2][tap[2]]
    return pltpu.roll(tile, (-move) % LANES, 1) * mask


def box(tile, along):
    for dimension, step in enumerate((BLK * BLK, BLK, 1)):
        ahead = pltpu.roll(tile, LANES - step, 1) * along[dimension][1]
        behind = pltpu.roll(tile, step, 1) * along[dimension][-1]
        tile = (behind + tile) + ahead
    return tile / 27.0


def sigmoid(values):
    return 1.0 / (1.0 + jnp.exp(-values))


PICKED = (0, 1, 2, 3, 0, 1, 2, 3, 0, 1, 2, 0, 0, 1, -1, -1, 0, 1, 2, 1, 2, 2, -1, -1)


def pick_rows():
    out, field = iota((32, NF * ROWS), 0), iota((32, NF * ROWS), 1) // ROWS
    table = jnp.zeros((32, NF * ROWS), jnp.float32)
    for i, f in enumerate(PICKED):
        table = jnp.where((out == i) & (field == f), 1.0, table)
    return table.astype(jnp.bfloat16)


def pick_blocks(advanced, samples, count):
    _, _, rows, lanes = advanced.shape
    along_y, along_z = rows // BLK, lanes // BLK
    row = iota((ROWS, LANES), 0)
    lane_at = iota((ROWS, LANES), 1)
    pick = pick_rows()
    out = []
    for j in range(0, count, 2):
        parts = [jnp.zeros((ROWS, LANES), jnp.float32) for _ in range(NF)]
        uppers = []
        for half in range(2):
            block = samples[j + half]
            block_x = block // (along_y * along_z)
            block_y = block // along_z % along_y
            block_z = block % along_z
            uppers.append(block_y % 2)
            start = pl.multiple_of(block_y // 2 * ROWS, ROWS)
            for x in range(BLK):
                turn = lax.rem(VOL * half + BLK * BLK * x - BLK * block_z + LANES, LANES)
                wanted = lane_at // BLK == (VOL * half + BLK * BLK * x) // BLK
                for f in range(NF):
                    tile = advanced[f, block_x * BLK + x, pl.ds(start, ROWS), :]
                    parts[f] = jnp.where(wanted, pltpu.roll(tile, turn, 1), parts[f])
        upper = jnp.where(lane_at < VOL, uppers[0], uppers[1])
        valid = row // BLK == upper
        for f in range(NF):
            for bit in (1, 2):
                moved = pltpu.roll(parts[f], BLK * bit, 1)
                parts[f] = jnp.where(row // bit % 2 == 1, moved, parts[f])
            parts[f] = jnp.where(valid, parts[f], 0.0)
        stacked = jnp.concatenate(parts, 0).astype(jnp.bfloat16)
        out.append(jnp.dot(pick, stacked, preferred_element_type=jnp.float32))
    return out


def closure(advanced, samples, trainers, counts, w_first, w_second, w_second_t, w_third,
            w_third_t, devices_all, stack_first, stack_mid, rows_out, send, slots, inline, place):
    count = len(samples)
    pairs = count // 2
    cols = [slice(LANES * m, LANES * m + LANES) for m in range(pairs)]
    along = inside_masks()
    lane_at = iota((ROWS, LANES), 1)
    row = iota((ROWS, LANES), 0)

    picked = pick_blocks(advanced, samples, count)
    values = [p[:ROWS] for p in picked]
    targets = []
    for p in picked:
        first, second = p[ROWS : 2 * ROWS], p[2 * ROWS : 3 * ROWS]
        targets.append(box(first * second, along) - box(first, along) * box(second, along))

    for m, tile in enumerate(values):
        for t in range(0, 28, 2):
            piece = shifted(tile, TAPS[t], along)
            later = shifted(tile, TAPS[t + 1], along) if t + 1 < 27 else jnp.zeros_like(tile)
            stack_first[BLK * t : BLK * t + ROWS, cols[m]] = jnp.where(row < NF, piece, later)
    stack_in = stack_first[...].astype(jnp.bfloat16)
    pre_first = jnp.dot(w_first, stack_in, preferred_element_type=jnp.float32)
    gate_first = sigmoid(pre_first)
    hidden_first = (pre_first * gate_first).astype(jnp.bfloat16).astype(jnp.float32)
    for m in range(pairs):
        tile = hidden_first[:, cols[m]]
        for k, tap in enumerate(TAPS):
            stack_mid[CH * k : CH * k + CH, cols[m]] = shifted(tile, tap, along).astype(jnp.bfloat16)
    pre_second = jnp.dot(w_second, stack_mid[...], preferred_element_type=jnp.float32)
    gate_second = sigmoid(pre_second)
    hidden_second = (pre_second * gate_second).astype(jnp.bfloat16)
    predicted = jnp.dot(w_third, hidden_second, preferred_element_type=jnp.float32)

    misfit = predicted[:ROWS] - jnp.concatenate(targets, 1)
    square = jnp.sum(misfit * misfit, axis=0, keepdims=True)
    sample_at = iota((ROWS, count * VOL), 1) // VOL
    mine = sample_at == iota((ROWS, count * VOL), 0)
    losses = jnp.sum(jnp.where(mine, square, 0.0), axis=1, keepdims=True) / (NOUT * VOL)
    owner = jnp.zeros((ROWS, LANES), jnp.int32)
    for j in range(count):
        owner = jnp.where(row == j, trainers[j], owner)
    load = jnp.sum(jnp.where(lane_at == owner, counts, 0.0), axis=1, keepdims=True)
    share = 1.0 / (devices_all * jnp.maximum(load, 1.0))
    scale = share * (2.0 / (NOUT * VOL))
    scale_at = jnp.sum(jnp.where(mine, scale, 0.0), axis=0, keepdims=True)
    grad_pred = (misfit * scale_at).astype(jnp.bfloat16)
    grad_pred = jnp.concatenate([grad_pred, jnp.zeros_like(grad_pred)], 0)

    upper = jnp.dot(w_third_t, grad_pred, preferred_element_type=jnp.float32)
    slope = gate_second * (1.0 + pre_second * (1.0 - gate_second))
    grad_mid = (upper * slope).astype(jnp.bfloat16)
    grad_second = lax.dot_general(grad_mid, stack_mid[...], FULL, preferred_element_type=jnp.float32)
    third = jnp.concatenate([grad_pred, jnp.zeros((LANES - 16, count * VOL), jnp.bfloat16)], 0)
    grad_third = lax.dot_general(hidden_second, third, FULL, preferred_element_type=jnp.float32)

    spread = jnp.dot(w_second_t, grad_mid, preferred_element_type=jnp.float32)
    lower = []
    for m in range(pairs):
        terms = [
            shifted(spread[CH * k : CH * k + CH, cols[m]], tuple(-o for o in tap), along)
            for k, tap in enumerate(TAPS)
        ]
        lower.append(functools.reduce(jnp.add, terms))
    lower = jnp.concatenate(lower, 1)
    slope = gate_first * (1.0 + pre_first * (1.0 - gate_first))
    grad_entry = (lower * slope).astype(jnp.bfloat16)
    grad_first = lax.dot_general(grad_entry, stack_in, FULL, preferred_element_type=jnp.float32)

    whole = CH * 27 // LANES
    rest = CH * 27 - whole * LANES
    for t in range(whole):
        rows_out[:, t, :] = grad_second[:, LANES * t : LANES * t + LANES]
    mixed = jnp.concatenate([grad_second[:, whole * LANES :], jnp.zeros((CH, LANES - rest), jnp.float32)], 1)
    mixed = mixed + pltpu.roll(grad_third, rest, 1)
    tail = LANES - grad_first.shape[1]
    rows_out[:, whole + 1, :] = jnp.concatenate([grad_first, jnp.zeros((CH, tail), jnp.float32)], 1)

    pos_x, pos_y, pos_z, count_y, count_z = place
    offset = rest + ROWS if inline else 0
    height = CH if inline else slots.shape[0]
    slot_rows = iota((height, LANES), 0)
    slot_lanes = iota((height, LANES), 1)
    placed = jnp.zeros((height, LANES), jnp.float32)
    for j in range(count):
        name = trainers[j]
        rank = jnp.int32(0)
        for i in range(j):
            rank = rank + jnp.where(trainers[i] == name, 1, 0)
        target = (pos_x * count_y + name) * count_z + pos_z
        slot = offset + pos_y * CAP + rank
        hit = (slot_rows == target) & (slot_lanes == slot)
        placed = jnp.where(hit, losses[j : j + 1, :], placed)
    high = placed.astype(jnp.bfloat16).astype(jnp.float32)
    placed = high + pltpu.roll(placed - high, count_y * CAP, 1)
    if inline:
        mixed = mixed + placed
    else:
        slots[:, 0, :] = placed.astype(jnp.bfloat16)
    rows_out[:, whole, :] = mixed
    send[...] = rows_out[...].astype(jnp.bfloat16)


def second_step(sizes, inline, drawn, middle, visc, partial, vx_prev, vx_next, vy_prev,
                vy_next, vz_other, vz_own, x_prev, x_next, y_prev, y_next, z_other, z_own, *rest):
    counts = None if sizes["gy"] == 4 else rest[0]
    rest = rest if counts is None else rest[1:]
    w_first, w_second, w_second_t, w_third, w_third_t, advanced, send = rest[:7]
    slots = None if inline else rest[7]
    stack_first, stack_mid, rows_out, y_terms = rest[-4:]
    halo = halo_of(x_prev, x_next, y_prev, y_next, z_other)
    visc_halo = halo_of(vx_prev, vx_next, vy_prev, vy_next, vz_other)
    count = stack_mid.shape[1] // VOL
    samples = [drawn[0, j] for j in range(count)]
    trainers = [drawn[1, j] for j in range(count)]

    def emit(f, x, c, tile):
        advanced[f, x, ROWS * c : ROWS * c + ROWS, :] = tile

    close(middle, visc, partial, halo, visc_halo, z_own, vz_own, y_terms, emit)
    if counts is None:
        total = counts_of(trainers, count) + vy_prev[NF + 1] + vy_next[NF + 1] + y_prev[NF]
    else:
        total = counts[...]
    place = (lax.axis_index("gx"), lax.axis_index("gy"), lax.axis_index("gz"), sizes["gy"], sizes["gz"])
    closure(advanced, samples, trainers, total, w_first[...], w_second[...],
            w_second_t[...], w_third[...], w_third_t[...],
            float(sizes["gx"] * sizes["gy"] * sizes["gz"]), stack_first, stack_mid, rows_out,
            send, slots, inline, place)


def add_up(where, arrived, spread, losses):
    total = jnp.sum(arrived[...].astype(jnp.float32), axis=0)
    row, lane = where
    count = losses.shape[3]
    high = total[row : row + 1, lane : lane + count]
    losses[0, 0] = high + total[row : row + 1, lane + count : lane + 2 * count]
    rounded = total.astype(jnp.bfloat16)
    for i in range(spread.shape[0]):
        spread[i] = rounded


def unpack(gathered, first, second, third, wide):
    wide[...] = gathered[...].astype(jnp.float32)
    whole = second.shape[1] // LANES
    rest = second.shape[1] - whole * LANES
    for t in range(whole):
        second[:, LANES * t : LANES * t + LANES] = wide[:, t, :]
    mixed = wide[:, whole, :]
    second[:, LANES * whole :] = mixed[:, :rest]
    third[...] = mixed[:, rest : rest + ROWS].T[:NOUT]
    first[...] = wide[:, whole + 1, :][:, : first.shape[1]]


def shape_of(*dims, dtype=jnp.float32):
    return jax.ShapeDtypeStruct(dims, dtype)


def exchange(x_first, x_last, y_first, y_last, z_both, sizes):
    def ring(axis, step):
        count = sizes[axis]
        return [(i, (i + step) % count) for i in range(count)]

    x_prev = lax.ppermute(x_last, "gx", ring("gx", 1))
    x_next = lax.ppermute(x_first, "gx", ring("gx", -1))
    y_prev = lax.ppermute(y_last, "gy", ring("gy", 1))
    y_next = lax.ppermute(y_first, "gy", ring("gy", -1))
    z_other = lax.ppermute(z_both, "gz", ring("gz", 1))
    return x_prev, x_next, y_prev, y_next, z_other


def without_border(kernel, fields, visc, index=(), weights=()):
    cells = visc.size
    out_shape = [shape_of(*fields.shape)]
    if weights:
        sizes = ((CH, 28 * NF), (27 * CH, CH), (16, CH), (CH, 16))
        out_shape += [shape_of(*size, dtype=jnp.bfloat16) for size in sizes]
        out_shape.append(shape_of(ROWS, LANES, dtype=jnp.int32))
    return pl.pallas_call(
        kernel,
        out_shape=out_shape,
        in_specs=[SMEM] * len(index) + [VMEM] * (2 + len(weights)),
        out_specs=[VMEM] * len(out_shape),
        compiler_params=PARAMS,
        cost_estimate=pl.CostEstimate(flops=120 * cells, bytes_accessed=36 * cells, transcendentals=0),
        name=kernel.__name__,
    )(*index, fields, visc, *weights)


def on_device(sizes, fields, visc, samples, trainers, conv_first, conv_second, conv_third):
    _, planes, rows, lanes = fields.shape
    axes = ("gx", "gy", "gz")
    devices_all = sizes["gx"] * sizes["gy"] * sizes["gz"]
    pairs = planes * rows // ROWS
    half = LANES // 2
    samples = samples.reshape(-1)
    trainers = trainers.reshape(-1)

    faces = pl.pallas_call(
        pack_faces,
        out_shape=[
            shape_of(NF + 1, rows, lanes),
            shape_of(NF + 1, rows, lanes),
            shape_of(NF + 2, planes, lanes),
            shape_of(NF + 2, planes, lanes),
            shape_of(-(-(NF + 1) * pairs // half), ROWS, LANES),
        ],
        in_specs=[HBM, HBM, SMEM],
        out_specs=[VMEM] * 5,
        scratch_shapes=[
            pltpu.VMEM(fields.shape, jnp.float32),
            pltpu.VMEM(visc.shape, jnp.float32),
            pltpu.SemaphoreType.DMA((NF + 1,)),
        ],
        compiler_params=PACK,
        name="pack_faces",
    )(fields, visc, trainers)
    halo = exchange(*faces, sizes)

    own_counts = sizes["gy"] == 4
    counts = []
    if not own_counts:
        named = trainers.reshape(-1, 1) == jnp.arange(LANES, dtype=jnp.int32)[None, :]
        total = lax.psum(jnp.sum(named.astype(jnp.float32), axis=0, keepdims=True), "gy")
        counts = [jnp.broadcast_to(total, (ROWS, LANES))]
    z_own = faces[4]
    partial, w_first, w_second_t, w_third, w_third_t, drawn = without_border(
        interior_and_weights, fields, visc, (samples, trainers), (conv_first, conv_second, conv_third)
    )
    y_terms = pltpu.VMEM((2, NF, planes, lanes), jnp.float32)
    middle, *faces = pl.pallas_call(
        close_first,
        out_shape=[
            shape_of(*fields.shape),
            shape_of(NF, rows, lanes),
            shape_of(NF, rows, lanes),
            shape_of(NF, planes, lanes),
            shape_of(NF + 1, planes, lanes),
            shape_of(-(-NF * pairs // half), ROWS, LANES),
        ],
        in_specs=[VMEM] * 9,
        out_specs=[VMEM] * 6,
        scratch_shapes=[y_terms],
        compiler_params=PARAMS,
        name="close_first",
    )(fields, visc, partial, *halo, z_own)
    later = exchange(*faces, sizes)
    (partial,) = without_border(interior, middle, visc)

    count = samples.shape[0]
    slot_total = sizes["gy"] * CAP
    tiles = -(-27 * CH // LANES) + 1
    parts = devices_all // CH
    inline = parts == 1 and slot_total <= 12
    out_shape = [shape_of(*fields.shape), shape_of(CH, tiles, LANES, dtype=jnp.bfloat16)]
    if not inline:
        out_shape.append(shape_of(devices_all, 1, LANES, dtype=jnp.bfloat16))
    advanced, send, *slots = pl.pallas_call(
        functools.partial(second_step, sizes, inline),
        out_shape=out_shape,
        in_specs=[VMEM] * (21 if own_counts else 22),
        out_specs=[VMEM] * len(out_shape),
        scratch_shapes=[
            pltpu.VMEM((28 * NF, count * VOL), jnp.float32),
            pltpu.VMEM((27 * CH, count * VOL), jnp.bfloat16),
            pltpu.VMEM((CH, tiles, LANES), jnp.float32),
            y_terms,
        ],
        compiler_params=PARAMS,
        name="second_step",
    )(drawn, middle, visc, partial, *halo, z_own, *later, faces[4], *counts,
      w_first, conv_second, w_second_t, w_third, w_third_t)

    if not inline:
        send = jnp.concatenate([send.reshape(devices_all, tiles // parts, LANES), slots[0]], 1)
    arrived = lax.all_to_all(send, axes, split_axis=0, concat_axis=0, tiled=True)
    if inline:
        where = (27 * CH // LANES, 27 * CH % LANES + ROWS)
    else:
        where = (send.shape[1] - 1, 0)
    spread, block_losses = pl.pallas_call(
        functools.partial(add_up, where),
        out_shape=[shape_of(*send.shape, dtype=jnp.bfloat16), shape_of(1, 1, 1, slot_total)],
        in_specs=[VMEM],
        out_specs=[VMEM] * 2,
        compiler_params=PARAMS,
        name="add_up",
    )(arrived)
    if not inline:
        spread = spread[:, :-1, :]
    gathered = lax.all_to_all(spread, axes, split_axis=0, concat_axis=0, tiled=True)
    first, second, third = pl.pallas_call(
        unpack,
        out_shape=[shape_of(*conv_first.shape), shape_of(*conv_second.shape), shape_of(*conv_third.shape)],
        in_specs=[VMEM],
        out_specs=[VMEM] * 3,
        scratch_shapes=[pltpu.VMEM((CH, tiles, LANES), jnp.float32)],
        compiler_params=PARAMS,
        name="unpack",
    )(gathered.reshape(CH, tiles, LANES))
    return advanced, block_losses, first, second, third


def solution(mesh):
    sizes = dict(mesh.shape)
    in_specs = (
        P(None, "gx", "gy", "gz"),
        P("gx", "gy", "gz"),
        P("gx", "gy", "gz", None),
        P("gx", "gy", "gz", None, None),
        P(),
        P(),
        P(),
    )
    out_specs = (P(None, "gx", "gy", "gz"), P("gx", "gy", "gz", None), P(), P(), P())
    return jax.shard_map(
        functools.partial(on_device, sizes), mesh=mesh, in_specs=in_specs, out_specs=out_specs,
        check_vma=False,
    )
```

```python
import functools

import jax
import jax.numpy as jnp
from jax import lax
from jax.experimental import pallas as pl
from jax.experimental.pallas import tpu as pltpu
from jax.sharding import PartitionSpec as P

BLK = 4
CAP = 2
NF = 4
VOL = BLK**3
TAPS = [(x, y, z) for x in (-1, 0, 1) for y in (-1, 0, 1) for z in (-1, 0, 1)]
LANES = 128
ROWS = 8
NOUT = 6
CH = 32

time_step = 0.25
buoyancy = 0.5

VMEM = pl.BlockSpec(memory_space=pltpu.VMEM)
SMEM = pl.BlockSpec(memory_space=pltpu.SMEM)
HBM = pl.BlockSpec(memory_space=pltpu.HBM)
ANY = pl.BlockSpec(memory_space=pl.ANY)
PARAMS = pltpu.CompilerParams(vmem_limit_bytes=24 * 1024 * 1024)
PACK = pltpu.CompilerParams(vmem_limit_bytes=60 * 1024 * 1024)
FULL = (((1,), (1,)), ((), ()))


def iota(shape, axis):
    return lax.broadcasted_iota(jnp.int32, shape, axis)


def odd(axis):
    return lax.axis_index(axis) % 2 == 1


def lay_out(axis, first, last, swap_a, swap_b):
    turned = odd(axis)
    for (index, low), (_, high) in zip(first, last):
        swap_a[index] = jnp.where(turned, low, high)
        swap_b[index] = jnp.where(turned, high, low)


class Sides:
    def __init__(self, x_a, x_b, y_a, y_b, z_both):
        self.faces = dict(x=(x_a, x_b), y=(y_a, y_b))
        self.odd = dict(x=odd("gx"), y=odd("gy"))
        self.z_both = z_both

    def prev(self, axis, *index):
        a, b = self.faces[axis]
        return jnp.where(self.odd[axis], a[index], b[index])

    def next(self, axis, *index):
        a, b = self.faces[axis]
        return jnp.where(self.odd[axis], b[index], a[index])


def pair_of(f, c, planes, chunks):
    span = 2 * planes * chunks
    return f * span // LANES, f * span % LANES + 2 * planes * c


def add_pair(packed, tile, lane):
    moved = pltpu.roll(tile, lane + 1, 1)
    at = iota(tile.shape, 1)
    return jnp.where((at == lane) | (at == lane + 1), moved, packed)


def counts_of(trainers_ref, count):
    at = iota((ROWS, LANES), 1)
    total = jnp.zeros((ROWS, LANES), jnp.float32)
    for j in range(count):
        total = total + jnp.where(at == trainers_ref[j], 1.0, 0.0)
    return total


def pack_faces(fields_far, visc_far, trainers_far, x_a, x_b, y_a, y_b, z_both, fields, visc, trainers, sems):
    _, planes, rows, _ = fields.shape
    chunks = rows // ROWS
    copies = [pltpu.make_async_copy(fields_far.at[f], fields.at[f], sems.at[f]) for f in range(NF)]
    copies.append(pltpu.make_async_copy(visc_far, visc, sems.at[NF]))
    listed = pltpu.make_async_copy(trainers_far, trainers, sems.at[NF + 1])
    for copy in copies:
        copy.start()
    listed.start()
    arrays = [fields.at[f] for f in range(NF)] + [visc]
    packed = [jnp.zeros((ROWS, LANES), jnp.float32) for _ in range(z_both.shape[0])]
    for f, array in enumerate(arrays):
        copies[f].wait()
        lay_out("gx", [(f, array[0])], [(f, array[planes - 1])], x_a, x_b)
        lay_out("gy", [(f, array[:, 0, :])], [(f, array[:, rows - 1, :])], y_a, y_b)
        for c in range(chunks):
            tile, lane = pair_of(f, c, planes, chunks)
            for x in range(planes):
                cells = array[x, ROWS * c : ROWS * c + ROWS]
                packed[tile] = add_pair(packed[tile], cells, lane + 2 * x)
    for tile, value in enumerate(packed):
        z_both[tile] = value
    listed.wait()
    counts = counts_of(trainers, trainers.shape[0])
    y_a[NF + 1] = counts
    y_b[NF + 1] = counts


def flux(lower, upper, dimension):
    speed = 0.25 * (lower[dimension] + upper[dimension])
    mean_visc = 0.5 * (lower[NF] + upper[NF])
    return [speed * (a + b) - mean_visc * (b - a) for a, b in zip(lower[:NF], upper[:NF])]


def interior(fields, visc, partial):
    _, planes, rows, _ = fields.shape
    chunks = rows // ROWS
    end_row = iota((ROWS, LANES), 0) == ROWS - 1
    end_lane = iota((ROWS, LANES), 1) == LANES - 1
    every = range(NF + 1)

    def cell(f, x, part):
        return fields[f, x, part, :] if f < NF else visc[x, part, :]

    def plane(x, lowers):
        uppers = []
        last = x == planes - 1
        beyond = jnp.minimum(x + 1, planes - 1)
        behind = [jnp.zeros((ROWS, LANES), jnp.float32)] * NF
        for c in range(chunks):
            part = slice(ROWS * c, ROWS * c + ROWS)
            here = [cell(f, x, part) for f in every]
            after = [cell(f, beyond, part) for f in every]
            upper = flux(here, after, 0)
            upper = [jnp.where(last, 0.0, u) for u in upper]
            total = [b - a for a, b in zip(lowers[c], upper)]
            uppers.append(upper)
            above = [pltpu.roll(h, ROWS - 1, 0) for h in here]
            if c + 1 < chunks:
                first = slice(ROWS * c + ROWS, ROWS * c + ROWS + 1)
                above = [jnp.where(end_row, cell(f, x, first), above[f]) for f in every]
            upper = flux(here, above, 1)
            lower = [pltpu.roll(jnp.where(end_row, b, u), 1, 0) for b, u in zip(behind, upper)]
            if c + 1 == chunks:
                upper = [jnp.where(end_row, 0.0, u) for u in upper]
            behind = upper
            total = [t + (b - a) for t, a, b in zip(total, lower, upper)]
            right = [pltpu.roll(h, LANES - 1, 1) for h in here]
            upper = [jnp.where(end_lane, 0.0, u) for u in flux(here, right, 2)]
            lower = [pltpu.roll(u, 1, 1) for u in upper]
            total = [t + (b - a) for t, a, b in zip(total, lower, upper)]
            updated = [q - time_step * t for q, t in zip(here[:NF], total)]
            updated[2] = updated[2] + (time_step * buoyancy) * here[3]
            for f in range(NF):
                partial[f, x, part, :] = updated[f]
        return uppers

    zeros = [[jnp.zeros((ROWS, LANES), jnp.float32)] * NF for _ in range(chunks)]
    lax.fori_loop(0, planes, plane, zeros)


def interior_and_weights(samples_far, trainers_far, fields, visc, conv_first, conv_second, conv_third,
                         partial, w_first, w_second_t, w_third, w_third_t, drawn, samples, trainers, sems):
    copies = [
        pltpu.make_async_copy(samples_far, samples, sems.at[0]),
        pltpu.make_async_copy(trainers_far, trainers, sems.at[1]),
    ]
    for copy in copies:
        copy.start()
    interior(fields, visc, partial)
    ahead = conv_first.shape[1]
    w_first[:, :ahead] = conv_first[...]
    w_first[:, ahead:] = jnp.zeros((CH, w_first.shape[1] - ahead), jnp.bfloat16)
    w_second_t[...] = conv_second[...].astype(jnp.float32).T.astype(jnp.bfloat16)
    third = conv_third[...].astype(jnp.float32)
    third = jnp.concatenate([third, jnp.zeros((w_third.shape[0] - NOUT, CH), jnp.float32)], 0)
    w_third[...] = third.astype(jnp.bfloat16)
    w_third_t[...] = third.T.astype(jnp.bfloat16)
    for copy in copies:
        copy.wait()
    at, row = iota((ROWS, LANES), 1), iota((ROWS, LANES), 0)
    table = jnp.zeros((ROWS, LANES), jnp.int32)
    for j in range(samples.shape[0]):
        table = jnp.where(at == j, jnp.where(row == 0, samples[j], trainers[j]), table)
    drawn[...] = table


def z_terms(own, other, visc_own, visc_other):
    lane = iota((ROWS, LANES), 1)
    second = lane % 2 == 1
    span = LANES // 2

    def ends(mine, theirs):
        lower = jnp.where(second, pltpu.roll(theirs, 1, 1), mine)
        return lower, jnp.where(second, mine, pltpu.roll(theirs, LANES - 1, 1))

    def twice(tile):
        return jnp.where(lane < span, tile, pltpu.roll(tile, span, 1))

    pairs = [ends(a, b) for a, b in zip(own, other)]
    speed = [twice(end) for end in pairs[2 * span // LANES]]
    visc = [twice(end) for end in ends(visc_own, visc_other)]
    speed = 0.25 * (speed[0] + speed[1])
    mean_visc = 0.5 * (visc[0] + visc[1])
    through = [speed * (a + b) - mean_visc * (b - a) for a, b in pairs]
    return [jnp.where(second, time_step, -time_step) * t for t in through]


def close(fields, visc, partial, halo, visc_halo, z_own, visc_z_own, y_terms, emit):
    _, planes, rows, _ = fields.shape
    chunks = rows // ROWS
    every = range(NF + 1)
    row = iota((ROWS, LANES), 0)
    lane_at = iota((ROWS, LANES), 1)
    ends = (lane_at == 0) | (lane_at == LANES - 1)

    def cell(f, *index):
        return fields[(f,) + index] if f < NF else visc[index]

    def sides(f):
        return halo if f < NF else visc_halo

    lower = flux([sides(f).prev("y", f) for f in every], [cell(f, slice(None), 0) for f in every], 1)
    upper = flux([cell(f, slice(None), rows - 1) for f in every], [sides(f).next("y", f) for f in every], 1)
    for f in range(NF):
        y_terms[0, f] = time_step * lower[f]
        y_terms[1, f] = -time_step * upper[f]
    tiles = z_own.shape[0] if z_own.shape[0] * LANES == 2 * NF * planes * chunks else z_own.shape[0] - 1
    terms = z_terms([z_own[t] for t in range(tiles)], [halo.z_both[t] for t in range(tiles)],
                    visc_z_own[tiles], visc_halo.z_both[tiles])
    for c in range(chunks):
        part = slice(ROWS * c, ROWS * c + ROWS)
        low = flux([sides(f).prev("x", f, part) for f in every], [cell(f, 0, part) for f in every], 0)
        high = flux([cell(f, planes - 1, part) for f in every], [sides(f).next("x", f, part) for f in every], 0)
        for x in range(planes):
            for f in range(NF):
                tile, lane = pair_of(f, c, planes, chunks)
                moved = pltpu.roll(terms[tile], LANES - 1 - lane - 2 * x, 1)
                value = partial[f, x, part, :] + jnp.where(ends, moved, 0.0)
                if x == 0:
                    value = value + time_step * low[f]
                if x == planes - 1:
                    value = value - time_step * high[f]
                if c == 0:
                    value = value + jnp.where(row == 0, y_terms[0, f, x : x + 1, :], 0.0)
                if c == chunks - 1:
                    value = value + jnp.where(row == ROWS - 1, y_terms[1, f, x : x + 1, :], 0.0)
                emit(f, x, c, value)


def close_first(fields, visc, partial, y_from_b, x_from_b, y_from_a, z_other, x_from_a, z_own,
                middle, x_a, x_b, y_a, y_b, z_both, y_terms):
    _, planes, rows, _ = fields.shape
    chunks = rows // ROWS
    halo = Sides(x_from_a, x_from_b, y_from_a, y_from_b, z_other)
    packed = [jnp.zeros((ROWS, LANES), jnp.float32) for _ in range(z_both.shape[0])]

    def emit(f, x, c, tile):
        middle[f, x, ROWS * c : ROWS * c + ROWS, :] = tile
        at, lane = pair_of(f, c, planes, chunks)
        packed[at] = add_pair(packed[at], tile, lane + 2 * x)

    close(fields, visc, partial, halo, halo, z_own, z_own, y_terms, emit)
    for at, value in enumerate(packed):
        z_both[at] = value
    for f in range(NF):
        lay_out("gx", [(f, middle[f, 0])], [(f, middle[f, planes - 1])], x_a, x_b)
        lay_out("gy", [(f, middle[f, :, 0, :])], [(f, middle[f, :, rows - 1, :])], y_a, y_b)
    y_b[NF] = y_from_a[NF + 1]


def inside_masks():
    at = iota((1, LANES), 1) % VOL
    coords = (at // (BLK * BLK), at // BLK % BLK, at % BLK)
    along = []
    for coord in coords:
        along.append({
            -1: jnp.where(coord > 0, 1.0, 0.0),
            0: jnp.ones((1, LANES), jnp.float32),
            1: jnp.where(coord < BLK - 1, 1.0, 0.0),
        })
    return along


def move_of(tap):
    return tap[0] * BLK * BLK + tap[1] * BLK + tap[2]


def shifted(tile, tap, along):
    move = move_of(tap)
    if move == 0:
        return tile
    mask = along[0][tap[0]] * along[1][tap[1]] * along[2][tap[2]]
    return pltpu.roll(tile, (-move) % LANES, 1) * mask


def box(tile, along):
    for dimension, step in enumerate((BLK * BLK, BLK, 1)):
        ahead = pltpu.roll(tile, LANES - step, 1) * along[dimension][1]
        behind = pltpu.roll(tile, step, 1) * along[dimension][-1]
        tile = (behind + tile) + ahead
    return tile / 27.0


def sigmoid(values):
    return 1.0 / (1.0 + jnp.exp(-values))


PICKED = (0, 1, 2, 3, 0, 1, 2, 3, 0, 1, 2, 0, 0, 1, -1, -1, 0, 1, 2, 1, 2, 2, -1, -1)


def pick_rows():
    out, field = iota((32, NF * ROWS), 0), iota((32, NF * ROWS), 1) // ROWS
    table = jnp.zeros((32, NF * ROWS), jnp.float32)
    for i, f in enumerate(PICKED):
        table = jnp.where((out == i) & (field == f), 1.0, table)
    return table.astype(jnp.bfloat16)


def pick_blocks(advanced, samples, count):
    _, _, rows, lanes = advanced.shape
    along_y, along_z = rows // BLK, lanes // BLK
    row = iota((ROWS, LANES), 0)
    lane_at = iota((ROWS, LANES), 1)
    pick = pick_rows()
    out = []
    for j in range(0, count, 2):
        parts = [jnp.zeros((ROWS, LANES), jnp.float32) for _ in range(NF)]
        uppers = []
        for half in range(2):
            block = samples[j + half]
            block_x = block // (along_y * along_z)
            block_y = block // along_z % along_y
            block_z = block % along_z
            uppers.append(block_y % 2)
            start = pl.multiple_of(block_y // 2 * ROWS, ROWS)
            for x in range(BLK):
                turn = lax.rem(VOL * half + BLK * BLK * x - BLK * block_z + LANES, LANES)
                wanted = lane_at // BLK == (VOL * half + BLK * BLK * x) // BLK
                for f in range(NF):
                    tile = advanced[f, block_x * BLK + x, pl.ds(start, ROWS), :]
                    parts[f] = jnp.where(wanted, pltpu.roll(tile, turn, 1), parts[f])
        upper = jnp.where(lane_at < VOL, uppers[0], uppers[1])
        valid = row // BLK == upper
        for f in range(NF):
            for bit in (1, 2):
                moved = pltpu.roll(parts[f], BLK * bit, 1)
                parts[f] = jnp.where(row // bit % 2 == 1, moved, parts[f])
            parts[f] = jnp.where(valid, parts[f], 0.0)
        stacked = jnp.concatenate(parts, 0).astype(jnp.bfloat16)
        out.append(jnp.dot(pick, stacked, preferred_element_type=jnp.float32))
    return out


def closure(advanced, samples, trainers, counts, w_first, w_second, w_second_t, w_third,
            w_third_t, devices_all, stack_first, stack_mid, rows_out, send, slots, inline, place):
    count = len(samples)
    pairs = count // 2
    cols = [slice(LANES * m, LANES * m + LANES) for m in range(pairs)]
    along = inside_masks()
    lane_at = iota((ROWS, LANES), 1)
    row = iota((ROWS, LANES), 0)

    picked = pick_blocks(advanced, samples, count)
    values = [p[:ROWS] for p in picked]
    targets = []
    for p in picked:
        first, second = p[ROWS : 2 * ROWS], p[2 * ROWS : 3 * ROWS]
        targets.append(box(first * second, along) - box(first, along) * box(second, along))

    for m, tile in enumerate(values):
        for t in range(0, 28, 2):
            piece = shifted(tile, TAPS[t], along)
            later = shifted(tile, TAPS[t + 1], along) if t + 1 < 27 else jnp.zeros_like(tile)
            stack_first[BLK * t : BLK * t + ROWS, cols[m]] = jnp.where(row < NF, piece, later)
    stack_in = stack_first[...].astype(jnp.bfloat16)
    pre_first = jnp.dot(w_first, stack_in, preferred_element_type=jnp.float32)
    gate_first = sigmoid(pre_first)
    hidden_first = (pre_first * gate_first).astype(jnp.bfloat16).astype(jnp.float32)
    for m in range(pairs):
        tile = hidden_first[:, cols[m]]
        for k, tap in enumerate(TAPS):
            stack_mid[CH * k : CH * k + CH, cols[m]] = shifted(tile, tap, along).astype(jnp.bfloat16)
    pre_second = jnp.dot(w_second, stack_mid[...], preferred_element_type=jnp.float32)
    gate_second = sigmoid(pre_second)
    hidden_second = (pre_second * gate_second).astype(jnp.bfloat16)
    predicted = jnp.dot(w_third, hidden_second, preferred_element_type=jnp.float32)

    misfit = predicted[:ROWS] - jnp.concatenate(targets, 1)
    square = jnp.sum(misfit * misfit, axis=0, keepdims=True)
    sample_at = iota((ROWS, count * VOL), 1) // VOL
    mine = sample_at == iota((ROWS, count * VOL), 0)
    losses = jnp.sum(jnp.where(mine, square, 0.0), axis=1, keepdims=True) / (NOUT * VOL)
    owner = jnp.zeros((ROWS, LANES), jnp.int32)
    for j in range(count):
        owner = jnp.where(row == j, trainers[j], owner)
    load = jnp.sum(jnp.where(lane_at == owner, counts, 0.0), axis=1, keepdims=True)
    share = 1.0 / (devices_all * jnp.maximum(load, 1.0))
    scale = share * (2.0 / (NOUT * VOL))
    scale_at = jnp.sum(jnp.where(mine, scale, 0.0), axis=0, keepdims=True)
    grad_pred = (misfit * scale_at).astype(jnp.bfloat16)
    grad_pred = jnp.concatenate([grad_pred, jnp.zeros_like(grad_pred)], 0)

    upper = jnp.dot(w_third_t, grad_pred, preferred_element_type=jnp.float32)
    slope = gate_second * (1.0 + pre_second * (1.0 - gate_second))
    grad_mid = (upper * slope).astype(jnp.bfloat16)
    grad_second = lax.dot_general(grad_mid, stack_mid[...], FULL, preferred_element_type=jnp.float32)
    third = jnp.concatenate([grad_pred, jnp.zeros((LANES - 16, count * VOL), jnp.bfloat16)], 0)
    grad_third = lax.dot_general(hidden_second, third, FULL, preferred_element_type=jnp.float32)

    spread = jnp.dot(w_second_t, grad_mid, preferred_element_type=jnp.float32)
    lower = []
    for m in range(pairs):
        terms = [
            shifted(spread[CH * k : CH * k + CH, cols[m]], tuple(-o for o in tap), along)
            for k, tap in enumerate(TAPS)
        ]
        lower.append(functools.reduce(jnp.add, terms))
    lower = jnp.concatenate(lower, 1)
    slope = gate_first * (1.0 + pre_first * (1.0 - gate_first))
    grad_entry = (lower * slope).astype(jnp.bfloat16)
    grad_first = lax.dot_general(grad_entry, stack_in, FULL, preferred_element_type=jnp.float32)

    whole = CH * 27 // LANES
    rest = CH * 27 - whole * LANES
    for t in range(whole):
        rows_out[:, t, :] = grad_second[:, LANES * t : LANES * t + LANES]
    mixed = jnp.concatenate([grad_second[:, whole * LANES :], jnp.zeros((CH, LANES - rest), jnp.float32)], 1)
    mixed = mixed + pltpu.roll(grad_third, rest, 1)
    tail = LANES - grad_first.shape[1]
    rows_out[:, whole + 1, :] = jnp.concatenate([grad_first, jnp.zeros((CH, tail), jnp.float32)], 1)

    pos_x, pos_y, pos_z, count_y, count_z = place
    offset = rest + ROWS if inline else 0
    height = CH if inline else slots.shape[0]
    slot_rows = iota((height, LANES), 0)
    slot_lanes = iota((height, LANES), 1)
    placed = jnp.zeros((height, LANES), jnp.float32)
    for j in range(count):
        name = trainers[j]
        rank = jnp.int32(0)
        for i in range(j):
            rank = rank + jnp.where(trainers[i] == name, 1, 0)
        target = (pos_x * count_y + name) * count_z + pos_z
        slot = offset + pos_y * CAP + rank
        hit = (slot_rows == target) & (slot_lanes == slot)
        placed = jnp.where(hit, losses[j : j + 1, :], placed)
    high = placed.astype(jnp.bfloat16).astype(jnp.float32)
    placed = high + pltpu.roll(placed - high, count_y * CAP, 1)
    if inline:
        mixed = mixed + placed
    else:
        slots[:, 0, :] = placed.astype(jnp.bfloat16)
    rows_out[:, whole, :] = mixed
    send[...] = rows_out[...].astype(jnp.bfloat16)


def second_step(sizes, inline, drawn, middle, visc, partial, vy_b, vx_b, vy_a, vz_other, vx_a, vz_own,
                y_b, x_b, y_a, z_other, x_a, z_own, *rest):
    counts = None if sizes["gy"] == 4 else rest[0]
    rest = rest if counts is None else rest[1:]
    w_first, w_second, w_second_t, w_third, w_third_t, advanced, send = rest[:7]
    slots = None if inline else rest[7]
    stack_first, stack_mid, rows_out, y_terms = rest[-4:]
    halo = Sides(x_a, x_b, y_a, y_b, z_other)
    visc_halo = Sides(vx_a, vx_b, vy_a, vy_b, vz_other)
    count = stack_mid.shape[1] // VOL
    samples = [drawn[0, j] for j in range(count)]
    trainers = [drawn[1, j] for j in range(count)]

    def emit(f, x, c, tile):
        advanced[f, x, ROWS * c : ROWS * c + ROWS, :] = tile

    close(middle, visc, partial, halo, visc_halo, z_own, vz_own, y_terms, emit)
    if counts is None:
        total = counts_of(trainers, count) + vy_a[NF + 1] + vy_b[NF + 1] + y_b[NF]
    else:
        total = counts[...]
    place = (lax.axis_index("gx"), lax.axis_index("gy"), lax.axis_index("gz"), sizes["gy"], sizes["gz"])
    closure(advanced, samples, trainers, total, w_first[...], w_second[...],
            w_second_t[...], w_third[...], w_third_t[...],
            float(sizes["gx"] * sizes["gy"] * sizes["gz"]), stack_first, stack_mid, rows_out,
            send, slots, inline, place)


def add_up(where, arrived, spread, losses):
    total = jnp.sum(arrived[...].astype(jnp.float32), axis=0)
    row, lane = where
    count = losses.shape[3]
    high = total[row : row + 1, lane : lane + count]
    losses[0, 0] = high + total[row : row + 1, lane + count : lane + 2 * count]
    rounded = total.astype(jnp.bfloat16)
    for i in range(spread.shape[0]):
        spread[i] = rounded


def unpack(gathered, first, second, third, wide):
    wide[...] = gathered[...].astype(jnp.float32)
    whole = second.shape[1] // LANES
    rest = second.shape[1] - whole * LANES
    for t in range(whole):
        second[:, LANES * t : LANES * t + LANES] = wide[:, t, :]
    mixed = wide[:, whole, :]
    second[:, LANES * whole :] = mixed[:, :rest]
    third[...] = mixed[:, rest : rest + ROWS].T[:NOUT]
    first[...] = wide[:, whole + 1, :][:, : first.shape[1]]


def shape_of(*dims, dtype=jnp.float32):
    return jax.ShapeDtypeStruct(dims, dtype)


def exchange(x_a, x_b, y_a, y_b, z_both, sizes):
    def swap_a(axis):
        return [(i, i ^ 1) for i in range(sizes[axis])]

    def swap_b(axis):
        return [(i, (i + (1 if i % 2 else -1)) % sizes[axis]) for i in range(sizes[axis])]

    y_b = lax.ppermute(y_b, "gy", swap_b("gy"))
    x_b = lax.ppermute(x_b, "gx", swap_b("gx"))
    y_a = lax.ppermute(y_a, "gy", swap_a("gy"))
    z_both = lax.ppermute(z_both, "gz", swap_a("gz"))
    x_a = lax.ppermute(x_a, "gx", swap_a("gx"))
    return y_b, x_b, y_a, z_both, x_a


def without_border(kernel, fields, visc, index=(), weights=()):
    cells = visc.size
    out_shape = [shape_of(*fields.shape)]
    scratch = [pltpu.SMEM(array.shape, jnp.int32) for array in index]
    if weights:
        scratch.append(pltpu.SemaphoreType.DMA((len(index),)))
        sizes = ((CH, 28 * NF), (27 * CH, CH), (16, CH), (CH, 16))
        out_shape += [shape_of(*size, dtype=jnp.bfloat16) for size in sizes]
        out_shape.append(shape_of(ROWS, LANES, dtype=jnp.int32))
    return pl.pallas_call(
        kernel,
        out_shape=out_shape,
        in_specs=[ANY] * len(index) + [VMEM] * (2 + len(weights)),
        out_specs=[VMEM] * len(out_shape),
        scratch_shapes=scratch,
        compiler_params=PARAMS,
        cost_estimate=pl.CostEstimate(flops=120 * cells, bytes_accessed=36 * cells, transcendentals=0),
        name=kernel.__name__,
    )(*index, fields, visc, *weights)


def on_device(sizes, fields, visc, samples, trainers, conv_first, conv_second, conv_third):
    _, planes, rows, lanes = fields.shape
    axes = ("gx", "gy", "gz")
    devices_all = sizes["gx"] * sizes["gy"] * sizes["gz"]
    pairs = planes * rows // ROWS
    half = LANES // 2
    samples = samples.reshape(-1)
    trainers = trainers.reshape(-1)

    faces = pl.pallas_call(
        pack_faces,
        out_shape=[
            shape_of(NF + 1, rows, lanes),
            shape_of(NF + 1, rows, lanes),
            shape_of(NF + 2, planes, lanes),
            shape_of(NF + 2, planes, lanes),
            shape_of(-(-(NF + 1) * pairs // half), ROWS, LANES),
        ],
        in_specs=[HBM, HBM, HBM],
        out_specs=[VMEM] * 5,
        scratch_shapes=[
            pltpu.VMEM(fields.shape, jnp.float32),
            pltpu.VMEM(visc.shape, jnp.float32),
            pltpu.SMEM(trainers.shape, jnp.int32),
            pltpu.SemaphoreType.DMA((NF + 2,)),
        ],
        compiler_params=PACK,
        name="pack_faces",
    )(fields, visc, trainers)
    halo = exchange(*faces, sizes)

    own_counts = sizes["gy"] == 4
    counts = []
    if not own_counts:
        named = trainers.reshape(-1, 1) == jnp.arange(LANES, dtype=jnp.int32)[None, :]
        total = lax.psum(jnp.sum(named.astype(jnp.float32), axis=0, keepdims=True), "gy")
        counts = [jnp.broadcast_to(total, (ROWS, LANES))]
    z_own = faces[4]
    y_terms = pltpu.VMEM((2, NF, planes, lanes), jnp.float32)
    middle, *faces = pl.pallas_call(
        close_first,
        out_shape=[
            shape_of(*fields.shape),
            shape_of(NF, rows, lanes),
            shape_of(NF, rows, lanes),
            shape_of(NF, planes, lanes),
            shape_of(NF + 1, planes, lanes),
            shape_of(-(-NF * pairs // half), ROWS, LANES),
        ],
        in_specs=[VMEM] * 9,
        out_specs=[VMEM] * 6,
        scratch_shapes=[y_terms],
        compiler_params=PARAMS,
        name="close_first",
    )(fields, visc, *without_border(interior, fields, visc), *halo, z_own)
    later = exchange(*faces, sizes)
    partial, w_first, w_second_t, w_third, w_third_t, drawn = without_border(
        interior_and_weights, middle, visc, (samples, trainers), (conv_first, conv_second, conv_third)
    )

    count = samples.shape[0]
    slot_total = sizes["gy"] * CAP
    tiles = -(-27 * CH // LANES) + 1
    parts = devices_all // CH
    inline = parts == 1 and slot_total <= 12
    out_shape = [shape_of(*fields.shape), shape_of(CH, tiles, LANES, dtype=jnp.bfloat16)]
    if not inline:
        out_shape.append(shape_of(devices_all, 1, LANES, dtype=jnp.bfloat16))
    advanced, send, *slots = pl.pallas_call(
        functools.partial(second_step, sizes, inline),
        out_shape=out_shape,
        in_specs=[VMEM] * (21 if own_counts else 22),
        out_specs=[VMEM] * len(out_shape),
        scratch_shapes=[
            pltpu.VMEM((28 * NF, count * VOL), jnp.float32),
            pltpu.VMEM((27 * CH, count * VOL), jnp.bfloat16),
            pltpu.VMEM((CH, tiles, LANES), jnp.float32),
            y_terms,
        ],
        compiler_params=PARAMS,
        name="second_step",
    )(drawn, middle, visc, partial, *halo, z_own, *later, faces[4], *counts,
      w_first, conv_second, w_second_t, w_third, w_third_t)

    if not inline:
        send = jnp.concatenate([send.reshape(devices_all, tiles // parts, LANES), slots[0]], 1)
    arrived = lax.all_to_all(send, axes, split_axis=0, concat_axis=0, tiled=True)
    if inline:
        where = (27 * CH // LANES, 27 * CH % LANES + ROWS)
    else:
        where = (send.shape[1] - 1, 0)
    spread, block_losses = pl.pallas_call(
        functools.partial(add_up, where),
        out_shape=[shape_of(*send.shape, dtype=jnp.bfloat16), shape_of(1, 1, 1, slot_total)],
        in_specs=[VMEM],
        out_specs=[VMEM] * 2,
        compiler_params=PARAMS,
        name="add_up",
    )(arrived)
    if not inline:
        spread = spread[:, :-1, :]
    gathered = lax.all_to_all(spread, axes, split_axis=0, concat_axis=0, tiled=True)
    first, second, third = pl.pallas_call(
        unpack,
        out_shape=[shape_of(*conv_first.shape), shape_of(*conv_second.shape), shape_of(*conv_third.shape)],
        in_specs=[VMEM],
        out_specs=[VMEM] * 3,
        scratch_shapes=[pltpu.VMEM((CH, tiles, LANES), jnp.float32)],
        compiler_params=PARAMS,
        name="unpack",
    )(gathered.reshape(CH, tiles, LANES))
    return advanced, block_losses, first, second, third


def solution(mesh):
    sizes = dict(mesh.shape)
    in_specs = (
        P(None, "gx", "gy", "gz"),
        P("gx", "gy", "gz"),
        P("gx", "gy", "gz", None),
        P("gx", "gy", "gz", None, None),
        P(),
        P(),
        P(),
    )
    out_specs = (P(None, "gx", "gy", "gz"), P("gx", "gy", "gz", None), P(), P(), P())
    return jax.shard_map(
        functools.partial(on_device, sizes), mesh=mesh, in_specs=in_specs, out_specs=out_specs,
        check_vma=False,
    )
```

```python
import functools

import jax
import jax.numpy as jnp
from jax import lax
from jax.experimental import pallas as pl
from jax.experimental.pallas import tpu as pltpu
from jax.sharding import PartitionSpec as P

BLK = 4
CAP = 2
NF = 4
VOL = BLK**3
TAPS = [(x, y, z) for x in (-1, 0, 1) for y in (-1, 0, 1) for z in (-1, 0, 1)]
LANES = 128
ROWS = 8
NOUT = 6
CH = 32

time_step = 0.25
buoyancy = 0.5

VMEM = pl.BlockSpec(memory_space=pltpu.VMEM)
SMEM = pl.BlockSpec(memory_space=pltpu.SMEM)
HBM = pl.BlockSpec(memory_space=pltpu.HBM)
ANY = pl.BlockSpec(memory_space=pl.ANY)
PARAMS = pltpu.CompilerParams(vmem_limit_bytes=24 * 1024 * 1024)
PACK = pltpu.CompilerParams(vmem_limit_bytes=54944 * 1024)
FULL = (((1,), (1,)), ((), ()))


def iota(shape, axis):
    return lax.broadcasted_iota(jnp.int32, shape, axis)


def odd(axis):
    return lax.axis_index(axis) % 2 == 1


def lay_out(axis, first, last, swap_a, swap_b):
    turned = odd(axis)
    for (index, low), (_, high) in zip(first, last):
        swap_a[index] = jnp.where(turned, low, high)
        swap_b[index] = jnp.where(turned, high, low)


class Sides:
    def __init__(self, x_a, x_b, y_a, y_b, z_both):
        self.faces = dict(x=(x_a, x_b), y=(y_a, y_b))
        self.odd = dict(x=odd("gx"), y=odd("gy"))
        self.z_both = z_both

    def prev(self, axis, *index):
        a, b = self.faces[axis]
        return jnp.where(self.odd[axis], a[index], b[index])

    def next(self, axis, *index):
        a, b = self.faces[axis]
        return jnp.where(self.odd[axis], b[index], a[index])


def pair_of(f, c, planes, chunks):
    span = 2 * planes * chunks
    return f * span // LANES, f * span % LANES + 2 * planes * c


def add_pair(packed, tile, lane):
    moved = pltpu.roll(tile, lane + 1, 1)
    at = iota(tile.shape, 1)
    return jnp.where((at == lane) | (at == lane + 1), moved, packed)


def counts_of(trainers_ref, count):
    at = iota((ROWS, LANES), 1)
    total = jnp.zeros((ROWS, LANES), jnp.float32)
    for j in range(count):
        total = total + jnp.where(at == trainers_ref[j], 1.0, 0.0)
    return total


def pack_faces(fields_far, visc_far, trainers_far, x_a, x_b, y_a, y_b, z_both, fields, visc, trainers, sems):
    _, planes, rows, _ = fields.shape
    chunks = rows // ROWS
    copies = [pltpu.make_async_copy(fields_far.at[f], fields.at[f], sems.at[f]) for f in range(NF)]
    copies.append(pltpu.make_async_copy(visc_far, visc, sems.at[NF]))
    listed = pltpu.make_async_copy(trainers_far, trainers, sems.at[NF + 1])
    for copy in copies:
        copy.start()
    listed.start()
    arrays = [fields.at[f] for f in range(NF)] + [visc]
    packed = [jnp.zeros((ROWS, LANES), jnp.float32) for _ in range(z_both.shape[0])]
    for f, array in enumerate(arrays):
        copies[f].wait()
        lay_out("gx", [(f, array[0])], [(f, array[planes - 1])], x_a, x_b)
        lay_out("gy", [(f, array[:, 0, :])], [(f, array[:, rows - 1, :])], y_a, y_b)
        for c in range(chunks):
            tile, lane = pair_of(f, c, planes, chunks)
            for x in range(planes):
                cells = array[x, ROWS * c : ROWS * c + ROWS]
                packed[tile] = add_pair(packed[tile], cells, lane + 2 * x)
    for tile, value in enumerate(packed):
        z_both[tile] = value
    listed.wait()
    counts = counts_of(trainers, trainers.shape[0])
    y_a[NF + 1] = counts
    y_b[NF + 1] = counts


def flux(lower, upper, dimension):
    speed = 0.25 * (lower[dimension] + upper[dimension])
    mean_visc = 0.5 * (lower[NF] + upper[NF])
    return [speed * (a + b) - mean_visc * (b - a) for a, b in zip(lower[:NF], upper[:NF])]


def interior(fields, visc, partial):
    _, planes, rows, _ = fields.shape
    chunks = rows // ROWS
    end_row = iota((ROWS, LANES), 0) == ROWS - 1
    end_lane = iota((ROWS, LANES), 1) == LANES - 1
    every = range(NF + 1)

    def cell(f, x, part):
        return fields[f, x, part, :] if f < NF else visc[x, part, :]

    def plane(x, lowers):
        uppers = []
        last = x == planes - 1
        beyond = jnp.minimum(x + 1, planes - 1)
        behind = [jnp.zeros((ROWS, LANES), jnp.float32)] * NF
        for c in range(chunks):
            part = slice(ROWS * c, ROWS * c + ROWS)
            here = [cell(f, x, part) for f in every]
            after = [cell(f, beyond, part) for f in every]
            upper = flux(here, after, 0)
            upper = [jnp.where(last, 0.0, u) for u in upper]
            total = [b - a for a, b in zip(lowers[c], upper)]
            uppers.append(upper)
            above = [pltpu.roll(h, ROWS - 1, 0) for h in here]
            if c + 1 < chunks:
                first = slice(ROWS * c + ROWS, ROWS * c + ROWS + 1)
                above = [jnp.where(end_row, cell(f, x, first), above[f]) for f in every]
            upper = flux(here, above, 1)
            lower = [pltpu.roll(jnp.where(end_row, b, u), 1, 0) for b, u in zip(behind, upper)]
            if c + 1 == chunks:
                upper = [jnp.where(end_row, 0.0, u) for u in upper]
            behind = upper
            total = [t + (b - a) for t, a, b in zip(total, lower, upper)]
            right = [pltpu.roll(h, LANES - 1, 1) for h in here]
            upper = [jnp.where(end_lane, 0.0, u) for u in flux(here, right, 2)]
            lower = [pltpu.roll(u, 1, 1) for u in upper]
            total = [t + (b - a) for t, a, b in zip(total, lower, upper)]
            updated = [q - time_step * t for q, t in zip(here[:NF], total)]
            updated[2] = updated[2] + (time_step * buoyancy) * here[3]
            for f in range(NF):
                partial[f, x, part, :] = updated[f]
        return uppers

    zeros = [[jnp.zeros((ROWS, LANES), jnp.float32)] * NF for _ in range(chunks)]
    lax.fori_loop(0, planes, plane, zeros)


def interior_and_weights(samples_far, trainers_far, fields, visc, conv_first, conv_second, conv_third,
                         partial, w_first, w_second_t, w_third, w_third_t, drawn, samples, trainers, sems):
    copies = [
        pltpu.make_async_copy(samples_far, samples, sems.at[0]),
        pltpu.make_async_copy(trainers_far, trainers, sems.at[1]),
    ]
    for copy in copies:
        copy.start()
    interior(fields, visc, partial)
    ahead = conv_first.shape[1]
    w_first[:, :ahead] = conv_first[...]
    w_first[:, ahead:] = jnp.zeros((CH, w_first.shape[1] - ahead), jnp.bfloat16)
    w_second_t[...] = conv_second[...].astype(jnp.float32).T.astype(jnp.bfloat16)
    third = conv_third[...].astype(jnp.float32)
    third = jnp.concatenate([third, jnp.zeros((w_third.shape[0] - NOUT, CH), jnp.float32)], 0)
    w_third[...] = third.astype(jnp.bfloat16)
    w_third_t[...] = third.T.astype(jnp.bfloat16)
    for copy in copies:
        copy.wait()
    at, row = iota((ROWS, LANES), 1), iota((ROWS, LANES), 0)
    table = jnp.zeros((ROWS, LANES), jnp.int32)
    for j in range(samples.shape[0]):
        table = jnp.where(at == j, jnp.where(row == 0, samples[j], trainers[j]), table)
    drawn[...] = table


def z_terms(own, other, visc_own, visc_other):
    lane = iota((ROWS, LANES), 1)
    second = lane % 2 == 1
    span = LANES // 2

    def ends(mine, theirs):
        lower = jnp.where(second, pltpu.roll(theirs, 1, 1), mine)
        return lower, jnp.where(second, mine, pltpu.roll(theirs, LANES - 1, 1))

    def twice(tile):
        return jnp.where(lane < span, tile, pltpu.roll(tile, span, 1))

    pairs = [ends(a, b) for a, b in zip(own, other)]
    speed = [twice(end) for end in pairs[2 * span // LANES]]
    visc = [twice(end) for end in ends(visc_own, visc_other)]
    speed = 0.25 * (speed[0] + speed[1])
    mean_visc = 0.5 * (visc[0] + visc[1])
    through = [speed * (a + b) - mean_visc * (b - a) for a, b in pairs]
    return [jnp.where(second, time_step, -time_step) * t for t in through]


def close(fields, visc, partial, halo, visc_halo, z_own, visc_z_own, y_terms, emit):
    _, planes, rows, _ = fields.shape
    chunks = rows // ROWS
    every = range(NF + 1)
    row = iota((ROWS, LANES), 0)
    lane_at = iota((ROWS, LANES), 1)
    ends = (lane_at == 0) | (lane_at == LANES - 1)

    def cell(f, *index):
        return fields[(f,) + index] if f < NF else visc[index]

    def sides(f):
        return halo if f < NF else visc_halo

    lower = flux([sides(f).prev("y", f) for f in every], [cell(f, slice(None), 0) for f in every], 1)
    upper = flux([cell(f, slice(None), rows - 1) for f in every], [sides(f).next("y", f) for f in every], 1)
    for f in range(NF):
        y_terms[0, f] = time_step * lower[f]
        y_terms[1, f] = -time_step * upper[f]
    tiles = z_own.shape[0] if z_own.shape[0] * LANES == 2 * NF * planes * chunks else z_own.shape[0] - 1
    terms = z_terms([z_own[t] for t in range(tiles)], [halo.z_both[t] for t in range(tiles)],
                    visc_z_own[tiles], visc_halo.z_both[tiles])
    for c in range(chunks):
        part = slice(ROWS * c, ROWS * c + ROWS)
        low = flux([sides(f).prev("x", f, part) for f in every], [cell(f, 0, part) for f in every], 0)
        high = flux([cell(f, planes - 1, part) for f in every], [sides(f).next("x", f, part) for f in every], 0)
        for x in range(planes):
            for f in range(NF):
                tile, lane = pair_of(f, c, planes, chunks)
                moved = pltpu.roll(terms[tile], LANES - 1 - lane - 2 * x, 1)
                value = partial[f, x, part, :] + jnp.where(ends, moved, 0.0)
                if x == 0:
                    value = value + time_step * low[f]
                if x == planes - 1:
                    value = value - time_step * high[f]
                if c == 0:
                    value = value + jnp.where(row == 0, y_terms[0, f, x : x + 1, :], 0.0)
                if c == chunks - 1:
                    value = value + jnp.where(row == ROWS - 1, y_terms[1, f, x : x + 1, :], 0.0)
                emit(f, x, c, value)


def close_first(fields, visc, partial, y_from_b, x_from_b, y_from_a, z_other, x_from_a, z_own,
                middle, x_a, x_b, y_a, y_b, z_both, y_terms):
    _, planes, rows, _ = fields.shape
    chunks = rows // ROWS
    halo = Sides(x_from_a, x_from_b, y_from_a, y_from_b, z_other)
    packed = [jnp.zeros((ROWS, LANES), jnp.float32) for _ in range(z_both.shape[0])]

    def emit(f, x, c, tile):
        middle[f, x, ROWS * c : ROWS * c + ROWS, :] = tile
        at, lane = pair_of(f, c, planes, chunks)
        packed[at] = add_pair(packed[at], tile, lane + 2 * x)

    close(fields, visc, partial, halo, halo, z_own, z_own, y_terms, emit)
    for at, value in enumerate(packed):
        z_both[at] = value
    for f in range(NF):
        lay_out("gx", [(f, middle[f, 0])], [(f, middle[f, planes - 1])], x_a, x_b)
        lay_out("gy", [(f, middle[f, :, 0, :])], [(f, middle[f, :, rows - 1, :])], y_a, y_b)
    y_b[NF] = y_from_a[NF + 1]


def inside_masks():
    at = iota((1, LANES), 1) % VOL
    coords = (at // (BLK * BLK), at // BLK % BLK, at % BLK)
    along = []
    for coord in coords:
        along.append({
            -1: jnp.where(coord > 0, 1.0, 0.0),
            0: jnp.ones((1, LANES), jnp.float32),
            1: jnp.where(coord < BLK - 1, 1.0, 0.0),
        })
    return along


def move_of(tap):
    return tap[0] * BLK * BLK + tap[1] * BLK + tap[2]


def shifted(tile, tap, along):
    move = move_of(tap)
    if move == 0:
        return tile
    mask = along[0][tap[0]] * along[1][tap[1]] * along[2][tap[2]]
    return pltpu.roll(tile, (-move) % LANES, 1) * mask


def box(tile, along):
    for dimension, step in enumerate((BLK * BLK, BLK, 1)):
        ahead = pltpu.roll(tile, LANES - step, 1) * along[dimension][1]
        behind = pltpu.roll(tile, step, 1) * along[dimension][-1]
        tile = (behind + tile) + ahead
    return tile / 27.0


def sigmoid(values):
    return 1.0 / (1.0 + jnp.exp(-values))


PICKED = (0, 1, 2, 3, 0, 1, 2, 3, 0, 1, 2, 0, 0, 1, -1, -1, 0, 1, 2, 1, 2, 2, -1, -1)


def pick_rows():
    out, field = iota((32, NF * ROWS), 0), iota((32, NF * ROWS), 1) // ROWS
    table = jnp.zeros((32, NF * ROWS), jnp.float32)
    for i, f in enumerate(PICKED):
        table = jnp.where((out == i) & (field == f), 1.0, table)
    return table.astype(jnp.bfloat16)


def pick_blocks(advanced, samples, count):
    _, _, rows, lanes = advanced.shape
    along_y, along_z = rows // BLK, lanes // BLK
    row = iota((ROWS, LANES), 0)
    lane_at = iota((ROWS, LANES), 1)
    pick = pick_rows()
    out = []
    for j in range(0, count, 2):
        parts = [jnp.zeros((ROWS, LANES), jnp.float32) for _ in range(NF)]
        uppers = []
        for half in range(2):
            block = samples[j + half]
            block_x = block // (along_y * along_z)
            block_y = block // along_z % along_y
            block_z = block % along_z
            uppers.append(block_y % 2)
            start = pl.multiple_of(block_y // 2 * ROWS, ROWS)
            for x in range(BLK):
                turn = lax.rem(VOL * half + BLK * BLK * x - BLK * block_z + LANES, LANES)
                wanted = lane_at // BLK == (VOL * half + BLK * BLK * x) // BLK
                for f in range(NF):
                    tile = advanced[f, block_x * BLK + x, pl.ds(start, ROWS), :]
                    parts[f] = jnp.where(wanted, pltpu.roll(tile, turn, 1), parts[f])
        upper = jnp.where(lane_at < VOL, uppers[0], uppers[1])
        valid = row // BLK == upper
        for f in range(NF):
            for bit in (1, 2):
                moved = pltpu.roll(parts[f], BLK * bit, 1)
                parts[f] = jnp.where(row // bit % 2 == 1, moved, parts[f])
            parts[f] = jnp.where(valid, parts[f], 0.0)
        stacked = jnp.concatenate(parts, 0).astype(jnp.bfloat16)
        out.append(jnp.dot(pick, stacked, preferred_element_type=jnp.float32))
    return out


def closure(advanced, samples, trainers, counts, w_first, w_second, w_second_t, w_third,
            w_third_t, devices_all, stack_first, stack_mid, rows_out, send, slots, inline, place):
    count = len(samples)
    pairs = count // 2
    cols = [slice(LANES * m, LANES * m + LANES) for m in range(pairs)]
    along = inside_masks()
    lane_at = iota((ROWS, LANES), 1)
    row = iota((ROWS, LANES), 0)

    picked = pick_blocks(advanced, samples, count)
    values = [p[:ROWS] for p in picked]
    targets = []
    for p in picked:
        first, second = p[ROWS : 2 * ROWS], p[2 * ROWS : 3 * ROWS]
        targets.append(box(first * second, along) - box(first, along) * box(second, along))

    for m, tile in enumerate(values):
        for t in range(0, 28, 2):
            piece = shifted(tile, TAPS[t], along)
            later = shifted(tile, TAPS[t + 1], along) if t + 1 < 27 else jnp.zeros_like(tile)
            stack_first[BLK * t : BLK * t + ROWS, cols[m]] = jnp.where(row < NF, piece, later)
    stack_in = stack_first[...].astype(jnp.bfloat16)
    pre_first = jnp.dot(w_first, stack_in, preferred_element_type=jnp.float32)
    gate_first = sigmoid(pre_first)
    hidden_first = (pre_first * gate_first).astype(jnp.bfloat16).astype(jnp.float32)
    for m in range(pairs):
        tile = hidden_first[:, cols[m]]
        for k, tap in enumerate(TAPS):
            stack_mid[CH * k : CH * k + CH, cols[m]] = shifted(tile, tap, along).astype(jnp.bfloat16)
    pre_second = jnp.dot(w_second, stack_mid[...], preferred_element_type=jnp.float32)
    gate_second = sigmoid(pre_second)
    hidden_second = (pre_second * gate_second).astype(jnp.bfloat16)
    predicted = jnp.dot(w_third, hidden_second, preferred_element_type=jnp.float32)

    misfit = predicted[:ROWS] - jnp.concatenate(targets, 1)
    square = jnp.sum(misfit * misfit, axis=0, keepdims=True)
    sample_at = iota((ROWS, count * VOL), 1) // VOL
    mine = sample_at == iota((ROWS, count * VOL), 0)
    losses = jnp.sum(jnp.where(mine, square, 0.0), axis=1, keepdims=True) / (NOUT * VOL)
    owner = jnp.zeros((ROWS, LANES), jnp.int32)
    for j in range(count):
        owner = jnp.where(row == j, trainers[j], owner)
    load = jnp.sum(jnp.where(lane_at == owner, counts, 0.0), axis=1, keepdims=True)
    share = 1.0 / (devices_all * jnp.maximum(load, 1.0))
    scale = share * (2.0 / (NOUT * VOL))
    scale_at = jnp.sum(jnp.where(mine, scale, 0.0), axis=0, keepdims=True)
    grad_pred = (misfit * scale_at).astype(jnp.bfloat16)
    grad_pred = jnp.concatenate([grad_pred, jnp.zeros_like(grad_pred)], 0)

    upper = jnp.dot(w_third_t, grad_pred, preferred_element_type=jnp.float32)
    slope = gate_second * (1.0 + pre_second * (1.0 - gate_second))
    grad_mid = (upper * slope).astype(jnp.bfloat16)
    grad_second = lax.dot_general(grad_mid, stack_mid[...], FULL, preferred_element_type=jnp.float32)
    third = jnp.concatenate([grad_pred, jnp.zeros((LANES - 16, count * VOL), jnp.bfloat16)], 0)
    grad_third = lax.dot_general(hidden_second, third, FULL, preferred_element_type=jnp.float32)

    spread = jnp.dot(w_second_t, grad_mid, preferred_element_type=jnp.float32)
    lower = []
    for m in range(pairs):
        terms = [
            shifted(spread[CH * k : CH * k + CH, cols[m]], tuple(-o for o in tap), along)
            for k, tap in enumerate(TAPS)
        ]
        lower.append(functools.reduce(jnp.add, terms))
    lower = jnp.concatenate(lower, 1)
    slope = gate_first * (1.0 + pre_first * (1.0 - gate_first))
    grad_entry = (lower * slope).astype(jnp.bfloat16)
    grad_first = lax.dot_general(grad_entry, stack_in, FULL, preferred_element_type=jnp.float32)

    whole = CH * 27 // LANES
    rest = CH * 27 - whole * LANES
    for t in range(whole):
        rows_out[:, t, :] = grad_second[:, LANES * t : LANES * t + LANES]
    mixed = jnp.concatenate([grad_second[:, whole * LANES :], jnp.zeros((CH, LANES - rest), jnp.float32)], 1)
    mixed = mixed + pltpu.roll(grad_third, rest, 1)
    tail = LANES - grad_first.shape[1]
    rows_out[:, whole + 1, :] = jnp.concatenate([grad_first, jnp.zeros((CH, tail), jnp.float32)], 1)

    pos_x, pos_y, pos_z, count_y, count_z = place
    offset = rest + ROWS if inline else 0
    height = CH if inline else slots.shape[0]
    slot_rows = iota((height, LANES), 0)
    slot_lanes = iota((height, LANES), 1)
    placed = jnp.zeros((height, LANES), jnp.float32)
    for j in range(count):
        name = trainers[j]
        rank = jnp.int32(0)
        for i in range(j):
            rank = rank + jnp.where(trainers[i] == name, 1, 0)
        target = (pos_x * count_y + name) * count_z + pos_z
        slot = offset + pos_y * CAP + rank
        hit = (slot_rows == target) & (slot_lanes == slot)
        placed = jnp.where(hit, losses[j : j + 1, :], placed)
    high = placed.astype(jnp.bfloat16).astype(jnp.float32)
    placed = high + pltpu.roll(placed - high, count_y * CAP, 1)
    if inline:
        mixed = mixed + placed
    else:
        slots[:, 0, :] = placed.astype(jnp.bfloat16)
    rows_out[:, whole, :] = mixed
    send[...] = rows_out[...].astype(jnp.bfloat16)


def second_step(sizes, inline, drawn, middle, visc, partial, vy_b, vx_b, vy_a, vz_other, vx_a, vz_own,
                y_b, x_b, y_a, z_other, x_a, z_own, *rest):
    counts = None if sizes["gy"] == 4 else rest[0]
    rest = rest if counts is None else rest[1:]
    w_first, w_second, w_second_t, w_third, w_third_t, advanced_far, send = rest[:7]
    slots = None if inline else rest[7]
    stack_first, stack_mid, rows_out, y_terms, advanced, sems = rest[-6:]
    halo = Sides(x_a, x_b, y_a, y_b, z_other)
    visc_halo = Sides(vx_a, vx_b, vy_a, vy_b, vz_other)
    count = stack_mid.shape[1] // VOL
    samples = [drawn[0, j] for j in range(count)]
    trainers = [drawn[1, j] for j in range(count)]

    def emit(f, x, c, tile):
        advanced[f, x, ROWS * c : ROWS * c + ROWS, :] = tile

    close(middle, visc, partial, halo, visc_halo, z_own, vz_own, y_terms, emit)
    copies = [pltpu.make_async_copy(advanced.at[f], advanced_far.at[f], sems.at[f]) for f in range(NF)]
    for copy in copies:
        copy.start()
    if counts is None:
        total = counts_of(trainers, count) + vy_a[NF + 1] + vy_b[NF + 1] + y_b[NF]
    else:
        total = counts[...]
    place = (lax.axis_index("gx"), lax.axis_index("gy"), lax.axis_index("gz"), sizes["gy"], sizes["gz"])
    closure(advanced, samples, trainers, total, w_first[...], w_second[...],
            w_second_t[...], w_third[...], w_third_t[...],
            float(sizes["gx"] * sizes["gy"] * sizes["gz"]), stack_first, stack_mid, rows_out,
            send, slots, inline, place)
    for copy in copies:
        copy.wait()


def add_up(arrived, spread, own):
    total = jnp.sum(arrived[...].astype(jnp.float32), axis=0)
    own[...] = total
    rounded = total.astype(jnp.bfloat16)
    for i in range(spread.shape[0]):
        spread[i] = rounded


def unpack(where, gathered, own, first, second, third, losses, wide):
    row, lane = where
    count = losses.shape[3]
    high = own[row : row + 1, lane : lane + count]
    losses[0, 0] = high + own[row : row + 1, lane + count : lane + 2 * count]
    wide[...] = gathered[...].astype(jnp.float32)
    whole = second.shape[1] // LANES
    rest = second.shape[1] - whole * LANES
    for t in range(whole):
        second[:, LANES * t : LANES * t + LANES] = wide[:, t, :]
    mixed = wide[:, whole, :]
    second[:, LANES * whole :] = mixed[:, :rest]
    third[...] = mixed[:, rest : rest + ROWS].T[:NOUT]
    first[...] = wide[:, whole + 1, :][:, : first.shape[1]]


def shape_of(*dims, dtype=jnp.float32):
    return jax.ShapeDtypeStruct(dims, dtype)


def exchange(x_a, x_b, y_a, y_b, z_both, sizes):
    def swap_a(axis):
        return [(i, i ^ 1) for i in range(sizes[axis])]

    def swap_b(axis):
        return [(i, (i + (1 if i % 2 else -1)) % sizes[axis]) for i in range(sizes[axis])]

    y_b = lax.ppermute(y_b, "gy", swap_b("gy"))
    x_b = lax.ppermute(x_b, "gx", swap_b("gx"))
    y_a = lax.ppermute(y_a, "gy", swap_a("gy"))
    z_both = lax.ppermute(z_both, "gz", swap_a("gz"))
    x_a = lax.ppermute(x_a, "gx", swap_a("gx"))
    return y_b, x_b, y_a, z_both, x_a


def without_border(kernel, fields, visc, index=(), weights=()):
    cells = visc.size
    out_shape = [shape_of(*fields.shape)]
    scratch = [pltpu.SMEM(array.shape, jnp.int32) for array in index]
    if weights:
        scratch.append(pltpu.SemaphoreType.DMA((len(index),)))
        sizes = ((CH, 28 * NF), (27 * CH, CH), (16, CH), (CH, 16))
        out_shape += [shape_of(*size, dtype=jnp.bfloat16) for size in sizes]
        out_shape.append(shape_of(ROWS, LANES, dtype=jnp.int32))
    return pl.pallas_call(
        kernel,
        out_shape=out_shape,
        in_specs=[ANY] * len(index) + [VMEM] * (2 + len(weights)),
        out_specs=[VMEM] * len(out_shape),
        scratch_shapes=scratch,
        compiler_params=PARAMS,
        cost_estimate=pl.CostEstimate(flops=120 * cells, bytes_accessed=36 * cells, transcendentals=0),
        name=kernel.__name__,
    )(*index, fields, visc, *weights)


def on_device(sizes, fields, visc, samples, trainers, conv_first, conv_second, conv_third):
    _, planes, rows, lanes = fields.shape
    axes = ("gx", "gy", "gz")
    devices_all = sizes["gx"] * sizes["gy"] * sizes["gz"]
    pairs = planes * rows // ROWS
    half = LANES // 2
    samples = samples.reshape(-1)
    trainers = trainers.reshape(-1)

    faces = pl.pallas_call(
        pack_faces,
        out_shape=[
            shape_of(NF + 1, rows, lanes),
            shape_of(NF + 1, rows, lanes),
            shape_of(NF + 2, planes, lanes),
            shape_of(NF + 2, planes, lanes),
            shape_of(-(-(NF + 1) * pairs // half), ROWS, LANES),
        ],
        in_specs=[HBM, HBM, HBM],
        out_specs=[VMEM] * 5,
        scratch_shapes=[
            pltpu.VMEM(fields.shape, jnp.float32),
            pltpu.VMEM(visc.shape, jnp.float32),
            pltpu.SMEM(trainers.shape, jnp.int32),
            pltpu.SemaphoreType.DMA((NF + 2,)),
        ],
        compiler_params=PACK,
        name="pack_faces",
    )(fields, visc, trainers)
    halo = exchange(*faces, sizes)

    own_counts = sizes["gy"] == 4
    counts = []
    if not own_counts:
        named = trainers.reshape(-1, 1) == jnp.arange(LANES, dtype=jnp.int32)[None, :]
        total = lax.psum(jnp.sum(named.astype(jnp.float32), axis=0, keepdims=True), "gy")
        counts = [jnp.broadcast_to(total, (ROWS, LANES))]
    z_own = faces[4]
    y_terms = pltpu.VMEM((2, NF, planes, lanes), jnp.float32)
    middle, *faces = pl.pallas_call(
        close_first,
        out_shape=[
            shape_of(*fields.shape),
            shape_of(NF, rows, lanes),
            shape_of(NF, rows, lanes),
            shape_of(NF, planes, lanes),
            shape_of(NF + 1, planes, lanes),
            shape_of(-(-NF * pairs // half), ROWS, LANES),
        ],
        in_specs=[VMEM] * 9,
        out_specs=[VMEM] * 6,
        scratch_shapes=[y_terms],
        compiler_params=PARAMS,
        name="close_first",
    )(fields, visc, *without_border(interior, fields, visc), *halo, z_own)
    later = exchange(*faces, sizes)
    partial, w_first, w_second_t, w_third, w_third_t, drawn = without_border(
        interior_and_weights, middle, visc, (samples, trainers), (conv_first, conv_second, conv_third)
    )

    count = samples.shape[0]
    slot_total = sizes["gy"] * CAP
    tiles = -(-27 * CH // LANES) + 1
    parts = devices_all // CH
    inline = parts == 1 and slot_total <= 12
    out_shape = [shape_of(*fields.shape), shape_of(CH, tiles, LANES, dtype=jnp.bfloat16)]
    if not inline:
        out_shape.append(shape_of(devices_all, 1, LANES, dtype=jnp.bfloat16))
    advanced, send, *slots = pl.pallas_call(
        functools.partial(second_step, sizes, inline),
        out_shape=out_shape,
        in_specs=[VMEM] * (21 if own_counts else 22),
        out_specs=[HBM] + [VMEM] * (len(out_shape) - 1),
        scratch_shapes=[
            pltpu.VMEM((28 * NF, count * VOL), jnp.float32),
            pltpu.VMEM((27 * CH, count * VOL), jnp.bfloat16),
            pltpu.VMEM((CH, tiles, LANES), jnp.float32),
            y_terms,
            pltpu.VMEM(fields.shape, jnp.float32),
            pltpu.SemaphoreType.DMA((NF,)),
        ],
        compiler_params=PARAMS,
        name="second_step",
    )(drawn, middle, visc, partial, *halo, z_own, *later, faces[4], *counts,
      w_first, conv_second, w_second_t, w_third, w_third_t)

    if not inline:
        send = jnp.concatenate([send.reshape(devices_all, tiles // parts, LANES), slots[0]], 1)
    arrived = lax.all_to_all(send, axes, split_axis=0, concat_axis=0, tiled=True)
    if inline:
        where = (27 * CH // LANES, 27 * CH % LANES + ROWS)
    else:
        where = (send.shape[1] - 1, 0)
    spread, own = pl.pallas_call(
        add_up,
        out_shape=[shape_of(*send.shape, dtype=jnp.bfloat16), shape_of(*send.shape[1:])],
        in_specs=[VMEM],
        out_specs=[VMEM] * 2,
        compiler_params=PARAMS,
        name="add_up",
    )(arrived)
    if not inline:
        spread = spread[:, :-1, :]
    gathered = lax.all_to_all(spread, axes, split_axis=0, concat_axis=0, tiled=True)
    first, second, third, block_losses = pl.pallas_call(
        functools.partial(unpack, where),
        out_shape=[
            shape_of(*conv_first.shape),
            shape_of(*conv_second.shape),
            shape_of(*conv_third.shape),
            shape_of(1, 1, 1, slot_total),
        ],
        in_specs=[VMEM] * 2,
        out_specs=[VMEM] * 4,
        scratch_shapes=[pltpu.VMEM((CH, tiles, LANES), jnp.float32)],
        compiler_params=PARAMS,
        name="unpack",
    )(gathered.reshape(CH, tiles, LANES), own)
    return advanced, block_losses, first, second, third


def solution(mesh):
    sizes = dict(mesh.shape)
    in_specs = (
        P(None, "gx", "gy", "gz"),
        P("gx", "gy", "gz"),
        P("gx", "gy", "gz", None),
        P("gx", "gy", "gz", None, None),
        P(),
        P(),
        P(),
    )
    out_specs = (P(None, "gx", "gy", "gz"), P("gx", "gy", "gz", None), P(), P(), P())
    return jax.shard_map(
        functools.partial(on_device, sizes), mesh=mesh, in_specs=in_specs, out_specs=out_specs,
        check_vma=False,
    )
```

```python
import functools

import jax
import jax.numpy as jnp
from jax import lax
from jax.experimental import pallas as pl
from jax.experimental.pallas import tpu as pltpu
from jax.sharding import PartitionSpec as P

BLK = 4
CAP = 2
SAMP = 8
NF = 4
VOL = BLK**3
TAPS = [(x, y, z) for x in (-1, 0, 1) for y in (-1, 0, 1) for z in (-1, 0, 1)]
LANES = 128
ROWS = 8
NOUT = 6
CH = 32

time_step = 0.25
buoyancy = 0.5

VMEM = pl.BlockSpec(memory_space=pltpu.VMEM)
SMEM = pl.BlockSpec(memory_space=pltpu.SMEM)
HBM = pl.BlockSpec(memory_space=pltpu.HBM)
ANY = pl.BlockSpec(memory_space=pl.ANY)
PARAMS = pltpu.CompilerParams(vmem_limit_bytes=24 * 1024 * 1024)
PACK = pltpu.CompilerParams(vmem_limit_bytes=54944 * 1024)
FULL = (((1,), (1,)), ((), ()))


def iota(shape, axis):
    return lax.broadcasted_iota(jnp.int32, shape, axis)


def odd(axis):
    return lax.axis_index(axis) % 2 == 1


def lay_out(axis, first, last, swap_a, swap_b):
    turned = odd(axis)
    for (index, low), (_, high) in zip(first, last):
        swap_a[index] = jnp.where(turned, low, high)
        swap_b[index] = jnp.where(turned, high, low)


class Sides:
    def __init__(self, x_a, x_b, y_a, y_b, z_both):
        self.faces = dict(x=(x_a, x_b), y=(y_a, y_b))
        self.odd = dict(x=odd("gx"), y=odd("gy"))
        self.z_both = z_both

    def prev(self, axis, *index):
        a, b = self.faces[axis]
        return jnp.where(self.odd[axis], a[index], b[index])

    def next(self, axis, *index):
        a, b = self.faces[axis]
        return jnp.where(self.odd[axis], b[index], a[index])


def pair_of(f, c, planes, chunks):
    span = 2 * planes * chunks
    return f * span // LANES, f * span % LANES + 2 * planes * c


def add_pair(packed, tile, lane):
    moved = pltpu.roll(tile, lane + 1, 1)
    at = iota(tile.shape, 1)
    return jnp.where((at == lane) | (at == lane + 1), moved, packed)


def pack_faces(fields_far, visc_far, x_a, x_b, y_a, y_b, z_both, fields, visc, sems):
    _, planes, rows, _ = fields.shape
    chunks = rows // ROWS
    copies = [pltpu.make_async_copy(fields_far.at[f], fields.at[f], sems.at[f]) for f in range(NF)]
    copies.append(pltpu.make_async_copy(visc_far, visc, sems.at[NF]))
    for copy in copies:
        copy.start()
    arrays = [fields.at[f] for f in range(NF)] + [visc]
    packed = [jnp.zeros((ROWS, LANES), jnp.float32) for _ in range(z_both.shape[0])]
    for f, array in enumerate(arrays):
        copies[f].wait()
        lay_out("gx", [(f, array[0])], [(f, array[planes - 1])], x_a, x_b)
        lay_out("gy", [(f, array[:, 0, :])], [(f, array[:, rows - 1, :])], y_a, y_b)
        for c in range(chunks):
            tile, lane = pair_of(f, c, planes, chunks)
            for x in range(planes):
                cells = array[x, ROWS * c : ROWS * c + ROWS]
                packed[tile] = add_pair(packed[tile], cells, lane + 2 * x)
    for tile, value in enumerate(packed):
        z_both[tile] = value


def flux(lower, upper, dimension):
    speed = 0.25 * (lower[dimension] + upper[dimension])
    mean_visc = 0.5 * (lower[NF] + upper[NF])
    return [speed * (a + b) - mean_visc * (b - a) for a, b in zip(lower[:NF], upper[:NF])]


def interior(fields, visc, partial):
    _, planes, rows, _ = fields.shape
    chunks = rows // ROWS
    end_row = iota((ROWS, LANES), 0) == ROWS - 1
    end_lane = iota((ROWS, LANES), 1) == LANES - 1
    every = range(NF + 1)

    def cell(f, x, part):
        return fields[f, x, part, :] if f < NF else visc[x, part, :]

    def plane(x, lowers):
        uppers = []
        last = x == planes - 1
        beyond = jnp.minimum(x + 1, planes - 1)
        behind = [jnp.zeros((ROWS, LANES), jnp.float32)] * NF
        for c in range(chunks):
            part = slice(ROWS * c, ROWS * c + ROWS)
            here = [cell(f, x, part) for f in every]
            after = [cell(f, beyond, part) for f in every]
            upper = flux(here, after, 0)
            upper = [jnp.where(last, 0.0, u) for u in upper]
            total = [b - a for a, b in zip(lowers[c], upper)]
            uppers.append(upper)
            above = [pltpu.roll(h, ROWS - 1, 0) for h in here]
            if c + 1 < chunks:
                first = slice(ROWS * c + ROWS, ROWS * c + ROWS + 1)
                above = [jnp.where(end_row, cell(f, x, first), above[f]) for f in every]
            upper = flux(here, above, 1)
            lower = [pltpu.roll(jnp.where(end_row, b, u), 1, 0) for b, u in zip(behind, upper)]
            if c + 1 == chunks:
                upper = [jnp.where(end_row, 0.0, u) for u in upper]
            behind = upper
            total = [t + (b - a) for t, a, b in zip(total, lower, upper)]
            right = [pltpu.roll(h, LANES - 1, 1) for h in here]
            upper = [jnp.where(end_lane, 0.0, u) for u in flux(here, right, 2)]
            lower = [pltpu.roll(u, 1, 1) for u in upper]
            total = [t + (b - a) for t, a, b in zip(total, lower, upper)]
            updated = [q - time_step * t for q, t in zip(here[:NF], total)]
            updated[2] = updated[2] + (time_step * buoyancy) * here[3]
            for f in range(NF):
                partial[f, x, part, :] = updated[f]
        return uppers

    zeros = [[jnp.zeros((ROWS, LANES), jnp.float32)] * NF for _ in range(chunks)]
    lax.fori_loop(0, planes, plane, zeros)


def interior_and_weights(samples_far, trainers_far, fields, visc, conv_first, conv_second, conv_third,
                         partial, w_first, w_second_t, w_third, w_third_t, drawn, samples, trainers, sems):
    copies = [
        pltpu.make_async_copy(samples_far, samples, sems.at[0]),
        pltpu.make_async_copy(trainers_far, trainers, sems.at[1]),
    ]
    for copy in copies:
        copy.start()
    interior(fields, visc, partial)
    ahead = conv_first.shape[1]
    w_first[:, :ahead] = conv_first[...]
    w_first[:, ahead:] = jnp.zeros((CH, w_first.shape[1] - ahead), jnp.bfloat16)
    w_second_t[...] = conv_second[...].astype(jnp.float32).T.astype(jnp.bfloat16)
    third = conv_third[...].astype(jnp.float32)
    third = jnp.concatenate([third, jnp.zeros((w_third.shape[0] - NOUT, CH), jnp.float32)], 0)
    w_third[...] = third.astype(jnp.bfloat16)
    w_third_t[...] = third.T.astype(jnp.bfloat16)
    for copy in copies:
        copy.wait()
    at, row = iota((ROWS, LANES), 1), iota((ROWS, LANES), 0)
    table = jnp.zeros((ROWS, LANES), jnp.int32)
    for j in range(samples.shape[0]):
        table = jnp.where(at == j, jnp.where(row == 0, samples[j], trainers[j]), table)
    drawn[...] = table


def z_terms(own, other, visc_own, visc_other):
    lane = iota((ROWS, LANES), 1)
    second = lane % 2 == 1
    span = LANES // 2

    def ends(mine, theirs):
        lower = jnp.where(second, pltpu.roll(theirs, 1, 1), mine)
        return lower, jnp.where(second, mine, pltpu.roll(theirs, LANES - 1, 1))

    def twice(tile):
        return jnp.where(lane < span, tile, pltpu.roll(tile, span, 1))

    pairs = [ends(a, b) for a, b in zip(own, other)]
    speed = [twice(end) for end in pairs[2 * span // LANES]]
    visc = [twice(end) for end in ends(visc_own, visc_other)]
    speed = 0.25 * (speed[0] + speed[1])
    mean_visc = 0.5 * (visc[0] + visc[1])
    through = [speed * (a + b) - mean_visc * (b - a) for a, b in pairs]
    return [jnp.where(second, time_step, -time_step) * t for t in through]


def close(fields, visc, partial, halo, visc_halo, z_own, visc_z_own, y_terms, emit):
    _, planes, rows, _ = fields.shape
    chunks = rows // ROWS
    every = range(NF + 1)
    row = iota((ROWS, LANES), 0)
    lane_at = iota((ROWS, LANES), 1)
    ends = (lane_at == 0) | (lane_at == LANES - 1)

    def cell(f, *index):
        return fields[(f,) + index] if f < NF else visc[index]

    def sides(f):
        return halo if f < NF else visc_halo

    lower = flux([sides(f).prev("y", f) for f in every], [cell(f, slice(None), 0) for f in every], 1)
    upper = flux([cell(f, slice(None), rows - 1) for f in every], [sides(f).next("y", f) for f in every], 1)
    for f in range(NF):
        y_terms[0, f] = time_step * lower[f]
        y_terms[1, f] = -time_step * upper[f]
    tiles = z_own.shape[0] if z_own.shape[0] * LANES == 2 * NF * planes * chunks else z_own.shape[0] - 1
    terms = z_terms([z_own[t] for t in range(tiles)], [halo.z_both[t] for t in range(tiles)],
                    visc_z_own[tiles], visc_halo.z_both[tiles])
    for c in range(chunks):
        part = slice(ROWS * c, ROWS * c + ROWS)
        low = flux([sides(f).prev("x", f, part) for f in every], [cell(f, 0, part) for f in every], 0)
        high = flux([cell(f, planes - 1, part) for f in every], [sides(f).next("x", f, part) for f in every], 0)
        for x in range(planes):
            for f in range(NF):
                tile, lane = pair_of(f, c, planes, chunks)
                moved = pltpu.roll(terms[tile], LANES - 1 - lane - 2 * x, 1)
                value = partial[f, x, part, :] + jnp.where(ends, moved, 0.0)
                if x == 0:
                    value = value + time_step * low[f]
                if x == planes - 1:
                    value = value - time_step * high[f]
                if c == 0:
                    value = value + jnp.where(row == 0, y_terms[0, f, x : x + 1, :], 0.0)
                if c == chunks - 1:
                    value = value + jnp.where(row == ROWS - 1, y_terms[1, f, x : x + 1, :], 0.0)
                emit(f, x, c, value)


def close_first(fields, visc, partial, y_from_b, x_from_b, y_from_a, z_other, x_from_a, z_own,
                middle, x_a, x_b, y_a, y_b, z_both, y_terms):
    _, planes, rows, _ = fields.shape
    chunks = rows // ROWS
    halo = Sides(x_from_a, x_from_b, y_from_a, y_from_b, z_other)
    packed = [jnp.zeros((ROWS, LANES), jnp.float32) for _ in range(z_both.shape[0])]

    def emit(f, x, c, tile):
        middle[f, x, ROWS * c : ROWS * c + ROWS, :] = tile
        at, lane = pair_of(f, c, planes, chunks)
        packed[at] = add_pair(packed[at], tile, lane + 2 * x)

    close(fields, visc, partial, halo, halo, z_own, z_own, y_terms, emit)
    for at, value in enumerate(packed):
        z_both[at] = value
    for f in range(NF):
        lay_out("gx", [(f, middle[f, 0])], [(f, middle[f, planes - 1])], x_a, x_b)
        lay_out("gy", [(f, middle[f, :, 0, :])], [(f, middle[f, :, rows - 1, :])], y_a, y_b)


def inside_masks():
    at = iota((1, LANES), 1) % VOL
    coords = (at // (BLK * BLK), at // BLK % BLK, at % BLK)
    along = []
    for coord in coords:
        along.append({
            -1: jnp.where(coord > 0, 1.0, 0.0),
            0: jnp.ones((1, LANES), jnp.float32),
            1: jnp.where(coord < BLK - 1, 1.0, 0.0),
        })
    return along


def move_of(tap):
    return tap[0] * BLK * BLK + tap[1] * BLK + tap[2]


def shifted(tile, tap, along):
    move = move_of(tap)
    if move == 0:
        return tile
    mask = along[0][tap[0]] * along[1][tap[1]] * along[2][tap[2]]
    return pltpu.roll(tile, (-move) % LANES, 1) * mask


def box(tile, along):
    for dimension, step in enumerate((BLK * BLK, BLK, 1)):
        ahead = pltpu.roll(tile, LANES - step, 1) * along[dimension][1]
        behind = pltpu.roll(tile, step, 1) * along[dimension][-1]
        tile = (behind + tile) + ahead
    return tile / 27.0


def sigmoid(values):
    return 1.0 / (1.0 + jnp.exp(-values))


PICKED = (0, 1, 2, 3, 0, 1, 2, 3, 0, 1, 2, 0, 0, 1, -1, -1, 0, 1, 2, 1, 2, 2, -1, -1)


def pick_rows():
    out, field = iota((32, NF * ROWS), 0), iota((32, NF * ROWS), 1) // ROWS
    table = jnp.zeros((32, NF * ROWS), jnp.float32)
    for i, f in enumerate(PICKED):
        table = jnp.where((out == i) & (field == f), 1.0, table)
    return table.astype(jnp.bfloat16)


def pick_blocks(advanced, samples, count):
    _, _, rows, lanes = advanced.shape
    along_y, along_z = rows // BLK, lanes // BLK
    row = iota((ROWS, LANES), 0)
    lane_at = iota((ROWS, LANES), 1)
    pick = pick_rows()
    out = []
    for j in range(0, count, 2):
        parts = [jnp.zeros((ROWS, LANES), jnp.float32) for _ in range(NF)]
        uppers = []
        for half in range(2):
            block = samples[j + half]
            block_x = block // (along_y * along_z)
            block_y = block // along_z % along_y
            block_z = block % along_z
            uppers.append(block_y % 2)
            start = pl.multiple_of(block_y // 2 * ROWS, ROWS)
            for x in range(BLK):
                turn = lax.rem(VOL * half + BLK * BLK * x - BLK * block_z + LANES, LANES)
                wanted = lane_at // BLK == (VOL * half + BLK * BLK * x) // BLK
                for f in range(NF):
                    tile = advanced[f, block_x * BLK + x, pl.ds(start, ROWS), :]
                    parts[f] = jnp.where(wanted, pltpu.roll(tile, turn, 1), parts[f])
        upper = jnp.where(lane_at < VOL, uppers[0], uppers[1])
        valid = row // BLK == upper
        for f in range(NF):
            for bit in (1, 2):
                moved = pltpu.roll(parts[f], BLK * bit, 1)
                parts[f] = jnp.where(row // bit % 2 == 1, moved, parts[f])
            parts[f] = jnp.where(valid, parts[f], 0.0)
        stacked = jnp.concatenate(parts, 0).astype(jnp.bfloat16)
        out.append(jnp.dot(pick, stacked, preferred_element_type=jnp.float32))
    return out


def closure(advanced, samples, trainers, loads, w_first, w_second, w_second_t, w_third,
            w_third_t, devices_all, stack_first, stack_mid, rows_out, send, slots, inline, place, leave):
    count = len(samples)
    pairs = count // 2
    cols = [slice(LANES * m, LANES * m + LANES) for m in range(pairs)]
    along = inside_masks()
    lane_at = iota((ROWS, LANES), 1)
    row = iota((ROWS, LANES), 0)

    pos_x, pos_y, pos_z, count_y, count_z = place
    picked = pick_blocks(advanced, samples, count)
    values = [p[:ROWS] for p in picked]
    targets = []
    for p in picked:
        first, second = p[ROWS : 2 * ROWS], p[2 * ROWS : 3 * ROWS]
        targets.append(box(first * second, along) - box(first, along) * box(second, along))

    for m, tile in enumerate(values):
        for t in range(0, 28, 2):
            piece = shifted(tile, TAPS[t], along)
            later = shifted(tile, TAPS[t + 1], along) if t + 1 < 27 else jnp.zeros_like(tile)
            stack_first[BLK * t : BLK * t + ROWS, cols[m]] = jnp.where(row < NF, piece, later)
    stack_in = stack_first[...].astype(jnp.bfloat16)
    pre_first = jnp.dot(w_first, stack_in, preferred_element_type=jnp.float32)
    gate_first = sigmoid(pre_first)
    hidden_first = (pre_first * gate_first).astype(jnp.bfloat16).astype(jnp.float32)
    for m in range(pairs):
        tile = hidden_first[:, cols[m]]
        for k, tap in enumerate(TAPS):
            stack_mid[CH * k : CH * k + CH, cols[m]] = shifted(tile, tap, along).astype(jnp.bfloat16)
    leave()
    pre_second = jnp.dot(w_second, stack_mid[...], preferred_element_type=jnp.float32)
    gate_second = sigmoid(pre_second)
    hidden_second = (pre_second * gate_second).astype(jnp.bfloat16)
    predicted = jnp.dot(w_third, hidden_second, preferred_element_type=jnp.float32)

    misfit = predicted[:ROWS] - jnp.concatenate(targets, 1)
    square = jnp.sum(misfit * misfit, axis=0, keepdims=True)
    sample_at = iota((ROWS, count * VOL), 1) // VOL
    mine = sample_at == iota((ROWS, count * VOL), 0)
    losses = jnp.sum(jnp.where(mine, square, 0.0), axis=1, keepdims=True) / (NOUT * VOL)
    if loads is None:
        load = jnp.full((ROWS, 1), float(count_y * CAP), jnp.float32)
    else:
        owner = jnp.zeros((ROWS, LANES), jnp.int32)
        for j in range(count):
            owner = jnp.where(row == j, trainers[j], owner)
        load = jnp.sum(jnp.where(lane_at == owner, loads, 0.0), axis=1, keepdims=True)
    share = 1.0 / (devices_all * jnp.maximum(load, 1.0))
    scale = share * (2.0 / (NOUT * VOL))
    scale_at = jnp.sum(jnp.where(mine, scale, 0.0), axis=0, keepdims=True)
    grad_pred = (misfit * scale_at).astype(jnp.bfloat16)
    grad_pred = jnp.concatenate([grad_pred, jnp.zeros_like(grad_pred)], 0)

    upper = jnp.dot(w_third_t, grad_pred, preferred_element_type=jnp.float32)
    slope = gate_second * (1.0 + pre_second * (1.0 - gate_second))
    grad_mid = (upper * slope).astype(jnp.bfloat16)
    grad_second = lax.dot_general(grad_mid, stack_mid[...], FULL, preferred_element_type=jnp.float32)
    third = jnp.concatenate([grad_pred, jnp.zeros((LANES - 16, count * VOL), jnp.bfloat16)], 0)
    grad_third = lax.dot_general(hidden_second, third, FULL, preferred_element_type=jnp.float32)

    spread = jnp.dot(w_second_t, grad_mid, preferred_element_type=jnp.float32)
    lower = []
    for m in range(pairs):
        terms = [
            shifted(spread[CH * k : CH * k + CH, cols[m]], tuple(-o for o in tap), along)
            for k, tap in enumerate(TAPS)
        ]
        lower.append(functools.reduce(jnp.add, terms))
    lower = jnp.concatenate(lower, 1)
    slope = gate_first * (1.0 + pre_first * (1.0 - gate_first))
    grad_entry = (lower * slope).astype(jnp.bfloat16)
    grad_first = lax.dot_general(grad_entry, stack_in, FULL, preferred_element_type=jnp.float32)

    whole = CH * 27 // LANES
    rest = CH * 27 - whole * LANES
    for t in range(whole):
        rows_out[:, t, :] = grad_second[:, LANES * t : LANES * t + LANES]
    mixed = jnp.concatenate([grad_second[:, whole * LANES :], jnp.zeros((CH, LANES - rest), jnp.float32)], 1)
    mixed = mixed + pltpu.roll(grad_third, rest, 1)
    tail = LANES - grad_first.shape[1]
    rows_out[:, whole + 1, :] = jnp.concatenate([grad_first, jnp.zeros((CH, tail), jnp.float32)], 1)

    offset = rest + ROWS if inline else 0
    height = CH if inline else slots.shape[0]
    slot_rows = iota((height, LANES), 0)
    slot_lanes = iota((height, LANES), 1)
    placed = jnp.zeros((height, LANES), jnp.float32)
    for j in range(count):
        name = trainers[j]
        rank = jnp.int32(0)
        for i in range(j):
            rank = rank + jnp.where(trainers[i] == name, 1, 0)
        target = (pos_x * count_y + name) * count_z + pos_z
        slot = offset + pos_y * CAP + rank
        hit = (slot_rows == target) & (slot_lanes == slot)
        placed = jnp.where(hit, losses[j : j + 1, :], placed)
    high = placed.astype(jnp.bfloat16).astype(jnp.float32)
    placed = high + pltpu.roll(placed - high, count_y * CAP, 1)
    if inline:
        mixed = mixed + placed
    else:
        slots[:, 0, :] = placed.astype(jnp.bfloat16)
    rows_out[:, whole, :] = mixed
    send[...] = rows_out[...].astype(jnp.bfloat16)


def second_step(sizes, inline, drawn, middle, visc, partial, vy_b, vx_b, vy_a, vz_other, vx_a, vz_own,
                y_b, x_b, y_a, z_other, x_a, z_own, *rest):
    loads, rest = (None, rest) if sizes["gy"] * CAP == SAMP else (rest[0][...], rest[1:])
    w_first, w_second, w_second_t, w_third, w_third_t, advanced_far, send = rest[:7]
    slots = None if inline else rest[7]
    stack_first, stack_mid, rows_out, y_terms, advanced, sems = rest[-6:]
    halo = Sides(x_a, x_b, y_a, y_b, z_other)
    visc_halo = Sides(vx_a, vx_b, vy_a, vy_b, vz_other)
    count = stack_mid.shape[1] // VOL
    samples = [drawn[0, j] for j in range(count)]
    trainers = [drawn[1, j] for j in range(count)]

    def emit(f, x, c, tile):
        advanced[f, x, ROWS * c : ROWS * c + ROWS, :] = tile

    close(middle, visc, partial, halo, visc_halo, z_own, vz_own, y_terms, emit)
    copies = [pltpu.make_async_copy(advanced.at[f], advanced_far.at[f], sems.at[f]) for f in range(NF)]

    def leave():
        for copy in copies:
            copy.start()

    place = (lax.axis_index("gx"), lax.axis_index("gy"), lax.axis_index("gz"), sizes["gy"], sizes["gz"])
    closure(advanced, samples, trainers, loads, w_first[...], w_second[...],
            w_second_t[...], w_third[...], w_third_t[...],
            float(sizes["gx"] * sizes["gy"] * sizes["gz"]), stack_first, stack_mid, rows_out,
            send, slots, inline, place, leave)
    for copy in copies:
        copy.wait()


def add_up(arrived, spread, own):
    total = jnp.sum(arrived[...].astype(jnp.float32), axis=0)
    own[...] = total
    rounded = total.astype(jnp.bfloat16)
    for i in range(spread.shape[0]):
        spread[i] = rounded


def unpack(where, gathered, own, first, second, third, losses, wide):
    row, lane = where
    count = losses.shape[3]
    high = own[row : row + 1, lane : lane + count]
    losses[0, 0] = high + own[row : row + 1, lane + count : lane + 2 * count]
    wide[...] = gathered[...].astype(jnp.float32)
    whole = second.shape[1] // LANES
    rest = second.shape[1] - whole * LANES
    for t in range(whole):
        second[:, LANES * t : LANES * t + LANES] = wide[:, t, :]
    mixed = wide[:, whole, :]
    second[:, LANES * whole :] = mixed[:, :rest]
    third[...] = mixed[:, rest : rest + ROWS].T[:NOUT]
    first[...] = wide[:, whole + 1, :][:, : first.shape[1]]


def shape_of(*dims, dtype=jnp.float32):
    return jax.ShapeDtypeStruct(dims, dtype)


def exchange(x_a, x_b, y_a, y_b, z_both, sizes):
    def swap_a(axis):
        return [(i, i ^ 1) for i in range(sizes[axis])]

    def swap_b(axis):
        return [(i, (i + (1 if i % 2 else -1)) % sizes[axis]) for i in range(sizes[axis])]

    y_b = lax.ppermute(y_b, "gy", swap_b("gy"))
    x_b = lax.ppermute(x_b, "gx", swap_b("gx"))
    y_a = lax.ppermute(y_a, "gy", swap_a("gy"))
    z_both = lax.ppermute(z_both, "gz", swap_a("gz"))
    x_a = lax.ppermute(x_a, "gx", swap_a("gx"))
    return y_b, x_b, y_a, z_both, x_a


def without_border(kernel, fields, visc, index=(), weights=()):
    cells = visc.size
    out_shape = [shape_of(*fields.shape)]
    scratch = [pltpu.SMEM(array.shape, jnp.int32) for array in index]
    if weights:
        scratch.append(pltpu.SemaphoreType.DMA((len(index),)))
        sizes = ((CH, 28 * NF), (27 * CH, CH), (16, CH), (CH, 16))
        out_shape += [shape_of(*size, dtype=jnp.bfloat16) for size in sizes]
        out_shape.append(shape_of(ROWS, LANES, dtype=jnp.int32))
    return pl.pallas_call(
        kernel,
        out_shape=out_shape,
        in_specs=[ANY] * len(index) + [VMEM] * (2 + len(weights)),
        out_specs=[VMEM] * len(out_shape),
        scratch_shapes=scratch,
        compiler_params=PARAMS,
        cost_estimate=pl.CostEstimate(flops=120 * cells, bytes_accessed=36 * cells, transcendentals=0),
        name=kernel.__name__,
    )(*index, fields, visc, *weights)


def on_device(sizes, fields, visc, samples, trainers, conv_first, conv_second, conv_third):
    _, planes, rows, lanes = fields.shape
    axes = ("gx", "gy", "gz")
    devices_all = sizes["gx"] * sizes["gy"] * sizes["gz"]
    pairs = planes * rows // ROWS
    half = LANES // 2
    samples = samples.reshape(-1)
    trainers = trainers.reshape(-1)

    faces = pl.pallas_call(
        pack_faces,
        out_shape=[
            shape_of(NF + 1, rows, lanes),
            shape_of(NF + 1, rows, lanes),
            shape_of(NF + 1, planes, lanes),
            shape_of(NF + 1, planes, lanes),
            shape_of(-(-(NF + 1) * pairs // half), ROWS, LANES),
        ],
        in_specs=[HBM, HBM],
        out_specs=[VMEM] * 5,
        scratch_shapes=[
            pltpu.VMEM(fields.shape, jnp.float32),
            pltpu.VMEM(visc.shape, jnp.float32),
            pltpu.SemaphoreType.DMA((NF + 1,)),
        ],
        compiler_params=PACK,
        name="pack_faces",
    )(fields, visc)
    halo = exchange(*faces, sizes)

    own_counts = sizes["gy"] * CAP == SAMP
    counts = []
    if not own_counts:
        named = trainers.reshape(-1, 1) == jnp.arange(LANES, dtype=jnp.int32)[None, :]
        total = lax.psum(jnp.sum(named.astype(jnp.float32), axis=0, keepdims=True), "gy")
        counts = [jnp.broadcast_to(total, (ROWS, LANES))]
    z_own = faces[4]
    y_terms = pltpu.VMEM((2, NF, planes, lanes), jnp.float32)
    middle, *faces = pl.pallas_call(
        close_first,
        out_shape=[
            shape_of(*fields.shape),
            shape_of(NF, rows, lanes),
            shape_of(NF, rows, lanes),
            shape_of(NF, planes, lanes),
            shape_of(NF, planes, lanes),
            shape_of(-(-NF * pairs // half), ROWS, LANES),
        ],
        in_specs=[VMEM] * 9,
        out_specs=[VMEM] * 6,
        scratch_shapes=[y_terms],
        compiler_params=PARAMS,
        name="close_first",
    )(fields, visc, *without_border(interior, fields, visc), *halo, z_own)
    later = exchange(*faces, sizes)
    partial, w_first, w_second_t, w_third, w_third_t, drawn = without_border(
        interior_and_weights, middle, visc, (samples, trainers), (conv_first, conv_second, conv_third)
    )

    count = samples.shape[0]
    slot_total = sizes["gy"] * CAP
    tiles = -(-27 * CH // LANES) + 1
    parts = devices_all // CH
    inline = parts == 1 and slot_total <= 12
    out_shape = [shape_of(*fields.shape), shape_of(CH, tiles, LANES, dtype=jnp.bfloat16)]
    if not inline:
        out_shape.append(shape_of(devices_all, 1, LANES, dtype=jnp.bfloat16))
    advanced, send, *slots = pl.pallas_call(
        functools.partial(second_step, sizes, inline),
        out_shape=out_shape,
        in_specs=[VMEM] * (21 if own_counts else 22),
        out_specs=[HBM] + [VMEM] * (len(out_shape) - 1),
        scratch_shapes=[
            pltpu.VMEM((28 * NF, count * VOL), jnp.float32),
            pltpu.VMEM((27 * CH, count * VOL), jnp.bfloat16),
            pltpu.VMEM((CH, tiles, LANES), jnp.float32),
            y_terms,
            pltpu.VMEM(fields.shape, jnp.float32),
            pltpu.SemaphoreType.DMA((NF,)),
        ],
        compiler_params=PARAMS,
        name="second_step",
    )(drawn, middle, visc, partial, *halo, z_own, *later, faces[4], *counts,
      w_first, conv_second, w_second_t, w_third, w_third_t)

    if not inline:
        send = jnp.concatenate([send.reshape(devices_all, tiles // parts, LANES), slots[0]], 1)
    arrived = lax.all_to_all(send, axes, split_axis=0, concat_axis=0, tiled=True)
    if inline:
        where = (27 * CH // LANES, 27 * CH % LANES + ROWS)
    else:
        where = (send.shape[1] - 1, 0)
    spread, own = pl.pallas_call(
        add_up,
        out_shape=[shape_of(*send.shape, dtype=jnp.bfloat16), shape_of(*send.shape[1:])],
        in_specs=[VMEM],
        out_specs=[VMEM] * 2,
        compiler_params=PARAMS,
        name="add_up",
    )(arrived)
    if not inline:
        spread = spread[:, :-1, :]
    gathered = lax.all_to_all(spread, axes, split_axis=0, concat_axis=0, tiled=True)
    first, second, third, block_losses = pl.pallas_call(
        functools.partial(unpack, where),
        out_shape=[
            shape_of(*conv_first.shape),
            shape_of(*conv_second.shape),
            shape_of(*conv_third.shape),
            shape_of(1, 1, 1, slot_total),
        ],
        in_specs=[VMEM] * 2,
        out_specs=[VMEM] * 4,
        scratch_shapes=[pltpu.VMEM((CH, tiles, LANES), jnp.float32)],
        compiler_params=PARAMS,
        name="unpack",
    )(gathered.reshape(CH, tiles, LANES), own)
    return advanced, block_losses, first, second, third


def solution(mesh):
    sizes = dict(mesh.shape)
    in_specs = (
        P(None, "gx", "gy", "gz"),
        P("gx", "gy", "gz"),
        P("gx", "gy", "gz", None),
        P("gx", "gy", "gz", None, None),
        P(),
        P(),
        P(),
    )
    out_specs = (P(None, "gx", "gy", "gz"), P("gx", "gy", "gz", None), P(), P(), P())
    return jax.shard_map(
        functools.partial(on_device, sizes), mesh=mesh, in_specs=in_specs, out_specs=out_specs,
        check_vma=False,
    )
```

```python
import functools

import jax
import jax.numpy as jnp
from jax import lax
from jax.experimental import pallas as pl
from jax.experimental.pallas import tpu as pltpu
from jax.sharding import PartitionSpec as P

BLK = 4
CAP = 2
SAMP = 8
NF = 4
VOL = BLK**3
TAPS = [(x, y, z) for x in (-1, 0, 1) for y in (-1, 0, 1) for z in (-1, 0, 1)]
LANES = 128
ROWS = 8
NOUT = 6
CH = 32

time_step = 0.25
buoyancy = 0.5

VMEM = pl.BlockSpec(memory_space=pltpu.VMEM)
SMEM = pl.BlockSpec(memory_space=pltpu.SMEM)
HBM = pl.BlockSpec(memory_space=pltpu.HBM)
ANY = pl.BlockSpec(memory_space=pl.ANY)
PARAMS = pltpu.CompilerParams(vmem_limit_bytes=24 * 1024 * 1024)
PACK = pltpu.CompilerParams(vmem_limit_bytes=54944 * 1024)
FULL = (((1,), (1,)), ((), ()))


def iota(shape, axis):
    return lax.broadcasted_iota(jnp.int32, shape, axis)


def odd(axis):
    return lax.axis_index(axis) % 2 == 1


def facing(axis, swap, first, last):
    return jnp.where(odd(axis), first, last) if swap == "a" else jnp.where(odd(axis), last, first)


def prev_next(axis, from_a, from_b):
    return jnp.where(odd(axis), from_a, from_b), jnp.where(odd(axis), from_b, from_a)


class Sides:
    def __init__(self, chunks, x_b, x_a, z_both, y_b=None, y_a=None):
        self.chunks = chunks
        self.x_a, self.x_b, self.y_a, self.y_b, self.z_both = x_a, x_b, y_a, y_b, z_both

    def along_x(self, f, c):
        tile = f * self.chunks + c
        return prev_next("gx", self.x_a[tile], self.x_b[tile])

    def along_y(self, f, depth=0):
        tile = depth * (NF + 1) + f
        return prev_next("gy", self.y_a[tile], self.y_b[tile])


def pair_of(f, c, planes, chunks):
    span = 2 * planes * chunks
    return f * span // LANES, f * span % LANES + 2 * planes * c


def add_pair(packed, tile, lane):
    moved = pltpu.roll(tile, lane + 1, 1)
    at = iota(tile.shape, 1)
    return jnp.where((at == lane) | (at == lane + 1), moved, packed)


def cut_x(f, array, x_b, x_a):
    planes, rows, _ = array.shape
    chunks = rows // ROWS
    for c in range(chunks):
        part = slice(ROWS * c, ROWS * c + ROWS)
        ends = array[0, part], array[planes - 1, part]
        x_b[f * chunks + c] = facing("gx", "b", *ends)
        x_a[f * chunks + c] = facing("gx", "a", *ends)


def pack_faces(fields_far, visc_far, x_b, x_a, z_both, y_b, y_a, fields, visc, sems):
    _, planes, rows, _ = fields.shape
    chunks = rows // ROWS
    copies = [pltpu.make_async_copy(fields_far.at[f], fields.at[f], sems.at[f]) for f in range(NF)]
    copies.append(pltpu.make_async_copy(visc_far, visc, sems.at[NF]))
    for copy in copies:
        copy.start()
    arrays = [fields.at[f] for f in range(NF)] + [visc]
    packed = [jnp.zeros((ROWS, LANES), jnp.float32) for _ in range(z_both.shape[0])]
    for f, array in enumerate(arrays):
        copies[f].wait()
        cut_x(f, array, x_b, x_a)
        for depth in range(2):
            ends = array[:, depth, :], array[:, rows - 1 - depth, :]
            y_b[depth * (NF + 1) + f] = facing("gy", "b", *ends)
            y_a[depth * (NF + 1) + f] = facing("gy", "a", *ends)
        for c in range(chunks):
            tile, lane = pair_of(f, c, planes, chunks)
            for x in range(planes):
                cells = array[x, ROWS * c : ROWS * c + ROWS]
                packed[tile] = add_pair(packed[tile], cells, lane + 2 * x)
    for tile, value in enumerate(packed):
        z_both[tile] = value


def flux(lower, upper, dimension):
    speed = 0.25 * (lower[dimension] + upper[dimension])
    mean_visc = 0.5 * (lower[NF] + upper[NF])
    return [speed * (a + b) - mean_visc * (b - a) for a, b in zip(lower[:NF], upper[:NF])]


def interior(fields, visc, partial):
    _, planes, rows, _ = fields.shape
    chunks = rows // ROWS
    end_row = iota((ROWS, LANES), 0) == ROWS - 1
    end_lane = iota((ROWS, LANES), 1) == LANES - 1
    every = range(NF + 1)

    def cell(f, x, part):
        return fields[f, x, part, :] if f < NF else visc[x, part, :]

    def plane(x, lowers):
        uppers = []
        last = x == planes - 1
        beyond = jnp.minimum(x + 1, planes - 1)
        behind = [jnp.zeros((ROWS, LANES), jnp.float32)] * NF
        for c in range(chunks):
            part = slice(ROWS * c, ROWS * c + ROWS)
            here = [cell(f, x, part) for f in every]
            after = [cell(f, beyond, part) for f in every]
            upper = flux(here, after, 0)
            upper = [jnp.where(last, 0.0, u) for u in upper]
            total = [b - a for a, b in zip(lowers[c], upper)]
            uppers.append(upper)
            above = [pltpu.roll(h, ROWS - 1, 0) for h in here]
            if c + 1 < chunks:
                first = slice(ROWS * c + ROWS, ROWS * c + ROWS + 1)
                above = [jnp.where(end_row, cell(f, x, first), above[f]) for f in every]
            upper = flux(here, above, 1)
            lower = [pltpu.roll(jnp.where(end_row, b, u), 1, 0) for b, u in zip(behind, upper)]
            if c + 1 == chunks:
                upper = [jnp.where(end_row, 0.0, u) for u in upper]
            behind = upper
            total = [t + (b - a) for t, a, b in zip(total, lower, upper)]
            right = [pltpu.roll(h, LANES - 1, 1) for h in here]
            upper = [jnp.where(end_lane, 0.0, u) for u in flux(here, right, 2)]
            lower = [pltpu.roll(u, 1, 1) for u in upper]
            total = [t + (b - a) for t, a, b in zip(total, lower, upper)]
            updated = [q - time_step * t for q, t in zip(here[:NF], total)]
            updated[2] = updated[2] + (time_step * buoyancy) * here[3]
            for f in range(NF):
                partial[f, x, part, :] = updated[f]
        return uppers

    zeros = [[jnp.zeros((ROWS, LANES), jnp.float32)] * NF for _ in range(chunks)]
    lax.fori_loop(0, planes, plane, zeros)


def rims_without_ends(fields, visc, sides, rims):
    rows = fields.shape[2]
    every = range(NF + 1)
    end_row = iota((ROWS, LANES), 0) == ROWS - 1
    end_lane = iota((ROWS, LANES), 1) == LANES - 1

    def own(row):
        return [fields[f, :, row, :] for f in range(NF)] + [visc[:, row, :]]

    for side in range(2):
        here = [sides.along_y(f)[side] for f in every]
        beyond = [sides.along_y(f, 1)[side] for f in every]
        below, above = (beyond, own(0)) if side == 0 else (own(rows - 1), beyond)
        total = [b - a for a, b in zip(flux(below, here, 1), flux(here, above, 1))]
        for dimension, axis, end in ((0, 0, end_row), (2, 1, end_lane)):
            after = [pltpu.roll(h, h.shape[axis] - 1, axis) for h in here]
            upper = [jnp.where(end, 0.0, u) for u in flux(here, after, dimension)]
            total = [t + (u - pltpu.roll(u, 1, axis)) for t, u in zip(total, upper)]
        updated = [q - time_step * t for q, t in zip(here[:NF], total)]
        updated[2] = updated[2] + (time_step * buoyancy) * here[3]
        for f in range(NF):
            rims[side * NF + f] = updated[f]


def rims_with_ends(rims, sides, later):
    row = iota((ROWS, LANES), 0)
    lane = iota((ROWS, LANES), 1)
    every = range(NF + 1)
    whole = []
    for side in range(2):
        here = [sides.along_y(f)[side] for f in every]
        tile = NF * later.chunks + side
        before, after = prev_next("gx", later.x_a[tile], later.x_b[tile])
        low = flux([before[f : f + 1] for f in every], [h[:1] for h in here], 0)
        high = flux([h[ROWS - 1 :] for h in here], [after[f : f + 1] for f in every], 0)
        columns = later.z_both[later.z_both.shape[0] - 1]
        left, right = [], []
        for f in every:
            both = pltpu.roll(columns, LANES - 1 - 2 * (side * (NF + 1) + f), 1)
            left.append(pltpu.roll(jnp.where(lane == LANES - 1, both, here[f]), 1, 1))
            right.append(pltpu.roll(jnp.where(lane == 0, both, here[f]), LANES - 1, 1))
        lower, upper = flux(left, here, 2), flux(here, right, 2)
        ends = []
        for f in range(NF):
            value = rims[side * NF + f]
            value = value + time_step * jnp.where(row == 0, low[f], 0.0)
            value = value - time_step * jnp.where(row == ROWS - 1, high[f], 0.0)
            value = value + time_step * jnp.where(lane == 0, lower[f], 0.0)
            ends.append(value - time_step * jnp.where(lane == LANES - 1, upper[f], 0.0))
        whole.append(ends)
    return whole


def interior_and_weights(samples_far, trainers_far, middle, visc, fields, y_b, y_a, conv_first, conv_second,
                         conv_third, partial, rims, w_first, w_second_t, w_third, w_third_t, drawn, samples, trainers, sems):
    copies = [
        pltpu.make_async_copy(samples_far, samples, sems.at[0]),
        pltpu.make_async_copy(trainers_far, trainers, sems.at[1]),
    ]
    for copy in copies:
        copy.start()
    interior(middle, visc, partial)
    rims_without_ends(fields, visc, Sides(0, None, None, None, y_b, y_a), rims)
    ahead = conv_first.shape[1]
    w_first[:, :ahead] = conv_first[...]
    w_first[:, ahead:] = jnp.zeros((CH, w_first.shape[1] - ahead), jnp.bfloat16)
    w_second_t[...] = conv_second[...].astype(jnp.float32).T.astype(jnp.bfloat16)
    third = conv_third[...].astype(jnp.float32)
    third = jnp.concatenate([third, jnp.zeros((w_third.shape[0] - NOUT, CH), jnp.float32)], 0)
    w_third[...] = third.astype(jnp.bfloat16)
    w_third_t[...] = third.T.astype(jnp.bfloat16)
    for copy in copies:
        copy.wait()
    at, row = iota((ROWS, LANES), 1), iota((ROWS, LANES), 0)
    table = jnp.zeros((ROWS, LANES), jnp.int32)
    for j in range(samples.shape[0]):
        table = jnp.where(at == j, jnp.where(row == 0, samples[j], trainers[j]), table)
    drawn[...] = table


def z_terms(own, other, visc_own, visc_other):
    lane = iota((ROWS, LANES), 1)
    second = lane % 2 == 1
    span = LANES // 2

    def ends(mine, theirs):
        lower = jnp.where(second, pltpu.roll(theirs, 1, 1), mine)
        return lower, jnp.where(second, mine, pltpu.roll(theirs, LANES - 1, 1))

    def twice(tile):
        return jnp.where(lane < span, tile, pltpu.roll(tile, span, 1))

    pairs = [ends(a, b) for a, b in zip(own, other)]
    speed = [twice(end) for end in pairs[2 * span // LANES]]
    visc = [twice(end) for end in ends(visc_own, visc_other)]
    speed = 0.25 * (speed[0] + speed[1])
    mean_visc = 0.5 * (visc[0] + visc[1])
    through = [speed * (a + b) - mean_visc * (b - a) for a, b in pairs]
    return [jnp.where(second, time_step, -time_step) * t for t in through]


def close(fields, visc, partial, halo, visc_halo, y_faces, z_own, visc_z_own, y_terms, emit):
    _, planes, rows, _ = fields.shape
    chunks = rows // ROWS
    every = range(NF + 1)
    row = iota((ROWS, LANES), 0)
    lane_at = iota((ROWS, LANES), 1)
    ends = (lane_at == 0) | (lane_at == LANES - 1)

    def cell(f, *index):
        return fields[(f,) + index] if f < NF else visc[index]

    def sides(f):
        return halo if f < NF else visc_halo

    lower = flux(y_faces[0], [cell(f, slice(None), 0) for f in every], 1)
    upper = flux([cell(f, slice(None), rows - 1) for f in every], y_faces[1], 1)
    for f in range(NF):
        y_terms[0, f] = time_step * lower[f]
        y_terms[1, f] = -time_step * upper[f]
    tiles = 2 * NF * planes * chunks // LANES
    terms = z_terms([z_own[t] for t in range(tiles)], [halo.z_both[t] for t in range(tiles)],
                    visc_z_own[tiles], visc_halo.z_both[tiles])
    for c in range(chunks):
        part = slice(ROWS * c, ROWS * c + ROWS)
        before, after = zip(*[sides(f).along_x(f, c) for f in every])
        low = flux(before, [cell(f, 0, part) for f in every], 0)
        high = flux([cell(f, planes - 1, part) for f in every], after, 0)
        for x in range(planes):
            for f in range(NF):
                tile, lane = pair_of(f, c, planes, chunks)
                moved = pltpu.roll(terms[tile], LANES - 1 - lane - 2 * x, 1)
                value = partial[f, x, part, :] + jnp.where(ends, moved, 0.0)
                if x == 0:
                    value = value + time_step * low[f]
                if x == planes - 1:
                    value = value - time_step * high[f]
                if c == 0:
                    value = value + jnp.where(row == 0, y_terms[0, f, x : x + 1, :], 0.0)
                if c == chunks - 1:
                    value = value + jnp.where(row == ROWS - 1, y_terms[1, f, x : x + 1, :], 0.0)
                emit(f, x, c, value)


def close_first(fields, visc, partial, z_own, x_from_b, x_from_a, z_other, y_from_b, y_from_a,
                middle, x_b, x_a, z_both, y_terms):
    _, planes, rows, _ = fields.shape
    chunks = rows // ROWS
    halo = Sides(chunks, x_from_b, x_from_a, z_other, y_from_b, y_from_a)
    packed = [jnp.zeros((ROWS, LANES), jnp.float32) for _ in range(z_both.shape[0])]
    y_faces = list(zip(*[halo.along_y(f) for f in range(NF + 1)]))

    def emit(f, x, c, tile):
        middle[f, x, ROWS * c : ROWS * c + ROWS, :] = tile
        at, lane = pair_of(f, c, planes, chunks)
        packed[at] = add_pair(packed[at], tile, lane + 2 * x)

    for side in range(2):
        for f in range(NF + 1):
            face = y_faces[side][f]
            packed[-1] = add_pair(packed[-1], face, 2 * (side * (NF + 1) + f))
            x_b[NF * chunks + side, f : f + 1, :] = facing("gx", "b", face[:1], face[planes - 1 :])
            x_a[NF * chunks + side, f : f + 1, :] = facing("gx", "a", face[:1], face[planes - 1 :])
    close(fields, visc, partial, halo, halo, y_faces, z_own, z_own, y_terms, emit)
    for at, value in enumerate(packed):
        z_both[at] = value
    for f in range(NF):
        cut_x(f, middle.at[f], x_b, x_a)


def inside_masks():
    at = iota((1, LANES), 1) % VOL
    coords = (at // (BLK * BLK), at // BLK % BLK, at % BLK)
    along = []
    for coord in coords:
        along.append({
            -1: jnp.where(coord > 0, 1.0, 0.0),
            0: jnp.ones((1, LANES), jnp.float32),
            1: jnp.where(coord < BLK - 1, 1.0, 0.0),
        })
    return along


def move_of(tap):
    return tap[0] * BLK * BLK + tap[1] * BLK + tap[2]


def shifted(tile, tap, along):
    move = move_of(tap)
    if move == 0:
        return tile
    mask = along[0][tap[0]] * along[1][tap[1]] * along[2][tap[2]]
    return pltpu.roll(tile, (-move) % LANES, 1) * mask


def box(tile, along):
    for dimension, step in enumerate((BLK * BLK, BLK, 1)):
        ahead = pltpu.roll(tile, LANES - step, 1) * along[dimension][1]
        behind = pltpu.roll(tile, step, 1) * along[dimension][-1]
        tile = (behind + tile) + ahead
    return tile / 27.0


def sigmoid(values):
    return 1.0 / (1.0 + jnp.exp(-values))


PICKED = (0, 1, 2, 3, 0, 1, 2, 3, 0, 1, 2, 0, 0, 1, -1, -1, 0, 1, 2, 1, 2, 2, -1, -1)


def pick_rows():
    out, field = iota((32, NF * ROWS), 0), iota((32, NF * ROWS), 1) // ROWS
    table = jnp.zeros((32, NF * ROWS), jnp.float32)
    for i, f in enumerate(PICKED):
        table = jnp.where((out == i) & (field == f), 1.0, table)
    return table.astype(jnp.bfloat16)


def pick_blocks(advanced, samples, count):
    _, _, rows, lanes = advanced.shape
    along_y, along_z = rows // BLK, lanes // BLK
    row = iota((ROWS, LANES), 0)
    lane_at = iota((ROWS, LANES), 1)
    pick = pick_rows()
    out = []
    for j in range(0, count, 2):
        parts = [jnp.zeros((ROWS, LANES), jnp.float32) for _ in range(NF)]
        uppers = []
        for half in range(2):
            block = samples[j + half]
            block_x = block // (along_y * along_z)
            block_y = block // along_z % along_y
            block_z = block % along_z
            uppers.append(block_y % 2)
            start = pl.multiple_of(block_y // 2 * ROWS, ROWS)
            for x in range(BLK):
                turn = lax.rem(VOL * half + BLK * BLK * x - BLK * block_z + LANES, LANES)
                wanted = lane_at // BLK == (VOL * half + BLK * BLK * x) // BLK
                for f in range(NF):
                    tile = advanced[f, block_x * BLK + x, pl.ds(start, ROWS), :]
                    parts[f] = jnp.where(wanted, pltpu.roll(tile, turn, 1), parts[f])
        upper = jnp.where(lane_at < VOL, uppers[0], uppers[1])
        valid = row // BLK == upper
        for f in range(NF):
            for bit in (1, 2):
                moved = pltpu.roll(parts[f], BLK * bit, 1)
                parts[f] = jnp.where(row // bit % 2 == 1, moved, parts[f])
            parts[f] = jnp.where(valid, parts[f], 0.0)
        stacked = jnp.concatenate(parts, 0).astype(jnp.bfloat16)
        out.append(jnp.dot(pick, stacked, preferred_element_type=jnp.float32))
    return out


def closure(advanced, samples, trainers, loads, w_first, w_second, w_second_t, w_third,
            w_third_t, devices_all, stack_first, stack_mid, rows_out, send, slots, inline, place):
    count = len(samples)
    pairs = count // 2
    cols = [slice(LANES * m, LANES * m + LANES) for m in range(pairs)]
    along = inside_masks()
    lane_at = iota((ROWS, LANES), 1)
    row = iota((ROWS, LANES), 0)

    pos_x, pos_y, pos_z, count_y, count_z = place
    picked = pick_blocks(advanced, samples, count)
    values = [p[:ROWS] for p in picked]
    targets = []
    for p in picked:
        first, second = p[ROWS : 2 * ROWS], p[2 * ROWS : 3 * ROWS]
        targets.append(box(first * second, along) - box(first, along) * box(second, along))

    for m, tile in enumerate(values):
        for t in range(0, 28, 2):
            piece = shifted(tile, TAPS[t], along)
            later = shifted(tile, TAPS[t + 1], along) if t + 1 < 27 else jnp.zeros_like(tile)
            stack_first[BLK * t : BLK * t + ROWS, cols[m]] = jnp.where(row < NF, piece, later)
    stack_in = stack_first[...].astype(jnp.bfloat16)
    pre_first = jnp.dot(w_first, stack_in, preferred_element_type=jnp.float32)
    gate_first = sigmoid(pre_first)
    hidden_first = (pre_first * gate_first).astype(jnp.bfloat16).astype(jnp.float32)
    for m in range(pairs):
        tile = hidden_first[:, cols[m]]
        for k, tap in enumerate(TAPS):
            stack_mid[CH * k : CH * k + CH, cols[m]] = shifted(tile, tap, along).astype(jnp.bfloat16)
    pre_second = jnp.dot(w_second, stack_mid[...], preferred_element_type=jnp.float32)
    gate_second = sigmoid(pre_second)
    hidden_second = (pre_second * gate_second).astype(jnp.bfloat16)
    predicted = jnp.dot(w_third, hidden_second, preferred_element_type=jnp.float32)

    misfit = predicted[:ROWS] - jnp.concatenate(targets, 1)
    square = jnp.sum(misfit * misfit, axis=0, keepdims=True)
    sample_at = iota((ROWS, count * VOL), 1) // VOL
    mine = sample_at == iota((ROWS, count * VOL), 0)
    losses = jnp.sum(jnp.where(mine, square, 0.0), axis=1, keepdims=True) / (NOUT * VOL)
    if loads is None:
        load = jnp.full((ROWS, 1), float(count_y * CAP), jnp.float32)
    else:
        owner = jnp.zeros((ROWS, LANES), jnp.int32)
        for j in range(count):
            owner = jnp.where(row == j, trainers[j], owner)
        load = jnp.sum(jnp.where(lane_at == owner, loads, 0.0), axis=1, keepdims=True)
    share = 1.0 / (devices_all * jnp.maximum(load, 1.0))
    scale = share * (2.0 / (NOUT * VOL))
    scale_at = jnp.sum(jnp.where(mine, scale, 0.0), axis=0, keepdims=True)
    grad_pred = (misfit * scale_at).astype(jnp.bfloat16)
    grad_pred = jnp.concatenate([grad_pred, jnp.zeros_like(grad_pred)], 0)

    upper = jnp.dot(w_third_t, grad_pred, preferred_element_type=jnp.float32)
    slope = gate_second * (1.0 + pre_second * (1.0 - gate_second))
    grad_mid = (upper * slope).astype(jnp.bfloat16)
    grad_second = lax.dot_general(grad_mid, stack_mid[...], FULL, preferred_element_type=jnp.float32)
    third = jnp.concatenate([grad_pred, jnp.zeros((LANES - 16, count * VOL), jnp.bfloat16)], 0)
    grad_third = lax.dot_general(hidden_second, third, FULL, preferred_element_type=jnp.float32)

    spread = jnp.dot(w_second_t, grad_mid, preferred_element_type=jnp.float32)
    lower = []
    for m in range(pairs):
        terms = [
            shifted(spread[CH * k : CH * k + CH, cols[m]], tuple(-o for o in tap), along)
            for k, tap in enumerate(TAPS)
        ]
        lower.append(functools.reduce(jnp.add, terms))
    lower = jnp.concatenate(lower, 1)
    slope = gate_first * (1.0 + pre_first * (1.0 - gate_first))
    grad_entry = (lower * slope).astype(jnp.bfloat16)
    grad_first = lax.dot_general(grad_entry, stack_in, FULL, preferred_element_type=jnp.float32)

    whole = CH * 27 // LANES
    rest = CH * 27 - whole * LANES
    for t in range(whole):
        rows_out[:, t, :] = grad_second[:, LANES * t : LANES * t + LANES]
    mixed = jnp.concatenate([grad_second[:, whole * LANES :], jnp.zeros((CH, LANES - rest), jnp.float32)], 1)
    mixed = mixed + pltpu.roll(grad_third, rest, 1)
    tail = LANES - grad_first.shape[1]
    rows_out[:, whole + 1, :] = jnp.concatenate([grad_first, jnp.zeros((CH, tail), jnp.float32)], 1)

    offset = rest + ROWS if inline else 0
    height = CH if inline else slots.shape[0]
    slot_rows = iota((height, LANES), 0)
    slot_lanes = iota((height, LANES), 1)
    placed = jnp.zeros((height, LANES), jnp.float32)
    for j in range(count):
        name = trainers[j]
        rank = jnp.int32(0)
        for i in range(j):
            rank = rank + jnp.where(trainers[i] == name, 1, 0)
        target = (pos_x * count_y + name) * count_z + pos_z
        slot = offset + pos_y * CAP + rank
        hit = (slot_rows == target) & (slot_lanes == slot)
        placed = jnp.where(hit, losses[j : j + 1, :], placed)
    high = placed.astype(jnp.bfloat16).astype(jnp.float32)
    placed = high + pltpu.roll(placed - high, count_y * CAP, 1)
    if inline:
        mixed = mixed + placed
    else:
        slots[:, 0, :] = placed.astype(jnp.bfloat16)
    rows_out[:, whole, :] = mixed
    send[...] = rows_out[...].astype(jnp.bfloat16)


def second_step(sizes, inline, drawn, middle, visc, partial, rims, vz_own, vx_b, vx_a, vz_other, vy_b, vy_a,
                z_own, x_b, x_a, z_other, *rest):
    loads, rest = (None, rest) if sizes["gy"] * CAP == SAMP else (rest[0][...], rest[1:])
    w_first, w_second, w_second_t, w_third, w_third_t, advanced, send = rest[:7]
    slots = None if inline else rest[7]
    stack_first, stack_mid, rows_out, y_terms = rest[-4:]
    chunks = middle.shape[2] // ROWS
    halo = Sides(chunks, x_b, x_a, z_other)
    visc_halo = Sides(chunks, vx_b, vx_a, vz_other, vy_b, vy_a)
    y_faces = rims_with_ends(rims, visc_halo, halo)
    y_faces = [face + [visc_halo.along_y(NF)[side]] for side, face in enumerate(y_faces)]
    count = stack_mid.shape[1] // VOL
    samples = [drawn[0, j] for j in range(count)]
    trainers = [drawn[1, j] for j in range(count)]

    def emit(f, x, c, tile):
        advanced[f, x, ROWS * c : ROWS * c + ROWS, :] = tile

    close(middle, visc, partial, halo, visc_halo, y_faces, z_own, vz_own, y_terms, emit)
    place = (lax.axis_index("gx"), lax.axis_index("gy"), lax.axis_index("gz"), sizes["gy"], sizes["gz"])
    closure(advanced, samples, trainers, loads, w_first[...], w_second[...],
            w_second_t[...], w_third[...], w_third_t[...],
            float(sizes["gx"] * sizes["gy"] * sizes["gz"]), stack_first, stack_mid, rows_out,
            send, slots, inline, place)


def add_up(arrived, spread, own):
    total = jnp.sum(arrived[...].astype(jnp.float32), axis=0)
    own[...] = total
    rounded = total.astype(jnp.bfloat16)
    for i in range(spread.shape[0]):
        spread[i] = rounded


def unpack(where, gathered, own, first, second, third, losses, wide):
    row, lane = where
    count = losses.shape[3]
    high = own[row : row + 1, lane : lane + count]
    losses[0, 0] = high + own[row : row + 1, lane + count : lane + 2 * count]
    wide[...] = gathered[...].astype(jnp.float32)
    whole = second.shape[1] // LANES
    rest = second.shape[1] - whole * LANES
    for t in range(whole):
        second[:, LANES * t : LANES * t + LANES] = wide[:, t, :]
    mixed = wide[:, whole, :]
    second[:, LANES * whole :] = mixed[:, :rest]
    third[...] = mixed[:, rest : rest + ROWS].T[:NOUT]
    first[...] = wide[:, whole + 1, :][:, : first.shape[1]]


def shape_of(*dims, dtype=jnp.float32):
    return jax.ShapeDtypeStruct(dims, dtype)


def exchange(x_b, x_a, z_both, y_b=None, y_a=None, sizes=None):
    def swap_a(face, axis):
        return lax.ppermute(face, axis, [(i, i ^ 1) for i in range(sizes[axis])])

    def swap_b(face, axis):
        count = sizes[axis]
        return lax.ppermute(face, axis, [(i, (i + (1 if i % 2 else -1)) % count) for i in range(count)])

    faces = [swap_b(x_b, "gx"), swap_a(x_a, "gx"), swap_a(z_both, "gz")]
    return faces if y_b is None else faces + [swap_b(y_b, "gy"), swap_a(y_a, "gy")]


def without_border(kernel, fields, visc, index=(), first=(), weights=()):
    cells = visc.size
    out_shape = [shape_of(*fields.shape)]
    scratch = [pltpu.SMEM(array.shape, jnp.int32) for array in index]
    if weights:
        scratch.append(pltpu.SemaphoreType.DMA((len(index),)))
        sizes = ((CH, 28 * NF), (27 * CH, CH), (16, CH), (CH, 16))
        out_shape.append(shape_of(2 * NF, ROWS, LANES))
        out_shape += [shape_of(*size, dtype=jnp.bfloat16) for size in sizes]
        out_shape.append(shape_of(ROWS, LANES, dtype=jnp.int32))
    return pl.pallas_call(
        kernel,
        out_shape=out_shape,
        in_specs=[ANY] * len(index) + [VMEM] * (2 + len(first) + len(weights)),
        out_specs=[VMEM] * len(out_shape),
        scratch_shapes=scratch,
        compiler_params=PARAMS,
        cost_estimate=pl.CostEstimate(flops=120 * cells, bytes_accessed=36 * cells, transcendentals=0),
        name=kernel.__name__,
    )(*index, fields, visc, *first, *weights)


def on_device(sizes, fields, visc, samples, trainers, conv_first, conv_second, conv_third):
    _, planes, rows, lanes = fields.shape
    axes = ("gx", "gy", "gz")
    devices_all = sizes["gx"] * sizes["gy"] * sizes["gz"]
    chunks = rows // ROWS
    pairs = planes * chunks
    half = LANES // 2
    samples = samples.reshape(-1)
    trainers = trainers.reshape(-1)

    faces = pl.pallas_call(
        pack_faces,
        out_shape=[
            shape_of((NF + 1) * chunks, ROWS, lanes),
            shape_of((NF + 1) * chunks, ROWS, lanes),
            shape_of(-(-(NF + 1) * pairs // half), ROWS, LANES),
            shape_of(2 * (NF + 1), planes, lanes),
            shape_of(2 * (NF + 1), planes, lanes),
        ],
        in_specs=[HBM, HBM],
        out_specs=[VMEM] * 5,
        scratch_shapes=[
            pltpu.VMEM(fields.shape, jnp.float32),
            pltpu.VMEM(visc.shape, jnp.float32),
            pltpu.SemaphoreType.DMA((NF + 1,)),
        ],
        compiler_params=PACK,
        name="pack_faces",
    )(fields, visc)
    halo = exchange(*faces, sizes=sizes)

    own_counts = sizes["gy"] * CAP == SAMP
    counts = []
    if not own_counts:
        named = trainers.reshape(-1, 1) == jnp.arange(LANES, dtype=jnp.int32)[None, :]
        total = lax.psum(jnp.sum(named.astype(jnp.float32), axis=0, keepdims=True), "gy")
        counts = [jnp.broadcast_to(total, (ROWS, LANES))]
    z_own = faces[2]
    y_terms = pltpu.VMEM((2, NF, planes, lanes), jnp.float32)
    middle, *faces = pl.pallas_call(
        close_first,
        out_shape=[
            shape_of(*fields.shape),
            shape_of(NF * chunks + 2, ROWS, lanes),
            shape_of(NF * chunks + 2, ROWS, lanes),
            shape_of(-(-NF * pairs // half) + 1, ROWS, LANES),
        ],
        in_specs=[VMEM] * 9,
        out_specs=[VMEM] * 4,
        scratch_shapes=[y_terms],
        compiler_params=PARAMS,
        name="close_first",
    )(fields, visc, *without_border(interior, fields, visc), z_own, *halo)
    later = exchange(*faces, sizes=sizes)
    partial, rims, w_first, w_second_t, w_third, w_third_t, drawn = without_border(
        interior_and_weights, middle, visc, (samples, trainers), (fields, *halo[3:]),
        (conv_first, conv_second, conv_third),
    )

    count = samples.shape[0]
    slot_total = sizes["gy"] * CAP
    tiles = -(-27 * CH // LANES) + 1
    parts = devices_all // CH
    inline = parts == 1 and slot_total <= 12
    out_shape = [shape_of(*fields.shape), shape_of(CH, tiles, LANES, dtype=jnp.bfloat16)]
    if not inline:
        out_shape.append(shape_of(devices_all, 1, LANES, dtype=jnp.bfloat16))
    advanced, send, *slots = pl.pallas_call(
        functools.partial(second_step, sizes, inline),
        out_shape=out_shape,
        in_specs=[VMEM] * (20 + len(counts)),
        out_specs=[VMEM] * len(out_shape),
        scratch_shapes=[
            pltpu.VMEM((28 * NF, count * VOL), jnp.float32),
            pltpu.VMEM((27 * CH, count * VOL), jnp.bfloat16),
            pltpu.VMEM((CH, tiles, LANES), jnp.float32),
            y_terms,
        ],
        compiler_params=PARAMS,
        name="second_step",
    )(drawn, middle, visc, partial, rims, z_own, *halo, faces[2], *later, *counts,
      w_first, conv_second, w_second_t, w_third, w_third_t)

    if not inline:
        send = jnp.concatenate([send.reshape(devices_all, tiles // parts, LANES), slots[0]], 1)
    arrived = lax.all_to_all(send, axes, split_axis=0, concat_axis=0, tiled=True)
    if inline:
        where = (27 * CH // LANES, 27 * CH % LANES + ROWS)
    else:
        where = (send.shape[1] - 1, 0)
    spread, own = pl.pallas_call(
        add_up,
        out_shape=[shape_of(*send.shape, dtype=jnp.bfloat16), shape_of(*send.shape[1:])],
        in_specs=[VMEM],
        out_specs=[VMEM] * 2,
        compiler_params=PARAMS,
        name="add_up",
    )(arrived)
    if not inline:
        spread = spread[:, :-1, :]
    gathered = lax.all_to_all(spread, axes, split_axis=0, concat_axis=0, tiled=True)
    first, second, third, block_losses = pl.pallas_call(
        functools.partial(unpack, where),
        out_shape=[
            shape_of(*conv_first.shape),
            shape_of(*conv_second.shape),
            shape_of(*conv_third.shape),
            shape_of(1, 1, 1, slot_total),
        ],
        in_specs=[VMEM] * 2,
        out_specs=[VMEM] * 4,
        scratch_shapes=[pltpu.VMEM((CH, tiles, LANES), jnp.float32)],
        compiler_params=PARAMS,
        name="unpack",
    )(gathered.reshape(CH, tiles, LANES), own)
    return advanced, block_losses, first, second, third


def solution(mesh):
    sizes = dict(mesh.shape)
    in_specs = (
        P(None, "gx", "gy", "gz"),
        P("gx", "gy", "gz"),
        P("gx", "gy", "gz", None),
        P("gx", "gy", "gz", None, None),
        P(),
        P(),
        P(),
    )
    out_specs = (P(None, "gx", "gy", "gz"), P("gx", "gy", "gz", None), P(), P(), P())
    return jax.shard_map(
        functools.partial(on_device, sizes), mesh=mesh, in_specs=in_specs, out_specs=out_specs,
        check_vma=False,
    )
```

```python
import functools

import jax
import jax.numpy as jnp
from jax import lax
from jax.experimental import pallas as pl
from jax.experimental.pallas import tpu as pltpu
from jax.sharding import PartitionSpec as P

BLK = 4
CAP = 2
SAMP = 8
Z_TILES = 2
NF = 4
VOL = BLK**3
TAPS = [(x, y, z) for x in (-1, 0, 1) for y in (-1, 0, 1) for z in (-1, 0, 1)]
LANES = 128
ROWS = 8
NOUT = 6
CH = 32

time_step = 0.25
buoyancy = 0.5

VMEM = pl.BlockSpec(memory_space=pltpu.VMEM)
SMEM = pl.BlockSpec(memory_space=pltpu.SMEM)
HBM = pl.BlockSpec(memory_space=pltpu.HBM)
ANY = pl.BlockSpec(memory_space=pl.ANY)
PARAMS = pltpu.CompilerParams(vmem_limit_bytes=24 * 1024 * 1024)
PACK = pltpu.CompilerParams(vmem_limit_bytes=54944 * 1024)
FULL = (((1,), (1,)), ((), ()))


def iota(shape, axis):
    return lax.broadcasted_iota(jnp.int32, shape, axis)


def odd(axis):
    return lax.axis_index(axis) % 2 == 1


def facing(axis, swap, first, last):
    return jnp.where(odd(axis), first, last) if swap == "a" else jnp.where(odd(axis), last, first)


def prev_next(axis, from_a, from_b):
    return jnp.where(odd(axis), from_a, from_b), jnp.where(odd(axis), from_b, from_a)


class Parts:
    def __init__(self, *parts):
        self.parts, self.tiles = parts, parts[0].shape[0]

    def at_tile(self, index):
        tile, rest = (index[0], index[1:]) if isinstance(index, tuple) else (index, ())
        return self.parts[tile // self.tiles], (tile % self.tiles,) + rest

    def __getitem__(self, index):
        part, place = self.at_tile(index)
        return part[place]

    def __setitem__(self, index, value):
        part, place = self.at_tile(index)
        part[place] = value


class Sides:
    def __init__(self, chunks, x_b, x_a, z_both, y_b=None, y_a=None):
        self.chunks = chunks
        self.x_a, self.x_b, self.y_a, self.y_b, self.z_both = x_a, x_b, y_a, y_b, z_both

    def along_x(self, f, c):
        tile = f * self.chunks + c
        return prev_next("gx", self.x_a[tile], self.x_b[tile])

    def along_y(self, f, depth=0):
        tile = depth * (NF + 1) + f
        return prev_next("gy", self.y_a[tile], self.y_b[tile])


def pair_of(f, c, planes, chunks):
    span = 2 * planes * chunks
    return f * span // LANES, f * span % LANES + 2 * planes * c


def add_pair(packed, tile, lane):
    moved = pltpu.roll(tile, lane + 1, 1)
    at = iota(tile.shape, 1)
    return jnp.where((at == lane) | (at == lane + 1), moved, packed)


def cut_x(f, array, x_b, x_a):
    planes, rows, _ = array.shape
    chunks = rows // ROWS
    for c in range(chunks):
        part = slice(ROWS * c, ROWS * c + ROWS)
        ends = array[0, part], array[planes - 1, part]
        x_b[f * chunks + c] = facing("gx", "b", *ends)
        x_a[f * chunks + c] = facing("gx", "a", *ends)


def pack_faces(fields_far, visc_far, x_b, x_a, z_both, y_b, y_a, fields, visc, sems):
    _, planes, rows, _ = fields.shape
    chunks = rows // ROWS
    copies = [pltpu.make_async_copy(fields_far.at[f], fields.at[f], sems.at[f]) for f in range(NF)]
    copies.append(pltpu.make_async_copy(visc_far, visc, sems.at[NF]))
    for copy in copies:
        copy.start()
    arrays = [fields.at[f] for f in range(NF)] + [visc]
    packed = [jnp.zeros((ROWS, LANES), jnp.float32) for _ in range(z_both.shape[0])]
    for f, array in enumerate(arrays):
        copies[f].wait()
        cut_x(f, array, x_b, x_a)
        for depth in range(2):
            ends = array[:, depth, :], array[:, rows - 1 - depth, :]
            y_b[depth * (NF + 1) + f] = facing("gy", "b", *ends)
            y_a[depth * (NF + 1) + f] = facing("gy", "a", *ends)
        for c in range(chunks):
            tile, lane = pair_of(f, c, planes, chunks)
            for x in range(planes):
                cells = array[x, ROWS * c : ROWS * c + ROWS]
                packed[tile] = add_pair(packed[tile], cells, lane + 2 * x)
    for tile, value in enumerate(packed):
        z_both[tile] = value


def flux(lower, upper, dimension):
    speed = 0.25 * (lower[dimension] + upper[dimension])
    mean_visc = 0.5 * (lower[NF] + upper[NF])
    return [speed * (a + b) - mean_visc * (b - a) for a, b in zip(lower[:NF], upper[:NF])]


def interior(fields, visc, partial):
    _, planes, rows, _ = fields.shape
    chunks = rows // ROWS
    end_row = iota((ROWS, LANES), 0) == ROWS - 1
    end_lane = iota((ROWS, LANES), 1) == LANES - 1
    every = range(NF + 1)

    def cell(f, x, part):
        return fields[f, x, part, :] if f < NF else visc[x, part, :]

    def plane(x, lowers):
        uppers = []
        last = x == planes - 1
        beyond = jnp.minimum(x + 1, planes - 1)
        behind = [jnp.zeros((ROWS, LANES), jnp.float32)] * NF
        for c in range(chunks):
            part = slice(ROWS * c, ROWS * c + ROWS)
            here = [cell(f, x, part) for f in every]
            after = [cell(f, beyond, part) for f in every]
            upper = flux(here, after, 0)
            upper = [jnp.where(last, 0.0, u) for u in upper]
            total = [b - a for a, b in zip(lowers[c], upper)]
            uppers.append(upper)
            above = [pltpu.roll(h, ROWS - 1, 0) for h in here]
            if c + 1 < chunks:
                first = slice(ROWS * c + ROWS, ROWS * c + ROWS + 1)
                above = [jnp.where(end_row, cell(f, x, first), above[f]) for f in every]
            upper = flux(here, above, 1)
            lower = [pltpu.roll(jnp.where(end_row, b, u), 1, 0) for b, u in zip(behind, upper)]
            if c + 1 == chunks:
                upper = [jnp.where(end_row, 0.0, u) for u in upper]
            behind = upper
            total = [t + (b - a) for t, a, b in zip(total, lower, upper)]
            right = [pltpu.roll(h, LANES - 1, 1) for h in here]
            upper = [jnp.where(end_lane, 0.0, u) for u in flux(here, right, 2)]
            lower = [pltpu.roll(u, 1, 1) for u in upper]
            total = [t + (b - a) for t, a, b in zip(total, lower, upper)]
            updated = [q - time_step * t for q, t in zip(here[:NF], total)]
            updated[2] = updated[2] + (time_step * buoyancy) * here[3]
            for f in range(NF):
                partial[f, x, part, :] = updated[f]
        return uppers

    zeros = [[jnp.zeros((ROWS, LANES), jnp.float32)] * NF for _ in range(chunks)]
    lax.fori_loop(0, planes, plane, zeros)


def rims_without_ends(fields, visc, sides, rims):
    rows = fields.shape[2]
    every = range(NF + 1)
    end_row = iota((ROWS, LANES), 0) == ROWS - 1
    end_lane = iota((ROWS, LANES), 1) == LANES - 1

    def own(row):
        return [fields[f, :, row, :] for f in range(NF)] + [visc[:, row, :]]

    for side in range(2):
        here = [sides.along_y(f)[side] for f in every]
        beyond = [sides.along_y(f, 1)[side] for f in every]
        below, above = (beyond, own(0)) if side == 0 else (own(rows - 1), beyond)
        total = [b - a for a, b in zip(flux(below, here, 1), flux(here, above, 1))]
        for dimension, axis, end in ((0, 0, end_row), (2, 1, end_lane)):
            after = [pltpu.roll(h, h.shape[axis] - 1, axis) for h in here]
            upper = [jnp.where(end, 0.0, u) for u in flux(here, after, dimension)]
            total = [t + (u - pltpu.roll(u, 1, axis)) for t, u in zip(total, upper)]
        updated = [q - time_step * t for q, t in zip(here[:NF], total)]
        updated[2] = updated[2] + (time_step * buoyancy) * here[3]
        for f in range(NF):
            rims[side * NF + f] = updated[f]


def rims_with_ends(rims, sides, later):
    row = iota((ROWS, LANES), 0)
    lane = iota((ROWS, LANES), 1)
    every = range(NF + 1)
    whole = []
    for side in range(2):
        here = [sides.along_y(f)[side] for f in every]
        tile = NF * later.chunks + side
        before, after = prev_next("gx", later.x_a[tile], later.x_b[tile])
        low = flux([before[f : f + 1] for f in every], [h[:1] for h in here], 0)
        high = flux([h[ROWS - 1 :] for h in here], [after[f : f + 1] for f in every], 0)
        columns = later.z_both[Z_TILES]
        left, right = [], []
        for f in every:
            both = pltpu.roll(columns, LANES - 1 - 2 * (side * (NF + 1) + f), 1)
            left.append(pltpu.roll(jnp.where(lane == LANES - 1, both, here[f]), 1, 1))
            right.append(pltpu.roll(jnp.where(lane == 0, both, here[f]), LANES - 1, 1))
        lower, upper = flux(left, here, 2), flux(here, right, 2)
        ends = []
        for f in range(NF):
            value = rims[side * NF + f]
            value = value + time_step * jnp.where(row == 0, low[f], 0.0)
            value = value - time_step * jnp.where(row == ROWS - 1, high[f], 0.0)
            value = value + time_step * jnp.where(lane == 0, lower[f], 0.0)
            ends.append(value - time_step * jnp.where(lane == LANES - 1, upper[f], 0.0))
        whole.append(ends)
    return whole


def interior_and_weights(samples_far, trainers_far, middle, visc, fields, y_b, y_a, conv_first, conv_second,
                         conv_third, partial, rims, w_first, w_second_t, w_third, w_third_t, drawn, samples, trainers, sems):
    copies = [
        pltpu.make_async_copy(samples_far, samples, sems.at[0]),
        pltpu.make_async_copy(trainers_far, trainers, sems.at[1]),
    ]
    for copy in copies:
        copy.start()
    interior(middle, visc, partial)
    rims_without_ends(fields, visc, Sides(0, None, None, None, y_b, y_a), rims)
    ahead = conv_first.shape[1]
    w_first[:, :ahead] = conv_first[...]
    w_first[:, ahead:] = jnp.zeros((CH, w_first.shape[1] - ahead), jnp.bfloat16)
    w_second_t[...] = conv_second[...].astype(jnp.float32).T.astype(jnp.bfloat16)
    third = conv_third[...].astype(jnp.float32)
    third = jnp.concatenate([third, jnp.zeros((w_third.shape[0] - NOUT, CH), jnp.float32)], 0)
    w_third[...] = third.astype(jnp.bfloat16)
    w_third_t[...] = third.T.astype(jnp.bfloat16)
    for copy in copies:
        copy.wait()
    at, row = iota((ROWS, LANES), 1), iota((ROWS, LANES), 0)
    table = jnp.zeros((ROWS, LANES), jnp.int32)
    for j in range(samples.shape[0]):
        table = jnp.where(at == j, jnp.where(row == 0, samples[j], trainers[j]), table)
    drawn[...] = table


def z_terms(own, other, visc_own, visc_other):
    lane = iota((ROWS, LANES), 1)
    second = lane % 2 == 1
    span = LANES // 2

    def ends(mine, theirs):
        lower = jnp.where(second, pltpu.roll(theirs, 1, 1), mine)
        return lower, jnp.where(second, mine, pltpu.roll(theirs, LANES - 1, 1))

    def twice(tile):
        return jnp.where(lane < span, tile, pltpu.roll(tile, span, 1))

    pairs = [ends(a, b) for a, b in zip(own, other)]
    speed = [twice(end) for end in pairs[2 * span // LANES]]
    visc = [twice(end) for end in ends(visc_own, visc_other)]
    speed = 0.25 * (speed[0] + speed[1])
    mean_visc = 0.5 * (visc[0] + visc[1])
    through = [speed * (a + b) - mean_visc * (b - a) for a, b in pairs]
    return [jnp.where(second, time_step, -time_step) * t for t in through]


def close(fields, visc, partial, halo, visc_halo, y_faces, z_own, visc_z_own, y_terms, emit):
    _, planes, rows, _ = fields.shape
    chunks = rows // ROWS
    every = range(NF + 1)
    row = iota((ROWS, LANES), 0)
    lane_at = iota((ROWS, LANES), 1)
    ends = (lane_at == 0) | (lane_at == LANES - 1)

    def cell(f, *index):
        return fields[(f,) + index] if f < NF else visc[index]

    def sides(f):
        return halo if f < NF else visc_halo

    lower = flux(y_faces[0], [cell(f, slice(None), 0) for f in every], 1)
    upper = flux([cell(f, slice(None), rows - 1) for f in every], y_faces[1], 1)
    for f in range(NF):
        y_terms[0, f] = time_step * lower[f]
        y_terms[1, f] = -time_step * upper[f]
    tiles = 2 * NF * planes * chunks // LANES
    terms = z_terms([z_own[t] for t in range(tiles)], [halo.z_both[t] for t in range(tiles)],
                    visc_z_own[tiles], visc_halo.z_both[tiles])
    for c in range(chunks):
        part = slice(ROWS * c, ROWS * c + ROWS)
        before, after = zip(*[sides(f).along_x(f, c) for f in every])
        low = flux(before, [cell(f, 0, part) for f in every], 0)
        high = flux([cell(f, planes - 1, part) for f in every], after, 0)
        for x in range(planes):
            for f in range(NF):
                tile, lane = pair_of(f, c, planes, chunks)
                moved = pltpu.roll(terms[tile], LANES - 1 - lane - 2 * x, 1)
                value = partial[f, x, part, :] + jnp.where(ends, moved, 0.0)
                if x == 0:
                    value = value + time_step * low[f]
                if x == planes - 1:
                    value = value - time_step * high[f]
                if c == 0:
                    value = value + jnp.where(row == 0, y_terms[0, f, x : x + 1, :], 0.0)
                if c == chunks - 1:
                    value = value + jnp.where(row == ROWS - 1, y_terms[1, f, x : x + 1, :], 0.0)
                emit(f, x, c, value)


def close_first(fields, visc, partial, z_own, x_from_b, x_from_a, z_other, y_from_b, y_from_a,
                middle, x_b, x_a_low, x_a_high, z_both, y_terms):
    x_a = Parts(x_a_low, x_a_high)
    _, planes, rows, _ = fields.shape
    chunks = rows // ROWS
    halo = Sides(chunks, x_from_b, x_from_a, z_other, y_from_b, y_from_a)
    packed = [jnp.zeros((ROWS, LANES), jnp.float32) for _ in range(Z_TILES + 1)]
    y_faces = list(zip(*[halo.along_y(f) for f in range(NF + 1)]))

    def emit(f, x, c, tile):
        middle[f, x, ROWS * c : ROWS * c + ROWS, :] = tile
        at, lane = pair_of(f, c, planes, chunks)
        packed[at] = add_pair(packed[at], tile, lane + 2 * x)

    for side in range(2):
        for f in range(NF + 1):
            face = y_faces[side][f]
            packed[-1] = add_pair(packed[-1], face, 2 * (side * (NF + 1) + f))
            x_b[NF * chunks + side, f : f + 1, :] = facing("gx", "b", face[:1], face[planes - 1 :])
            x_a[NF * chunks + side, f : f + 1, :] = facing("gx", "a", face[:1], face[planes - 1 :])
    close(fields, visc, partial, halo, halo, y_faces, z_own, z_own, y_terms, emit)
    for at in range(z_both.shape[0]):
        z_both[at] = packed[at] if at <= Z_TILES else jnp.zeros((ROWS, LANES), jnp.float32)
    for f in range(NF):
        cut_x(f, middle.at[f], x_b, x_a)


def inside_masks():
    at = iota((1, LANES), 1) % VOL
    coords = (at // (BLK * BLK), at // BLK % BLK, at % BLK)
    along = []
    for coord in coords:
        along.append({
            -1: jnp.where(coord > 0, 1.0, 0.0),
            0: jnp.ones((1, LANES), jnp.float32),
            1: jnp.where(coord < BLK - 1, 1.0, 0.0),
        })
    return along


def move_of(tap):
    return tap[0] * BLK * BLK + tap[1] * BLK + tap[2]


def shifted(tile, tap, along):
    move = move_of(tap)
    if move == 0:
        return tile
    mask = along[0][tap[0]] * along[1][tap[1]] * along[2][tap[2]]
    return pltpu.roll(tile, (-move) % LANES, 1) * mask


def box(tile, along):
    for dimension, step in enumerate((BLK * BLK, BLK, 1)):
        ahead = pltpu.roll(tile, LANES - step, 1) * along[dimension][1]
        behind = pltpu.roll(tile, step, 1) * along[dimension][-1]
        tile = (behind + tile) + ahead
    return tile / 27.0


def sigmoid(values):
    return 1.0 / (1.0 + jnp.exp(-values))


PICKED = (0, 1, 2, 3, 0, 1, 2, 3, 0, 1, 2, 0, 0, 1, -1, -1, 0, 1, 2, 1, 2, 2, -1, -1)


def pick_rows():
    out, field = iota((32, NF * ROWS), 0), iota((32, NF * ROWS), 1) // ROWS
    table = jnp.zeros((32, NF * ROWS), jnp.float32)
    for i, f in enumerate(PICKED):
        table = jnp.where((out == i) & (field == f), 1.0, table)
    return table.astype(jnp.bfloat16)


def pick_blocks(advanced, samples, count):
    _, _, rows, lanes = advanced.shape
    along_y, along_z = rows // BLK, lanes // BLK
    row = iota((ROWS, LANES), 0)
    lane_at = iota((ROWS, LANES), 1)
    pick = pick_rows()
    out = []
    for j in range(0, count, 2):
        parts = [jnp.zeros((ROWS, LANES), jnp.float32) for _ in range(NF)]
        uppers = []
        for half in range(2):
            block = samples[j + half]
            block_x = block // (along_y * along_z)
            block_y = block // along_z % along_y
            block_z = block % along_z
            uppers.append(block_y % 2)
            start = pl.multiple_of(block_y // 2 * ROWS, ROWS)
            for x in range(BLK):
                turn = lax.rem(VOL * half + BLK * BLK * x - BLK * block_z + LANES, LANES)
                wanted = lane_at // BLK == (VOL * half + BLK * BLK * x) // BLK
                for f in range(NF):
                    tile = advanced[f, block_x * BLK + x, pl.ds(start, ROWS), :]
                    parts[f] = jnp.where(wanted, pltpu.roll(tile, turn, 1), parts[f])
        upper = jnp.where(lane_at < VOL, uppers[0], uppers[1])
        valid = row // BLK == upper
        for f in range(NF):
            for bit in (1, 2):
                moved = pltpu.roll(parts[f], BLK * bit, 1)
                parts[f] = jnp.where(row // bit % 2 == 1, moved, parts[f])
            parts[f] = jnp.where(valid, parts[f], 0.0)
        stacked = jnp.concatenate(parts, 0).astype(jnp.bfloat16)
        out.append(jnp.dot(pick, stacked, preferred_element_type=jnp.float32))
    return out


def closure(advanced, samples, trainers, loads, w_first, w_second, w_second_t, w_third,
            w_third_t, devices_all, stack_first, stack_mid, rows_out, send, slots, inline, place):
    count = len(samples)
    pairs = count // 2
    cols = [slice(LANES * m, LANES * m + LANES) for m in range(pairs)]
    along = inside_masks()
    lane_at = iota((ROWS, LANES), 1)
    row = iota((ROWS, LANES), 0)

    pos_x, pos_y, pos_z, count_y, count_z = place
    picked = pick_blocks(advanced, samples, count)
    values = [p[:ROWS] for p in picked]
    targets = []
    for p in picked:
        first, second = p[ROWS : 2 * ROWS], p[2 * ROWS : 3 * ROWS]
        targets.append(box(first * second, along) - box(first, along) * box(second, along))

    for m, tile in enumerate(values):
        for t in range(0, 28, 2):
            piece = shifted(tile, TAPS[t], along)
            later = shifted(tile, TAPS[t + 1], along) if t + 1 < 27 else jnp.zeros_like(tile)
            stack_first[BLK * t : BLK * t + ROWS, cols[m]] = jnp.where(row < NF, piece, later)
    stack_in = stack_first[...].astype(jnp.bfloat16)
    pre_first = jnp.dot(w_first, stack_in, preferred_element_type=jnp.float32)
    gate_first = sigmoid(pre_first)
    hidden_first = (pre_first * gate_first).astype(jnp.bfloat16).astype(jnp.float32)
    for m in range(pairs):
        tile = hidden_first[:, cols[m]]
        for k, tap in enumerate(TAPS):
            stack_mid[CH * k : CH * k + CH, cols[m]] = shifted(tile, tap, along).astype(jnp.bfloat16)
    pre_second = jnp.dot(w_second, stack_mid[...], preferred_element_type=jnp.float32)
    gate_second = sigmoid(pre_second)
    hidden_second = (pre_second * gate_second).astype(jnp.bfloat16)
    predicted = jnp.dot(w_third, hidden_second, preferred_element_type=jnp.float32)

    misfit = predicted[:ROWS] - jnp.concatenate(targets, 1)
    square = jnp.sum(misfit * misfit, axis=0, keepdims=True)
    sample_at = iota((ROWS, count * VOL), 1) // VOL
    mine = sample_at == iota((ROWS, count * VOL), 0)
    losses = jnp.sum(jnp.where(mine, square, 0.0), axis=1, keepdims=True) / (NOUT * VOL)
    if loads is None:
        load = jnp.full((ROWS, 1), float(count_y * CAP), jnp.float32)
    else:
        owner = jnp.zeros((ROWS, LANES), jnp.int32)
        for j in range(count):
            owner = jnp.where(row == j, trainers[j], owner)
        load = jnp.sum(jnp.where(lane_at == owner, loads, 0.0), axis=1, keepdims=True)
    share = 1.0 / (devices_all * jnp.maximum(load, 1.0))
    scale = share * (2.0 / (NOUT * VOL))
    scale_at = jnp.sum(jnp.where(mine, scale, 0.0), axis=0, keepdims=True)
    grad_pred = (misfit * scale_at).astype(jnp.bfloat16)
    grad_pred = jnp.concatenate([grad_pred, jnp.zeros_like(grad_pred)], 0)

    upper = jnp.dot(w_third_t, grad_pred, preferred_element_type=jnp.float32)
    slope = gate_second * (1.0 + pre_second * (1.0 - gate_second))
    grad_mid = (upper * slope).astype(jnp.bfloat16)
    grad_second = lax.dot_general(grad_mid, stack_mid[...], FULL, preferred_element_type=jnp.float32)
    third = jnp.concatenate([grad_pred, jnp.zeros((LANES - 16, count * VOL), jnp.bfloat16)], 0)
    grad_third = lax.dot_general(hidden_second, third, FULL, preferred_element_type=jnp.float32)

    spread = jnp.dot(w_second_t, grad_mid, preferred_element_type=jnp.float32)
    lower = []
    for m in range(pairs):
        terms = [
            shifted(spread[CH * k : CH * k + CH, cols[m]], tuple(-o for o in tap), along)
            for k, tap in enumerate(TAPS)
        ]
        lower.append(functools.reduce(jnp.add, terms))
    lower = jnp.concatenate(lower, 1)
    slope = gate_first * (1.0 + pre_first * (1.0 - gate_first))
    grad_entry = (lower * slope).astype(jnp.bfloat16)
    grad_first = lax.dot_general(grad_entry, stack_in, FULL, preferred_element_type=jnp.float32)

    whole = CH * 27 // LANES
    rest = CH * 27 - whole * LANES
    for t in range(whole):
        rows_out[:, t, :] = grad_second[:, LANES * t : LANES * t + LANES]
    mixed = jnp.concatenate([grad_second[:, whole * LANES :], jnp.zeros((CH, LANES - rest), jnp.float32)], 1)
    mixed = mixed + pltpu.roll(grad_third, rest, 1)
    tail = LANES - grad_first.shape[1]
    rows_out[:, whole + 1, :] = jnp.concatenate([grad_first, jnp.zeros((CH, tail), jnp.float32)], 1)

    offset = rest + ROWS if inline else 0
    height = CH if inline else slots.shape[0]
    slot_rows = iota((height, LANES), 0)
    slot_lanes = iota((height, LANES), 1)
    placed = jnp.zeros((height, LANES), jnp.float32)
    for j in range(count):
        name = trainers[j]
        rank = jnp.int32(0)
        for i in range(j):
            rank = rank + jnp.where(trainers[i] == name, 1, 0)
        target = (pos_x * count_y + name) * count_z + pos_z
        slot = offset + pos_y * CAP + rank
        hit = (slot_rows == target) & (slot_lanes == slot)
        placed = jnp.where(hit, losses[j : j + 1, :], placed)
    high = placed.astype(jnp.bfloat16).astype(jnp.float32)
    placed = high + pltpu.roll(placed - high, count_y * CAP, 1)
    if inline:
        mixed = mixed + placed
    else:
        slots[:, 0, :] = placed.astype(jnp.bfloat16)
    rows_out[:, whole, :] = mixed
    send[...] = rows_out[...].astype(jnp.bfloat16)


def second_step(sizes, inline, drawn, middle, visc, partial, rims, vz_own, vx_b, vx_a, vz_other, vy_b, vy_a,
                z_own, x_b, z_other, x_a_low, x_a_high, *rest):
    loads, rest = (None, rest) if sizes["gy"] * CAP == SAMP else (rest[0][...], rest[1:])
    w_first, w_second, w_second_t, w_third, w_third_t, advanced, send = rest[:7]
    slots = None if inline else rest[7]
    stack_first, stack_mid, rows_out, y_terms = rest[-4:]
    chunks = middle.shape[2] // ROWS
    halo = Sides(chunks, x_b, Parts(x_a_low, x_a_high), z_other)
    visc_halo = Sides(chunks, vx_b, vx_a, vz_other, vy_b, vy_a)
    y_faces = rims_with_ends(rims, visc_halo, halo)
    y_faces = [face + [visc_halo.along_y(NF)[side]] for side, face in enumerate(y_faces)]
    count = stack_mid.shape[1] // VOL
    samples = [drawn[0, j] for j in range(count)]
    trainers = [drawn[1, j] for j in range(count)]

    def emit(f, x, c, tile):
        advanced[f, x, ROWS * c : ROWS * c + ROWS, :] = tile

    close(middle, visc, partial, halo, visc_halo, y_faces, z_own, vz_own, y_terms, emit)
    place = (lax.axis_index("gx"), lax.axis_index("gy"), lax.axis_index("gz"), sizes["gy"], sizes["gz"])
    closure(advanced, samples, trainers, loads, w_first[...], w_second[...],
            w_second_t[...], w_third[...], w_third_t[...],
            float(sizes["gx"] * sizes["gy"] * sizes["gz"]), stack_first, stack_mid, rows_out,
            send, slots, inline, place)


def add_up(arrived, spread, own):
    total = jnp.sum(arrived[...].astype(jnp.float32), axis=0)
    own[...] = total
    rounded = total.astype(jnp.bfloat16)
    for i in range(spread.shape[0]):
        spread[i] = rounded


def unpack(where, gathered, own, kept, first, second, third, losses, advanced, wide, sems):
    copies = [pltpu.make_async_copy(kept.at[f], advanced.at[f], sems.at[f]) for f in range(NF)]
    for copy in copies:
        copy.start()
    row, lane = where
    count = losses.shape[3]
    high = own[row : row + 1, lane : lane + count]
    losses[0, 0] = high + own[row : row + 1, lane + count : lane + 2 * count]
    wide[...] = gathered[...].astype(jnp.float32)
    whole = second.shape[1] // LANES
    rest = second.shape[1] - whole * LANES
    for t in range(whole):
        second[:, LANES * t : LANES * t + LANES] = wide[:, t, :]
    mixed = wide[:, whole, :]
    second[:, LANES * whole :] = mixed[:, :rest]
    third[...] = mixed[:, rest : rest + ROWS].T[:NOUT]
    first[...] = wide[:, whole + 1, :][:, : first.shape[1]]
    for copy in copies:
        copy.wait()


def shape_of(*dims, dtype=jnp.float32):
    return jax.ShapeDtypeStruct(dims, dtype)


def swap_a(face, axis, sizes):
    return lax.ppermute(face, axis, [(i, i ^ 1) for i in range(sizes[axis])])


def swap_b(face, axis, sizes):
    count = sizes[axis]
    return lax.ppermute(face, axis, [(i, (i + (1 if i % 2 else -1)) % count) for i in range(count)])


def without_border(kernel, fields, visc, index=(), first=(), weights=()):
    cells = visc.size
    out_shape = [shape_of(*fields.shape)]
    scratch = [pltpu.SMEM(array.shape, jnp.int32) for array in index]
    if weights:
        scratch.append(pltpu.SemaphoreType.DMA((len(index),)))
        sizes = ((CH, 28 * NF), (27 * CH, CH), (16, CH), (CH, 16))
        out_shape.append(shape_of(2 * NF, ROWS, LANES))
        out_shape += [shape_of(*size, dtype=jnp.bfloat16) for size in sizes]
        out_shape.append(shape_of(ROWS, LANES, dtype=jnp.int32))
    return pl.pallas_call(
        kernel,
        out_shape=out_shape,
        in_specs=[ANY] * len(index) + [VMEM] * (2 + len(first) + len(weights)),
        out_specs=[VMEM] * len(out_shape),
        scratch_shapes=scratch,
        compiler_params=PARAMS,
        cost_estimate=pl.CostEstimate(flops=120 * cells, bytes_accessed=36 * cells, transcendentals=0),
        name=kernel.__name__,
    )(*index, fields, visc, *first, *weights)


def on_device(sizes, fields, visc, samples, trainers, conv_first, conv_second, conv_third):
    _, planes, rows, lanes = fields.shape
    axes = ("gx", "gy", "gz")
    devices_all = sizes["gx"] * sizes["gy"] * sizes["gz"]
    chunks = rows // ROWS
    pairs = planes * chunks
    half = LANES // 2
    samples = samples.reshape(-1)
    trainers = trainers.reshape(-1)

    faces = pl.pallas_call(
        pack_faces,
        out_shape=[
            shape_of((NF + 1) * chunks, ROWS, lanes),
            shape_of((NF + 1) * chunks, ROWS, lanes),
            shape_of(-(-(NF + 1) * pairs // half), ROWS, LANES),
            shape_of(2 * (NF + 1), planes, lanes),
            shape_of(2 * (NF + 1), planes, lanes),
        ],
        in_specs=[HBM, HBM],
        out_specs=[VMEM] * 5,
        scratch_shapes=[
            pltpu.VMEM(fields.shape, jnp.float32),
            pltpu.VMEM(visc.shape, jnp.float32),
            pltpu.SemaphoreType.DMA((NF + 1,)),
        ],
        compiler_params=PACK,
        name="pack_faces",
    )(fields, visc)
    x_b, x_a, z_own, y_b, y_a = faces
    halo = [
        swap_b(x_b, "gx", sizes), swap_a(x_a, "gx", sizes), swap_a(z_own, "gz", sizes),
        swap_b(y_b, "gy", sizes), swap_a(y_a, "gy", sizes),
    ]

    own_counts = sizes["gy"] * CAP == SAMP
    counts = []
    if not own_counts:
        named = trainers.reshape(-1, 1) == jnp.arange(LANES, dtype=jnp.int32)[None, :]
        total = lax.psum(jnp.sum(named.astype(jnp.float32), axis=0, keepdims=True), "gy")
        counts = [jnp.broadcast_to(total, (ROWS, LANES))]
    y_terms = pltpu.VMEM((2, NF, planes, lanes), jnp.float32)
    middle, x_b, x_a_low, x_a_high, z_later = pl.pallas_call(
        close_first,
        out_shape=[
            shape_of(*fields.shape),
            shape_of(NF * chunks + 2, ROWS, lanes),
            shape_of(NF * chunks // 2 + 1, ROWS, lanes),
            shape_of(NF * chunks // 2 + 1, ROWS, lanes),
            shape_of(NF * chunks // 2 + 2, ROWS, LANES),
        ],
        in_specs=[VMEM] * 9,
        out_specs=[VMEM] * 5,
        scratch_shapes=[y_terms],
        compiler_params=PARAMS,
        name="close_first",
    )(fields, visc, *without_border(interior, fields, visc), z_own, *halo)
    later = [
        swap_b(x_b, "gx", sizes), swap_a(z_later, "gz", sizes),
        swap_a(x_a_low, "gx", sizes), swap_a(x_a_high, "gx", sizes),
    ]
    partial, rims, w_first, w_second_t, w_third, w_third_t, drawn = without_border(
        interior_and_weights, middle, visc, (samples, trainers), (fields, *halo[3:]),
        (conv_first, conv_second, conv_third),
    )

    count = samples.shape[0]
    slot_total = sizes["gy"] * CAP
    tiles = -(-27 * CH // LANES) + 1
    parts = devices_all // CH
    inline = parts == 1 and slot_total <= 12
    out_shape = [shape_of(*fields.shape), shape_of(CH, tiles, LANES, dtype=jnp.bfloat16)]
    if not inline:
        out_shape.append(shape_of(devices_all, 1, LANES, dtype=jnp.bfloat16))
    kept, send, *slots = pl.pallas_call(
        functools.partial(second_step, sizes, inline),
        out_shape=out_shape,
        in_specs=[VMEM] * (21 + len(counts)),
        out_specs=[VMEM] * len(out_shape),
        scratch_shapes=[
            pltpu.VMEM((28 * NF, count * VOL), jnp.float32),
            pltpu.VMEM((27 * CH, count * VOL), jnp.bfloat16),
            pltpu.VMEM((CH, tiles, LANES), jnp.float32),
            y_terms,
        ],
        compiler_params=PARAMS,
        name="second_step",
    )(drawn, middle, visc, partial, rims, z_own, *halo, z_later, *later, *counts,
      w_first, conv_second, w_second_t, w_third, w_third_t)

    if not inline:
        send = jnp.concatenate([send.reshape(devices_all, tiles // parts, LANES), slots[0]], 1)
    arrived = lax.all_to_all(send, axes, split_axis=0, concat_axis=0, tiled=True)
    if inline:
        where = (27 * CH // LANES, 27 * CH % LANES + ROWS)
    else:
        where = (send.shape[1] - 1, 0)
    spread, own = pl.pallas_call(
        add_up,
        out_shape=[shape_of(*send.shape, dtype=jnp.bfloat16), shape_of(*send.shape[1:])],
        in_specs=[VMEM],
        out_specs=[VMEM] * 2,
        compiler_params=PARAMS,
        name="add_up",
    )(arrived)
    if not inline:
        spread = spread[:, :-1, :]
    gathered = lax.all_to_all(spread, axes, split_axis=0, concat_axis=0, tiled=True)
    first, second, third, block_losses, advanced = pl.pallas_call(
        functools.partial(unpack, where),
        out_shape=[
            shape_of(*conv_first.shape),
            shape_of(*conv_second.shape),
            shape_of(*conv_third.shape),
            shape_of(1, 1, 1, slot_total),
            shape_of(*fields.shape),
        ],
        in_specs=[VMEM, VMEM, ANY],
        out_specs=[VMEM] * 4 + [ANY],
        scratch_shapes=[pltpu.VMEM((CH, tiles, LANES), jnp.float32), pltpu.SemaphoreType.DMA((NF,))],
        compiler_params=PARAMS,
        name="unpack",
    )(gathered.reshape(CH, tiles, LANES), own, kept)
    return advanced, block_losses, first, second, third


def solution(mesh):
    sizes = dict(mesh.shape)
    in_specs = (
        P(None, "gx", "gy", "gz"),
        P("gx", "gy", "gz"),
        P("gx", "gy", "gz", None),
        P("gx", "gy", "gz", None, None),
        P(),
        P(),
        P(),
    )
    out_specs = (P(None, "gx", "gy", "gz"), P("gx", "gy", "gz", None), P(), P(), P())
    return jax.shard_map(
        functools.partial(on_device, sizes), mesh=mesh, in_specs=in_specs, out_specs=out_specs,
        check_vma=False,
    )
```

```python
import functools

import jax
import jax.numpy as jnp
from jax import lax
from jax.experimental import pallas as pl
from jax.experimental.pallas import tpu as pltpu
from jax.sharding import PartitionSpec as P

BLK = 4
CAP = 2
SAMP = 8
Z_TILES = 2
NF = 4
VOL = BLK**3
TAPS = [(x, y, z) for x in (-1, 0, 1) for y in (-1, 0, 1) for z in (-1, 0, 1)]
LANES = 128
ROWS = 8
NOUT = 6
CH = 32

time_step = 0.25
buoyancy = 0.5

VMEM = pl.BlockSpec(memory_space=pltpu.VMEM)
SMEM = pl.BlockSpec(memory_space=pltpu.SMEM)
HBM = pl.BlockSpec(memory_space=pltpu.HBM)
ANY = pl.BlockSpec(memory_space=pl.ANY)
PARAMS = pltpu.CompilerParams(vmem_limit_bytes=24 * 1024 * 1024)
PACK = pltpu.CompilerParams(vmem_limit_bytes=54944 * 1024)
FULL = (((1,), (1,)), ((), ()))


def iota(shape, axis):
    return lax.broadcasted_iota(jnp.int32, shape, axis)


def odd(axis):
    return lax.axis_index(axis) % 2 == 1


def facing(axis, swap, first, last):
    return jnp.where(odd(axis), first, last) if swap == "a" else jnp.where(odd(axis), last, first)


def prev_next(axis, from_a, from_b):
    return jnp.where(odd(axis), from_a, from_b), jnp.where(odd(axis), from_b, from_a)


class Parts:
    def __init__(self, *parts):
        self.parts, self.tiles = parts, parts[0].shape[0]

    def at_tile(self, index):
        tile, rest = (index[0], index[1:]) if isinstance(index, tuple) else (index, ())
        return self.parts[tile // self.tiles], (tile % self.tiles,) + rest

    def __getitem__(self, index):
        part, place = self.at_tile(index)
        return part[place]

    def __setitem__(self, index, value):
        part, place = self.at_tile(index)
        part[place] = value


class Sides:
    def __init__(self, chunks, x_b, x_a, z_both, y_b=None, y_a=None):
        self.chunks = chunks
        self.x_a, self.x_b, self.y_a, self.y_b, self.z_both = x_a, x_b, y_a, y_b, z_both

    def along_x(self, f, c):
        tile = f * self.chunks + c
        return prev_next("gx", self.x_a[tile], self.x_b[tile])

    def along_y(self, f, depth=0):
        tile = depth * (NF + 1) + f
        return prev_next("gy", self.y_a[tile], self.y_b[tile])


def pair_of(f, c, planes, chunks):
    span = 2 * planes * chunks
    return f * span // LANES, f * span % LANES + 2 * planes * c


def add_pair(packed, tile, lane):
    moved = pltpu.roll(tile, lane + 1, 1)
    at = iota(tile.shape, 1)
    return jnp.where((at == lane) | (at == lane + 1), moved, packed)


def cut_x(f, array, x_b, x_a):
    planes, rows, _ = array.shape
    chunks = rows // ROWS
    for c in range(chunks):
        part = slice(ROWS * c, ROWS * c + ROWS)
        ends = array[0, part], array[planes - 1, part]
        x_b[f * chunks + c] = facing("gx", "b", *ends)
        x_a[f * chunks + c] = facing("gx", "a", *ends)


def pack_faces(fields_far, visc_far, x_b, x_a, z_both, y_b, y_a, fields, visc, sems):
    _, planes, rows, _ = fields.shape
    chunks = rows // ROWS
    copies = [
        pltpu.make_async_copy(fields_far, fields, sems.at[0]),
        pltpu.make_async_copy(visc_far, visc, sems.at[1]),
    ]
    for copy in copies:
        copy.start()
    arrays = [fields.at[f] for f in range(NF)] + [visc]
    packed = [jnp.zeros((ROWS, LANES), jnp.float32) for _ in range(z_both.shape[0])]
    for f, array in enumerate(arrays):
        if f == 0 or f == NF:
            copies[f // NF].wait()
        cut_x(f, array, x_b, x_a)
        for depth in range(2):
            ends = array[:, depth, :], array[:, rows - 1 - depth, :]
            y_b[depth * (NF + 1) + f] = facing("gy", "b", *ends)
            y_a[depth * (NF + 1) + f] = facing("gy", "a", *ends)
        for c in range(chunks):
            tile, lane = pair_of(f, c, planes, chunks)
            for x in range(planes):
                cells = array[x, ROWS * c : ROWS * c + ROWS]
                packed[tile] = add_pair(packed[tile], cells, lane + 2 * x)
    for tile, value in enumerate(packed):
        z_both[tile] = value


def flux(lower, upper, dimension):
    speed = 0.25 * (lower[dimension] + upper[dimension])
    mean_visc = 0.5 * (lower[NF] + upper[NF])
    return [speed * (a + b) - mean_visc * (b - a) for a, b in zip(lower[:NF], upper[:NF])]


def interior(fields, visc, partial):
    _, planes, rows, _ = fields.shape
    chunks = rows // ROWS
    end_row = iota((ROWS, LANES), 0) == ROWS - 1
    end_lane = iota((ROWS, LANES), 1) == LANES - 1
    every = range(NF + 1)

    def cell(f, x, part):
        return fields[f, x, part, :] if f < NF else visc[x, part, :]

    def plane(x, lowers):
        uppers = []
        last = x == planes - 1
        beyond = jnp.minimum(x + 1, planes - 1)
        behind = [jnp.zeros((ROWS, LANES), jnp.float32)] * NF
        for c in range(chunks):
            part = slice(ROWS * c, ROWS * c + ROWS)
            here = [cell(f, x, part) for f in every]
            after = [cell(f, beyond, part) for f in every]
            upper = flux(here, after, 0)
            upper = [jnp.where(last, 0.0, u) for u in upper]
            total = [b - a for a, b in zip(lowers[c], upper)]
            uppers.append(upper)
            above = [pltpu.roll(h, ROWS - 1, 0) for h in here]
            if c + 1 < chunks:
                first = slice(ROWS * c + ROWS, ROWS * c + ROWS + 1)
                above = [jnp.where(end_row, cell(f, x, first), above[f]) for f in every]
            upper = flux(here, above, 1)
            lower = [pltpu.roll(jnp.where(end_row, b, u), 1, 0) for b, u in zip(behind, upper)]
            if c + 1 == chunks:
                upper = [jnp.where(end_row, 0.0, u) for u in upper]
            behind = upper
            total = [t + (b - a) for t, a, b in zip(total, lower, upper)]
            right = [pltpu.roll(h, LANES - 1, 1) for h in here]
            upper = [jnp.where(end_lane, 0.0, u) for u in flux(here, right, 2)]
            lower = [pltpu.roll(u, 1, 1) for u in upper]
            total = [t + (b - a) for t, a, b in zip(total, lower, upper)]
            updated = [q - time_step * t for q, t in zip(here[:NF], total)]
            updated[2] = updated[2] + (time_step * buoyancy) * here[3]
            for f in range(NF):
                partial[f, x, part, :] = updated[f]
        return uppers

    zeros = [[jnp.zeros((ROWS, LANES), jnp.float32)] * NF for _ in range(chunks)]
    lax.fori_loop(0, planes, plane, zeros)


def rims_without_ends(fields, visc, sides, rims):
    rows = fields.shape[2]
    every = range(NF + 1)
    end_row = iota((ROWS, LANES), 0) == ROWS - 1
    end_lane = iota((ROWS, LANES), 1) == LANES - 1

    def own(row):
        return [fields[f, :, row, :] for f in range(NF)] + [visc[:, row, :]]

    for side in range(2):
        here = [sides.along_y(f)[side] for f in every]
        beyond = [sides.along_y(f, 1)[side] for f in every]
        below, above = (beyond, own(0)) if side == 0 else (own(rows - 1), beyond)
        total = [b - a for a, b in zip(flux(below, here, 1), flux(here, above, 1))]
        for dimension, axis, end in ((0, 0, end_row), (2, 1, end_lane)):
            after = [pltpu.roll(h, h.shape[axis] - 1, axis) for h in here]
            upper = [jnp.where(end, 0.0, u) for u in flux(here, after, dimension)]
            total = [t + (u - pltpu.roll(u, 1, axis)) for t, u in zip(total, upper)]
        updated = [q - time_step * t for q, t in zip(here[:NF], total)]
        updated[2] = updated[2] + (time_step * buoyancy) * here[3]
        for f in range(NF):
            rims[side * NF + f] = updated[f]


def rims_with_ends(rims, sides, later):
    row = iota((ROWS, LANES), 0)
    lane = iota((ROWS, LANES), 1)
    every = range(NF + 1)
    whole = []
    for side in range(2):
        here = [sides.along_y(f)[side] for f in every]
        tile = NF * later.chunks + side
        before, after = prev_next("gx", later.x_a[tile], later.x_b[tile])
        low = flux([before[f : f + 1] for f in every], [h[:1] for h in here], 0)
        high = flux([h[ROWS - 1 :] for h in here], [after[f : f + 1] for f in every], 0)
        columns = later.z_both[Z_TILES]
        left, right = [], []
        for f in every:
            both = pltpu.roll(columns, LANES - 1 - 2 * (side * (NF + 1) + f), 1)
            left.append(pltpu.roll(jnp.where(lane == LANES - 1, both, here[f]), 1, 1))
            right.append(pltpu.roll(jnp.where(lane == 0, both, here[f]), LANES - 1, 1))
        lower, upper = flux(left, here, 2), flux(here, right, 2)
        ends = []
        for f in range(NF):
            value = rims[side * NF + f]
            value = value + time_step * jnp.where(row == 0, low[f], 0.0)
            value = value - time_step * jnp.where(row == ROWS - 1, high[f], 0.0)
            value = value + time_step * jnp.where(lane == 0, lower[f], 0.0)
            ends.append(value - time_step * jnp.where(lane == LANES - 1, upper[f], 0.0))
        whole.append(ends)
    return whole


def interior_first(samples_far, trainers_far, fields, visc, conv_first, conv_third, partial, w_first,
                   w_third, w_third_t, drawn, samples, trainers, sems):
    copies = [
        pltpu.make_async_copy(samples_far, samples, sems.at[0]),
        pltpu.make_async_copy(trainers_far, trainers, sems.at[1]),
    ]
    for copy in copies:
        copy.start()
    interior(fields, visc, partial)
    ahead = conv_first.shape[1]
    w_first[:, :ahead] = conv_first[...]
    w_first[:, ahead:] = jnp.zeros((CH, w_first.shape[1] - ahead), jnp.bfloat16)
    third = conv_third[...].astype(jnp.float32)
    third = jnp.concatenate([third, jnp.zeros((w_third.shape[0] - NOUT, CH), jnp.float32)], 0)
    w_third[...] = third.astype(jnp.bfloat16)
    w_third_t[...] = third.T.astype(jnp.bfloat16)
    for copy in copies:
        copy.wait()
    at, row = iota((ROWS, LANES), 1), iota((ROWS, LANES), 0)
    table = jnp.zeros((ROWS, LANES), jnp.int32)
    for j in range(samples.shape[0]):
        table = jnp.where(at == j, jnp.where(row == 0, samples[j], trainers[j]), table)
    drawn[...] = table


def interior_second(middle, visc, fields, y_b, y_a, conv_second, partial, rims, w_second_t):
    interior(middle, visc, partial)
    rims_without_ends(fields, visc, Sides(0, None, None, None, y_b, y_a), rims)
    w_second_t[...] = conv_second[...].astype(jnp.float32).T.astype(jnp.bfloat16)


def z_terms(own, other, visc_own, visc_other):
    lane = iota((ROWS, LANES), 1)
    second = lane % 2 == 1
    span = LANES // 2

    def ends(mine, theirs):
        lower = jnp.where(second, pltpu.roll(theirs, 1, 1), mine)
        return lower, jnp.where(second, mine, pltpu.roll(theirs, LANES - 1, 1))

    def twice(tile):
        return jnp.where(lane < span, tile, pltpu.roll(tile, span, 1))

    pairs = [ends(a, b) for a, b in zip(own, other)]
    speed = [twice(end) for end in pairs[2 * span // LANES]]
    visc = [twice(end) for end in ends(visc_own, visc_other)]
    speed = 0.25 * (speed[0] + speed[1])
    mean_visc = 0.5 * (visc[0] + visc[1])
    through = [speed * (a + b) - mean_visc * (b - a) for a, b in pairs]
    return [jnp.where(second, time_step, -time_step) * t for t in through]


def close(fields, visc, partial, halo, visc_halo, y_faces, z_own, visc_z_own, y_terms, emit):
    _, planes, rows, _ = fields.shape
    chunks = rows // ROWS
    every = range(NF + 1)
    row = iota((ROWS, LANES), 0)
    lane_at = iota((ROWS, LANES), 1)
    ends = (lane_at == 0) | (lane_at == LANES - 1)

    def cell(f, *index):
        return fields[(f,) + index] if f < NF else visc[index]

    def sides(f):
        return halo if f < NF else visc_halo

    lower = flux(y_faces[0], [cell(f, slice(None), 0) for f in every], 1)
    upper = flux([cell(f, slice(None), rows - 1) for f in every], y_faces[1], 1)
    for f in range(NF):
        y_terms[0, f] = time_step * lower[f]
        y_terms[1, f] = -time_step * upper[f]
    tiles = 2 * NF * planes * chunks // LANES
    terms = z_terms([z_own[t] for t in range(tiles)], [halo.z_both[t] for t in range(tiles)],
                    visc_z_own[tiles], visc_halo.z_both[tiles])
    for c in range(chunks):
        part = slice(ROWS * c, ROWS * c + ROWS)
        before, after = zip(*[sides(f).along_x(f, c) for f in every])
        low = flux(before, [cell(f, 0, part) for f in every], 0)
        high = flux([cell(f, planes - 1, part) for f in every], after, 0)
        for x in range(planes):
            for f in range(NF):
                tile, lane = pair_of(f, c, planes, chunks)
                moved = pltpu.roll(terms[tile], LANES - 1 - lane - 2 * x, 1)
                value = partial[f, x, part, :] + jnp.where(ends, moved, 0.0)
                if x == 0:
                    value = value + time_step * low[f]
                if x == planes - 1:
                    value = value - time_step * high[f]
                if c == 0:
                    value = value + jnp.where(row == 0, y_terms[0, f, x : x + 1, :], 0.0)
                if c == chunks - 1:
                    value = value + jnp.where(row == ROWS - 1, y_terms[1, f, x : x + 1, :], 0.0)
                emit(f, x, c, value)


def close_first(fields, visc, partial, z_own, x_from_b, x_from_a, z_other, y_from_b, y_from_a,
                middle, x_b, x_a_low, x_a_high, z_both, y_terms):
    x_a = Parts(x_a_low, x_a_high)
    _, planes, rows, _ = fields.shape
    chunks = rows // ROWS
    halo = Sides(chunks, x_from_b, x_from_a, z_other, y_from_b, y_from_a)
    packed = [jnp.zeros((ROWS, LANES), jnp.float32) for _ in range(Z_TILES + 1)]
    y_faces = list(zip(*[halo.along_y(f) for f in range(NF + 1)]))

    def emit(f, x, c, tile):
        middle[f, x, ROWS * c : ROWS * c + ROWS, :] = tile
        at, lane = pair_of(f, c, planes, chunks)
        packed[at] = add_pair(packed[at], tile, lane + 2 * x)

    for side in range(2):
        for f in range(NF + 1):
            face = y_faces[side][f]
            packed[-1] = add_pair(packed[-1], face, 2 * (side * (NF + 1) + f))
            x_b[NF * chunks + side, f : f + 1, :] = facing("gx", "b", face[:1], face[planes - 1 :])
            x_a[NF * chunks + side, f : f + 1, :] = facing("gx", "a", face[:1], face[planes - 1 :])
    close(fields, visc, partial, halo, halo, y_faces, z_own, z_own, y_terms, emit)
    for at in range(z_both.shape[0]):
        z_both[at] = packed[at] if at <= Z_TILES else jnp.zeros((ROWS, LANES), jnp.float32)
    for f in range(NF):
        cut_x(f, middle.at[f], x_b, x_a)


def inside_masks():
    at = iota((1, LANES), 1) % VOL
    coords = (at // (BLK * BLK), at // BLK % BLK, at % BLK)
    along = []
    for coord in coords:
        along.append({
            -1: jnp.where(coord > 0, 1.0, 0.0),
            0: jnp.ones((1, LANES), jnp.float32),
            1: jnp.where(coord < BLK - 1, 1.0, 0.0),
        })
    return along


def move_of(tap):
    return tap[0] * BLK * BLK + tap[1] * BLK + tap[2]


def shifted(tile, tap, along):
    move = move_of(tap)
    if move == 0:
        return tile
    mask = along[0][tap[0]] * along[1][tap[1]] * along[2][tap[2]]
    return pltpu.roll(tile, (-move) % LANES, 1) * mask


def box(tile, along):
    for dimension, step in enumerate((BLK * BLK, BLK, 1)):
        ahead = pltpu.roll(tile, LANES - step, 1) * along[dimension][1]
        behind = pltpu.roll(tile, step, 1) * along[dimension][-1]
        tile = (behind + tile) + ahead
    return tile / 27.0


def sigmoid(values):
    return 1.0 / (1.0 + jnp.exp(-values))


PICKED = (0, 1, 2, 3, 0, 1, 2, 3, 0, 1, 2, 0, 0, 1, -1, -1, 0, 1, 2, 1, 2, 2, -1, -1)


def pick_rows():
    out, field = iota((32, NF * ROWS), 0), iota((32, NF * ROWS), 1) // ROWS
    table = jnp.zeros((32, NF * ROWS), jnp.float32)
    for i, f in enumerate(PICKED):
        table = jnp.where((out == i) & (field == f), 1.0, table)
    return table.astype(jnp.bfloat16)


def pick_blocks(advanced, samples, count):
    _, _, rows, lanes = advanced.shape
    along_y, along_z = rows // BLK, lanes // BLK
    row = iota((ROWS, LANES), 0)
    lane_at = iota((ROWS, LANES), 1)
    pick = pick_rows()
    out = []
    for j in range(0, count, 2):
        parts = [jnp.zeros((ROWS, LANES), jnp.float32) for _ in range(NF)]
        uppers = []
        for half in range(2):
            block = samples[j + half]
            block_x = block // (along_y * along_z)
            block_y = block // along_z % along_y
            block_z = block % along_z
            uppers.append(block_y % 2)
            start = pl.multiple_of(block_y // 2 * ROWS, ROWS)
            for x in range(BLK):
                turn = lax.rem(VOL * half + BLK * BLK * x - BLK * block_z + LANES, LANES)
                wanted = lane_at // BLK == (VOL * half + BLK * BLK * x) // BLK
                for f in range(NF):
                    tile = advanced[f, block_x * BLK + x, pl.ds(start, ROWS), :]
                    parts[f] = jnp.where(wanted, pltpu.roll(tile, turn, 1), parts[f])
        upper = jnp.where(lane_at < VOL, uppers[0], uppers[1])
        valid = row // BLK == upper
        for f in range(NF):
            for bit in (1, 2):
                moved = pltpu.roll(parts[f], BLK * bit, 1)
                parts[f] = jnp.where(row // bit % 2 == 1, moved, parts[f])
            parts[f] = jnp.where(valid, parts[f], 0.0)
        stacked = jnp.concatenate(parts, 0).astype(jnp.bfloat16)
        out.append(jnp.dot(pick, stacked, preferred_element_type=jnp.float32))
    return out


def closure(advanced, samples, trainers, loads, w_first, w_second, w_second_t, w_third,
            w_third_t, devices_all, stack_first, stack_mid, rows_out, send, slots, inline, place, leaving):
    count = len(samples)
    pairs = count // 2
    cols = [slice(LANES * m, LANES * m + LANES) for m in range(pairs)]
    along = inside_masks()
    lane_at = iota((ROWS, LANES), 1)
    row = iota((ROWS, LANES), 0)

    pos_x, pos_y, pos_z, count_y, count_z = place
    picked = pick_blocks(advanced, samples, count)
    values = [p[:ROWS] for p in picked]
    targets = []
    for p in picked:
        first, second = p[ROWS : 2 * ROWS], p[2 * ROWS : 3 * ROWS]
        targets.append(box(first * second, along) - box(first, along) * box(second, along))

    for m, tile in enumerate(values):
        for t in range(0, 28, 2):
            piece = shifted(tile, TAPS[t], along)
            later = shifted(tile, TAPS[t + 1], along) if t + 1 < 27 else jnp.zeros_like(tile)
            stack_first[BLK * t : BLK * t + ROWS, cols[m]] = jnp.where(row < NF, piece, later)
    stack_in = stack_first[...].astype(jnp.bfloat16)
    pre_first = jnp.dot(w_first, stack_in, preferred_element_type=jnp.float32)
    gate_first = sigmoid(pre_first)
    hidden_first = (pre_first * gate_first).astype(jnp.bfloat16).astype(jnp.float32)
    for m in range(pairs):
        tile = hidden_first[:, cols[m]]
        for k, tap in enumerate(TAPS):
            stack_mid[CH * k : CH * k + CH, cols[m]] = shifted(tile, tap, along).astype(jnp.bfloat16)
    leaving.start()
    pre_second = jnp.dot(w_second, stack_mid[...], preferred_element_type=jnp.float32)
    gate_second = sigmoid(pre_second)
    hidden_second = (pre_second * gate_second).astype(jnp.bfloat16)
    predicted = jnp.dot(w_third, hidden_second, preferred_element_type=jnp.float32)

    misfit = predicted[:ROWS] - jnp.concatenate(targets, 1)
    square = jnp.sum(misfit * misfit, axis=0, keepdims=True)
    sample_at = iota((ROWS, count * VOL), 1) // VOL
    mine = sample_at == iota((ROWS, count * VOL), 0)
    losses = jnp.sum(jnp.where(mine, square, 0.0), axis=1, keepdims=True) / (NOUT * VOL)
    if loads is None:
        load = jnp.full((ROWS, 1), float(count_y * CAP), jnp.float32)
    else:
        owner = jnp.zeros((ROWS, LANES), jnp.int32)
        for j in range(count):
            owner = jnp.where(row == j, trainers[j], owner)
        load = jnp.sum(jnp.where(lane_at == owner, loads, 0.0), axis=1, keepdims=True)
    share = 1.0 / (devices_all * jnp.maximum(load, 1.0))
    scale = share * (2.0 / (NOUT * VOL))
    scale_at = jnp.sum(jnp.where(mine, scale, 0.0), axis=0, keepdims=True)
    grad_pred = (misfit * scale_at).astype(jnp.bfloat16)
    grad_pred = jnp.concatenate([grad_pred, jnp.zeros_like(grad_pred)], 0)

    upper = jnp.dot(w_third_t, grad_pred, preferred_element_type=jnp.float32)
    slope = gate_second * (1.0 + pre_second * (1.0 - gate_second))
    grad_mid = (upper * slope).astype(jnp.bfloat16)
    grad_second = lax.dot_general(grad_mid, stack_mid[...], FULL, preferred_element_type=jnp.float32)
    third = jnp.concatenate([grad_pred, jnp.zeros((LANES - 16, count * VOL), jnp.bfloat16)], 0)
    grad_third = lax.dot_general(hidden_second, third, FULL, preferred_element_type=jnp.float32)

    spread = jnp.dot(w_second_t, grad_mid, preferred_element_type=jnp.float32)
    lower = []
    for m in range(pairs):
        terms = [
            shifted(spread[CH * k : CH * k + CH, cols[m]], tuple(-o for o in tap), along)
            for k, tap in enumerate(TAPS)
        ]
        lower.append(functools.reduce(jnp.add, terms))
    lower = jnp.concatenate(lower, 1)
    slope = gate_first * (1.0 + pre_first * (1.0 - gate_first))
    grad_entry = (lower * slope).astype(jnp.bfloat16)
    grad_first = lax.dot_general(grad_entry, stack_in, FULL, preferred_element_type=jnp.float32)

    whole = CH * 27 // LANES
    rest = CH * 27 - whole * LANES
    for t in range(whole):
        rows_out[:, t, :] = grad_second[:, LANES * t : LANES * t + LANES]
    mixed = jnp.concatenate([grad_second[:, whole * LANES :], jnp.zeros((CH, LANES - rest), jnp.float32)], 1)
    mixed = mixed + pltpu.roll(grad_third, rest, 1)
    tail = LANES - grad_first.shape[1]
    rows_out[:, whole + 1, :] = jnp.concatenate([grad_first, jnp.zeros((CH, tail), jnp.float32)], 1)

    offset = rest + ROWS if inline else 0
    height = CH if inline else slots.shape[0]
    slot_rows = iota((height, LANES), 0)
    slot_lanes = iota((height, LANES), 1)
    placed = jnp.zeros((height, LANES), jnp.float32)
    for j in range(count):
        name = trainers[j]
        rank = jnp.int32(0)
        for i in range(j):
            rank = rank + jnp.where(trainers[i] == name, 1, 0)
        target = (pos_x * count_y + name) * count_z + pos_z
        slot = offset + pos_y * CAP + rank
        hit = (slot_rows == target) & (slot_lanes == slot)
        placed = jnp.where(hit, losses[j : j + 1, :], placed)
    high = placed.astype(jnp.bfloat16).astype(jnp.float32)
    placed = high + pltpu.roll(placed - high, count_y * CAP, 1)
    if inline:
        mixed = mixed + placed
    else:
        slots[:, 0, :] = placed.astype(jnp.bfloat16)
    rows_out[:, whole, :] = mixed
    send[...] = rows_out[...].astype(jnp.bfloat16)


def second_step(sizes, inline, drawn, middle, visc, partial, rims, vz_own, vx_b, vx_a, vz_other, vy_b, vy_a,
                z_own, x_b, z_other, x_a_low, x_a_high, *rest):
    loads, rest = (None, rest) if sizes["gy"] * CAP == SAMP else (rest[0][...], rest[1:])
    w_first, w_second, w_second_t, w_third, w_third_t, advanced_far, send = rest[:7]
    slots = None if inline else rest[7]
    stack_first, stack_mid, rows_out, y_terms, advanced, sem = rest[-6:]
    chunks = middle.shape[2] // ROWS
    halo = Sides(chunks, x_b, Parts(x_a_low, x_a_high), z_other)
    visc_halo = Sides(chunks, vx_b, vx_a, vz_other, vy_b, vy_a)
    y_faces = rims_with_ends(rims, visc_halo, halo)
    y_faces = [face + [visc_halo.along_y(NF)[side]] for side, face in enumerate(y_faces)]
    count = stack_mid.shape[1] // VOL
    samples = [drawn[0, j] for j in range(count)]
    trainers = [drawn[1, j] for j in range(count)]

    def emit(f, x, c, tile):
        advanced[f, x, ROWS * c : ROWS * c + ROWS, :] = tile

    close(middle, visc, partial, halo, visc_halo, y_faces, z_own, vz_own, y_terms, emit)
    leaving = pltpu.make_async_copy(advanced, advanced_far, sem)
    place = (lax.axis_index("gx"), lax.axis_index("gy"), lax.axis_index("gz"), sizes["gy"], sizes["gz"])
    closure(advanced, samples, trainers, loads, w_first[...], w_second[...],
            w_second_t[...], w_third[...], w_third_t[...],
            float(sizes["gx"] * sizes["gy"] * sizes["gz"]), stack_first, stack_mid, rows_out,
            send, slots, inline, place, leaving)
    leaving.wait()


def add_up(arrived, spread, own):
    total = jnp.sum(arrived[...].astype(jnp.float32), axis=0)
    own[...] = total
    rounded = total.astype(jnp.bfloat16)
    for i in range(spread.shape[0]):
        spread[i] = rounded


def unpack(where, gathered, own, first, second, third, losses, wide):
    row, lane = where
    count = losses.shape[3]
    high = own[row : row + 1, lane : lane + count]
    losses[0, 0] = high + own[row : row + 1, lane + count : lane + 2 * count]
    wide[...] = gathered[...].astype(jnp.float32)
    whole = second.shape[1] // LANES
    rest = second.shape[1] - whole * LANES
    for t in range(whole):
        second[:, LANES * t : LANES * t + LANES] = wide[:, t, :]
    mixed = wide[:, whole, :]
    second[:, LANES * whole :] = mixed[:, :rest]
    third[...] = mixed[:, rest : rest + ROWS].T[:NOUT]
    first[...] = wide[:, whole + 1, :][:, : first.shape[1]]


def shape_of(*dims, dtype=jnp.float32):
    return jax.ShapeDtypeStruct(dims, dtype)


def swap_a(face, axis, sizes):
    return lax.ppermute(face, axis, [(i, i ^ 1) for i in range(sizes[axis])])


def swap_b(face, axis, sizes):
    count = sizes[axis]
    return lax.ppermute(face, axis, [(i, (i + (1 if i % 2 else -1)) % count) for i in range(count)])


def beside(kernel, cells, more_shapes, index, arrays):
    scratch = [pltpu.SMEM(array.shape, jnp.int32) for array in index]
    if index:
        scratch.append(pltpu.SemaphoreType.DMA((len(index),)))
    return pl.pallas_call(
        kernel,
        out_shape=[shape_of(*arrays[0].shape)] + more_shapes,
        in_specs=[ANY] * len(index) + [VMEM] * len(arrays),
        out_specs=[VMEM] * (1 + len(more_shapes)),
        scratch_shapes=scratch,
        compiler_params=PARAMS,
        cost_estimate=pl.CostEstimate(flops=120 * cells, bytes_accessed=36 * cells, transcendentals=0),
        name=kernel.__name__,
    )(*index, *arrays)


def on_device(sizes, fields, visc, samples, trainers, conv_first, conv_second, conv_third):
    _, planes, rows, lanes = fields.shape
    axes = ("gx", "gy", "gz")
    devices_all = sizes["gx"] * sizes["gy"] * sizes["gz"]
    chunks = rows // ROWS
    pairs = planes * chunks
    half = LANES // 2
    samples = samples.reshape(-1)
    trainers = trainers.reshape(-1)

    faces = pl.pallas_call(
        pack_faces,
        out_shape=[
            shape_of((NF + 1) * chunks, ROWS, lanes),
            shape_of((NF + 1) * chunks, ROWS, lanes),
            shape_of(-(-(NF + 1) * pairs // half), ROWS, LANES),
            shape_of(2 * (NF + 1), planes, lanes),
            shape_of(2 * (NF + 1), planes, lanes),
        ],
        in_specs=[HBM, HBM],
        out_specs=[VMEM] * 5,
        scratch_shapes=[
            pltpu.VMEM(fields.shape, jnp.float32),
            pltpu.VMEM(visc.shape, jnp.float32),
            pltpu.SemaphoreType.DMA((2,)),
        ],
        compiler_params=PACK,
        name="pack_faces",
    )(fields, visc)
    x_b, x_a, z_own, y_b, y_a = faces
    halo = [
        swap_b(x_b, "gx", sizes), swap_a(x_a, "gx", sizes), swap_a(z_own, "gz", sizes),
        swap_b(y_b, "gy", sizes), swap_a(y_a, "gy", sizes),
    ]

    own_counts = sizes["gy"] * CAP == SAMP
    counts = []
    if not own_counts:
        named = trainers.reshape(-1, 1) == jnp.arange(LANES, dtype=jnp.int32)[None, :]
        total = lax.psum(jnp.sum(named.astype(jnp.float32), axis=0, keepdims=True), "gy")
        counts = [jnp.broadcast_to(total, (ROWS, LANES))]
    sizes_of = [shape_of(*size, dtype=jnp.bfloat16) for size in ((CH, 28 * NF), (16, CH), (CH, 16))]
    partial, w_first, w_third, w_third_t, drawn = beside(
        interior_first, visc.size, sizes_of + [shape_of(ROWS, LANES, dtype=jnp.int32)],
        (samples, trainers), (fields, visc, conv_first, conv_third),
    )
    y_terms = pltpu.VMEM((2, NF, planes, lanes), jnp.float32)
    middle, x_b, x_a_low, x_a_high, z_later = pl.pallas_call(
        close_first,
        out_shape=[
            shape_of(*fields.shape),
            shape_of(NF * chunks + 2, ROWS, lanes),
            shape_of(NF * chunks // 2 + 1, ROWS, lanes),
            shape_of(NF * chunks // 2 + 1, ROWS, lanes),
            shape_of(NF * chunks // 2 + 2, ROWS, LANES),
        ],
        in_specs=[VMEM] * 9,
        out_specs=[VMEM] * 5,
        scratch_shapes=[y_terms],
        compiler_params=PARAMS,
        name="close_first",
    )(fields, visc, partial, z_own, *halo)
    later = [
        swap_b(x_b, "gx", sizes), swap_a(z_later, "gz", sizes),
        swap_a(x_a_low, "gx", sizes), swap_a(x_a_high, "gx", sizes),
    ]
    partial, rims, w_second_t = beside(
        interior_second, visc.size,
        [shape_of(2 * NF, ROWS, LANES), shape_of(27 * CH, CH, dtype=jnp.bfloat16)],
        (), (middle, visc, fields, *halo[3:], conv_second),
    )

    count = samples.shape[0]
    slot_total = sizes["gy"] * CAP
    tiles = -(-27 * CH // LANES) + 1
    parts = devices_all // CH
    inline = parts == 1 and slot_total <= 12
    out_shape = [shape_of(*fields.shape), shape_of(CH, tiles, LANES, dtype=jnp.bfloat16)]
    if not inline:
        out_shape.append(shape_of(devices_all, 1, LANES, dtype=jnp.bfloat16))
    advanced, send, *slots = pl.pallas_call(
        functools.partial(second_step, sizes, inline),
        out_shape=out_shape,
        in_specs=[VMEM] * (21 + len(counts)),
        out_specs=[ANY] + [VMEM] * (len(out_shape) - 1),
        scratch_shapes=[
            pltpu.VMEM((28 * NF, count * VOL), jnp.float32),
            pltpu.VMEM((27 * CH, count * VOL), jnp.bfloat16),
            pltpu.VMEM((CH, tiles, LANES), jnp.float32),
            y_terms,
            pltpu.VMEM(fields.shape, jnp.float32),
            pltpu.SemaphoreType.DMA,
        ],
        compiler_params=PARAMS,
        name="second_step",
    )(drawn, middle, visc, partial, rims, z_own, *halo, z_later, *later, *counts,
      w_first, conv_second, w_second_t, w_third, w_third_t)

    if not inline:
        send = jnp.concatenate([send.reshape(devices_all, tiles // parts, LANES), slots[0]], 1)
    arrived = lax.all_to_all(send, axes, split_axis=0, concat_axis=0, tiled=True)
    if inline:
        where = (27 * CH // LANES, 27 * CH % LANES + ROWS)
    else:
        where = (send.shape[1] - 1, 0)
    spread, own = pl.pallas_call(
        add_up,
        out_shape=[shape_of(*send.shape, dtype=jnp.bfloat16), shape_of(*send.shape[1:])],
        in_specs=[VMEM],
        out_specs=[VMEM] * 2,
        compiler_params=PARAMS,
        name="add_up",
    )(arrived)
    if not inline:
        spread = spread[:, :-1, :]
    gathered = lax.all_to_all(spread, axes, split_axis=0, concat_axis=0, tiled=True)
    first, second, third, block_losses = pl.pallas_call(
        functools.partial(unpack, where),
        out_shape=[
            shape_of(*conv_first.shape),
            shape_of(*conv_second.shape),
            shape_of(*conv_third.shape),
            shape_of(1, 1, 1, slot_total),
        ],
        in_specs=[VMEM] * 2,
        out_specs=[VMEM] * 4,
        scratch_shapes=[pltpu.VMEM((CH, tiles, LANES), jnp.float32)],
        compiler_params=PARAMS,
        name="unpack",
    )(gathered.reshape(CH, tiles, LANES), own)
    return advanced, block_losses, first, second, third


def solution(mesh):
    sizes = dict(mesh.shape)
    in_specs = (
        P(None, "gx", "gy", "gz"),
        P("gx", "gy", "gz"),
        P("gx", "gy", "gz", None),
        P("gx", "gy", "gz", None, None),
        P(),
        P(),
        P(),
    )
    out_specs = (P(None, "gx", "gy", "gz"), P("gx", "gy", "gz", None), P(), P(), P())
    return jax.shard_map(
        functools.partial(on_device, sizes), mesh=mesh, in_specs=in_specs, out_specs=out_specs,
        check_vma=False,
    )
```

```python
import functools

import jax
import jax.numpy as jnp
from jax import lax
from jax.experimental import pallas as pl
from jax.experimental.pallas import tpu as pltpu
from jax.sharding import PartitionSpec as P

BLK = 4
CAP = 2
SAMP = 8
Z_TILES = 2
NF = 4
VOL = BLK**3
TAPS = [(x, y, z) for x in (-1, 0, 1) for y in (-1, 0, 1) for z in (-1, 0, 1)]
LANES = 128
ROWS = 8
NOUT = 6
CH = 32

time_step = 0.25
buoyancy = 0.5

VMEM = pl.BlockSpec(memory_space=pltpu.VMEM)
SMEM = pl.BlockSpec(memory_space=pltpu.SMEM)
HBM = pl.BlockSpec(memory_space=pltpu.HBM)
ANY = pl.BlockSpec(memory_space=pl.ANY)
PARAMS = pltpu.CompilerParams(vmem_limit_bytes=24 * 1024 * 1024)
PACK = pltpu.CompilerParams(vmem_limit_bytes=54944 * 1024)
FULL = (((1,), (1,)), ((), ()))


def iota(shape, axis):
    return lax.broadcasted_iota(jnp.int32, shape, axis)


def odd(axis):
    return lax.axis_index(axis) % 2 == 1


def facing(axis, swap, first, last):
    return jnp.where(odd(axis), first, last) if swap == "a" else jnp.where(odd(axis), last, first)


def prev_next(axis, from_a, from_b):
    return jnp.where(odd(axis), from_a, from_b), jnp.where(odd(axis), from_b, from_a)


class Parts:
    def __init__(self, *parts):
        self.parts, self.tiles = parts, parts[0].shape[0]

    def at_tile(self, index):
        tile, rest = (index[0], index[1:]) if isinstance(index, tuple) else (index, ())
        return self.parts[tile // self.tiles], (tile % self.tiles,) + rest

    def __getitem__(self, index):
        part, place = self.at_tile(index)
        return part[place]

    def __setitem__(self, index, value):
        part, place = self.at_tile(index)
        part[place] = value


class Sides:
    def __init__(self, chunks, x_b, x_a, z_both, y_b=None, y_a=None):
        self.chunks = chunks
        self.x_a, self.x_b, self.y_a, self.y_b, self.z_both = x_a, x_b, y_a, y_b, z_both

    def along_x(self, f, c):
        tile = f * self.chunks + c
        return prev_next("gx", self.x_a[tile], self.x_b[tile])

    def along_y(self, f, depth=0):
        tile = depth * (NF + 1) + f
        return prev_next("gy", self.y_a[tile], self.y_b[tile])


def pair_of(f, c, planes, chunks):
    span = 2 * planes * chunks
    return f * span // LANES, f * span % LANES + 2 * planes * c


def add_pair(packed, tile, lane):
    moved = pltpu.roll(tile, lane + 1, 1)
    at = iota(tile.shape, 1)
    return jnp.where((at == lane) | (at == lane + 1), moved, packed)


def cut_x(f, array, x_b, x_a):
    planes, rows, _ = array.shape
    chunks = rows // ROWS
    for c in range(chunks):
        part = slice(ROWS * c, ROWS * c + ROWS)
        ends = array[0, part], array[planes - 1, part]
        x_b[f * chunks + c] = facing("gx", "b", *ends)
        x_a[f * chunks + c] = facing("gx", "a", *ends)


def pack_faces(fields_far, visc_far, x_b, x_a, z_both, y_b, y_a, fields, visc, sems):
    _, planes, rows, _ = fields.shape
    chunks = rows // ROWS
    copies = [
        pltpu.make_async_copy(fields_far, fields, sems.at[0]),
        pltpu.make_async_copy(visc_far, visc, sems.at[1]),
    ]
    for copy in copies:
        copy.start()
    arrays = [fields.at[f] for f in range(NF)] + [visc]
    packed = [jnp.zeros((ROWS, LANES), jnp.float32) for _ in range(z_both.shape[0])]
    for f, array in enumerate(arrays):
        if f == 0 or f == NF:
            copies[f // NF].wait()
        cut_x(f, array, x_b, x_a)
        for depth in range(2):
            ends = array[:, depth, :], array[:, rows - 1 - depth, :]
            y_b[depth * (NF + 1) + f] = facing("gy", "b", *ends)
            y_a[depth * (NF + 1) + f] = facing("gy", "a", *ends)
        for c in range(chunks):
            tile, lane = pair_of(f, c, planes, chunks)
            for x in range(planes):
                cells = array[x, ROWS * c : ROWS * c + ROWS]
                packed[tile] = add_pair(packed[tile], cells, lane + 2 * x)
    for tile, value in enumerate(packed):
        z_both[tile] = value


def flux(lower, upper, dimension):
    speed = 0.25 * (lower[dimension] + upper[dimension])
    mean_visc = 0.5 * (lower[NF] + upper[NF])
    return [speed * (a + b) - mean_visc * (b - a) for a, b in zip(lower[:NF], upper[:NF])]


def interior(fields, visc, partial):
    _, planes, rows, _ = fields.shape
    chunks = rows // ROWS
    end_row = iota((ROWS, LANES), 0) == ROWS - 1
    end_lane = iota((ROWS, LANES), 1) == LANES - 1
    every = range(NF + 1)

    def cell(f, x, part):
        return fields[f, x, part, :] if f < NF else visc[x, part, :]

    def plane(x, lowers):
        uppers = []
        last = x == planes - 1
        beyond = jnp.minimum(x + 1, planes - 1)
        behind = [jnp.zeros((ROWS, LANES), jnp.float32)] * NF
        for c in range(chunks):
            part = slice(ROWS * c, ROWS * c + ROWS)
            here = [cell(f, x, part) for f in every]
            after = [cell(f, beyond, part) for f in every]
            upper = flux(here, after, 0)
            upper = [jnp.where(last, 0.0, u) for u in upper]
            total = [b - a for a, b in zip(lowers[c], upper)]
            uppers.append(upper)
            above = [pltpu.roll(h, ROWS - 1, 0) for h in here]
            if c + 1 < chunks:
                first = slice(ROWS * c + ROWS, ROWS * c + ROWS + 1)
                above = [jnp.where(end_row, cell(f, x, first), above[f]) for f in every]
            upper = flux(here, above, 1)
            lower = [pltpu.roll(jnp.where(end_row, b, u), 1, 0) for b, u in zip(behind, upper)]
            if c + 1 == chunks:
                upper = [jnp.where(end_row, 0.0, u) for u in upper]
            behind = upper
            total = [t + (b - a) for t, a, b in zip(total, lower, upper)]
            right = [pltpu.roll(h, LANES - 1, 1) for h in here]
            upper = [jnp.where(end_lane, 0.0, u) for u in flux(here, right, 2)]
            lower = [pltpu.roll(u, 1, 1) for u in upper]
            total = [t + (b - a) for t, a, b in zip(total, lower, upper)]
            updated = [q - time_step * t for q, t in zip(here[:NF], total)]
            updated[2] = updated[2] + (time_step * buoyancy) * here[3]
            for f in range(NF):
                partial[f, x, part, :] = updated[f]
        return uppers

    zeros = [[jnp.zeros((ROWS, LANES), jnp.float32)] * NF for _ in range(chunks)]
    lax.fori_loop(0, planes, plane, zeros)


def rims_without_ends(fields, visc, sides, rims):
    rows = fields.shape[2]
    every = range(NF + 1)
    end_row = iota((ROWS, LANES), 0) == ROWS - 1
    end_lane = iota((ROWS, LANES), 1) == LANES - 1

    def own(row):
        return [fields[f, :, row, :] for f in range(NF)] + [visc[:, row, :]]

    for side in range(2):
        here = [sides.along_y(f)[side] for f in every]
        beyond = [sides.along_y(f, 1)[side] for f in every]
        below, above = (beyond, own(0)) if side == 0 else (own(rows - 1), beyond)
        total = [b - a for a, b in zip(flux(below, here, 1), flux(here, above, 1))]
        for dimension, axis, end in ((0, 0, end_row), (2, 1, end_lane)):
            after = [pltpu.roll(h, h.shape[axis] - 1, axis) for h in here]
            upper = [jnp.where(end, 0.0, u) for u in flux(here, after, dimension)]
            total = [t + (u - pltpu.roll(u, 1, axis)) for t, u in zip(total, upper)]
        updated = [q - time_step * t for q, t in zip(here[:NF], total)]
        updated[2] = updated[2] + (time_step * buoyancy) * here[3]
        for f in range(NF):
            rims[side * NF + f] = updated[f]


def rims_with_ends(rims, sides, later):
    row = iota((ROWS, LANES), 0)
    lane = iota((ROWS, LANES), 1)
    every = range(NF + 1)
    whole = []
    for side in range(2):
        here = [sides.along_y(f)[side] for f in every]
        tile = NF * later.chunks + side
        before, after = prev_next("gx", later.x_a[tile], later.x_b[tile])
        low = flux([before[f : f + 1] for f in every], [h[:1] for h in here], 0)
        high = flux([h[ROWS - 1 :] for h in here], [after[f : f + 1] for f in every], 0)
        columns = later.z_both[Z_TILES]
        left, right = [], []
        for f in every:
            both = pltpu.roll(columns, LANES - 1 - 2 * (side * (NF + 1) + f), 1)
            left.append(pltpu.roll(jnp.where(lane == LANES - 1, both, here[f]), 1, 1))
            right.append(pltpu.roll(jnp.where(lane == 0, both, here[f]), LANES - 1, 1))
        lower, upper = flux(left, here, 2), flux(here, right, 2)
        ends = []
        for f in range(NF):
            value = rims[side * NF + f]
            value = value + time_step * jnp.where(row == 0, low[f], 0.0)
            value = value - time_step * jnp.where(row == ROWS - 1, high[f], 0.0)
            value = value + time_step * jnp.where(lane == 0, lower[f], 0.0)
            ends.append(value - time_step * jnp.where(lane == LANES - 1, upper[f], 0.0))
        whole.append(ends)
    return whole


def interior_first(samples_far, trainers_far, fields, visc, conv_first, conv_third, partial, w_first,
                   w_third, w_third_t, drawn, samples, trainers, sems):
    copies = [
        pltpu.make_async_copy(samples_far, samples, sems.at[0]),
        pltpu.make_async_copy(trainers_far, trainers, sems.at[1]),
    ]
    for copy in copies:
        copy.start()
    interior(fields, visc, partial)
    ahead = conv_first.shape[1]
    w_first[:, :ahead] = conv_first[...]
    w_first[:, ahead:] = jnp.zeros((CH, w_first.shape[1] - ahead), jnp.bfloat16)
    third = conv_third[...].astype(jnp.float32)
    third = jnp.concatenate([third, jnp.zeros((w_third.shape[0] - NOUT, CH), jnp.float32)], 0)
    w_third[...] = third.astype(jnp.bfloat16)
    w_third_t[...] = third.T.astype(jnp.bfloat16)
    for copy in copies:
        copy.wait()
    at, row = iota((ROWS, LANES), 1), iota((ROWS, LANES), 0)
    table = jnp.zeros((ROWS, LANES), jnp.int32)
    for j in range(samples.shape[0]):
        table = jnp.where(at == j, jnp.where(row == 0, samples[j], trainers[j]), table)
    drawn[...] = table


def interior_second(middle, visc, fields, y_b, y_a, conv_second, partial, rims, w_second_t):
    interior(middle, visc, partial)
    rims_without_ends(fields, visc, Sides(0, None, None, None, y_b, y_a), rims)
    w_second_t[...] = conv_second[...].astype(jnp.float32).T.astype(jnp.bfloat16)


def z_terms(own, other, visc_own, visc_other):
    lane = iota((ROWS, LANES), 1)
    second = lane % 2 == 1
    span = LANES // 2

    def ends(mine, theirs):
        lower = jnp.where(second, pltpu.roll(theirs, 1, 1), mine)
        return lower, jnp.where(second, mine, pltpu.roll(theirs, LANES - 1, 1))

    def twice(tile):
        return jnp.where(lane < span, tile, pltpu.roll(tile, span, 1))

    pairs = [ends(a, b) for a, b in zip(own, other)]
    speed = [twice(end) for end in pairs[2 * span // LANES]]
    visc = [twice(end) for end in ends(visc_own, visc_other)]
    speed = 0.25 * (speed[0] + speed[1])
    mean_visc = 0.5 * (visc[0] + visc[1])
    through = [speed * (a + b) - mean_visc * (b - a) for a, b in pairs]
    return [jnp.where(second, time_step, -time_step) * t for t in through]


def close(fields, visc, partial, halo, visc_halo, y_faces, z_own, visc_z_own, y_terms, emit):
    _, planes, rows, _ = fields.shape
    chunks = rows // ROWS
    every = range(NF + 1)
    row = iota((ROWS, LANES), 0)
    lane_at = iota((ROWS, LANES), 1)
    ends = (lane_at == 0) | (lane_at == LANES - 1)

    def cell(f, *index):
        return fields[(f,) + index] if f < NF else visc[index]

    def sides(f):
        return halo if f < NF else visc_halo

    lower = flux(y_faces[0], [cell(f, slice(None), 0) for f in every], 1)
    upper = flux([cell(f, slice(None), rows - 1) for f in every], y_faces[1], 1)
    for f in range(NF):
        y_terms[0, f] = time_step * lower[f]
        y_terms[1, f] = -time_step * upper[f]
    tiles = 2 * NF * planes * chunks // LANES
    terms = z_terms([z_own[t] for t in range(tiles)], [halo.z_both[t] for t in range(tiles)],
                    visc_z_own[tiles], visc_halo.z_both[tiles])
    for c in range(chunks):
        part = slice(ROWS * c, ROWS * c + ROWS)
        before, after = zip(*[sides(f).along_x(f, c) for f in every])
        low = flux(before, [cell(f, 0, part) for f in every], 0)
        high = flux([cell(f, planes - 1, part) for f in every], after, 0)
        for x in range(planes):
            for f in range(NF):
                tile, lane = pair_of(f, c, planes, chunks)
                moved = pltpu.roll(terms[tile], LANES - 1 - lane - 2 * x, 1)
                value = partial[f, x, part, :] + jnp.where(ends, moved, 0.0)
                if x == 0:
                    value = value + time_step * low[f]
                if x == planes - 1:
                    value = value - time_step * high[f]
                if c == 0:
                    value = value + jnp.where(row == 0, y_terms[0, f, x : x + 1, :], 0.0)
                if c == chunks - 1:
                    value = value + jnp.where(row == ROWS - 1, y_terms[1, f, x : x + 1, :], 0.0)
                emit(f, x, c, value)


def close_first(fields, visc, partial, z_own, x_from_b, x_from_a, z_other, y_from_b, y_from_a,
                middle, x_b, x_a_low, x_a_high, z_both, y_terms):
    x_a = Parts(x_a_low, x_a_high)
    _, planes, rows, _ = fields.shape
    chunks = rows // ROWS
    halo = Sides(chunks, x_from_b, x_from_a, z_other, y_from_b, y_from_a)
    packed = [jnp.zeros((ROWS, LANES), jnp.float32) for _ in range(Z_TILES + 1)]
    y_faces = list(zip(*[halo.along_y(f) for f in range(NF + 1)]))

    def emit(f, x, c, tile):
        middle[f, x, ROWS * c : ROWS * c + ROWS, :] = tile
        at, lane = pair_of(f, c, planes, chunks)
        packed[at] = add_pair(packed[at], tile, lane + 2 * x)

    for side in range(2):
        for f in range(NF + 1):
            face = y_faces[side][f]
            packed[-1] = add_pair(packed[-1], face, 2 * (side * (NF + 1) + f))
            x_b[NF * chunks + side, f : f + 1, :] = facing("gx", "b", face[:1], face[planes - 1 :])
            x_a[NF * chunks + side, f : f + 1, :] = facing("gx", "a", face[:1], face[planes - 1 :])
    close(fields, visc, partial, halo, halo, y_faces, z_own, z_own, y_terms, emit)
    for at in range(z_both.shape[0]):
        z_both[at] = packed[at] if at <= Z_TILES else jnp.zeros((ROWS, LANES), jnp.float32)
    for f in range(NF):
        cut_x(f, middle.at[f], x_b, x_a)


def inside_masks():
    at = iota((1, LANES), 1) % VOL
    coords = (at // (BLK * BLK), at // BLK % BLK, at % BLK)
    along = []
    for coord in coords:
        along.append({
            -1: jnp.where(coord > 0, 1.0, 0.0),
            0: jnp.ones((1, LANES), jnp.float32),
            1: jnp.where(coord < BLK - 1, 1.0, 0.0),
        })
    return along


def move_of(tap):
    return tap[0] * BLK * BLK + tap[1] * BLK + tap[2]


def shifted(tile, tap, along):
    move = move_of(tap)
    if move == 0:
        return tile
    mask = along[0][tap[0]] * along[1][tap[1]] * along[2][tap[2]]
    return pltpu.roll(tile, (-move) % LANES, 1) * mask


def box(tile, along):
    for dimension, step in enumerate((BLK * BLK, BLK, 1)):
        ahead = pltpu.roll(tile, LANES - step, 1) * along[dimension][1]
        behind = pltpu.roll(tile, step, 1) * along[dimension][-1]
        tile = (behind + tile) + ahead
    return tile / 27.0


def sigmoid(values):
    return 1.0 / (1.0 + jnp.exp(-values))


PICKED = (0, 1, 2, 3, 0, 1, 2, 3, 0, 1, 2, 0, 0, 1, -1, -1, 0, 1, 2, 1, 2, 2, -1, -1)


def pick_rows():
    out, field = iota((32, NF * ROWS), 0), iota((32, NF * ROWS), 1) // ROWS
    table = jnp.zeros((32, NF * ROWS), jnp.float32)
    for i, f in enumerate(PICKED):
        table = jnp.where((out == i) & (field == f), 1.0, table)
    return table.astype(jnp.bfloat16)


def pick_blocks(advanced, samples, count):
    _, _, rows, lanes = advanced.shape
    along_y, along_z = rows // BLK, lanes // BLK
    row = iota((ROWS, LANES), 0)
    lane_at = iota((ROWS, LANES), 1)
    pick = pick_rows()
    out = []
    for j in range(0, count, 2):
        parts = [jnp.zeros((ROWS, LANES), jnp.float32) for _ in range(NF)]
        uppers = []
        for half in range(2):
            block = samples[j + half]
            block_x = block // (along_y * along_z)
            block_y = block // along_z % along_y
            block_z = block % along_z
            uppers.append(block_y % 2)
            start = pl.multiple_of(block_y // 2 * ROWS, ROWS)
            for x in range(BLK):
                turn = lax.rem(VOL * half + BLK * BLK * x - BLK * block_z + LANES, LANES)
                wanted = lane_at // BLK == (VOL * half + BLK * BLK * x) // BLK
                for f in range(NF):
                    tile = advanced[f, block_x * BLK + x, pl.ds(start, ROWS), :]
                    parts[f] = jnp.where(wanted, pltpu.roll(tile, turn, 1), parts[f])
        upper = jnp.where(lane_at < VOL, uppers[0], uppers[1])
        valid = row // BLK == upper
        for f in range(NF):
            for bit in (1, 2):
                moved = pltpu.roll(parts[f], BLK * bit, 1)
                parts[f] = jnp.where(row // bit % 2 == 1, moved, parts[f])
            parts[f] = jnp.where(valid, parts[f], 0.0)
        stacked = jnp.concatenate(parts, 0).astype(jnp.bfloat16)
        out.append(jnp.dot(pick, stacked, preferred_element_type=jnp.float32))
    return out


def closure(advanced, samples, trainers, loads, w_first, w_second, w_second_t, w_third,
            w_third_t, devices_all, stack_first, stack_mid, rows_out, send, slots, inline, place):
    count = len(samples)
    pairs = count // 2
    cols = [slice(LANES * m, LANES * m + LANES) for m in range(pairs)]
    along = inside_masks()
    lane_at = iota((ROWS, LANES), 1)
    row = iota((ROWS, LANES), 0)

    pos_x, pos_y, pos_z, count_y, count_z = place
    picked = pick_blocks(advanced, samples, count)
    values = [p[:ROWS] for p in picked]
    targets = []
    for p in picked:
        first, second = p[ROWS : 2 * ROWS], p[2 * ROWS : 3 * ROWS]
        targets.append(box(first * second, along) - box(first, along) * box(second, along))

    for m, tile in enumerate(values):
        for t in range(0, 28, 2):
            piece = shifted(tile, TAPS[t], along)
            later = shifted(tile, TAPS[t + 1], along) if t + 1 < 27 else jnp.zeros_like(tile)
            stack_first[BLK * t : BLK * t + ROWS, cols[m]] = jnp.where(row < NF, piece, later)
    stack_in = stack_first[...].astype(jnp.bfloat16)
    pre_first = jnp.dot(w_first, stack_in, preferred_element_type=jnp.float32)
    gate_first = sigmoid(pre_first)
    hidden_first = (pre_first * gate_first).astype(jnp.bfloat16).astype(jnp.float32)
    for m in range(pairs):
        tile = hidden_first[:, cols[m]]
        for k, tap in enumerate(TAPS):
            stack_mid[CH * k : CH * k + CH, cols[m]] = shifted(tile, tap, along).astype(jnp.bfloat16)
    pre_second = jnp.dot(w_second, stack_mid[...], preferred_element_type=jnp.float32)
    gate_second = sigmoid(pre_second)
    hidden_second = (pre_second * gate_second).astype(jnp.bfloat16)
    predicted = jnp.dot(w_third, hidden_second, preferred_element_type=jnp.float32)

    misfit = predicted[:ROWS] - jnp.concatenate(targets, 1)
    square = jnp.sum(misfit * misfit, axis=0, keepdims=True)
    sample_at = iota((ROWS, count * VOL), 1) // VOL
    mine = sample_at == iota((ROWS, count * VOL), 0)
    losses = jnp.sum(jnp.where(mine, square, 0.0), axis=1, keepdims=True) / (NOUT * VOL)
    if loads is None:
        load = jnp.full((ROWS, 1), float(count_y * CAP), jnp.float32)
    else:
        owner = jnp.zeros((ROWS, LANES), jnp.int32)
        for j in range(count):
            owner = jnp.where(row == j, trainers[j], owner)
        load = jnp.sum(jnp.where(lane_at == owner, loads, 0.0), axis=1, keepdims=True)
    share = 1.0 / (devices_all * jnp.maximum(load, 1.0))
    scale = share * (2.0 / (NOUT * VOL))
    scale_at = jnp.sum(jnp.where(mine, scale, 0.0), axis=0, keepdims=True)
    grad_pred = (misfit * scale_at).astype(jnp.bfloat16)
    grad_pred = jnp.concatenate([grad_pred, jnp.zeros_like(grad_pred)], 0)

    upper = jnp.dot(w_third_t, grad_pred, preferred_element_type=jnp.float32)
    slope = gate_second * (1.0 + pre_second * (1.0 - gate_second))
    grad_mid = (upper * slope).astype(jnp.bfloat16)
    grad_second = lax.dot_general(grad_mid, stack_mid[...], FULL, preferred_element_type=jnp.float32)
    third = jnp.concatenate([grad_pred, jnp.zeros((LANES - 16, count * VOL), jnp.bfloat16)], 0)
    grad_third = lax.dot_general(hidden_second, third, FULL, preferred_element_type=jnp.float32)

    spread = jnp.dot(w_second_t, grad_mid, preferred_element_type=jnp.float32)
    lower = []
    for m in range(pairs):
        terms = [
            shifted(spread[CH * k : CH * k + CH, cols[m]], tuple(-o for o in tap), along)
            for k, tap in enumerate(TAPS)
        ]
        lower.append(functools.reduce(jnp.add, terms))
    lower = jnp.concatenate(lower, 1)
    slope = gate_first * (1.0 + pre_first * (1.0 - gate_first))
    grad_entry = (lower * slope).astype(jnp.bfloat16)
    grad_first = lax.dot_general(grad_entry, stack_in, FULL, preferred_element_type=jnp.float32)

    whole = CH * 27 // LANES
    rest = CH * 27 - whole * LANES
    for t in range(whole):
        rows_out[:, t, :] = grad_second[:, LANES * t : LANES * t + LANES]
    mixed = jnp.concatenate([grad_second[:, whole * LANES :], jnp.zeros((CH, LANES - rest), jnp.float32)], 1)
    mixed = mixed + pltpu.roll(grad_third, rest, 1)
    tail = LANES - grad_first.shape[1]
    rows_out[:, whole + 1, :] = jnp.concatenate([grad_first, jnp.zeros((CH, tail), jnp.float32)], 1)

    offset = rest + ROWS if inline else 0
    height = CH if inline else slots.shape[0]
    slot_rows = iota((height, LANES), 0)
    slot_lanes = iota((height, LANES), 1)
    placed = jnp.zeros((height, LANES), jnp.float32)
    for j in range(count):
        name = trainers[j]
        rank = jnp.int32(0)
        for i in range(j):
            rank = rank + jnp.where(trainers[i] == name, 1, 0)
        target = (pos_x * count_y + name) * count_z + pos_z
        slot = offset + pos_y * CAP + rank
        hit = (slot_rows == target) & (slot_lanes == slot)
        placed = jnp.where(hit, losses[j : j + 1, :], placed)
    high = placed.astype(jnp.bfloat16).astype(jnp.float32)
    placed = high + pltpu.roll(placed - high, count_y * CAP, 1)
    if inline:
        mixed = mixed + placed
    else:
        slots[:, 0, :] = placed.astype(jnp.bfloat16)
    rows_out[:, whole, :] = mixed
    send[...] = rows_out[...].astype(jnp.bfloat16)


def second_step(sizes, inline, drawn, middle, visc, partial, rims, vz_own, vx_b, vx_a, vz_other, vy_b, vy_a,
                z_own, x_b, z_other, x_a_low, x_a_high, *rest):
    loads, rest = (None, rest) if sizes["gy"] * CAP == SAMP else (rest[0][...], rest[1:])
    w_first, w_second, w_second_t, w_third, w_third_t, advanced, send = rest[:7]
    slots = None if inline else rest[7]
    stack_first, stack_mid, rows_out, y_terms = rest[-4:]
    chunks = middle.shape[2] // ROWS
    halo = Sides(chunks, x_b, Parts(x_a_low, x_a_high), z_other)
    visc_halo = Sides(chunks, vx_b, vx_a, vz_other, vy_b, vy_a)
    y_faces = rims_with_ends(rims, visc_halo, halo)
    y_faces = [face + [visc_halo.along_y(NF)[side]] for side, face in enumerate(y_faces)]
    count = stack_mid.shape[1] // VOL
    samples = [drawn[0, j] for j in range(count)]
    trainers = [drawn[1, j] for j in range(count)]

    def emit(f, x, c, tile):
        advanced[f, x, ROWS * c : ROWS * c + ROWS, :] = tile

    close(middle, visc, partial, halo, visc_halo, y_faces, z_own, vz_own, y_terms, emit)
    place = (lax.axis_index("gx"), lax.axis_index("gy"), lax.axis_index("gz"), sizes["gy"], sizes["gz"])
    closure(advanced, samples, trainers, loads, w_first[...], w_second[...],
            w_second_t[...], w_third[...], w_third_t[...],
            float(sizes["gx"] * sizes["gy"] * sizes["gz"]), stack_first, stack_mid, rows_out,
            send, slots, inline, place)


def write_out(kept, advanced, sem):
    copy = pltpu.make_async_copy(kept, advanced, sem)
    copy.start()
    copy.wait()


def add_up(arrived, spread, own):
    total = jnp.sum(arrived[...].astype(jnp.float32), axis=0)
    own[...] = total
    rounded = total.astype(jnp.bfloat16)
    for i in range(spread.shape[0]):
        spread[i] = rounded


def unpack(where, gathered, own, first, second, third, losses, wide):
    row, lane = where
    count = losses.shape[3]
    high = own[row : row + 1, lane : lane + count]
    losses[0, 0] = high + own[row : row + 1, lane + count : lane + 2 * count]
    wide[...] = gathered[...].astype(jnp.float32)
    whole = second.shape[1] // LANES
    rest = second.shape[1] - whole * LANES
    for t in range(whole):
        second[:, LANES * t : LANES * t + LANES] = wide[:, t, :]
    mixed = wide[:, whole, :]
    second[:, LANES * whole :] = mixed[:, :rest]
    third[...] = mixed[:, rest : rest + ROWS].T[:NOUT]
    first[...] = wide[:, whole + 1, :][:, : first.shape[1]]


def shape_of(*dims, dtype=jnp.float32):
    return jax.ShapeDtypeStruct(dims, dtype)


def swap_a(face, axis, sizes):
    return lax.ppermute(face, axis, [(i, i ^ 1) for i in range(sizes[axis])])


def swap_b(face, axis, sizes):
    count = sizes[axis]
    return lax.ppermute(face, axis, [(i, (i + (1 if i % 2 else -1)) % count) for i in range(count)])


def beside(kernel, cells, more_shapes, index, arrays):
    scratch = [pltpu.SMEM(array.shape, jnp.int32) for array in index]
    if index:
        scratch.append(pltpu.SemaphoreType.DMA((len(index),)))
    return pl.pallas_call(
        kernel,
        out_shape=[shape_of(*arrays[0].shape)] + more_shapes,
        in_specs=[ANY] * len(index) + [VMEM] * len(arrays),
        out_specs=[VMEM] * (1 + len(more_shapes)),
        scratch_shapes=scratch,
        compiler_params=PARAMS,
        cost_estimate=pl.CostEstimate(flops=120 * cells, bytes_accessed=36 * cells, transcendentals=0),
        name=kernel.__name__,
    )(*index, *arrays)


def on_device(sizes, fields, visc, samples, trainers, conv_first, conv_second, conv_third):
    _, planes, rows, lanes = fields.shape
    axes = ("gx", "gy", "gz")
    devices_all = sizes["gx"] * sizes["gy"] * sizes["gz"]
    chunks = rows // ROWS
    pairs = planes * chunks
    half = LANES // 2
    samples = samples.reshape(-1)
    trainers = trainers.reshape(-1)

    faces = pl.pallas_call(
        pack_faces,
        out_shape=[
            shape_of((NF + 1) * chunks, ROWS, lanes),
            shape_of((NF + 1) * chunks, ROWS, lanes),
            shape_of(-(-(NF + 1) * pairs // half), ROWS, LANES),
            shape_of(2 * (NF + 1), planes, lanes),
            shape_of(2 * (NF + 1), planes, lanes),
        ],
        in_specs=[HBM, HBM],
        out_specs=[VMEM] * 5,
        scratch_shapes=[
            pltpu.VMEM(fields.shape, jnp.float32),
            pltpu.VMEM(visc.shape, jnp.float32),
            pltpu.SemaphoreType.DMA((2,)),
        ],
        compiler_params=PACK,
        name="pack_faces",
    )(fields, visc)
    x_b, x_a, z_own, y_b, y_a = faces
    halo = [
        swap_b(x_b, "gx", sizes), swap_a(x_a, "gx", sizes), swap_a(z_own, "gz", sizes),
        swap_b(y_b, "gy", sizes), swap_a(y_a, "gy", sizes),
    ]

    own_counts = sizes["gy"] * CAP == SAMP
    counts = []
    if not own_counts:
        named = trainers.reshape(-1, 1) == jnp.arange(LANES, dtype=jnp.int32)[None, :]
        total = lax.psum(jnp.sum(named.astype(jnp.float32), axis=0, keepdims=True), "gy")
        counts = [jnp.broadcast_to(total, (ROWS, LANES))]
    sizes_of = [shape_of(*size, dtype=jnp.bfloat16) for size in ((CH, 28 * NF), (16, CH), (CH, 16))]
    partial, w_first, w_third, w_third_t, drawn = beside(
        interior_first, visc.size, sizes_of + [shape_of(ROWS, LANES, dtype=jnp.int32)],
        (samples, trainers), (fields, visc, conv_first, conv_third),
    )
    y_terms = pltpu.VMEM((2, NF, planes, lanes), jnp.float32)
    middle, x_b, x_a_low, x_a_high, z_later = pl.pallas_call(
        close_first,
        out_shape=[
            shape_of(*fields.shape),
            shape_of(NF * chunks + 2, ROWS, lanes),
            shape_of(NF * chunks // 2 + 1, ROWS, lanes),
            shape_of(NF * chunks // 2 + 1, ROWS, lanes),
            shape_of(NF * chunks // 2 + 2, ROWS, LANES),
        ],
        in_specs=[VMEM] * 9,
        out_specs=[VMEM] * 5,
        scratch_shapes=[y_terms],
        compiler_params=PARAMS,
        name="close_first",
    )(fields, visc, partial, z_own, *halo)
    later = [
        swap_b(x_b, "gx", sizes), swap_a(z_later, "gz", sizes),
        swap_a(x_a_low, "gx", sizes), swap_a(x_a_high, "gx", sizes),
    ]
    partial, rims, w_second_t = beside(
        interior_second, visc.size,
        [shape_of(2 * NF, ROWS, LANES), shape_of(27 * CH, CH, dtype=jnp.bfloat16)],
        (), (middle, visc, fields, *halo[3:], conv_second),
    )

    count = samples.shape[0]
    slot_total = sizes["gy"] * CAP
    tiles = -(-27 * CH // LANES) + 1
    parts = devices_all // CH
    inline = parts == 1 and slot_total <= 12
    out_shape = [shape_of(*fields.shape), shape_of(CH, tiles, LANES, dtype=jnp.bfloat16)]
    if not inline:
        out_shape.append(shape_of(devices_all, 1, LANES, dtype=jnp.bfloat16))
    kept, send, *slots = pl.pallas_call(
        functools.partial(second_step, sizes, inline),
        out_shape=out_shape,
        in_specs=[VMEM] * (21 + len(counts)),
        out_specs=[VMEM] * len(out_shape),
        scratch_shapes=[
            pltpu.VMEM((28 * NF, count * VOL), jnp.float32),
            pltpu.VMEM((27 * CH, count * VOL), jnp.bfloat16),
            pltpu.VMEM((CH, tiles, LANES), jnp.float32),
            y_terms,
        ],
        compiler_params=PARAMS,
        name="second_step",
    )(drawn, middle, visc, partial, rims, z_own, *halo, z_later, *later, *counts,
      w_first, conv_second, w_second_t, w_third, w_third_t)

    if not inline:
        send = jnp.concatenate([send.reshape(devices_all, tiles // parts, LANES), slots[0]], 1)
    advanced = pl.pallas_call(
        write_out,
        out_shape=shape_of(*fields.shape),
        in_specs=[ANY],
        out_specs=ANY,
        scratch_shapes=[pltpu.SemaphoreType.DMA],
        compiler_params=PARAMS,
        cost_estimate=pl.CostEstimate(flops=0, bytes_accessed=8 * fields.size, transcendentals=0),
        name="write_out",
    )(kept)
    arrived = lax.all_to_all(send, axes, split_axis=0, concat_axis=0, tiled=True)
    if inline:
        where = (27 * CH // LANES, 27 * CH % LANES + ROWS)
    else:
        where = (send.shape[1] - 1, 0)
    spread, own = pl.pallas_call(
        add_up,
        out_shape=[shape_of(*send.shape, dtype=jnp.bfloat16), shape_of(*send.shape[1:])],
        in_specs=[VMEM],
        out_specs=[VMEM] * 2,
        compiler_params=PARAMS,
        name="add_up",
    )(arrived)
    if not inline:
        spread = spread[:, :-1, :]
    gathered = lax.all_to_all(spread, axes, split_axis=0, concat_axis=0, tiled=True)
    first, second, third, block_losses = pl.pallas_call(
        functools.partial(unpack, where),
        out_shape=[
            shape_of(*conv_first.shape),
            shape_of(*conv_second.shape),
            shape_of(*conv_third.shape),
            shape_of(1, 1, 1, slot_total),
        ],
        in_specs=[VMEM] * 2,
        out_specs=[VMEM] * 4,
        scratch_shapes=[pltpu.VMEM((CH, tiles, LANES), jnp.float32)],
        compiler_params=PARAMS,
        name="unpack",
    )(gathered.reshape(CH, tiles, LANES), own)
    return advanced, block_losses, first, second, third


def solution(mesh):
    sizes = dict(mesh.shape)
    in_specs = (
        P(None, "gx", "gy", "gz"),
        P("gx", "gy", "gz"),
        P("gx", "gy", "gz", None),
        P("gx", "gy", "gz", None, None),
        P(),
        P(),
        P(),
    )
    out_specs = (P(None, "gx", "gy", "gz"), P("gx", "gy", "gz", None), P(), P(), P())
    return jax.shard_map(
        functools.partial(on_device, sizes), mesh=mesh, in_specs=in_specs, out_specs=out_specs,
        check_vma=False,
    )
```

```python
import functools

import jax
import jax.numpy as jnp
from jax import lax
from jax.experimental import pallas as pl
from jax.experimental.pallas import tpu as pltpu
from jax.sharding import PartitionSpec as P

BLK = 4
CAP = 2
SAMP = 8
Z_TILES = 2
NF = 4
VOL = BLK**3
TAPS = [(x, y, z) for x in (-1, 0, 1) for y in (-1, 0, 1) for z in (-1, 0, 1)]
LANES = 128
ROWS = 8
NOUT = 6
CH = 32

time_step = 0.25
buoyancy = 0.5

VMEM = pl.BlockSpec(memory_space=pltpu.VMEM)
SMEM = pl.BlockSpec(memory_space=pltpu.SMEM)
HBM = pl.BlockSpec(memory_space=pltpu.HBM)
ANY = pl.BlockSpec(memory_space=pl.ANY)
PARAMS = pltpu.CompilerParams(vmem_limit_bytes=24 * 1024 * 1024)
PACK = pltpu.CompilerParams(vmem_limit_bytes=54944 * 1024)
FULL = (((1,), (1,)), ((), ()))


def iota(shape, axis):
    return lax.broadcasted_iota(jnp.int32, shape, axis)


def odd(axis):
    return lax.axis_index(axis) % 2 == 1


def facing(axis, swap, first, last):
    return jnp.where(odd(axis), first, last) if swap == "a" else jnp.where(odd(axis), last, first)


def prev_next(axis, from_a, from_b):
    return jnp.where(odd(axis), from_a, from_b), jnp.where(odd(axis), from_b, from_a)


class Parts:
    def __init__(self, *parts):
        self.parts, self.tiles = parts, parts[0].shape[0]

    def at_tile(self, index):
        tile, rest = (index[0], index[1:]) if isinstance(index, tuple) else (index, ())
        return self.parts[tile // self.tiles], (tile % self.tiles,) + rest

    def __getitem__(self, index):
        part, place = self.at_tile(index)
        return part[place]

    def __setitem__(self, index, value):
        part, place = self.at_tile(index)
        part[place] = value


class Sides:
    def __init__(self, chunks, x_b, x_a, z_both, y_b=None, y_a=None):
        self.chunks = chunks
        self.x_a, self.x_b, self.y_a, self.y_b, self.z_both = x_a, x_b, y_a, y_b, z_both

    def along_x(self, f, c):
        tile = f * self.chunks + c
        return prev_next("gx", self.x_a[tile], self.x_b[tile])

    def along_y(self, f, depth=0):
        tile = depth * (NF + 1) + f
        return prev_next("gy", self.y_a[tile], self.y_b[tile])


def pair_of(f, c, planes, chunks):
    span = 2 * planes * chunks
    return f * span // LANES, f * span % LANES + 2 * planes * c


def add_pair(packed, tile, lane):
    moved = pltpu.roll(tile, lane + 1, 1)
    at = iota(tile.shape, 1)
    return jnp.where((at == lane) | (at == lane + 1), moved, packed)


def cut_x(f, array, x_b, x_a):
    planes, rows, _ = array.shape
    chunks = rows // ROWS
    for c in range(chunks):
        part = slice(ROWS * c, ROWS * c + ROWS)
        ends = array[0, part], array[planes - 1, part]
        x_b[f * chunks + c] = facing("gx", "b", *ends)
        x_a[f * chunks + c] = facing("gx", "a", *ends)


def pack_faces(fields_far, visc_far, x_b, x_a, z_both, y_b, y_a, fields, visc, sems):
    _, planes, rows, _ = fields.shape
    chunks = rows // ROWS
    copies = [
        pltpu.make_async_copy(fields_far, fields, sems.at[0]),
        pltpu.make_async_copy(visc_far, visc, sems.at[1]),
    ]
    for copy in copies:
        copy.start()
    arrays = [fields.at[f] for f in range(NF)] + [visc]
    packed = [jnp.zeros((ROWS, LANES), jnp.float32) for _ in range(z_both.shape[0])]
    for f, array in enumerate(arrays):
        if f == 0 or f == NF:
            copies[f // NF].wait()
        cut_x(f, array, x_b, x_a)
        for depth in range(2):
            ends = array[:, depth, :], array[:, rows - 1 - depth, :]
            y_b[depth * (NF + 1) + f] = facing("gy", "b", *ends)
            y_a[depth * (NF + 1) + f] = facing("gy", "a", *ends)
        for c in range(chunks):
            tile, lane = pair_of(f, c, planes, chunks)
            for x in range(planes):
                cells = array[x, ROWS * c : ROWS * c + ROWS]
                packed[tile] = add_pair(packed[tile], cells, lane + 2 * x)
    for tile, value in enumerate(packed):
        z_both[tile] = value


def flux(lower, upper, dimension):
    speed = 0.25 * (lower[dimension] + upper[dimension])
    mean_visc = 0.5 * (lower[NF] + upper[NF])
    return [speed * (a + b) - mean_visc * (b - a) for a, b in zip(lower[:NF], upper[:NF])]


def interior(fields, visc, partial):
    _, planes, rows, _ = fields.shape
    chunks = rows // ROWS
    end_row = iota((ROWS, LANES), 0) == ROWS - 1
    end_lane = iota((ROWS, LANES), 1) == LANES - 1
    every = range(NF + 1)

    def cell(f, x, part):
        return fields[f, x, part, :] if f < NF else visc[x, part, :]

    def plane(x, lowers):
        uppers = []
        last = x == planes - 1
        beyond = jnp.minimum(x + 1, planes - 1)
        behind = [jnp.zeros((ROWS, LANES), jnp.float32)] * NF
        for c in range(chunks):
            part = slice(ROWS * c, ROWS * c + ROWS)
            here = [cell(f, x, part) for f in every]
            after = [cell(f, beyond, part) for f in every]
            upper = flux(here, after, 0)
            upper = [jnp.where(last, 0.0, u) for u in upper]
            total = [b - a for a, b in zip(lowers[c], upper)]
            uppers.append(upper)
            above = [pltpu.roll(h, ROWS - 1, 0) for h in here]
            if c + 1 < chunks:
                first = slice(ROWS * c + ROWS, ROWS * c + ROWS + 1)
                above = [jnp.where(end_row, cell(f, x, first), above[f]) for f in every]
            upper = flux(here, above, 1)
            lower = [pltpu.roll(jnp.where(end_row, b, u), 1, 0) for b, u in zip(behind, upper)]
            if c + 1 == chunks:
                upper = [jnp.where(end_row, 0.0, u) for u in upper]
            behind = upper
            total = [t + (b - a) for t, a, b in zip(total, lower, upper)]
            right = [pltpu.roll(h, LANES - 1, 1) for h in here]
            upper = [jnp.where(end_lane, 0.0, u) for u in flux(here, right, 2)]
            lower = [pltpu.roll(u, 1, 1) for u in upper]
            total = [t + (b - a) for t, a, b in zip(total, lower, upper)]
            updated = [q - time_step * t for q, t in zip(here[:NF], total)]
            updated[2] = updated[2] + (time_step * buoyancy) * here[3]
            for f in range(NF):
                partial[f, x, part, :] = updated[f]
        return uppers

    zeros = [[jnp.zeros((ROWS, LANES), jnp.float32)] * NF for _ in range(chunks)]
    lax.fori_loop(0, planes, plane, zeros)


def rims_without_ends(fields, visc, sides, rims):
    rows = fields.shape[2]
    every = range(NF + 1)
    end_row = iota((ROWS, LANES), 0) == ROWS - 1
    end_lane = iota((ROWS, LANES), 1) == LANES - 1

    def own(row):
        return [fields[f, :, row, :] for f in range(NF)] + [visc[:, row, :]]

    for side in range(2):
        here = [sides.along_y(f)[side] for f in every]
        beyond = [sides.along_y(f, 1)[side] for f in every]
        below, above = (beyond, own(0)) if side == 0 else (own(rows - 1), beyond)
        total = [b - a for a, b in zip(flux(below, here, 1), flux(here, above, 1))]
        for dimension, axis, end in ((0, 0, end_row), (2, 1, end_lane)):
            after = [pltpu.roll(h, h.shape[axis] - 1, axis) for h in here]
            upper = [jnp.where(end, 0.0, u) for u in flux(here, after, dimension)]
            total = [t + (u - pltpu.roll(u, 1, axis)) for t, u in zip(total, upper)]
        updated = [q - time_step * t for q, t in zip(here[:NF], total)]
        updated[2] = updated[2] + (time_step * buoyancy) * here[3]
        for f in range(NF):
            rims[side * NF + f] = updated[f]


def rims_with_ends(rims, sides, later):
    row = iota((ROWS, LANES), 0)
    lane = iota((ROWS, LANES), 1)
    every = range(NF + 1)
    whole = []
    for side in range(2):
        here = [sides.along_y(f)[side] for f in every]
        tile = NF * later.chunks + side
        before, after = prev_next("gx", later.x_a[tile], later.x_b[tile])
        low = flux([before[f : f + 1] for f in every], [h[:1] for h in here], 0)
        high = flux([h[ROWS - 1 :] for h in here], [after[f : f + 1] for f in every], 0)
        columns = later.z_both[Z_TILES]
        left, right = [], []
        for f in every:
            both = pltpu.roll(columns, LANES - 1 - 2 * (side * (NF + 1) + f), 1)
            left.append(pltpu.roll(jnp.where(lane == LANES - 1, both, here[f]), 1, 1))
            right.append(pltpu.roll(jnp.where(lane == 0, both, here[f]), LANES - 1, 1))
        lower, upper = flux(left, here, 2), flux(here, right, 2)
        ends = []
        for f in range(NF):
            value = rims[side * NF + f]
            value = value + time_step * jnp.where(row == 0, low[f], 0.0)
            value = value - time_step * jnp.where(row == ROWS - 1, high[f], 0.0)
            value = value + time_step * jnp.where(lane == 0, lower[f], 0.0)
            ends.append(value - time_step * jnp.where(lane == LANES - 1, upper[f], 0.0))
        whole.append(ends)
    return whole


def interior_first(samples_far, trainers_far, fields, visc, conv_first, conv_third, partial, w_first,
                   w_third, w_third_t, drawn, samples, trainers, sems):
    copies = [
        pltpu.make_async_copy(samples_far, samples, sems.at[0]),
        pltpu.make_async_copy(trainers_far, trainers, sems.at[1]),
    ]
    for copy in copies:
        copy.start()
    interior(fields, visc, partial)
    ahead = conv_first.shape[1]
    w_first[:, :ahead] = conv_first[...]
    w_first[:, ahead:] = jnp.zeros((CH, w_first.shape[1] - ahead), jnp.bfloat16)
    third = conv_third[...].astype(jnp.float32)
    third = jnp.concatenate([third, jnp.zeros((w_third.shape[0] - NOUT, CH), jnp.float32)], 0)
    w_third[...] = third.astype(jnp.bfloat16)
    w_third_t[...] = third.T.astype(jnp.bfloat16)
    for copy in copies:
        copy.wait()
    at, row = iota((ROWS, LANES), 1), iota((ROWS, LANES), 0)
    table = jnp.zeros((ROWS, LANES), jnp.int32)
    for j in range(samples.shape[0]):
        table = jnp.where(at == j, jnp.where(row == 0, samples[j], trainers[j]), table)
    drawn[...] = table


def interior_second(middle, visc, fields, y_b, y_a, conv_second, partial, rims, w_second_t):
    interior(middle, visc, partial)
    rims_without_ends(fields, visc, Sides(0, None, None, None, y_b, y_a), rims)
    w_second_t[...] = conv_second[...].astype(jnp.float32).T.astype(jnp.bfloat16)


def z_terms(own, other, visc_own, visc_other):
    lane = iota((ROWS, LANES), 1)
    second = lane % 2 == 1
    span = LANES // 2

    def ends(mine, theirs):
        lower = jnp.where(second, pltpu.roll(theirs, 1, 1), mine)
        return lower, jnp.where(second, mine, pltpu.roll(theirs, LANES - 1, 1))

    def twice(tile):
        return jnp.where(lane < span, tile, pltpu.roll(tile, span, 1))

    pairs = [ends(a, b) for a, b in zip(own, other)]
    speed = [twice(end) for end in pairs[2 * span // LANES]]
    visc = [twice(end) for end in ends(visc_own, visc_other)]
    speed = 0.25 * (speed[0] + speed[1])
    mean_visc = 0.5 * (visc[0] + visc[1])
    through = [speed * (a + b) - mean_visc * (b - a) for a, b in pairs]
    return [jnp.where(second, time_step, -time_step) * t for t in through]


def close(fields, visc, partial, halo, visc_halo, y_faces, z_own, visc_z_own, y_terms, emit):
    _, planes, rows, _ = fields.shape
    chunks = rows // ROWS
    every = range(NF + 1)
    row = iota((ROWS, LANES), 0)
    lane_at = iota((ROWS, LANES), 1)
    ends = (lane_at == 0) | (lane_at == LANES - 1)

    def cell(f, *index):
        return fields[(f,) + index] if f < NF else visc[index]

    def sides(f):
        return halo if f < NF else visc_halo

    lower = flux(y_faces[0], [cell(f, slice(None), 0) for f in every], 1)
    upper = flux([cell(f, slice(None), rows - 1) for f in every], y_faces[1], 1)
    for f in range(NF):
        y_terms[0, f] = time_step * lower[f]
        y_terms[1, f] = -time_step * upper[f]
    tiles = 2 * NF * planes * chunks // LANES
    terms = z_terms([z_own[t] for t in range(tiles)], [halo.z_both[t] for t in range(tiles)],
                    visc_z_own[tiles], visc_halo.z_both[tiles])
    for c in range(chunks):
        part = slice(ROWS * c, ROWS * c + ROWS)
        before, after = zip(*[sides(f).along_x(f, c) for f in every])
        low = flux(before, [cell(f, 0, part) for f in every], 0)
        high = flux([cell(f, planes - 1, part) for f in every], after, 0)
        for x in range(planes):
            for f in range(NF):
                tile, lane = pair_of(f, c, planes, chunks)
                moved = pltpu.roll(terms[tile], LANES - 1 - lane - 2 * x, 1)
                value = partial[f, x, part, :] + jnp.where(ends, moved, 0.0)
                if x == 0:
                    value = value + time_step * low[f]
                if x == planes - 1:
                    value = value - time_step * high[f]
                if c == 0:
                    value = value + jnp.where(row == 0, y_terms[0, f, x : x + 1, :], 0.0)
                if c == chunks - 1:
                    value = value + jnp.where(row == ROWS - 1, y_terms[1, f, x : x + 1, :], 0.0)
                emit(f, x, c, value)


def close_first(fields, visc, partial, z_own, x_from_b, x_from_a, z_other, y_from_b, y_from_a,
                middle, x_b, x_a_low, x_a_high, z_both, y_terms):
    x_a = Parts(x_a_low, x_a_high)
    _, planes, rows, _ = fields.shape
    chunks = rows // ROWS
    halo = Sides(chunks, x_from_b, x_from_a, z_other, y_from_b, y_from_a)
    packed = [jnp.zeros((ROWS, LANES), jnp.float32) for _ in range(Z_TILES + 1)]
    y_faces = list(zip(*[halo.along_y(f) for f in range(NF + 1)]))

    def emit(f, x, c, tile):
        middle[f, x, ROWS * c : ROWS * c + ROWS, :] = tile
        at, lane = pair_of(f, c, planes, chunks)
        packed[at] = add_pair(packed[at], tile, lane + 2 * x)

    for side in range(2):
        for f in range(NF + 1):
            face = y_faces[side][f]
            packed[-1] = add_pair(packed[-1], face, 2 * (side * (NF + 1) + f))
            x_b[NF * chunks + side, f : f + 1, :] = facing("gx", "b", face[:1], face[planes - 1 :])
            x_a[NF * chunks + side, f : f + 1, :] = facing("gx", "a", face[:1], face[planes - 1 :])
    close(fields, visc, partial, halo, halo, y_faces, z_own, z_own, y_terms, emit)
    for at in range(z_both.shape[0]):
        z_both[at] = packed[at] if at <= Z_TILES else jnp.zeros((ROWS, LANES), jnp.float32)
    for f in range(NF):
        cut_x(f, middle.at[f], x_b, x_a)


def inside_masks():
    at = iota((1, LANES), 1) % VOL
    coords = (at // (BLK * BLK), at // BLK % BLK, at % BLK)
    along = []
    for coord in coords:
        along.append({
            -1: jnp.where(coord > 0, 1.0, 0.0),
            0: jnp.ones((1, LANES), jnp.float32),
            1: jnp.where(coord < BLK - 1, 1.0, 0.0),
        })
    return along


def move_of(tap):
    return tap[0] * BLK * BLK + tap[1] * BLK + tap[2]


def shifted(tile, tap, along):
    move = move_of(tap)
    if move == 0:
        return tile
    mask = along[0][tap[0]] * along[1][tap[1]] * along[2][tap[2]]
    return pltpu.roll(tile, (-move) % LANES, 1) * mask


def box(tile, along):
    for dimension, step in enumerate((BLK * BLK, BLK, 1)):
        ahead = pltpu.roll(tile, LANES - step, 1) * along[dimension][1]
        behind = pltpu.roll(tile, step, 1) * along[dimension][-1]
        tile = (behind + tile) + ahead
    return tile / 27.0


def sigmoid(values):
    return 1.0 / (1.0 + jnp.exp(-values))


PICKED = (0, 1, 2, 3, 0, 1, 2, 3, 0, 1, 2, 0, 0, 1, -1, -1, 0, 1, 2, 1, 2, 2, -1, -1)


def pick_rows():
    out, field = iota((32, NF * ROWS), 0), iota((32, NF * ROWS), 1) // ROWS
    table = jnp.zeros((32, NF * ROWS), jnp.float32)
    for i, f in enumerate(PICKED):
        table = jnp.where((out == i) & (field == f), 1.0, table)
    return table.astype(jnp.bfloat16)


def pick_blocks(advanced, samples, count):
    _, _, rows, lanes = advanced.shape
    along_y, along_z = rows // BLK, lanes // BLK
    row = iota((ROWS, LANES), 0)
    lane_at = iota((ROWS, LANES), 1)
    pick = pick_rows()
    out = []
    for j in range(0, count, 2):
        parts = [jnp.zeros((ROWS, LANES), jnp.float32) for _ in range(NF)]
        uppers = []
        for half in range(2):
            block = samples[j + half]
            block_x = block // (along_y * along_z)
            block_y = block // along_z % along_y
            block_z = block % along_z
            uppers.append(block_y % 2)
            start = pl.multiple_of(block_y // 2 * ROWS, ROWS)
            for x in range(BLK):
                turn = lax.rem(VOL * half + BLK * BLK * x - BLK * block_z + LANES, LANES)
                wanted = lane_at // BLK == (VOL * half + BLK * BLK * x) // BLK
                for f in range(NF):
                    tile = advanced[f, block_x * BLK + x, pl.ds(start, ROWS), :]
                    parts[f] = jnp.where(wanted, pltpu.roll(tile, turn, 1), parts[f])
        upper = jnp.where(lane_at < VOL, uppers[0], uppers[1])
        valid = row // BLK == upper
        for f in range(NF):
            for bit in (1, 2):
                moved = pltpu.roll(parts[f], BLK * bit, 1)
                parts[f] = jnp.where(row // bit % 2 == 1, moved, parts[f])
            parts[f] = jnp.where(valid, parts[f], 0.0)
        stacked = jnp.concatenate(parts, 0).astype(jnp.bfloat16)
        out.append(jnp.dot(pick, stacked, preferred_element_type=jnp.float32))
    return out


def closure(advanced, samples, trainers, loads, w_first, w_second, w_second_t, w_third,
            w_third_t, devices_all, stack_first, stack_mid, rows_out, send, slots, inline, place):
    count = len(samples)
    pairs = count // 2
    cols = [slice(LANES * m, LANES * m + LANES) for m in range(pairs)]
    along = inside_masks()
    lane_at = iota((ROWS, LANES), 1)
    row = iota((ROWS, LANES), 0)

    pos_x, pos_y, pos_z, count_y, count_z = place
    picked = pick_blocks(advanced, samples, count)
    values = [p[:ROWS] for p in picked]
    targets = []
    for p in picked:
        first, second = p[ROWS : 2 * ROWS], p[2 * ROWS : 3 * ROWS]
        targets.append(box(first * second, along) - box(first, along) * box(second, along))

    for m, tile in enumerate(values):
        for t in range(0, 28, 2):
            piece = shifted(tile, TAPS[t], along)
            later = shifted(tile, TAPS[t + 1], along) if t + 1 < 27 else jnp.zeros_like(tile)
            stack_first[BLK * t : BLK * t + ROWS, cols[m]] = jnp.where(row < NF, piece, later)
    stack_in = stack_first[...].astype(jnp.bfloat16)
    pre_first = jnp.dot(w_first, stack_in, preferred_element_type=jnp.float32)
    gate_first = sigmoid(pre_first)
    hidden_first = (pre_first * gate_first).astype(jnp.bfloat16).astype(jnp.float32)
    for m in range(pairs):
        tile = hidden_first[:, cols[m]]
        for k, tap in enumerate(TAPS):
            stack_mid[CH * k : CH * k + CH, cols[m]] = shifted(tile, tap, along).astype(jnp.bfloat16)
    pre_second = jnp.dot(w_second, stack_mid[...], preferred_element_type=jnp.float32)
    gate_second = sigmoid(pre_second)
    hidden_second = (pre_second * gate_second).astype(jnp.bfloat16)
    predicted = jnp.dot(w_third, hidden_second, preferred_element_type=jnp.float32)

    misfit = predicted[:ROWS] - jnp.concatenate(targets, 1)
    square = jnp.sum(misfit * misfit, axis=0, keepdims=True)
    sample_at = iota((ROWS, count * VOL), 1) // VOL
    mine = sample_at == iota((ROWS, count * VOL), 0)
    losses = jnp.sum(jnp.where(mine, square, 0.0), axis=1, keepdims=True) / (NOUT * VOL)
    if loads is None:
        load = jnp.full((ROWS, 1), float(count_y * CAP), jnp.float32)
    else:
        owner = jnp.zeros((ROWS, LANES), jnp.int32)
        for j in range(count):
            owner = jnp.where(row == j, trainers[j], owner)
        load = jnp.sum(jnp.where(lane_at == owner, loads, 0.0), axis=1, keepdims=True)
    share = 1.0 / (devices_all * jnp.maximum(load, 1.0))
    scale = share * (2.0 / (NOUT * VOL))
    scale_at = jnp.sum(jnp.where(mine, scale, 0.0), axis=0, keepdims=True)
    grad_pred = (misfit * scale_at).astype(jnp.bfloat16)
    grad_pred = jnp.concatenate([grad_pred, jnp.zeros_like(grad_pred)], 0)

    upper = jnp.dot(w_third_t, grad_pred, preferred_element_type=jnp.float32)
    slope = gate_second * (1.0 + pre_second * (1.0 - gate_second))
    grad_mid = (upper * slope).astype(jnp.bfloat16)
    grad_second = lax.dot_general(grad_mid, stack_mid[...], FULL, preferred_element_type=jnp.float32)
    third = jnp.concatenate([grad_pred, jnp.zeros((LANES - 16, count * VOL), jnp.bfloat16)], 0)
    grad_third = lax.dot_general(hidden_second, third, FULL, preferred_element_type=jnp.float32)

    spread = jnp.dot(w_second_t, grad_mid, preferred_element_type=jnp.float32)
    lower = []
    for m in range(pairs):
        terms = [
            shifted(spread[CH * k : CH * k + CH, cols[m]], tuple(-o for o in tap), along)
            for k, tap in enumerate(TAPS)
        ]
        lower.append(functools.reduce(jnp.add, terms))
    lower = jnp.concatenate(lower, 1)
    slope = gate_first * (1.0 + pre_first * (1.0 - gate_first))
    grad_entry = (lower * slope).astype(jnp.bfloat16)
    grad_first = lax.dot_general(grad_entry, stack_in, FULL, preferred_element_type=jnp.float32)

    whole = CH * 27 // LANES
    rest = CH * 27 - whole * LANES
    for t in range(whole):
        rows_out[:, t, :] = grad_second[:, LANES * t : LANES * t + LANES]
    mixed = jnp.concatenate([grad_second[:, whole * LANES :], jnp.zeros((CH, LANES - rest), jnp.float32)], 1)
    mixed = mixed + pltpu.roll(grad_third, rest, 1)
    tail = LANES - grad_first.shape[1]
    rows_out[:, whole + 1, :] = jnp.concatenate([grad_first, jnp.zeros((CH, tail), jnp.float32)], 1)

    offset = rest + ROWS if inline else 0
    height = CH if inline else slots.shape[0]
    slot_rows = iota((height, LANES), 0)
    slot_lanes = iota((height, LANES), 1)
    placed = jnp.zeros((height, LANES), jnp.float32)
    for j in range(count):
        name = trainers[j]
        rank = jnp.int32(0)
        for i in range(j):
            rank = rank + jnp.where(trainers[i] == name, 1, 0)
        target = (pos_x * count_y + name) * count_z + pos_z
        slot = offset + pos_y * CAP + rank
        hit = (slot_rows == target) & (slot_lanes == slot)
        placed = jnp.where(hit, losses[j : j + 1, :], placed)
    high = placed.astype(jnp.bfloat16).astype(jnp.float32)
    placed = high + pltpu.roll(placed - high, count_y * CAP, 1)
    if inline:
        mixed = mixed + placed
    else:
        slots[:, 0, :] = placed.astype(jnp.bfloat16)
    rows_out[:, whole, :] = mixed
    send[...] = rows_out[...].astype(jnp.bfloat16)


def second_step(sizes, inline, drawn, middle, visc, partial, rims, vz_own, vx_b, vx_a, vz_other, vy_b, vy_a,
                z_own, x_b, z_other, x_a_low, x_a_high, *rest):
    loads, rest = (None, rest) if sizes["gy"] * CAP == SAMP else (rest[0][...], rest[1:])
    w_first, w_second, w_second_t, w_third, w_third_t, advanced_far, send = rest[:7]
    slots = None if inline else rest[7]
    stack_first, stack_mid, rows_out, y_terms, advanced, sem = rest[-6:]
    chunks = middle.shape[2] // ROWS
    halo = Sides(chunks, x_b, Parts(x_a_low, x_a_high), z_other)
    visc_halo = Sides(chunks, vx_b, vx_a, vz_other, vy_b, vy_a)
    y_faces = rims_with_ends(rims, visc_halo, halo)
    y_faces = [face + [visc_halo.along_y(NF)[side]] for side, face in enumerate(y_faces)]
    count = stack_mid.shape[1] // VOL
    samples = [drawn[0, j] for j in range(count)]
    trainers = [drawn[1, j] for j in range(count)]

    def emit(f, x, c, tile):
        advanced[f, x, ROWS * c : ROWS * c + ROWS, :] = tile

    close(middle, visc, partial, halo, visc_halo, y_faces, z_own, vz_own, y_terms, emit)
    leaving = pltpu.make_async_copy(advanced, advanced_far, sem)
    leaving.start()
    place = (lax.axis_index("gx"), lax.axis_index("gy"), lax.axis_index("gz"), sizes["gy"], sizes["gz"])
    closure(advanced, samples, trainers, loads, w_first[...], w_second[...],
            w_second_t[...], w_third[...], w_third_t[...],
            float(sizes["gx"] * sizes["gy"] * sizes["gz"]), stack_first, stack_mid, rows_out,
            send, slots, inline, place)
    leaving.wait()


def add_up(arrived, spread, own):
    total = jnp.sum(arrived[...].astype(jnp.float32), axis=0)
    own[...] = total
    rounded = total.astype(jnp.bfloat16)
    for i in range(spread.shape[0]):
        spread[i] = rounded


def unpack(where, gathered, own, first, second, third, losses, wide):
    row, lane = where
    count = losses.shape[3]
    high = own[row : row + 1, lane : lane + count]
    losses[0, 0] = high + own[row : row + 1, lane + count : lane + 2 * count]
    wide[...] = gathered[...].astype(jnp.float32)
    whole = second.shape[1] // LANES
    rest = second.shape[1] - whole * LANES
    for t in range(whole):
        second[:, LANES * t : LANES * t + LANES] = wide[:, t, :]
    mixed = wide[:, whole, :]
    second[:, LANES * whole :] = mixed[:, :rest]
    third[...] = mixed[:, rest : rest + ROWS].T[:NOUT]
    first[...] = wide[:, whole + 1, :][:, : first.shape[1]]


def shape_of(*dims, dtype=jnp.float32):
    return jax.ShapeDtypeStruct(dims, dtype)


def swap_a(face, axis, sizes):
    return lax.ppermute(face, axis, [(i, i ^ 1) for i in range(sizes[axis])])


def swap_b(face, axis, sizes):
    count = sizes[axis]
    return lax.ppermute(face, axis, [(i, (i + (1 if i % 2 else -1)) % count) for i in range(count)])


def beside(kernel, cells, more_shapes, index, arrays):
    scratch = [pltpu.SMEM(array.shape, jnp.int32) for array in index]
    if index:
        scratch.append(pltpu.SemaphoreType.DMA((len(index),)))
    return pl.pallas_call(
        kernel,
        out_shape=[shape_of(*arrays[0].shape)] + more_shapes,
        in_specs=[ANY] * len(index) + [VMEM] * len(arrays),
        out_specs=[VMEM] * (1 + len(more_shapes)),
        scratch_shapes=scratch,
        compiler_params=PARAMS,
        cost_estimate=pl.CostEstimate(flops=120 * cells, bytes_accessed=36 * cells, transcendentals=0),
        name=kernel.__name__,
    )(*index, *arrays)


def on_device(sizes, fields, visc, samples, trainers, conv_first, conv_second, conv_third):
    _, planes, rows, lanes = fields.shape
    axes = ("gx", "gy", "gz")
    devices_all = sizes["gx"] * sizes["gy"] * sizes["gz"]
    chunks = rows // ROWS
    pairs = planes * chunks
    half = LANES // 2
    samples = samples.reshape(-1)
    trainers = trainers.reshape(-1)

    faces = pl.pallas_call(
        pack_faces,
        out_shape=[
            shape_of((NF + 1) * chunks, ROWS, lanes),
            shape_of((NF + 1) * chunks, ROWS, lanes),
            shape_of(-(-(NF + 1) * pairs // half), ROWS, LANES),
            shape_of(2 * (NF + 1), planes, lanes),
            shape_of(2 * (NF + 1), planes, lanes),
        ],
        in_specs=[HBM, HBM],
        out_specs=[VMEM] * 5,
        scratch_shapes=[
            pltpu.VMEM(fields.shape, jnp.float32),
            pltpu.VMEM(visc.shape, jnp.float32),
            pltpu.SemaphoreType.DMA((2,)),
        ],
        compiler_params=PACK,
        name="pack_faces",
    )(fields, visc)
    x_b, x_a, z_own, y_b, y_a = faces
    halo = [
        swap_b(x_b, "gx", sizes), swap_a(x_a, "gx", sizes), swap_a(z_own, "gz", sizes),
        swap_b(y_b, "gy", sizes), swap_a(y_a, "gy", sizes),
    ]

    own_counts = sizes["gy"] * CAP == SAMP
    counts = []
    if not own_counts:
        named = trainers.reshape(-1, 1) == jnp.arange(LANES, dtype=jnp.int32)[None, :]
        total = lax.psum(jnp.sum(named.astype(jnp.float32), axis=0, keepdims=True), "gy")
        counts = [jnp.broadcast_to(total, (ROWS, LANES))]
    sizes_of = [shape_of(*size, dtype=jnp.bfloat16) for size in ((CH, 28 * NF), (16, CH), (CH, 16))]
    partial, w_first, w_third, w_third_t, drawn = beside(
        interior_first, visc.size, sizes_of + [shape_of(ROWS, LANES, dtype=jnp.int32)],
        (samples, trainers), (fields, visc, conv_first, conv_third),
    )
    y_terms = pltpu.VMEM((2, NF, planes, lanes), jnp.float32)
    middle, x_b, x_a_low, x_a_high, z_later = pl.pallas_call(
        close_first,
        out_shape=[
            shape_of(*fields.shape),
            shape_of(NF * chunks + 2, ROWS, lanes),
            shape_of(NF * chunks // 2 + 1, ROWS, lanes),
            shape_of(NF * chunks // 2 + 1, ROWS, lanes),
            shape_of(NF * chunks // 2 + 2, ROWS, LANES),
        ],
        in_specs=[VMEM] * 9,
        out_specs=[VMEM] * 5,
        scratch_shapes=[y_terms],
        compiler_params=PARAMS,
        name="close_first",
    )(fields, visc, partial, z_own, *halo)
    later = [
        swap_b(x_b, "gx", sizes), swap_a(z_later, "gz", sizes),
        swap_a(x_a_low, "gx", sizes), swap_a(x_a_high, "gx", sizes),
    ]
    partial, rims, w_second_t = beside(
        interior_second, visc.size,
        [shape_of(2 * NF, ROWS, LANES), shape_of(27 * CH, CH, dtype=jnp.bfloat16)],
        (), (middle, visc, fields, *halo[3:], conv_second),
    )

    count = samples.shape[0]
    slot_total = sizes["gy"] * CAP
    tiles = -(-27 * CH // LANES) + 1
    parts = devices_all // CH
    inline = parts == 1 and slot_total <= 12
    out_shape = [shape_of(*fields.shape), shape_of(CH, tiles, LANES, dtype=jnp.bfloat16)]
    if not inline:
        out_shape.append(shape_of(devices_all, 1, LANES, dtype=jnp.bfloat16))
    advanced, send, *slots = pl.pallas_call(
        functools.partial(second_step, sizes, inline),
        out_shape=out_shape,
        in_specs=[VMEM] * (21 + len(counts)),
        out_specs=[ANY] + [VMEM] * (len(out_shape) - 1),
        scratch_shapes=[
            pltpu.VMEM((28 * NF, count * VOL), jnp.float32),
            pltpu.VMEM((27 * CH, count * VOL), jnp.bfloat16),
            pltpu.VMEM((CH, tiles, LANES), jnp.float32),
            y_terms,
            pltpu.VMEM(fields.shape, jnp.float32),
            pltpu.SemaphoreType.DMA,
        ],
        compiler_params=PARAMS,
        name="second_step",
    )(drawn, middle, visc, partial, rims, z_own, *halo, z_later, *later, *counts,
      w_first, conv_second, w_second_t, w_third, w_third_t)

    if not inline:
        send = jnp.concatenate([send.reshape(devices_all, tiles // parts, LANES), slots[0]], 1)
    arrived = lax.all_to_all(send, axes, split_axis=0, concat_axis=0, tiled=True)
    if inline:
        where = (27 * CH // LANES, 27 * CH % LANES + ROWS)
    else:
        where = (send.shape[1] - 1, 0)
    spread, own = pl.pallas_call(
        add_up,
        out_shape=[shape_of(*send.shape, dtype=jnp.bfloat16), shape_of(*send.shape[1:])],
        in_specs=[VMEM],
        out_specs=[VMEM] * 2,
        compiler_params=PARAMS,
        name="add_up",
    )(arrived)
    if not inline:
        spread = spread[:, :-1, :]
    gathered = lax.all_to_all(spread, axes, split_axis=0, concat_axis=0, tiled=True)
    first, second, third, block_losses = pl.pallas_call(
        functools.partial(unpack, where),
        out_shape=[
            shape_of(*conv_first.shape),
            shape_of(*conv_second.shape),
            shape_of(*conv_third.shape),
            shape_of(1, 1, 1, slot_total),
        ],
        in_specs=[VMEM] * 2,
        out_specs=[VMEM] * 4,
        scratch_shapes=[pltpu.VMEM((CH, tiles, LANES), jnp.float32)],
        compiler_params=PARAMS,
        name="unpack",
    )(gathered.reshape(CH, tiles, LANES), own)
    return advanced, block_losses, first, second, third


def solution(mesh):
    sizes = dict(mesh.shape)
    in_specs = (
        P(None, "gx", "gy", "gz"),
        P("gx", "gy", "gz"),
        P("gx", "gy", "gz", None),
        P("gx", "gy", "gz", None, None),
        P(),
        P(),
        P(),
    )
    out_specs = (P(None, "gx", "gy", "gz"), P("gx", "gy", "gz", None), P(), P(), P())
    return jax.shard_map(
        functools.partial(on_device, sizes), mesh=mesh, in_specs=in_specs, out_specs=out_specs,
        check_vma=False,
    )
```

```python
import functools

import jax
import jax.numpy as jnp
from jax import lax
from jax.experimental import pallas as pl
from jax.experimental.pallas import tpu as pltpu
from jax.sharding import PartitionSpec as P

BLK = 4
CAP = 2
SAMP = 8
Z_TILES = 2
NF = 4
VOL = BLK**3
TAPS = [(x, y, z) for x in (-1, 0, 1) for y in (-1, 0, 1) for z in (-1, 0, 1)]
LANES = 128
ROWS = 8
NOUT = 6
CH = 32

time_step = 0.25
buoyancy = 0.5

VMEM = pl.BlockSpec(memory_space=pltpu.VMEM)
SMEM = pl.BlockSpec(memory_space=pltpu.SMEM)
HBM = pl.BlockSpec(memory_space=pltpu.HBM)
ANY = pl.BlockSpec(memory_space=pl.ANY)
PARAMS = pltpu.CompilerParams(vmem_limit_bytes=24 * 1024 * 1024)
PACK = pltpu.CompilerParams(vmem_limit_bytes=54944 * 1024)
FULL = (((1,), (1,)), ((), ()))


def iota(shape, axis):
    return lax.broadcasted_iota(jnp.int32, shape, axis)


def odd(axis):
    return lax.axis_index(axis) % 2 == 1


def facing(axis, swap, first, last):
    return jnp.where(odd(axis), first, last) if swap == "a" else jnp.where(odd(axis), last, first)


def prev_next(axis, from_a, from_b):
    return jnp.where(odd(axis), from_a, from_b), jnp.where(odd(axis), from_b, from_a)


class Parts:
    def __init__(self, *parts):
        self.parts, self.tiles = parts, parts[0].shape[0]

    def at_tile(self, index):
        tile, rest = (index[0], index[1:]) if isinstance(index, tuple) else (index, ())
        return self.parts[tile // self.tiles], (tile % self.tiles,) + rest

    def __getitem__(self, index):
        part, place = self.at_tile(index)
        return part[place]

    def __setitem__(self, index, value):
        part, place = self.at_tile(index)
        part[place] = value


class Sides:
    def __init__(self, chunks, x_b, x_a, z_both, y_b=None, y_a=None):
        self.chunks = chunks
        self.x_a, self.x_b, self.y_a, self.y_b, self.z_both = x_a, x_b, y_a, y_b, z_both

    def along_x(self, f, c):
        tile = f * self.chunks + c
        return prev_next("gx", self.x_a[tile], self.x_b[tile])

    def along_y(self, f, depth=0):
        tile = depth * (NF + 1) + f
        return prev_next("gy", self.y_a[tile], self.y_b[tile])


def pair_of(f, c, planes, chunks):
    span = 2 * planes * chunks
    return f * span // LANES, f * span % LANES + 2 * planes * c


def add_pair(packed, tile, lane):
    moved = pltpu.roll(tile, lane + 1, 1)
    at = iota(tile.shape, 1)
    return jnp.where((at == lane) | (at == lane + 1), moved, packed)


def cut_x(f, array, x_b, x_a):
    planes, rows, _ = array.shape
    chunks = rows // ROWS
    for c in range(chunks):
        part = slice(ROWS * c, ROWS * c + ROWS)
        ends = array[0, part], array[planes - 1, part]
        x_b[f * chunks + c] = facing("gx", "b", *ends)
        x_a[f * chunks + c] = facing("gx", "a", *ends)


def pack_faces(fields_far, visc_far, x_b, x_a, z_both, y_b, y_a, fields, visc, sems):
    _, planes, rows, _ = fields.shape
    chunks = rows // ROWS
    copies = [
        pltpu.make_async_copy(fields_far, fields, sems.at[0]),
        pltpu.make_async_copy(visc_far, visc, sems.at[1]),
    ]
    for copy in copies:
        copy.start()
    arrays = [fields.at[f] for f in range(NF)] + [visc]
    packed = [jnp.zeros((ROWS, LANES), jnp.float32) for _ in range(z_both.shape[0])]
    for f, array in enumerate(arrays):
        if f == 0 or f == NF:
            copies[f // NF].wait()
        cut_x(f, array, x_b, x_a)
        for depth in range(2):
            ends = array[:, depth, :], array[:, rows - 1 - depth, :]
            y_b[depth * (NF + 1) + f] = facing("gy", "b", *ends)
            y_a[depth * (NF + 1) + f] = facing("gy", "a", *ends)
        for c in range(chunks):
            tile, lane = pair_of(f, c, planes, chunks)
            for x in range(planes):
                cells = array[x, ROWS * c : ROWS * c + ROWS]
                packed[tile] = add_pair(packed[tile], cells, lane + 2 * x)
    for tile, value in enumerate(packed):
        z_both[tile] = value


def flux(lower, upper, dimension):
    speed = 0.25 * (lower[dimension] + upper[dimension])
    mean_visc = 0.5 * (lower[NF] + upper[NF])
    return [speed * (a + b) - mean_visc * (b - a) for a, b in zip(lower[:NF], upper[:NF])]


def interior(fields, visc, partial):
    _, planes, rows, _ = fields.shape
    chunks = rows // ROWS
    end_row = iota((ROWS, LANES), 0) == ROWS - 1
    end_lane = iota((ROWS, LANES), 1) == LANES - 1
    every = range(NF + 1)

    def cell(f, x, part):
        return fields[f, x, part, :] if f < NF else visc[x, part, :]

    def plane(x, lowers):
        uppers = []
        last = x == planes - 1
        beyond = jnp.minimum(x + 1, planes - 1)
        behind = [jnp.zeros((ROWS, LANES), jnp.float32)] * NF
        for c in range(chunks):
            part = slice(ROWS * c, ROWS * c + ROWS)
            here = [cell(f, x, part) for f in every]
            after = [cell(f, beyond, part) for f in every]
            upper = flux(here, after, 0)
            upper = [jnp.where(last, 0.0, u) for u in upper]
            total = [b - a for a, b in zip(lowers[c], upper)]
            uppers.append(upper)
            above = [pltpu.roll(h, ROWS - 1, 0) for h in here]
            if c + 1 < chunks:
                first = slice(ROWS * c + ROWS, ROWS * c + ROWS + 1)
                above = [jnp.where(end_row, cell(f, x, first), above[f]) for f in every]
            upper = flux(here, above, 1)
            lower = [pltpu.roll(jnp.where(end_row, b, u), 1, 0) for b, u in zip(behind, upper)]
            if c + 1 == chunks:
                upper = [jnp.where(end_row, 0.0, u) for u in upper]
            behind = upper
            total = [t + (b - a) for t, a, b in zip(total, lower, upper)]
            right = [pltpu.roll(h, LANES - 1, 1) for h in here]
            upper = [jnp.where(end_lane, 0.0, u) for u in flux(here, right, 2)]
            lower = [pltpu.roll(u, 1, 1) for u in upper]
            total = [t + (b - a) for t, a, b in zip(total, lower, upper)]
            updated = [q - time_step * t for q, t in zip(here[:NF], total)]
            updated[2] = updated[2] + (time_step * buoyancy) * here[3]
            for f in range(NF):
                partial[f, x, part, :] = updated[f]
        return uppers

    zeros = [[jnp.zeros((ROWS, LANES), jnp.float32)] * NF for _ in range(chunks)]
    lax.fori_loop(0, planes, plane, zeros)


def rims_without_ends(fields, visc, sides, rims):
    rows = fields.shape[2]
    every = range(NF + 1)
    end_row = iota((ROWS, LANES), 0) == ROWS - 1
    end_lane = iota((ROWS, LANES), 1) == LANES - 1

    def own(row):
        return [fields[f, :, row, :] for f in range(NF)] + [visc[:, row, :]]

    for side in range(2):
        here = [sides.along_y(f)[side] for f in every]
        beyond = [sides.along_y(f, 1)[side] for f in every]
        below, above = (beyond, own(0)) if side == 0 else (own(rows - 1), beyond)
        total = [b - a for a, b in zip(flux(below, here, 1), flux(here, above, 1))]
        for dimension, axis, end in ((0, 0, end_row), (2, 1, end_lane)):
            after = [pltpu.roll(h, h.shape[axis] - 1, axis) for h in here]
            upper = [jnp.where(end, 0.0, u) for u in flux(here, after, dimension)]
            total = [t + (u - pltpu.roll(u, 1, axis)) for t, u in zip(total, upper)]
        updated = [q - time_step * t for q, t in zip(here[:NF], total)]
        updated[2] = updated[2] + (time_step * buoyancy) * here[3]
        for f in range(NF):
            rims[side * NF + f] = updated[f]


def rims_with_ends(rims, sides, later):
    row = iota((ROWS, LANES), 0)
    lane = iota((ROWS, LANES), 1)
    every = range(NF + 1)
    whole = []
    for side in range(2):
        here = [sides.along_y(f)[side] for f in every]
        tile = NF * later.chunks + side
        before, after = prev_next("gx", later.x_a[tile], later.x_b[tile])
        low = flux([before[f : f + 1] for f in every], [h[:1] for h in here], 0)
        high = flux([h[ROWS - 1 :] for h in here], [after[f : f + 1] for f in every], 0)
        columns = later.z_both[Z_TILES]
        left, right = [], []
        for f in every:
            both = pltpu.roll(columns, LANES - 1 - 2 * (side * (NF + 1) + f), 1)
            left.append(pltpu.roll(jnp.where(lane == LANES - 1, both, here[f]), 1, 1))
            right.append(pltpu.roll(jnp.where(lane == 0, both, here[f]), LANES - 1, 1))
        lower, upper = flux(left, here, 2), flux(here, right, 2)
        ends = []
        for f in range(NF):
            value = rims[side * NF + f]
            value = value + time_step * jnp.where(row == 0, low[f], 0.0)
            value = value - time_step * jnp.where(row == ROWS - 1, high[f], 0.0)
            value = value + time_step * jnp.where(lane == 0, lower[f], 0.0)
            ends.append(value - time_step * jnp.where(lane == LANES - 1, upper[f], 0.0))
        whole.append(ends)
    return whole


def interior_first(samples_far, trainers_far, fields, visc, conv_first, conv_third, partial, w_first,
                   w_third, w_third_t, drawn, samples, trainers, sems):
    copies = [
        pltpu.make_async_copy(samples_far, samples, sems.at[0]),
        pltpu.make_async_copy(trainers_far, trainers, sems.at[1]),
    ]
    for copy in copies:
        copy.start()
    interior(fields, visc, partial)
    ahead = conv_first.shape[1]
    w_first[:, :ahead] = conv_first[...]
    w_first[:, ahead:] = jnp.zeros((CH, w_first.shape[1] - ahead), jnp.bfloat16)
    third = conv_third[...].astype(jnp.float32)
    third = jnp.concatenate([third, jnp.zeros((w_third.shape[0] - NOUT, CH), jnp.float32)], 0)
    w_third[...] = third.astype(jnp.bfloat16)
    w_third_t[...] = third.T.astype(jnp.bfloat16)
    for copy in copies:
        copy.wait()
    at, row = iota((ROWS, LANES), 1), iota((ROWS, LANES), 0)
    table = jnp.zeros((ROWS, LANES), jnp.int32)
    for j in range(samples.shape[0]):
        table = jnp.where(at == j, jnp.where(row == 0, samples[j], trainers[j]), table)
    drawn[...] = table


def interior_second(middle, visc, fields, y_b, y_a, conv_second, partial, rims, w_second_t):
    interior(middle, visc, partial)
    rims_without_ends(fields, visc, Sides(0, None, None, None, y_b, y_a), rims)
    w_second_t[...] = conv_second[...].astype(jnp.float32).T.astype(jnp.bfloat16)


def z_terms(own, other, visc_own, visc_other):
    lane = iota((ROWS, LANES), 1)
    second = lane % 2 == 1
    span = LANES // 2

    def ends(mine, theirs):
        lower = jnp.where(second, pltpu.roll(theirs, 1, 1), mine)
        return lower, jnp.where(second, mine, pltpu.roll(theirs, LANES - 1, 1))

    def twice(tile):
        return jnp.where(lane < span, tile, pltpu.roll(tile, span, 1))

    pairs = [ends(a, b) for a, b in zip(own, other)]
    speed = [twice(end) for end in pairs[2 * span // LANES]]
    visc = [twice(end) for end in ends(visc_own, visc_other)]
    speed = 0.25 * (speed[0] + speed[1])
    mean_visc = 0.5 * (visc[0] + visc[1])
    through = [speed * (a + b) - mean_visc * (b - a) for a, b in pairs]
    return [jnp.where(second, time_step, -time_step) * t for t in through]


def close(fields, visc, partial, halo, visc_halo, y_faces, z_own, visc_z_own, y_terms, emit):
    _, planes, rows, _ = fields.shape
    chunks = rows // ROWS
    every = range(NF + 1)
    row = iota((ROWS, LANES), 0)
    lane_at = iota((ROWS, LANES), 1)
    ends = (lane_at == 0) | (lane_at == LANES - 1)

    def cell(f, *index):
        return fields[(f,) + index] if f < NF else visc[index]

    def sides(f):
        return halo if f < NF else visc_halo

    lower = flux(y_faces[0], [cell(f, slice(None), 0) for f in every], 1)
    upper = flux([cell(f, slice(None), rows - 1) for f in every], y_faces[1], 1)
    for f in range(NF):
        y_terms[0, f] = time_step * lower[f]
        y_terms[1, f] = -time_step * upper[f]
    tiles = 2 * NF * planes * chunks // LANES
    terms = z_terms([z_own[t] for t in range(tiles)], [halo.z_both[t] for t in range(tiles)],
                    visc_z_own[tiles], visc_halo.z_both[tiles])
    for c in range(chunks):
        part = slice(ROWS * c, ROWS * c + ROWS)
        before, after = zip(*[sides(f).along_x(f, c) for f in every])
        low = flux(before, [cell(f, 0, part) for f in every], 0)
        high = flux([cell(f, planes - 1, part) for f in every], after, 0)
        for x in range(planes):
            for f in range(NF):
                tile, lane = pair_of(f, c, planes, chunks)
                moved = pltpu.roll(terms[tile], LANES - 1 - lane - 2 * x, 1)
                value = partial[f, x, part, :] + jnp.where(ends, moved, 0.0)
                if x == 0:
                    value = value + time_step * low[f]
                if x == planes - 1:
                    value = value - time_step * high[f]
                if c == 0:
                    value = value + jnp.where(row == 0, y_terms[0, f, x : x + 1, :], 0.0)
                if c == chunks - 1:
                    value = value + jnp.where(row == ROWS - 1, y_terms[1, f, x : x + 1, :], 0.0)
                emit(f, x, c, value)


def close_first(fields, visc, partial, z_own, x_from_b, x_from_a, z_other, y_from_b, y_from_a,
                middle, x_b, x_a_low, x_a_high, z_both, y_terms):
    x_a = Parts(x_a_low, x_a_high)
    _, planes, rows, _ = fields.shape
    chunks = rows // ROWS
    halo = Sides(chunks, x_from_b, x_from_a, z_other, y_from_b, y_from_a)
    packed = [jnp.zeros((ROWS, LANES), jnp.float32) for _ in range(Z_TILES + 1)]
    y_faces = list(zip(*[halo.along_y(f) for f in range(NF + 1)]))

    def emit(f, x, c, tile):
        middle[f, x, ROWS * c : ROWS * c + ROWS, :] = tile
        at, lane = pair_of(f, c, planes, chunks)
        packed[at] = add_pair(packed[at], tile, lane + 2 * x)

    for side in range(2):
        for f in range(NF + 1):
            face = y_faces[side][f]
            packed[-1] = add_pair(packed[-1], face, 2 * (side * (NF + 1) + f))
            x_b[NF * chunks + side, f : f + 1, :] = facing("gx", "b", face[:1], face[planes - 1 :])
            x_a[NF * chunks + side, f : f + 1, :] = facing("gx", "a", face[:1], face[planes - 1 :])
    close(fields, visc, partial, halo, halo, y_faces, z_own, z_own, y_terms, emit)
    for at in range(z_both.shape[0]):
        z_both[at] = packed[at] if at <= Z_TILES else jnp.zeros((ROWS, LANES), jnp.float32)
    for f in range(NF):
        cut_x(f, middle.at[f], x_b, x_a)


def inside_masks():
    at = iota((1, LANES), 1) % VOL
    coords = (at // (BLK * BLK), at // BLK % BLK, at % BLK)
    along = []
    for coord in coords:
        along.append({
            -1: jnp.where(coord > 0, 1.0, 0.0),
            0: jnp.ones((1, LANES), jnp.float32),
            1: jnp.where(coord < BLK - 1, 1.0, 0.0),
        })
    return along


def move_of(tap):
    return tap[0] * BLK * BLK + tap[1] * BLK + tap[2]


def shifted(tile, tap, along):
    move = move_of(tap)
    if move == 0:
        return tile
    mask = along[0][tap[0]] * along[1][tap[1]] * along[2][tap[2]]
    return pltpu.roll(tile, (-move) % LANES, 1) * mask


def box(tile, along):
    for dimension, step in enumerate((BLK * BLK, BLK, 1)):
        ahead = pltpu.roll(tile, LANES - step, 1) * along[dimension][1]
        behind = pltpu.roll(tile, step, 1) * along[dimension][-1]
        tile = (behind + tile) + ahead
    return tile / 27.0


def sigmoid(values):
    return 1.0 / (1.0 + jnp.exp(-values))


PICKED = (0, 1, 2, 3, 0, 1, 2, 3, 0, 1, 2, 0, 0, 1, -1, -1, 0, 1, 2, 1, 2, 2, -1, -1)


def pick_rows():
    out, field = iota((32, NF * ROWS), 0), iota((32, NF * ROWS), 1) // ROWS
    table = jnp.zeros((32, NF * ROWS), jnp.float32)
    for i, f in enumerate(PICKED):
        table = jnp.where((out == i) & (field == f), 1.0, table)
    return table.astype(jnp.bfloat16)


def pick_blocks(advanced, samples, count):
    _, _, rows, lanes = advanced.shape
    along_y, along_z = rows // BLK, lanes // BLK
    row = iota((ROWS, LANES), 0)
    lane_at = iota((ROWS, LANES), 1)
    pick = pick_rows()
    out = []
    for j in range(0, count, 2):
        parts = [jnp.zeros((ROWS, LANES), jnp.float32) for _ in range(NF)]
        uppers = []
        for half in range(2):
            block = samples[j + half]
            block_x = block // (along_y * along_z)
            block_y = block // along_z % along_y
            block_z = block % along_z
            uppers.append(block_y % 2)
            start = pl.multiple_of(block_y // 2 * ROWS, ROWS)
            for x in range(BLK):
                turn = lax.rem(VOL * half + BLK * BLK * x - BLK * block_z + LANES, LANES)
                wanted = lane_at // BLK == (VOL * half + BLK * BLK * x) // BLK
                for f in range(NF):
                    tile = advanced[f, block_x * BLK + x, pl.ds(start, ROWS), :]
                    parts[f] = jnp.where(wanted, pltpu.roll(tile, turn, 1), parts[f])
        upper = jnp.where(lane_at < VOL, uppers[0], uppers[1])
        valid = row // BLK == upper
        for f in range(NF):
            for bit in (1, 2):
                moved = pltpu.roll(parts[f], BLK * bit, 1)
                parts[f] = jnp.where(row // bit % 2 == 1, moved, parts[f])
            parts[f] = jnp.where(valid, parts[f], 0.0)
        stacked = jnp.concatenate(parts, 0).astype(jnp.bfloat16)
        out.append(jnp.dot(pick, stacked, preferred_element_type=jnp.float32))
    return out


def closure(advanced, samples, trainers, loads, w_first, w_second, w_second_t, w_third,
            w_third_t, devices_all, stack_first, stack_mid, rows_out, send, slots, inline, place):
    count = len(samples)
    pairs = count // 2
    cols = [slice(LANES * m, LANES * m + LANES) for m in range(pairs)]
    along = inside_masks()
    lane_at = iota((ROWS, LANES), 1)
    row = iota((ROWS, LANES), 0)

    pos_x, pos_y, pos_z, count_y, count_z = place
    picked = pick_blocks(advanced, samples, count)
    values = [p[:ROWS] for p in picked]
    targets = []
    for p in picked:
        first, second = p[ROWS : 2 * ROWS], p[2 * ROWS : 3 * ROWS]
        targets.append(box(first * second, along) - box(first, along) * box(second, along))

    for m, tile in enumerate(values):
        for t in range(0, 28, 2):
            piece = shifted(tile, TAPS[t], along)
            later = shifted(tile, TAPS[t + 1], along) if t + 1 < 27 else jnp.zeros_like(tile)
            stack_first[BLK * t : BLK * t + ROWS, cols[m]] = jnp.where(row < NF, piece, later)
    stack_in = stack_first[...].astype(jnp.bfloat16)
    pre_first = jnp.dot(w_first, stack_in, preferred_element_type=jnp.float32)
    gate_first = sigmoid(pre_first)
    hidden_first = (pre_first * gate_first).astype(jnp.bfloat16).astype(jnp.float32)
    for m in range(pairs):
        tile = hidden_first[:, cols[m]]
        for k, tap in enumerate(TAPS):
            stack_mid[CH * k : CH * k + CH, cols[m]] = shifted(tile, tap, along).astype(jnp.bfloat16)
    pre_second = jnp.dot(w_second, stack_mid[...], preferred_element_type=jnp.float32)
    gate_second = sigmoid(pre_second)
    hidden_second = (pre_second * gate_second).astype(jnp.bfloat16)
    predicted = jnp.dot(w_third, hidden_second, preferred_element_type=jnp.float32)

    misfit = predicted[:ROWS] - jnp.concatenate(targets, 1)
    square = jnp.sum(misfit * misfit, axis=0, keepdims=True)
    sample_at = iota((ROWS, count * VOL), 1) // VOL
    mine = sample_at == iota((ROWS, count * VOL), 0)
    losses = jnp.sum(jnp.where(mine, square, 0.0), axis=1, keepdims=True) / (NOUT * VOL)
    if loads is None:
        load = jnp.full((ROWS, 1), float(count_y * CAP), jnp.float32)
    else:
        owner = jnp.zeros((ROWS, LANES), jnp.int32)
        for j in range(count):
            owner = jnp.where(row == j, trainers[j], owner)
        load = jnp.sum(jnp.where(lane_at == owner, loads, 0.0), axis=1, keepdims=True)
    share = 1.0 / (devices_all * jnp.maximum(load, 1.0))
    scale = share * (2.0 / (NOUT * VOL))
    scale_at = jnp.sum(jnp.where(mine, scale, 0.0), axis=0, keepdims=True)
    grad_pred = (misfit * scale_at).astype(jnp.bfloat16)
    grad_pred = jnp.concatenate([grad_pred, jnp.zeros_like(grad_pred)], 0)

    upper = jnp.dot(w_third_t, grad_pred, preferred_element_type=jnp.float32)
    slope = gate_second * (1.0 + pre_second * (1.0 - gate_second))
    grad_mid = (upper * slope).astype(jnp.bfloat16)
    grad_second = lax.dot_general(grad_mid, stack_mid[...], FULL, preferred_element_type=jnp.float32)
    third = jnp.concatenate([grad_pred, jnp.zeros((LANES - 16, count * VOL), jnp.bfloat16)], 0)
    grad_third = lax.dot_general(hidden_second, third, FULL, preferred_element_type=jnp.float32)

    spread = jnp.dot(w_second_t, grad_mid, preferred_element_type=jnp.float32)
    lower = []
    for m in range(pairs):
        terms = [
            shifted(spread[CH * k : CH * k + CH, cols[m]], tuple(-o for o in tap), along)
            for k, tap in enumerate(TAPS)
        ]
        lower.append(functools.reduce(jnp.add, terms))
    lower = jnp.concatenate(lower, 1)
    slope = gate_first * (1.0 + pre_first * (1.0 - gate_first))
    grad_entry = (lower * slope).astype(jnp.bfloat16)
    grad_first = lax.dot_general(grad_entry, stack_in, FULL, preferred_element_type=jnp.float32)

    whole = CH * 27 // LANES
    rest = CH * 27 - whole * LANES
    for t in range(whole):
        rows_out[:, t, :] = grad_second[:, LANES * t : LANES * t + LANES]
    mixed = jnp.concatenate([grad_second[:, whole * LANES :], jnp.zeros((CH, LANES - rest), jnp.float32)], 1)
    mixed = mixed + pltpu.roll(grad_third, rest, 1)
    tail = LANES - grad_first.shape[1]
    rows_out[:, whole + 1, :] = jnp.concatenate([grad_first, jnp.zeros((CH, tail), jnp.float32)], 1)

    offset = rest + ROWS if inline else 0
    height = CH if inline else slots.shape[0]
    slot_rows = iota((height, LANES), 0)
    slot_lanes = iota((height, LANES), 1)
    placed = jnp.zeros((height, LANES), jnp.float32)
    for j in range(count):
        name = trainers[j]
        rank = jnp.int32(0)
        for i in range(j):
            rank = rank + jnp.where(trainers[i] == name, 1, 0)
        target = (pos_x * count_y + name) * count_z + pos_z
        slot = offset + pos_y * CAP + rank
        hit = (slot_rows == target) & (slot_lanes == slot)
        placed = jnp.where(hit, losses[j : j + 1, :], placed)
    high = placed.astype(jnp.bfloat16).astype(jnp.float32)
    placed = high + pltpu.roll(placed - high, count_y * CAP, 1)
    if inline:
        mixed = mixed + placed
    else:
        slots[:, 0, :] = placed.astype(jnp.bfloat16)
    rows_out[:, whole, :] = mixed
    send[...] = rows_out[...].astype(jnp.bfloat16)


def second_step(sizes, inline, drawn, middle, visc, partial, rims, vz_own, vx_b, vx_a, vz_other, vy_b, vy_a,
                z_own, x_b, z_other, x_a_low, x_a_high, *rest):
    loads, rest = (None, rest) if sizes["gy"] * CAP == SAMP else (rest[0][...], rest[1:])
    w_first, w_second, w_second_t, w_third, w_third_t, advanced, send = rest[:7]
    slots = None if inline else rest[7]
    stack_first, stack_mid, rows_out, y_terms = rest[-4:]
    chunks = middle.shape[2] // ROWS
    halo = Sides(chunks, x_b, Parts(x_a_low, x_a_high), z_other)
    visc_halo = Sides(chunks, vx_b, vx_a, vz_other, vy_b, vy_a)
    y_faces = rims_with_ends(rims, visc_halo, halo)
    y_faces = [face + [visc_halo.along_y(NF)[side]] for side, face in enumerate(y_faces)]
    count = stack_mid.shape[1] // VOL
    samples = [drawn[0, j] for j in range(count)]
    trainers = [drawn[1, j] for j in range(count)]

    def emit(f, x, c, tile):
        advanced[f, x, ROWS * c : ROWS * c + ROWS, :] = tile

    close(middle, visc, partial, halo, visc_halo, y_faces, z_own, vz_own, y_terms, emit)
    place = (lax.axis_index("gx"), lax.axis_index("gy"), lax.axis_index("gz"), sizes["gy"], sizes["gz"])
    closure(advanced, samples, trainers, loads, w_first[...], w_second[...],
            w_second_t[...], w_third[...], w_third_t[...],
            float(sizes["gx"] * sizes["gy"] * sizes["gz"]), stack_first, stack_mid, rows_out,
            send, slots, inline, place)


def add_up(arrived, spread, own):
    total = jnp.sum(arrived[...].astype(jnp.float32), axis=0)
    own[...] = total
    rounded = total.astype(jnp.bfloat16)
    for i in range(spread.shape[0]):
        spread[i] = rounded


def unpack(where, gathered, own, kept, first, second, third, losses, advanced, wide, sem):
    leaving = pltpu.make_async_copy(kept, advanced, sem)
    leaving.start()
    row, lane = where
    count = losses.shape[3]
    high = own[row : row + 1, lane : lane + count]
    losses[0, 0] = high + own[row : row + 1, lane + count : lane + 2 * count]
    wide[...] = gathered[...].astype(jnp.float32)
    whole = second.shape[1] // LANES
    rest = second.shape[1] - whole * LANES
    for t in range(whole):
        second[:, LANES * t : LANES * t + LANES] = wide[:, t, :]
    mixed = wide[:, whole, :]
    second[:, LANES * whole :] = mixed[:, :rest]
    third[...] = mixed[:, rest : rest + ROWS].T[:NOUT]
    first[...] = wide[:, whole + 1, :][:, : first.shape[1]]
    leaving.wait()


def shape_of(*dims, dtype=jnp.float32):
    return jax.ShapeDtypeStruct(dims, dtype)


def swap_a(face, axis, sizes):
    return lax.ppermute(face, axis, [(i, i ^ 1) for i in range(sizes[axis])])


def swap_b(face, axis, sizes):
    count = sizes[axis]
    return lax.ppermute(face, axis, [(i, (i + (1 if i % 2 else -1)) % count) for i in range(count)])


def beside(kernel, cells, more_shapes, index, arrays):
    scratch = [pltpu.SMEM(array.shape, jnp.int32) for array in index]
    if index:
        scratch.append(pltpu.SemaphoreType.DMA((len(index),)))
    return pl.pallas_call(
        kernel,
        out_shape=[shape_of(*arrays[0].shape)] + more_shapes,
        in_specs=[ANY] * len(index) + [VMEM] * len(arrays),
        out_specs=[VMEM] * (1 + len(more_shapes)),
        scratch_shapes=scratch,
        compiler_params=PARAMS,
        cost_estimate=pl.CostEstimate(flops=120 * cells, bytes_accessed=36 * cells, transcendentals=0),
        name=kernel.__name__,
    )(*index, *arrays)


def on_device(sizes, fields, visc, samples, trainers, conv_first, conv_second, conv_third):
    _, planes, rows, lanes = fields.shape
    axes = ("gx", "gy", "gz")
    devices_all = sizes["gx"] * sizes["gy"] * sizes["gz"]
    chunks = rows // ROWS
    pairs = planes * chunks
    half = LANES // 2
    samples = samples.reshape(-1)
    trainers = trainers.reshape(-1)

    faces = pl.pallas_call(
        pack_faces,
        out_shape=[
            shape_of((NF + 1) * chunks, ROWS, lanes),
            shape_of((NF + 1) * chunks, ROWS, lanes),
            shape_of(-(-(NF + 1) * pairs // half), ROWS, LANES),
            shape_of(2 * (NF + 1), planes, lanes),
            shape_of(2 * (NF + 1), planes, lanes),
        ],
        in_specs=[HBM, HBM],
        out_specs=[VMEM] * 5,
        scratch_shapes=[
            pltpu.VMEM(fields.shape, jnp.float32),
            pltpu.VMEM(visc.shape, jnp.float32),
            pltpu.SemaphoreType.DMA((2,)),
        ],
        compiler_params=PACK,
        name="pack_faces",
    )(fields, visc)
    x_b, x_a, z_own, y_b, y_a = faces
    halo = [
        swap_b(x_b, "gx", sizes), swap_a(x_a, "gx", sizes), swap_a(z_own, "gz", sizes),
        swap_b(y_b, "gy", sizes), swap_a(y_a, "gy", sizes),
    ]

    own_counts = sizes["gy"] * CAP == SAMP
    counts = []
    if not own_counts:
        named = trainers.reshape(-1, 1) == jnp.arange(LANES, dtype=jnp.int32)[None, :]
        total = lax.psum(jnp.sum(named.astype(jnp.float32), axis=0, keepdims=True), "gy")
        counts = [jnp.broadcast_to(total, (ROWS, LANES))]
    sizes_of = [shape_of(*size, dtype=jnp.bfloat16) for size in ((CH, 28 * NF), (16, CH), (CH, 16))]
    partial, w_first, w_third, w_third_t, drawn = beside(
        interior_first, visc.size, sizes_of + [shape_of(ROWS, LANES, dtype=jnp.int32)],
        (samples, trainers), (fields, visc, conv_first, conv_third),
    )
    y_terms = pltpu.VMEM((2, NF, planes, lanes), jnp.float32)
    middle, x_b, x_a_low, x_a_high, z_later = pl.pallas_call(
        close_first,
        out_shape=[
            shape_of(*fields.shape),
            shape_of(NF * chunks + 2, ROWS, lanes),
            shape_of(NF * chunks // 2 + 1, ROWS, lanes),
            shape_of(NF * chunks // 2 + 1, ROWS, lanes),
            shape_of(NF * chunks // 2 + 2, ROWS, LANES),
        ],
        in_specs=[VMEM] * 9,
        out_specs=[VMEM] * 5,
        scratch_shapes=[y_terms],
        compiler_params=PARAMS,
        name="close_first",
    )(fields, visc, partial, z_own, *halo)
    later = [
        swap_b(x_b, "gx", sizes), swap_a(z_later, "gz", sizes),
        swap_a(x_a_low, "gx", sizes), swap_a(x_a_high, "gx", sizes),
    ]
    partial, rims, w_second_t = beside(
        interior_second, visc.size,
        [shape_of(2 * NF, ROWS, LANES), shape_of(27 * CH, CH, dtype=jnp.bfloat16)],
        (), (middle, visc, fields, *halo[3:], conv_second),
    )

    count = samples.shape[0]
    slot_total = sizes["gy"] * CAP
    tiles = -(-27 * CH // LANES) + 1
    parts = devices_all // CH
    inline = parts == 1 and slot_total <= 12
    out_shape = [shape_of(*fields.shape), shape_of(CH, tiles, LANES, dtype=jnp.bfloat16)]
    if not inline:
        out_shape.append(shape_of(devices_all, 1, LANES, dtype=jnp.bfloat16))
    kept, send, *slots = pl.pallas_call(
        functools.partial(second_step, sizes, inline),
        out_shape=out_shape,
        in_specs=[VMEM] * (21 + len(counts)),
        out_specs=[VMEM] * len(out_shape),
        scratch_shapes=[
            pltpu.VMEM((28 * NF, count * VOL), jnp.float32),
            pltpu.VMEM((27 * CH, count * VOL), jnp.bfloat16),
            pltpu.VMEM((CH, tiles, LANES), jnp.float32),
            y_terms,
        ],
        compiler_params=PARAMS,
        name="second_step",
    )(drawn, middle, visc, partial, rims, z_own, *halo, z_later, *later, *counts,
      w_first, conv_second, w_second_t, w_third, w_third_t)

    if not inline:
        send = jnp.concatenate([send.reshape(devices_all, tiles // parts, LANES), slots[0]], 1)
    arrived = lax.all_to_all(send, axes, split_axis=0, concat_axis=0, tiled=True)
    if inline:
        where = (27 * CH // LANES, 27 * CH % LANES + ROWS)
    else:
        where = (send.shape[1] - 1, 0)
    spread, own = pl.pallas_call(
        add_up,
        out_shape=[shape_of(*send.shape, dtype=jnp.bfloat16), shape_of(*send.shape[1:])],
        in_specs=[VMEM],
        out_specs=[VMEM] * 2,
        compiler_params=PARAMS,
        name="add_up",
    )(arrived)
    if not inline:
        spread = spread[:, :-1, :]
    gathered = lax.all_to_all(spread, axes, split_axis=0, concat_axis=0, tiled=True)
    first, second, third, block_losses, advanced = pl.pallas_call(
        functools.partial(unpack, where),
        out_shape=[
            shape_of(*conv_first.shape),
            shape_of(*conv_second.shape),
            shape_of(*conv_third.shape),
            shape_of(1, 1, 1, slot_total),
            shape_of(*fields.shape),
        ],
        in_specs=[VMEM, VMEM, ANY],
        out_specs=[VMEM] * 4 + [ANY],
        scratch_shapes=[pltpu.VMEM((CH, tiles, LANES), jnp.float32), pltpu.SemaphoreType.DMA],
        compiler_params=PARAMS,
        name="unpack",
    )(gathered.reshape(CH, tiles, LANES), own, kept)
    return advanced, block_losses, first, second, third


def solution(mesh):
    sizes = dict(mesh.shape)
    in_specs = (
        P(None, "gx", "gy", "gz"),
        P("gx", "gy", "gz"),
        P("gx", "gy", "gz", None),
        P("gx", "gy", "gz", None, None),
        P(),
        P(),
        P(),
    )
    out_specs = (P(None, "gx", "gy", "gz"), P("gx", "gy", "gz", None), P(), P(), P())
    return jax.shard_map(
        functools.partial(on_device, sizes), mesh=mesh, in_specs=in_specs, out_specs=out_specs,
        check_vma=False,
    )
```

```python
import functools

import jax
import jax.numpy as jnp
from jax import lax
from jax.experimental import pallas as pl
from jax.experimental.pallas import tpu as pltpu
from jax.sharding import PartitionSpec as P

BLK = 4
CAP = 2
SAMP = 8
Z_TILES = 2
NF = 4
VOL = BLK**3
TAPS = [(x, y, z) for x in (-1, 0, 1) for y in (-1, 0, 1) for z in (-1, 0, 1)]
LANES = 128
ROWS = 8
NOUT = 6
CH = 32

time_step = 0.25
buoyancy = 0.5

VMEM = pl.BlockSpec(memory_space=pltpu.VMEM)
SMEM = pl.BlockSpec(memory_space=pltpu.SMEM)
HBM = pl.BlockSpec(memory_space=pltpu.HBM)
ANY = pl.BlockSpec(memory_space=pl.ANY)
PARAMS = pltpu.CompilerParams(vmem_limit_bytes=24 * 1024 * 1024)
PACK = pltpu.CompilerParams(vmem_limit_bytes=54944 * 1024)
FULL = (((1,), (1,)), ((), ()))


def iota(shape, axis):
    return lax.broadcasted_iota(jnp.int32, shape, axis)


def odd(axis):
    return lax.axis_index(axis) % 2 == 1


def facing(axis, swap, first, last):
    return jnp.where(odd(axis), first, last) if swap == "a" else jnp.where(odd(axis), last, first)


def prev_next(axis, from_a, from_b):
    return jnp.where(odd(axis), from_a, from_b), jnp.where(odd(axis), from_b, from_a)


class Parts:
    def __init__(self, *parts):
        self.parts, self.tiles = parts, parts[0].shape[0]

    def at_tile(self, index):
        tile, rest = (index[0], index[1:]) if isinstance(index, tuple) else (index, ())
        return self.parts[tile // self.tiles], (tile % self.tiles,) + rest

    def __getitem__(self, index):
        part, place = self.at_tile(index)
        return part[place]

    def __setitem__(self, index, value):
        part, place = self.at_tile(index)
        part[place] = value


class Sides:
    def __init__(self, chunks, x_b, x_a, z_both, y_b=None, y_a=None):
        self.chunks = chunks
        self.x_a, self.x_b, self.y_a, self.y_b, self.z_both = x_a, x_b, y_a, y_b, z_both

    def along_x(self, f, c):
        tile = f * self.chunks + c
        return prev_next("gx", self.x_a[tile], self.x_b[tile])

    def along_y(self, f, depth=0):
        tile = depth * (NF + 1) + f
        return prev_next("gy", self.y_a[tile], self.y_b[tile])


def pair_of(f, c, planes, chunks):
    span = 2 * planes * chunks
    return f * span // LANES, f * span % LANES + 2 * planes * c


def add_pair(packed, tile, lane):
    moved = pltpu.roll(tile, lane + 1, 1)
    at = iota(tile.shape, 1)
    return jnp.where((at == lane) | (at == lane + 1), moved, packed)


def cut_x(f, array, x_b, x_a):
    planes, rows, _ = array.shape
    chunks = rows // ROWS
    for c in range(chunks):
        part = slice(ROWS * c, ROWS * c + ROWS)
        ends = array[0, part], array[planes - 1, part]
        x_b[f * chunks + c] = facing("gx", "b", *ends)
        x_a[f * chunks + c] = facing("gx", "a", *ends)


def pack_faces(fields_far, visc_far, x_b, x_a, z_both, y_b, y_a, fields, visc, sems):
    _, planes, rows, _ = fields.shape
    chunks = rows // ROWS
    copies = [
        pltpu.make_async_copy(fields_far, fields, sems.at[0]),
        pltpu.make_async_copy(visc_far, visc, sems.at[1]),
    ]
    for copy in copies:
        copy.start()
    arrays = [fields.at[f] for f in range(NF)] + [visc]
    packed = [jnp.zeros((ROWS, LANES), jnp.float32) for _ in range(z_both.shape[0])]
    for f, array in enumerate(arrays):
        if f == 0 or f == NF:
            copies[f // NF].wait()
        cut_x(f, array, x_b, x_a)
        for depth in range(2):
            ends = array[:, depth, :], array[:, rows - 1 - depth, :]
            y_b[depth * (NF + 1) + f] = facing("gy", "b", *ends)
            y_a[depth * (NF + 1) + f] = facing("gy", "a", *ends)
        for c in range(chunks):
            tile, lane = pair_of(f, c, planes, chunks)
            for x in range(planes):
                cells = array[x, ROWS * c : ROWS * c + ROWS]
                packed[tile] = add_pair(packed[tile], cells, lane + 2 * x)
    for tile, value in enumerate(packed):
        z_both[tile] = value


def flux(lower, upper, dimension):
    speed = 0.25 * (lower[dimension] + upper[dimension])
    mean_visc = 0.5 * (lower[NF] + upper[NF])
    return [speed * (a + b) - mean_visc * (b - a) for a, b in zip(lower[:NF], upper[:NF])]


def interior(fields, visc, partial):
    _, planes, rows, _ = fields.shape
    chunks = rows // ROWS
    end_row = iota((ROWS, LANES), 0) == ROWS - 1
    end_lane = iota((ROWS, LANES), 1) == LANES - 1
    every = range(NF + 1)

    def cell(f, x, part):
        return fields[f, x, part, :] if f < NF else visc[x, part, :]

    def plane(x, lowers):
        uppers = []
        last = x == planes - 1
        beyond = jnp.minimum(x + 1, planes - 1)
        behind = [jnp.zeros((ROWS, LANES), jnp.float32)] * NF
        for c in range(chunks):
            part = slice(ROWS * c, ROWS * c + ROWS)
            here = [cell(f, x, part) for f in every]
            after = [cell(f, beyond, part) for f in every]
            upper = flux(here, after, 0)
            upper = [jnp.where(last, 0.0, u) for u in upper]
            total = [b - a for a, b in zip(lowers[c], upper)]
            uppers.append(upper)
            above = [pltpu.roll(h, ROWS - 1, 0) for h in here]
            if c + 1 < chunks:
                first = slice(ROWS * c + ROWS, ROWS * c + ROWS + 1)
                above = [jnp.where(end_row, cell(f, x, first), above[f]) for f in every]
            upper = flux(here, above, 1)
            lower = [pltpu.roll(jnp.where(end_row, b, u), 1, 0) for b, u in zip(behind, upper)]
            if c + 1 == chunks:
                upper = [jnp.where(end_row, 0.0, u) for u in upper]
            behind = upper
            total = [t + (b - a) for t, a, b in zip(total, lower, upper)]
            right = [pltpu.roll(h, LANES - 1, 1) for h in here]
            upper = [jnp.where(end_lane, 0.0, u) for u in flux(here, right, 2)]
            lower = [pltpu.roll(u, 1, 1) for u in upper]
            total = [t + (b - a) for t, a, b in zip(total, lower, upper)]
            updated = [q - time_step * t for q, t in zip(here[:NF], total)]
            updated[2] = updated[2] + (time_step * buoyancy) * here[3]
            for f in range(NF):
                partial[f, x, part, :] = updated[f]
        return uppers

    zeros = [[jnp.zeros((ROWS, LANES), jnp.float32)] * NF for _ in range(chunks)]
    lax.fori_loop(0, planes, plane, zeros)


def rims_without_ends(fields, visc, sides, rims):
    rows = fields.shape[2]
    every = range(NF + 1)
    end_row = iota((ROWS, LANES), 0) == ROWS - 1
    end_lane = iota((ROWS, LANES), 1) == LANES - 1

    def own(row):
        return [fields[f, :, row, :] for f in range(NF)] + [visc[:, row, :]]

    for side in range(2):
        here = [sides.along_y(f)[side] for f in every]
        beyond = [sides.along_y(f, 1)[side] for f in every]
        below, above = (beyond, own(0)) if side == 0 else (own(rows - 1), beyond)
        total = [b - a for a, b in zip(flux(below, here, 1), flux(here, above, 1))]
        for dimension, axis, end in ((0, 0, end_row), (2, 1, end_lane)):
            after = [pltpu.roll(h, h.shape[axis] - 1, axis) for h in here]
            upper = [jnp.where(end, 0.0, u) for u in flux(here, after, dimension)]
            total = [t + (u - pltpu.roll(u, 1, axis)) for t, u in zip(total, upper)]
        updated = [q - time_step * t for q, t in zip(here[:NF], total)]
        updated[2] = updated[2] + (time_step * buoyancy) * here[3]
        for f in range(NF):
            rims[side * NF + f] = updated[f]


def rims_with_ends(rims, sides, later):
    row = iota((ROWS, LANES), 0)
    lane = iota((ROWS, LANES), 1)
    every = range(NF + 1)
    whole = []
    for side in range(2):
        here = [sides.along_y(f)[side] for f in every]
        tile = NF * later.chunks + side
        before, after = prev_next("gx", later.x_a[tile], later.x_b[tile])
        low = flux([before[f : f + 1] for f in every], [h[:1] for h in here], 0)
        high = flux([h[ROWS - 1 :] for h in here], [after[f : f + 1] for f in every], 0)
        columns = later.z_both[Z_TILES]
        left, right = [], []
        for f in every:
            both = pltpu.roll(columns, LANES - 1 - 2 * (side * (NF + 1) + f), 1)
            left.append(pltpu.roll(jnp.where(lane == LANES - 1, both, here[f]), 1, 1))
            right.append(pltpu.roll(jnp.where(lane == 0, both, here[f]), LANES - 1, 1))
        lower, upper = flux(left, here, 2), flux(here, right, 2)
        ends = []
        for f in range(NF):
            value = rims[side * NF + f]
            value = value + time_step * jnp.where(row == 0, low[f], 0.0)
            value = value - time_step * jnp.where(row == ROWS - 1, high[f], 0.0)
            value = value + time_step * jnp.where(lane == 0, lower[f], 0.0)
            ends.append(value - time_step * jnp.where(lane == LANES - 1, upper[f], 0.0))
        whole.append(ends)
    return whole


def interior_first(samples_far, trainers_far, fields, visc, conv_first, conv_third, partial, w_first,
                   w_third, w_third_t, drawn, samples, trainers, sems):
    copies = [
        pltpu.make_async_copy(samples_far, samples, sems.at[0]),
        pltpu.make_async_copy(trainers_far, trainers, sems.at[1]),
    ]
    for copy in copies:
        copy.start()
    interior(fields, visc, partial)
    ahead = conv_first.shape[1]
    w_first[:, :ahead] = conv_first[...]
    w_first[:, ahead:] = jnp.zeros((CH, w_first.shape[1] - ahead), jnp.bfloat16)
    third = conv_third[...].astype(jnp.float32)
    third = jnp.concatenate([third, jnp.zeros((w_third.shape[0] - NOUT, CH), jnp.float32)], 0)
    w_third[...] = third.astype(jnp.bfloat16)
    w_third_t[...] = third.T.astype(jnp.bfloat16)
    for copy in copies:
        copy.wait()
    at, row = iota((ROWS, LANES), 1), iota((ROWS, LANES), 0)
    table = jnp.zeros((ROWS, LANES), jnp.int32)
    for j in range(samples.shape[0]):
        table = jnp.where(at == j, jnp.where(row == 0, samples[j], trainers[j]), table)
    drawn[...] = table


def interior_second(middle, visc, fields, y_b, y_a, conv_second, partial, rims, w_second_t):
    interior(middle, visc, partial)
    rims_without_ends(fields, visc, Sides(0, None, None, None, y_b, y_a), rims)
    w_second_t[...] = conv_second[...].astype(jnp.float32).T.astype(jnp.bfloat16)


def z_terms(own, other, visc_own, visc_other):
    lane = iota((ROWS, LANES), 1)
    second = lane % 2 == 1
    span = LANES // 2

    def ends(mine, theirs):
        lower = jnp.where(second, pltpu.roll(theirs, 1, 1), mine)
        return lower, jnp.where(second, mine, pltpu.roll(theirs, LANES - 1, 1))

    def twice(tile):
        return jnp.where(lane < span, tile, pltpu.roll(tile, span, 1))

    pairs = [ends(a, b) for a, b in zip(own, other)]
    speed = [twice(end) for end in pairs[2 * span // LANES]]
    visc = [twice(end) for end in ends(visc_own, visc_other)]
    speed = 0.25 * (speed[0] + speed[1])
    mean_visc = 0.5 * (visc[0] + visc[1])
    through = [speed * (a + b) - mean_visc * (b - a) for a, b in pairs]
    return [jnp.where(second, time_step, -time_step) * t for t in through]


def close(fields, visc, partial, halo, visc_halo, y_faces, z_own, visc_z_own, y_terms, emit):
    _, planes, rows, _ = fields.shape
    chunks = rows // ROWS
    every = range(NF + 1)
    row = iota((ROWS, LANES), 0)
    lane_at = iota((ROWS, LANES), 1)
    ends = (lane_at == 0) | (lane_at == LANES - 1)

    def cell(f, *index):
        return fields[(f,) + index] if f < NF else visc[index]

    def sides(f):
        return halo if f < NF else visc_halo

    lower = flux(y_faces[0], [cell(f, slice(None), 0) for f in every], 1)
    upper = flux([cell(f, slice(None), rows - 1) for f in every], y_faces[1], 1)
    for f in range(NF):
        y_terms[0, f] = time_step * lower[f]
        y_terms[1, f] = -time_step * upper[f]
    tiles = 2 * NF * planes * chunks // LANES
    terms = z_terms([z_own[t] for t in range(tiles)], [halo.z_both[t] for t in range(tiles)],
                    visc_z_own[tiles], visc_halo.z_both[tiles])
    for c in range(chunks):
        part = slice(ROWS * c, ROWS * c + ROWS)
        before, after = zip(*[sides(f).along_x(f, c) for f in every])
        low = flux(before, [cell(f, 0, part) for f in every], 0)
        high = flux([cell(f, planes - 1, part) for f in every], after, 0)
        for x in range(planes):
            for f in range(NF):
                tile, lane = pair_of(f, c, planes, chunks)
                moved = pltpu.roll(terms[tile], LANES - 1 - lane - 2 * x, 1)
                value = partial[f, x, part, :] + jnp.where(ends, moved, 0.0)
                if x == 0:
                    value = value + time_step * low[f]
                if x == planes - 1:
                    value = value - time_step * high[f]
                if c == 0:
                    value = value + jnp.where(row == 0, y_terms[0, f, x : x + 1, :], 0.0)
                if c == chunks - 1:
                    value = value + jnp.where(row == ROWS - 1, y_terms[1, f, x : x + 1, :], 0.0)
                emit(f, x, c, value)


def close_first(fields, visc, partial, z_own, x_from_b, x_from_a, z_other, y_from_b, y_from_a,
                middle, x_b, x_a_low, x_a_mid, x_a_high, z_both, y_terms):
    x_a = Parts(x_a_low, x_a_mid, x_a_high)
    _, planes, rows, _ = fields.shape
    chunks = rows // ROWS
    halo = Sides(chunks, x_from_b, x_from_a, z_other, y_from_b, y_from_a)
    packed = [jnp.zeros((ROWS, LANES), jnp.float32) for _ in range(Z_TILES + 1)]
    y_faces = list(zip(*[halo.along_y(f) for f in range(NF + 1)]))

    def emit(f, x, c, tile):
        middle[f, x, ROWS * c : ROWS * c + ROWS, :] = tile
        at, lane = pair_of(f, c, planes, chunks)
        packed[at] = add_pair(packed[at], tile, lane + 2 * x)

    for side in range(2):
        for f in range(NF + 1):
            face = y_faces[side][f]
            packed[-1] = add_pair(packed[-1], face, 2 * (side * (NF + 1) + f))
            x_b[NF * chunks + side, f : f + 1, :] = facing("gx", "b", face[:1], face[planes - 1 :])
            x_a[NF * chunks + side, f : f + 1, :] = facing("gx", "a", face[:1], face[planes - 1 :])
    close(fields, visc, partial, halo, halo, y_faces, z_own, z_own, y_terms, emit)
    for at in range(z_both.shape[0]):
        z_both[at] = packed[at] if at <= Z_TILES else jnp.zeros((ROWS, LANES), jnp.float32)
    for f in range(NF):
        cut_x(f, middle.at[f], x_b, x_a)


def inside_masks():
    at = iota((1, LANES), 1) % VOL
    coords = (at // (BLK * BLK), at // BLK % BLK, at % BLK)
    along = []
    for coord in coords:
        along.append({
            -1: jnp.where(coord > 0, 1.0, 0.0),
            0: jnp.ones((1, LANES), jnp.float32),
            1: jnp.where(coord < BLK - 1, 1.0, 0.0),
        })
    return along


def move_of(tap):
    return tap[0] * BLK * BLK + tap[1] * BLK + tap[2]


def shifted(tile, tap, along):
    move = move_of(tap)
    if move == 0:
        return tile
    mask = along[0][tap[0]] * along[1][tap[1]] * along[2][tap[2]]
    return pltpu.roll(tile, (-move) % LANES, 1) * mask


def box(tile, along):
    for dimension, step in enumerate((BLK * BLK, BLK, 1)):
        ahead = pltpu.roll(tile, LANES - step, 1) * along[dimension][1]
        behind = pltpu.roll(tile, step, 1) * along[dimension][-1]
        tile = (behind + tile) + ahead
    return tile / 27.0


def sigmoid(values):
    return 1.0 / (1.0 + jnp.exp(-values))


PICKED = (0, 1, 2, 3, 0, 1, 2, 3, 0, 1, 2, 0, 0, 1, -1, -1, 0, 1, 2, 1, 2, 2, -1, -1)


def pick_rows():
    out, field = iota((32, NF * ROWS), 0), iota((32, NF * ROWS), 1) // ROWS
    table = jnp.zeros((32, NF * ROWS), jnp.float32)
    for i, f in enumerate(PICKED):
        table = jnp.where((out == i) & (field == f), 1.0, table)
    return table.astype(jnp.bfloat16)


def pick_blocks(advanced, samples, count):
    _, _, rows, lanes = advanced.shape
    along_y, along_z = rows // BLK, lanes // BLK
    row = iota((ROWS, LANES), 0)
    lane_at = iota((ROWS, LANES), 1)
    pick = pick_rows()
    out = []
    for j in range(0, count, 2):
        parts = [jnp.zeros((ROWS, LANES), jnp.float32) for _ in range(NF)]
        uppers = []
        for half in range(2):
            block = samples[j + half]
            block_x = block // (along_y * along_z)
            block_y = block // along_z % along_y
            block_z = block % along_z
            uppers.append(block_y % 2)
            start = pl.multiple_of(block_y // 2 * ROWS, ROWS)
            for x in range(BLK):
                turn = lax.rem(VOL * half + BLK * BLK * x - BLK * block_z + LANES, LANES)
                wanted = lane_at // BLK == (VOL * half + BLK * BLK * x) // BLK
                for f in range(NF):
                    tile = advanced[f, block_x * BLK + x, pl.ds(start, ROWS), :]
                    parts[f] = jnp.where(wanted, pltpu.roll(tile, turn, 1), parts[f])
        upper = jnp.where(lane_at < VOL, uppers[0], uppers[1])
        valid = row // BLK == upper
        for f in range(NF):
            for bit in (1, 2):
                moved = pltpu.roll(parts[f], BLK * bit, 1)
                parts[f] = jnp.where(row // bit % 2 == 1, moved, parts[f])
            parts[f] = jnp.where(valid, parts[f], 0.0)
        stacked = jnp.concatenate(parts, 0).astype(jnp.bfloat16)
        out.append(jnp.dot(pick, stacked, preferred_element_type=jnp.float32))
    return out


def closure(advanced, samples, trainers, loads, w_first, w_second, w_second_t, w_third,
            w_third_t, devices_all, stack_first, stack_mid, rows_out, send, slots, inline, place):
    count = len(samples)
    pairs = count // 2
    cols = [slice(LANES * m, LANES * m + LANES) for m in range(pairs)]
    along = inside_masks()
    lane_at = iota((ROWS, LANES), 1)
    row = iota((ROWS, LANES), 0)

    pos_x, pos_y, pos_z, count_y, count_z = place
    picked = pick_blocks(advanced, samples, count)
    values = [p[:ROWS] for p in picked]
    targets = []
    for p in picked:
        first, second = p[ROWS : 2 * ROWS], p[2 * ROWS : 3 * ROWS]
        targets.append(box(first * second, along) - box(first, along) * box(second, along))

    for m, tile in enumerate(values):
        for t in range(0, 28, 2):
            piece = shifted(tile, TAPS[t], along)
            later = shifted(tile, TAPS[t + 1], along) if t + 1 < 27 else jnp.zeros_like(tile)
            stack_first[BLK * t : BLK * t + ROWS, cols[m]] = jnp.where(row < NF, piece, later)
    stack_in = stack_first[...].astype(jnp.bfloat16)
    pre_first = jnp.dot(w_first, stack_in, preferred_element_type=jnp.float32)
    gate_first = sigmoid(pre_first)
    hidden_first = (pre_first * gate_first).astype(jnp.bfloat16).astype(jnp.float32)
    for m in range(pairs):
        tile = hidden_first[:, cols[m]]
        for k, tap in enumerate(TAPS):
            stack_mid[CH * k : CH * k + CH, cols[m]] = shifted(tile, tap, along).astype(jnp.bfloat16)
    pre_second = jnp.dot(w_second, stack_mid[...], preferred_element_type=jnp.float32)
    gate_second = sigmoid(pre_second)
    hidden_second = (pre_second * gate_second).astype(jnp.bfloat16)
    predicted = jnp.dot(w_third, hidden_second, preferred_element_type=jnp.float32)

    misfit = predicted[:ROWS] - jnp.concatenate(targets, 1)
    square = jnp.sum(misfit * misfit, axis=0, keepdims=True)
    sample_at = iota((ROWS, count * VOL), 1) // VOL
    mine = sample_at == iota((ROWS, count * VOL), 0)
    losses = jnp.sum(jnp.where(mine, square, 0.0), axis=1, keepdims=True) / (NOUT * VOL)
    if loads is None:
        load = jnp.full((ROWS, 1), float(count_y * CAP), jnp.float32)
    else:
        owner = jnp.zeros((ROWS, LANES), jnp.int32)
        for j in range(count):
            owner = jnp.where(row == j, trainers[j], owner)
        load = jnp.sum(jnp.where(lane_at == owner, loads, 0.0), axis=1, keepdims=True)
    share = 1.0 / (devices_all * jnp.maximum(load, 1.0))
    scale = share * (2.0 / (NOUT * VOL))
    scale_at = jnp.sum(jnp.where(mine, scale, 0.0), axis=0, keepdims=True)
    grad_pred = (misfit * scale_at).astype(jnp.bfloat16)
    grad_pred = jnp.concatenate([grad_pred, jnp.zeros_like(grad_pred)], 0)

    upper = jnp.dot(w_third_t, grad_pred, preferred_element_type=jnp.float32)
    slope = gate_second * (1.0 + pre_second * (1.0 - gate_second))
    grad_mid = (upper * slope).astype(jnp.bfloat16)
    grad_second = lax.dot_general(grad_mid, stack_mid[...], FULL, preferred_element_type=jnp.float32)
    third = jnp.concatenate([grad_pred, jnp.zeros((LANES - 16, count * VOL), jnp.bfloat16)], 0)
    grad_third = lax.dot_general(hidden_second, third, FULL, preferred_element_type=jnp.float32)

    spread = jnp.dot(w_second_t, grad_mid, preferred_element_type=jnp.float32)
    lower = []
    for m in range(pairs):
        terms = [
            shifted(spread[CH * k : CH * k + CH, cols[m]], tuple(-o for o in tap), along)
            for k, tap in enumerate(TAPS)
        ]
        lower.append(functools.reduce(jnp.add, terms))
    lower = jnp.concatenate(lower, 1)
    slope = gate_first * (1.0 + pre_first * (1.0 - gate_first))
    grad_entry = (lower * slope).astype(jnp.bfloat16)
    grad_first = lax.dot_general(grad_entry, stack_in, FULL, preferred_element_type=jnp.float32)

    whole = CH * 27 // LANES
    rest = CH * 27 - whole * LANES
    for t in range(whole):
        rows_out[:, t, :] = grad_second[:, LANES * t : LANES * t + LANES]
    mixed = jnp.concatenate([grad_second[:, whole * LANES :], jnp.zeros((CH, LANES - rest), jnp.float32)], 1)
    mixed = mixed + pltpu.roll(grad_third, rest, 1)
    tail = LANES - grad_first.shape[1]
    rows_out[:, whole + 1, :] = jnp.concatenate([grad_first, jnp.zeros((CH, tail), jnp.float32)], 1)

    offset = rest + ROWS if inline else 0
    height = CH if inline else slots.shape[0]
    slot_rows = iota((height, LANES), 0)
    slot_lanes = iota((height, LANES), 1)
    placed = jnp.zeros((height, LANES), jnp.float32)
    for j in range(count):
        name = trainers[j]
        rank = jnp.int32(0)
        for i in range(j):
            rank = rank + jnp.where(trainers[i] == name, 1, 0)
        target = (pos_x * count_y + name) * count_z + pos_z
        slot = offset + pos_y * CAP + rank
        hit = (slot_rows == target) & (slot_lanes == slot)
        placed = jnp.where(hit, losses[j : j + 1, :], placed)
    high = placed.astype(jnp.bfloat16).astype(jnp.float32)
    placed = high + pltpu.roll(placed - high, count_y * CAP, 1)
    if inline:
        mixed = mixed + placed
    else:
        slots[:, 0, :] = placed.astype(jnp.bfloat16)
    rows_out[:, whole, :] = mixed
    send[...] = rows_out[...].astype(jnp.bfloat16)


def second_step(sizes, inline, drawn, middle, visc, partial, rims, vz_own, vx_b, vx_a, vz_other, vy_b, vy_a,
                z_own, x_b, z_other, x_a_low, x_a_mid, x_a_high, *rest):
    loads, rest = (None, rest) if sizes["gy"] * CAP == SAMP else (rest[0][...], rest[1:])
    w_first, w_second, w_second_t, w_third, w_third_t, advanced_far, send = rest[:7]
    slots = None if inline else rest[7]
    stack_first, stack_mid, rows_out, y_terms, advanced, sem = rest[-6:]
    chunks = middle.shape[2] // ROWS
    halo = Sides(chunks, x_b, Parts(x_a_low, x_a_mid, x_a_high), z_other)
    visc_halo = Sides(chunks, vx_b, vx_a, vz_other, vy_b, vy_a)
    y_faces = rims_with_ends(rims, visc_halo, halo)
    y_faces = [face + [visc_halo.along_y(NF)[side]] for side, face in enumerate(y_faces)]
    count = stack_mid.shape[1] // VOL
    samples = [drawn[0, j] for j in range(count)]
    trainers = [drawn[1, j] for j in range(count)]

    def emit(f, x, c, tile):
        advanced[f, x, ROWS * c : ROWS * c + ROWS, :] = tile

    close(middle, visc, partial, halo, visc_halo, y_faces, z_own, vz_own, y_terms, emit)
    leaving = pltpu.make_async_copy(advanced, advanced_far, sem)
    leaving.start()
    place = (lax.axis_index("gx"), lax.axis_index("gy"), lax.axis_index("gz"), sizes["gy"], sizes["gz"])
    closure(advanced, samples, trainers, loads, w_first[...], w_second[...],
            w_second_t[...], w_third[...], w_third_t[...],
            float(sizes["gx"] * sizes["gy"] * sizes["gz"]), stack_first, stack_mid, rows_out,
            send, slots, inline, place)
    leaving.wait()


def add_up(arrived, spread, own):
    total = jnp.sum(arrived[...].astype(jnp.float32), axis=0)
    own[...] = total
    rounded = total.astype(jnp.bfloat16)
    for i in range(spread.shape[0]):
        spread[i] = rounded


def unpack(where, gathered, own, first, second, third, losses, wide):
    row, lane = where
    count = losses.shape[3]
    high = own[row : row + 1, lane : lane + count]
    losses[0, 0] = high + own[row : row + 1, lane + count : lane + 2 * count]
    wide[...] = gathered[...].astype(jnp.float32)
    whole = second.shape[1] // LANES
    rest = second.shape[1] - whole * LANES
    for t in range(whole):
        second[:, LANES * t : LANES * t + LANES] = wide[:, t, :]
    mixed = wide[:, whole, :]
    second[:, LANES * whole :] = mixed[:, :rest]
    third[...] = mixed[:, rest : rest + ROWS].T[:NOUT]
    first[...] = wide[:, whole + 1, :][:, : first.shape[1]]


def shape_of(*dims, dtype=jnp.float32):
    return jax.ShapeDtypeStruct(dims, dtype)


def swap_a(face, axis, sizes):
    return lax.ppermute(face, axis, [(i, i ^ 1) for i in range(sizes[axis])])


def swap_b(face, axis, sizes):
    count = sizes[axis]
    return lax.ppermute(face, axis, [(i, (i + (1 if i % 2 else -1)) % count) for i in range(count)])


def beside(kernel, cells, more_shapes, index, arrays):
    scratch = [pltpu.SMEM(array.shape, jnp.int32) for array in index]
    if index:
        scratch.append(pltpu.SemaphoreType.DMA((len(index),)))
    return pl.pallas_call(
        kernel,
        out_shape=[shape_of(*arrays[0].shape)] + more_shapes,
        in_specs=[ANY] * len(index) + [VMEM] * len(arrays),
        out_specs=[VMEM] * (1 + len(more_shapes)),
        scratch_shapes=scratch,
        compiler_params=PARAMS,
        cost_estimate=pl.CostEstimate(flops=120 * cells, bytes_accessed=36 * cells, transcendentals=0),
        name=kernel.__name__,
    )(*index, *arrays)


def on_device(sizes, fields, visc, samples, trainers, conv_first, conv_second, conv_third):
    _, planes, rows, lanes = fields.shape
    axes = ("gx", "gy", "gz")
    devices_all = sizes["gx"] * sizes["gy"] * sizes["gz"]
    chunks = rows // ROWS
    pairs = planes * chunks
    half = LANES // 2
    samples = samples.reshape(-1)
    trainers = trainers.reshape(-1)

    faces = pl.pallas_call(
        pack_faces,
        out_shape=[
            shape_of((NF + 1) * chunks, ROWS, lanes),
            shape_of((NF + 1) * chunks, ROWS, lanes),
            shape_of(-(-(NF + 1) * pairs // half), ROWS, LANES),
            shape_of(2 * (NF + 1), planes, lanes),
            shape_of(2 * (NF + 1), planes, lanes),
        ],
        in_specs=[HBM, HBM],
        out_specs=[VMEM] * 5,
        scratch_shapes=[
            pltpu.VMEM(fields.shape, jnp.float32),
            pltpu.VMEM(visc.shape, jnp.float32),
            pltpu.SemaphoreType.DMA((2,)),
        ],
        compiler_params=PACK,
        name="pack_faces",
    )(fields, visc)
    x_b, x_a, z_own, y_b, y_a = faces
    halo = [
        swap_b(x_b, "gx", sizes), swap_a(x_a, "gx", sizes), swap_a(z_own, "gz", sizes),
        swap_b(y_b, "gy", sizes), swap_a(y_a, "gy", sizes),
    ]

    own_counts = sizes["gy"] * CAP == SAMP
    counts = []
    if not own_counts:
        named = trainers.reshape(-1, 1) == jnp.arange(LANES, dtype=jnp.int32)[None, :]
        total = lax.psum(jnp.sum(named.astype(jnp.float32), axis=0, keepdims=True), "gy")
        counts = [jnp.broadcast_to(total, (ROWS, LANES))]
    sizes_of = [shape_of(*size, dtype=jnp.bfloat16) for size in ((CH, 28 * NF), (16, CH), (CH, 16))]
    partial, w_first, w_third, w_third_t, drawn = beside(
        interior_first, visc.size, sizes_of + [shape_of(ROWS, LANES, dtype=jnp.int32)],
        (samples, trainers), (fields, visc, conv_first, conv_third),
    )
    y_terms = pltpu.VMEM((2, NF, planes, lanes), jnp.float32)
    middle, x_b, x_a_low, x_a_mid, x_a_high, z_later = pl.pallas_call(
        close_first,
        out_shape=[
            shape_of(*fields.shape),
            shape_of(NF * chunks + 2, ROWS, lanes),
            *[shape_of((NF * chunks + 2) // 3, ROWS, lanes)] * 3,
            shape_of((NF * chunks + 2) // 3 + 1, ROWS, LANES),
        ],
        in_specs=[VMEM] * 9,
        out_specs=[VMEM] * 6,
        scratch_shapes=[y_terms],
        compiler_params=PARAMS,
        name="close_first",
    )(fields, visc, partial, z_own, *halo)
    later = [
        swap_b(x_b, "gx", sizes), swap_a(z_later, "gz", sizes),
        swap_a(x_a_low, "gx", sizes), swap_a(x_a_mid, "gx", sizes), swap_a(x_a_high, "gx", sizes),
    ]
    partial, rims, w_second_t = beside(
        interior_second, visc.size,
        [shape_of(2 * NF, ROWS, LANES), shape_of(27 * CH, CH, dtype=jnp.bfloat16)],
        (), (middle, visc, fields, *halo[3:], conv_second),
    )

    count = samples.shape[0]
    slot_total = sizes["gy"] * CAP
    tiles = -(-27 * CH // LANES) + 1
    parts = devices_all // CH
    inline = parts == 1 and slot_total <= 12
    out_shape = [shape_of(*fields.shape), shape_of(CH, tiles, LANES, dtype=jnp.bfloat16)]
    if not inline:
        out_shape.append(shape_of(devices_all, 1, LANES, dtype=jnp.bfloat16))
    advanced, send, *slots = pl.pallas_call(
        functools.partial(second_step, sizes, inline),
        out_shape=out_shape,
        in_specs=[VMEM] * (22 + len(counts)),
        out_specs=[ANY] + [VMEM] * (len(out_shape) - 1),
        scratch_shapes=[
            pltpu.VMEM((28 * NF, count * VOL), jnp.float32),
            pltpu.VMEM((27 * CH, count * VOL), jnp.bfloat16),
            pltpu.VMEM((CH, tiles, LANES), jnp.float32),
            y_terms,
            pltpu.VMEM(fields.shape, jnp.float32),
            pltpu.SemaphoreType.DMA,
        ],
        compiler_params=PARAMS,
        name="second_step",
    )(drawn, middle, visc, partial, rims, z_own, *halo, z_later, *later, *counts,
      w_first, conv_second, w_second_t, w_third, w_third_t)

    if not inline:
        send = jnp.concatenate([send.reshape(devices_all, tiles // parts, LANES), slots[0]], 1)
    arrived = lax.all_to_all(send, axes, split_axis=0, concat_axis=0, tiled=True)
    if inline:
        where = (27 * CH // LANES, 27 * CH % LANES + ROWS)
    else:
        where = (send.shape[1] - 1, 0)
    spread, own = pl.pallas_call(
        add_up,
        out_shape=[shape_of(*send.shape, dtype=jnp.bfloat16), shape_of(*send.shape[1:])],
        in_specs=[VMEM],
        out_specs=[VMEM] * 2,
        compiler_params=PARAMS,
        name="add_up",
    )(arrived)
    if not inline:
        spread = spread[:, :-1, :]
    gathered = lax.all_to_all(spread, axes, split_axis=0, concat_axis=0, tiled=True)
    first, second, third, block_losses = pl.pallas_call(
        functools.partial(unpack, where),
        out_shape=[
            shape_of(*conv_first.shape),
            shape_of(*conv_second.shape),
            shape_of(*conv_third.shape),
            shape_of(1, 1, 1, slot_total),
        ],
        in_specs=[VMEM] * 2,
        out_specs=[VMEM] * 4,
        scratch_shapes=[pltpu.VMEM((CH, tiles, LANES), jnp.float32)],
        compiler_params=PARAMS,
        name="unpack",
    )(gathered.reshape(CH, tiles, LANES), own)
    return advanced, block_losses, first, second, third


def solution(mesh):
    sizes = dict(mesh.shape)
    in_specs = (
        P(None, "gx", "gy", "gz"),
        P("gx", "gy", "gz"),
        P("gx", "gy", "gz", None),
        P("gx", "gy", "gz", None, None),
        P(),
        P(),
        P(),
    )
    out_specs = (P(None, "gx", "gy", "gz"), P("gx", "gy", "gz", None), P(), P(), P())
    return jax.shard_map(
        functools.partial(on_device, sizes), mesh=mesh, in_specs=in_specs, out_specs=out_specs,
        check_vma=False,
    )
```
